32 devices in a mesh: dp: 8 (over z, y), tensor: 4 (over x, core).
Axes of the slice: x: 2, y: 2, z: 4, core: 2. Of those that a mesh axis runs over, the one named last changes fastest.
Arguments:
- block_input: float32 [8192, 1536], P(('dp', 'tensor')), may hold values from -6 to 6
- cotangent: float32 [8192, 1536], P(('dp', 'tensor')), may hold values from -6 to 6
- norm_gain: float32 [1536], replicated, may hold values from 0.5 to 1.5
- gate_weight: float32 [1536, 3072], P('dp', 'tensor'), may hold values from -0.45927933 to 0.45927933
- input_weight: float32 [1536, 3072], P('dp', 'tensor'), may hold values from -0.15625 to 0.15625
- state_weight: float32 [1536, 256], P('dp'), may hold values from -0.15625 to 0.15625
- step_weight: float32 [1536, 48], P('dp', 'tensor'), may hold values from -0.15625 to 0.15625
- conv_input: float32 [4, 3072], P(None, 'tensor'), may hold values from -3 to 3
- conv_input_bias: float32 [3072], P('tensor'), may hold values from -0.5 to 0.5
- conv_state: float32 [4, 256], replicated, may hold values from -3 to 3
- conv_state_bias: float32 [256], replicated, may hold values from -0.5 to 0.5
- step_bias: float32 [48], P('tensor'), may hold values from -6 to -2
- decay_log: float32 [48], P('tensor'), may hold values from -3 to 1.5
- skip_scale: float32 [48], P('tensor'), may hold values from 0.5 to 2
- gate_gain: float32 [3072], P('tensor'), may hold values from 0.5 to 1.5
- out_weight: float32 [3072, 1536], P('tensor', 'dp'), may hold values from -0.109375 to 0.109375
Outputs:
- block_output: float32 [8192, 1536], P(('dp', 'tensor'))
- input_grad: float32 [8192, 1536], P(('dp', 'tensor'))
- norm_gain_grad: float32 [1536], replicated
- gate_weight_grad: float32 [1536, 3072], P('dp', 'tensor')
- input_weight_grad: float32 [1536, 3072], P('dp', 'tensor')
- state_weight_grad: float32 [1536, 256], P('dp')
- step_weight_grad: float32 [1536, 48], P('dp', 'tensor')
- conv_input_grad: float32 [4, 3072], P(None, 'tensor')
- conv_input_bias_grad: float32 [3072], P('tensor')
- conv_state_grad: float32 [4, 256], replicated
- conv_state_bias_grad: float32 [256], replicated
- step_bias_grad: float32 [48], P('tensor')
- decay_log_grad: float32 [48], P('tensor')
- skip_scale_grad: float32 [48], P('tensor')
- gate_gain_grad: float32 [3072], P('tensor')
- out_weight_grad: float32 [3072, 1536], P('tensor', 'dp')
The draws below stay inside these ranges and needn't reach their ends.
All inputs are finite; a program needn't handle non-finite values.
Results may differ from the reference program's by a relative error of at most 0.0013.
The reference program's roundings to bfloat16 on the way count: a program that leaves them out, or rounds other values in their place, can miss the bound.
Values may be sent and summed in bfloat16 or wider, within the bound.
No kernel may reach another device: no remote copies, remote signals or barrier semaphores. Data moves between devices by JAX's collectives and lax.ppermute only.
A program may use at most 128 MiB of HBM per device.

```python
import math
import jax
import jax.numpy as jnp
from jax import lax

D = 1536
HEADS = 48
HEAD_DIM = 64
STATE = 128
CONV = 4
BLOCK = 256
SEQ = 1024
TOK_DEV = 256
INNER = 3072
TOKENS = 8192
N_DP = 8
N_TENSOR = 4


def draw_gate_weight(key, part):
    key = jax.random.fold_in(key, 11)
    first_key, second_key = jax.random.split(key)
    column = jnp.arange(INNER, dtype=jnp.float32) / INNER
    base = jnp.clip(jax.random.normal(first_key, (D, INNER), jnp.float32), -4.0, 4.0)
    column_scale = 10.0 ** (0.5 * column) * jnp.exp(jax.random.uniform(second_key, (1, INNER), jnp.float32, -0.35, 0.35))
    return base * column_scale / math.sqrt(D)


def shard_levels(key, dims, cuts, smallest, high):
    level = 1.0
    for axis_at, shards_of in cuts:
        heights = jax.random.uniform(jax.random.fold_in(jax.random.fold_in(key, 6), axis_at), (shards_of,), jnp.float32, smallest / len(cuts), high / len(cuts))
        level = level * jnp.repeat(jnp.exp(heights), dims[axis_at] // shards_of).reshape((-1,) + (1,) * (len(dims) - 1 - axis_at))
    return level


def normal_values(rng, shape, width, reach, cuts=(), kind=jnp.bfloat16):
    factor_of = shard_levels(rng, shape, cuts, -0.22, 0.18) if cuts else 1.0
    values = jax.random.normal(rng, shape, jnp.float32) * width * factor_of
    return jnp.minimum(jnp.maximum(values, -reach), reach).astype(kind)


def setup_inputs(seed: int = 0) -> dict:
    streams_of = jax.random.split(jax.random.key(seed), 17)
    return {
        "block_input": normal_values(streams_of[0], (TOKENS, D), 1.0, 6.0, ((0, 32),), jnp.float32),
        "cotangent": normal_values(streams_of[1], (TOKENS, D), 1.0, 6.0, ((0, 32),), jnp.float32),
        "norm_gain": jnp.clip(1.0 + 0.1 * jax.random.normal(streams_of[2], (D,), jnp.float32), 0.5, 1.5),
        "gate_weight": draw_gate_weight(jax.random.fold_in(streams_of[16], 71), 0),
        "input_weight": normal_values(streams_of[4], (D, INNER), D ** -0.5, 0.15625, ((0, 8), (1, 4)), jnp.float32),
        "state_weight": normal_values(streams_of[5], (D, 2 * STATE), D ** -0.5, 0.15625, ((0, 8),), jnp.float32),
        "step_weight": normal_values(streams_of[6], (D, HEADS), D ** -0.5, 0.15625, ((0, 8), (1, 4)), jnp.float32),
        "conv_input": normal_values(streams_of[7], (CONV, INNER), CONV ** -0.5, 3.0, ((1, 4),), jnp.float32),
        "conv_input_bias": jnp.clip(jax.random.uniform(streams_of[8], (INNER,), jnp.float32, -0.5, 0.5) * shard_levels(streams_of[8], (INNER,), ((0, 4),), -0.4, 0.0), -0.5, 0.5),
        "conv_state": normal_values(streams_of[9], (CONV, 2 * STATE), CONV ** -0.5, 3.0, (), jnp.float32),
        "conv_state_bias": jnp.clip(jax.random.uniform(streams_of[10], (2 * STATE,), jnp.float32, -0.5, 0.5), -0.5, 0.5),
        "step_bias": jnp.clip(-6.0 + 4.0 * jax.random.uniform(streams_of[11], (HEADS,), jnp.float32) ** shard_levels(streams_of[11], (HEADS,), ((0, 4),), -0.2, 0.2), -6.0, -2.0),
        "decay_log": jnp.clip(-3.0 + 4.5 * jax.random.uniform(streams_of[12], (HEADS,), jnp.float32) ** shard_levels(streams_of[12], (HEADS,), ((0, 4),), -0.2, 0.2), -3.0, 1.5),
        "skip_scale": jnp.clip(0.5 + 1.5 * jax.random.uniform(streams_of[13], (HEADS,), jnp.float32) ** shard_levels(streams_of[13], (HEADS,), ((0, 4),), -0.2, 0.2), 0.5, 2.0),
        "gate_gain": jnp.clip(1.0 + 0.1 * jax.random.normal(streams_of[14], (INNER,), jnp.float32), 0.5, 1.5),
        "out_weight": normal_values(streams_of[15], (INNER, D), INNER ** -0.5, 0.109375, ((0, 4), (1, 8)), jnp.float32),
    }


epsilon = 1e-05
highest = lax.Precision.HIGHEST

@jax.custom_vjp
def low(v):
    return lax.optimization_barrier(v.astype(jnp.bfloat16)).astype(jnp.float32)

@jax.custom_vjp
def low_back(v):
    return v

def low_keep(v):
    return (low(v), None)

def low_pass(kept, grad):
    return (grad,)

def back_keep(v):
    return (v, None)

def back_low(kept, grad):
    return (low(grad),)
low.defvjp(low_keep, low_pass)
low_back.defvjp(back_keep, back_low)

def causal_conv(channel_rows, kernel, conv_bias, seq_count):
    row_count, channels = channel_rows.shape
    seq_len = row_count // seq_count
    tap_count = kernel.shape[0]
    shaped = channel_rows.reshape(seq_count, seq_len, channels)
    padded = jnp.pad(shaped, ((0, 0), (tap_count - 1, 0), (0, 0)))
    summed = jnp.zeros_like(shaped) + conv_bias
    for offset in range(tap_count):
        begin_at = tap_count - 1 - offset
        summed = summed + kernel[offset] * padded[:, begin_at:begin_at + seq_len]
    return summed.reshape(row_count, channels)

def scan_sequence(inputs, step_size, rates, write_vec, read_vec):
    seq_len, head_count, head_width = inputs.shape
    block_count = seq_len // BLOCK
    log_decay = (step_size * rates[None, :]).reshape(block_count, BLOCK, head_count)
    weighted = (inputs * step_size[:, :, None]).reshape(block_count, BLOCK, head_count, head_width)
    writes = write_vec.reshape(block_count, BLOCK, -1)
    reads = read_vec.reshape(block_count, BLOCK, -1)
    cumulative = jnp.cumsum(log_decay, axis=1)
    cum_heads = jnp.transpose(cumulative, (0, 2, 1))
    gaps = cum_heads[:, :, :, None] - cum_heads[:, :, None, :]
    position = jnp.arange(BLOCK)
    causal = position[:, None] >= position[None, :]
    within = jnp.where(causal, jnp.exp(jnp.where(causal, gaps, 0.0)), 0.0)
    intersection = jnp.einsum('kqn,ksn->kqs', reads, writes, precision=highest)
    mixing = within * intersection[:, None]
    local_out = jnp.einsum('khqs,kshp->kqhp', mixing, weighted, precision=highest)
    to_end = jnp.exp(cumulative[:, -1:, :] - cumulative)
    block_states = jnp.einsum('ksn,kshp->khpn', writes, weighted * to_end[..., None], precision=highest)
    block_decay = jnp.exp(cumulative[:, -1, :])

    def carry_step(state_in, step_pair):
        decay_now, fresh_state = step_pair
        return (decay_now[:, None, None] * state_in + fresh_state, state_in)
    zero_state = jnp.zeros((head_count, head_width, write_vec.shape[1]), jnp.float32)
    unused, entering = lax.scan(carry_step, zero_state, (block_decay, block_states))
    carried = jnp.einsum('kqn,khpn->kqhp', reads, entering, precision=highest) * jnp.exp(cumulative)[..., None]
    return (local_out + carried).reshape(seq_len, head_count, head_width)

def mixer(seq_count, gate_proj, input_proj, state_proj, step_proj, conv_input, conv_input_bias, conv_state, conv_state_bias, step_bias, decay_log, skip_scale):
    inputs = jax.nn.silu(causal_conv(input_proj, conv_input, conv_input_bias, seq_count))
    state_rows = jax.nn.silu(causal_conv(state_proj, conv_state, conv_state_bias, seq_count))
    write_vec = state_rows[:, :STATE]
    read_vec = state_rows[:, STATE:]
    step_size = jax.nn.softplus(step_proj + step_bias)
    rates = -jnp.exp(decay_log)
    row_count = input_proj.shape[0]
    head_count = step_bias.shape[0]
    seq_len = row_count // seq_count
    per_head = inputs.reshape(seq_count, seq_len, head_count, HEAD_DIM)

    def one_sequence(pieces):
        return scan_sequence(pieces[0], pieces[1], rates, pieces[2], pieces[3])
    scanned = lax.map(jax.checkpoint(one_sequence), (per_head, step_size.reshape(seq_count, seq_len, head_count), write_vec.reshape(seq_count, seq_len, STATE), read_vec.reshape(seq_count, seq_len, STATE)))
    mixed = scanned.reshape(row_count, head_count, HEAD_DIM) + skip_scale[:, None] * inputs.reshape(row_count, head_count, HEAD_DIM)
    return mixed.reshape(row_count, head_count * HEAD_DIM) * jax.nn.silu(gate_proj)

def block_forward(rows_in, norm_gain, gate_weight, input_weight, state_weight, step_weight, conv_input, conv_input_bias, conv_state, conv_state_bias, step_bias, decay_log, skip_scale, gate_gain, out_weight):
    row_scale = lax.rsqrt(lax.optimization_barrier(jnp.mean(rows_in * rows_in, axis=1, keepdims=True)) + epsilon)
    normed = low(rows_in * row_scale * norm_gain)
    gate_proj = low_back(jnp.dot(normed, low(gate_weight), precision=highest))
    input_proj = low_back(jnp.dot(normed, low(input_weight), precision=highest))
    state_proj = low_back(jnp.dot(normed, low(state_weight), precision=highest))
    step_proj = low_back(jnp.dot(normed, low(step_weight), precision=highest))
    seq_count = rows_in.shape[0] // SEQ
    gated_rows = mixer(seq_count, gate_proj, input_proj, state_proj, step_proj, conv_input, conv_input_bias, conv_state, conv_state_bias, step_bias, decay_log, skip_scale)
    gate_scale = lax.rsqrt(lax.optimization_barrier(jnp.mean(gated_rows * gated_rows, axis=1, keepdims=True)) + epsilon)
    gate_out = low(gated_rows * gate_scale * gate_gain)
    branch = low_back(jnp.dot(gate_out, low(out_weight), precision=highest))
    return rows_in + branch

def reference(block_input, cotangent, norm_gain, gate_weight, input_weight, state_weight, step_weight, conv_input, conv_input_bias, conv_state, conv_state_bias, step_bias, decay_log, skip_scale, gate_gain, out_weight):
    group_rows = TOK_DEV * N_TENSOR
    params = (norm_gain, gate_weight, input_weight, state_weight, step_weight, conv_input, conv_input_bias, conv_state, conv_state_bias, step_bias, decay_log, skip_scale, gate_gain, out_weight)

    def group_step(grad_sums, inputs_pair):
        rows_in, cot_rows = inputs_pair
        result, pullback = jax.vjp(block_forward, rows_in, *params)
        pulled = pullback(cot_rows)
        return (jax.tree.map(jnp.add, grad_sums, tuple(pulled[1:])), (result, pulled[0]))
    zero_grads = jax.tree.map(jnp.zeros_like, params)
    sums, outputs = lax.scan(group_step, zero_grads, (block_input.reshape(N_DP, group_rows, D), cotangent.reshape(N_DP, group_rows, D)))
    return (outputs[0].reshape(TOKENS, D), outputs[1].reshape(TOKENS, D), sums[0], sums[1], sums[2], sums[3], sums[4], sums[5], sums[6], sums[7], sums[8], sums[9], sums[10], sums[11], sums[12], sums[13])
```

```python
import jax
import jax.numpy as jnp
from jax import lax
from jax.experimental import pallas as pl
from jax.experimental.pallas import tpu as pltpu
from jax.sharding import PartitionSpec as P

HEAD_DIM = 64
STATE = 128
BLOCK = 256
SEQ = 1024
LANES = 128

epsilon = 1e-05
high = lax.Precision.HIGH
highest = lax.Precision.HIGHEST
f32 = jnp.float32
bf16 = jnp.bfloat16


def dot(left, right, dims, precision=None):
    return lax.dot_general(
        left, right, (dims, ((), ())), precision=precision, preferred_element_type=f32
    )


def sigmoid(v):
    return 1.0 / (1.0 + jnp.exp(-v))


def softplus(v):
    return jnp.maximum(v, 0.0) + jnp.log1p(jnp.exp(-jnp.abs(v)))


def iota(shape, axis):
    return lax.broadcasted_iota(jnp.int32, shape, axis)


def pair_columns(table, pair):
    lane = iota((table.shape[0], LANES), 1)
    return jnp.where(lane < HEAD_DIM, table[:, 2 * pair : 2 * pair + 1], table[:, 2 * pair + 1 : 2 * pair + 2])


def decay_tables(step_rows, step_bias, rates):
    step_size = softplus(step_rows + step_bias)
    earlier = (iota((BLOCK, BLOCK), 0) >= iota((BLOCK, BLOCK), 1)).astype(f32)
    cumulative = dot(earlier, step_size * rates, ((1,), (0,)), highest)
    return step_size, cumulative, jnp.exp(cumulative), jnp.exp(cumulative[BLOCK - 1 : BLOCK, :] - cumulative)


def state_decay(from_start, pair):
    last = from_start[BLOCK - 1 : BLOCK, :]
    row = iota((LANES, STATE), 0)
    return jnp.where(row < HEAD_DIM, last[:, 2 * pair : 2 * pair + 1], last[:, 2 * pair + 1 : 2 * pair + 2])


def shifted_conv(rows_ref, buffer, taps, conv_bias, first):
    @pl.when(first)
    def _():
        buffer[0:8, :] = jnp.zeros((8, buffer.shape[1]), f32)

    @pl.when(jnp.logical_not(first))
    def _():
        buffer[0:8, :] = buffer[BLOCK : BLOCK + 8, :]

    buffer[8 : BLOCK + 8, :] = rows_ref[...]
    total = conv_bias[...] + taps[0:1, :] * buffer[8 : BLOCK + 8, :]
    for tap in range(1, 4):
        total = total + taps[tap : tap + 1, :] * buffer[8 - tap : BLOCK + 8 - tap, :]
    return total


def scan_kernel(
    input_rows, state_rows, step_rows, conv_input, conv_input_bias, conv_state, conv_state_bias,
    step_bias, rates, skip, mixed, input_conv, state_conv, entering, input_buffer, state_buffer, carried,
):
    first = pl.program_id(0) == 0
    pairs = input_rows.shape[1] // LANES

    @pl.when(first)
    def _():
        carried[...] = jnp.zeros(carried.shape, f32)

    input_conv[...] = shifted_conv(input_rows, input_buffer, conv_input, conv_input_bias, first)
    state_pre = shifted_conv(state_rows, state_buffer, conv_state, conv_state_bias, first)
    state_conv[...] = state_pre
    state_act = state_pre * sigmoid(state_pre)
    writes, reads = state_act[:, :STATE], state_act[:, STATE:]
    meeting = dot(reads, writes, ((1,), (1,)), high)
    step_size, cumulative, from_start, to_end = decay_tables(step_rows[...], step_bias[...], rates[...])
    cumulative_t = cumulative.T
    causal = iota((BLOCK, BLOCK), 0) >= iota((BLOCK, BLOCK), 1)
    lane = iota((BLOCK, LANES), 1)
    for pair in range(pairs):
        columns = slice(pair * LANES, pair * LANES + LANES)
        pre = input_conv[:, columns]
        inputs = pre * sigmoid(pre)
        weighted = inputs * pair_columns(step_size, pair)
        state_in = carried[pair]
        entering[0, pair] = state_in
        out = dot(reads, state_in, ((1,), (1,)), high) * pair_columns(from_start, pair)
        for side in range(2):
            head = 2 * pair + side
            gap = cumulative[:, head : head + 1] - cumulative_t[head : head + 1, :]
            mixing = jnp.exp(jnp.where(causal, gap, -1e30)) * meeting
            mine = (lane < HEAD_DIM) if side == 0 else (lane >= HEAD_DIM)
            out = out + dot(mixing, jnp.where(mine, weighted, 0.0), ((1,), (0,)), high)
        fresh = dot(weighted * pair_columns(to_end, pair), writes, ((0,), (0,)), high)
        carried[pair] = state_decay(from_start, pair) * state_in + fresh
        mixed[:, columns] = out + skip[:, columns] * inputs


def scan_back_kernel(
    input_rows, state_rows, step_rows, input_conv, state_conv, mixed, entering, mixed_grad,
    conv_input, conv_state, step_bias, rates, skip, head_of,
    input_grad, state_grad, step_grad, input_sums, state_sums, step_sums,
    input_buffer, state_buffer, carried, later, gap_grad, out_products, in_products,
):
    first = pl.program_id(0) == 0
    pairs = input_rows.shape[1] // LANES

    @pl.when(first)
    def _():
        carried[...] = jnp.zeros(carried.shape, f32)
        later[...] = jnp.zeros(later.shape, f32)
        input_sums[...] = jnp.zeros(input_sums.shape, f32)
        state_sums[...] = jnp.zeros(state_sums.shape, f32)
        step_sums[...] = jnp.zeros(step_sums.shape, f32)
        input_buffer[BLOCK : BLOCK + 8, :] = jnp.zeros((8, input_buffer.shape[1]), f32)
        state_buffer[BLOCK : BLOCK + 8, :] = jnp.zeros((8, state_buffer.shape[1]), f32)

    @pl.when(jnp.logical_not(first))
    def _():
        input_buffer[BLOCK : BLOCK + 8, :] = input_buffer[0:8, :]
        state_buffer[BLOCK : BLOCK + 8, :] = state_buffer[0:8, :]

    state_pre = state_conv[...]
    state_sig = sigmoid(state_pre)
    state_act = state_pre * state_sig
    writes, reads = state_act[:, :STATE], state_act[:, STATE:]
    meeting_t = dot(writes, reads, ((1,), (1,)), high)
    step_size, cumulative, from_start, to_end = decay_tables(step_rows[...], step_bias[...], rates[...])
    cumulative_t = cumulative.T
    causal_t = iota((BLOCK, BLOCK), 0) <= iota((BLOCK, BLOCK), 1)
    lane = iota((BLOCK, LANES), 1)
    gap_grad[...] = jnp.zeros(gap_grad.shape, f32)
    writes_grad = jnp.zeros((BLOCK, STATE), f32)
    reads_grad = jnp.zeros((BLOCK, STATE), f32)
    for pair in range(pairs):
        columns = slice(pair * LANES, pair * LANES + LANES)
        pre = input_conv[:, columns]
        sig = sigmoid(pre)
        inputs = pre * sig
        step_pair = pair_columns(step_size, pair)
        weighted = inputs * step_pair
        out_grad = mixed_grad[:, columns]
        skip_product = out_grad * inputs
        input_sums[5:6, columns] += jnp.sum(skip_product, axis=0, keepdims=True)
        end_pair = pair_columns(to_end, pair)
        leaving_grad = carried[pair]
        weighted_grad = dot(writes, leaving_grad, ((1,), (1,)), high) * end_pair
        for side in range(2):
            head = 2 * pair + side
            gap = cumulative_t[head : head + 1, :] - cumulative[:, head : head + 1]
            within = jnp.exp(jnp.where(causal_t, gap, -1e30))
            mine = (lane < HEAD_DIM) if side == 0 else (lane >= HEAD_DIM)
            own_grad = jnp.where(mine, out_grad, 0.0)
            weighted_grad = weighted_grad + dot(within * meeting_t, own_grad, ((1,), (0,)), high)
            gap_grad[...] += within * dot(weighted, own_grad, ((1,), (1,)), high)
        start_grad = out_grad * pair_columns(from_start, pair)
        reads_grad = reads_grad + dot(start_grad, entering[0, pair], ((1,), (0,)), high)
        writes_grad = writes_grad + dot(weighted * end_pair, leaving_grad, ((1,), (0,)), high)
        carried[pair] = state_decay(from_start, pair) * leaving_grad + dot(start_grad, reads, ((0,), (0,)), high)
        out_products[:, columns] = out_grad * mixed[:, columns] - skip[:, columns] * skip_product
        in_products[:, columns] = inputs * weighted_grad
        inputs_grad = skip[:, columns] * out_grad + step_pair * weighted_grad
        input_buffer[0:BLOCK, columns] = inputs_grad * (sig * (1.0 + pre * (1.0 - sig)))
    reads_grad = reads_grad + dot(gap_grad[...], writes, ((0,), (0,)), high)
    writes_grad = writes_grad + dot(gap_grad[...], reads, ((1,), (0,)), high)
    state_slope = state_sig * (1.0 + state_pre * (1.0 - state_sig))
    state_buffer[0:BLOCK, 0:STATE] = writes_grad * state_slope[:, :STATE]
    state_buffer[0:BLOCK, STATE : 2 * STATE] = reads_grad * state_slope[:, STATE:]

    for buffer, rows, taps, sums, result in (
        (input_buffer, input_rows, conv_input, input_sums, input_grad),
        (state_buffer, state_rows, conv_state, state_sums, state_grad),
    ):
        raw = rows[...]
        total = jnp.zeros(raw.shape, f32)
        for tap in range(4):
            ahead = buffer[tap : tap + BLOCK, :]
            total = total + taps[tap : tap + 1, :] * ahead
            sums[tap : tap + 1, :] += jnp.sum(ahead * raw, axis=0, keepdims=True)
        sums[4:5, :] += jnp.sum(buffer[0:BLOCK, :], axis=0, keepdims=True)
        result[...] = total.astype(result.dtype)

    out_head = dot(out_products[...], head_of[...], ((1,), (0,)), high)
    in_head = dot(in_products[...], head_of[...], ((1,), (0,)), high)
    upper = (iota((BLOCK, BLOCK), 0) <= iota((BLOCK, BLOCK), 1)).astype(f32)
    decay_grad = dot(upper, out_head - step_size * in_head, ((1,), (0,)), highest) + later[0:1, :]
    later[0:1, :] = decay_grad[0:1, :]
    step_sig = sigmoid(step_rows[...] + step_bias[...])
    step_back = (rates[...] * decay_grad + in_head) * step_sig
    step_grad[...] = step_back.astype(step_grad.dtype)
    step_sums[0:1, :] += jnp.sum(step_back, axis=0, keepdims=True)
    step_sums[1:2, :] += jnp.sum(step_size * decay_grad, axis=0, keepdims=True)


def whole(array):
    zeros = (0,) * array.ndim
    return pl.BlockSpec(array.shape, lambda k: zeros)


params = pltpu.CompilerParams(dimension_semantics=("arbitrary",), vmem_limit_bytes=48 * 1024 * 1024)


def run_scan(input_rows, state_rows, step_rows, consts):
    rows, channels = input_rows.shape
    blocks, pairs = rows // BLOCK, channels // LANES

    def tokens(width):
        return pl.BlockSpec((BLOCK, width), lambda k: (k, 0))

    return pl.pallas_call(
        scan_kernel,
        grid=(blocks,),
        in_specs=[tokens(channels), tokens(2 * STATE), tokens(LANES)] + [whole(c) for c in consts],
        out_specs=[
            tokens(channels),
            tokens(channels),
            tokens(2 * STATE),
            pl.BlockSpec((1, pairs, LANES, STATE), lambda k: (k, 0, 0, 0)),
        ],
        out_shape=[
            jax.ShapeDtypeStruct((rows, channels), f32),
            jax.ShapeDtypeStruct((rows, channels), f32),
            jax.ShapeDtypeStruct((rows, 2 * STATE), f32),
            jax.ShapeDtypeStruct((blocks, pairs, LANES, STATE), f32),
        ],
        scratch_shapes=[
            pltpu.VMEM((BLOCK + 8, channels), f32),
            pltpu.VMEM((BLOCK + 8, 2 * STATE), f32),
            pltpu.VMEM((pairs, LANES, STATE), f32),
        ],
        compiler_params=params,
        name="scan",
    )(input_rows, state_rows, step_rows, *consts)


def run_scan_back(input_rows, state_rows, step_rows, input_conv, state_conv, mixed, entering, mixed_grad, consts):
    rows, channels = input_rows.shape
    blocks, pairs = rows // BLOCK, channels // LANES

    def tokens(width):
        return pl.BlockSpec((BLOCK, width), lambda k: (blocks - 1 - k, 0))

    def fixed(height, width):
        return pl.BlockSpec((height, width), lambda k: (0, 0))

    return pl.pallas_call(
        scan_back_kernel,
        grid=(blocks,),
        in_specs=[
            tokens(channels), tokens(2 * STATE), tokens(LANES), tokens(channels), tokens(2 * STATE), tokens(channels),
            pl.BlockSpec((1, pairs, LANES, STATE), lambda k: (blocks - 1 - k, 0, 0, 0)),
            tokens(channels),
        ] + [whole(c) for c in consts],
        out_specs=[
            tokens(channels), tokens(2 * STATE), tokens(LANES),
            fixed(8, channels), fixed(8, 2 * STATE), fixed(8, LANES),
        ],
        out_shape=[
            jax.ShapeDtypeStruct((rows, channels), bf16),
            jax.ShapeDtypeStruct((rows, 2 * STATE), f32),
            jax.ShapeDtypeStruct((rows, LANES), bf16),
            jax.ShapeDtypeStruct((8, channels), f32),
            jax.ShapeDtypeStruct((8, 2 * STATE), f32),
            jax.ShapeDtypeStruct((8, LANES), f32),
        ],
        scratch_shapes=[
            pltpu.VMEM((BLOCK + 8, channels), f32),
            pltpu.VMEM((BLOCK + 8, 2 * STATE), f32),
            pltpu.VMEM((pairs, LANES, STATE), f32),
            pltpu.VMEM((8, LANES), f32),
            pltpu.VMEM((BLOCK, BLOCK), f32),
            pltpu.VMEM((BLOCK, channels), f32),
            pltpu.VMEM((BLOCK, channels), f32),
        ],
        compiler_params=params,
        name="scan_back",
    )(input_rows, state_rows, step_rows, input_conv, state_conv, mixed, entering, mixed_grad, *consts)


def shards(
    block_input, cotangent, norm_gain, gate_weight, input_weight, state_weight, step_weight, conv_input,
    conv_input_bias, conv_state, conv_state_bias, step_bias, decay_log, skip_scale, gate_gain, out_weight,
):
    group_count = lax.axis_size("tensor")
    my_index = lax.axis_index("tensor")
    local_rows = block_input.shape[0]
    channels = gate_gain.shape[0]
    heads = step_bias.shape[0]
    inner_total = channels * group_count
    share = 2 * STATE // group_count

    row_scale = lax.rsqrt(jnp.mean(block_input * block_input, axis=1, keepdims=True) + epsilon)
    normed_local = (block_input * row_scale * norm_gain).astype(bf16)
    normed_all = lax.all_gather(normed_local, "tensor", axis=0, tiled=True)
    first_weight = jnp.concatenate(
        [input_weight, state_weight, jnp.pad(step_weight, ((0, 0), (0, LANES - heads)))], axis=1
    ).astype(bf16)
    first_full = lax.all_gather(first_weight, "dp", axis=0, tiled=True)
    gate_full = lax.all_gather(gate_weight.astype(bf16), "dp", axis=0, tiled=True)
    out_full = lax.all_gather(out_weight.T.astype(bf16), "dp", axis=0, tiled=True)
    cot_all = lax.all_gather(cotangent.astype(bf16), "tensor", axis=0, tiled=True)

    rows_dot = ((1,), (0,))
    first_proj = dot(normed_all, first_full, rows_dot)
    input_proj = first_proj[:, :channels]
    state_proj = first_proj[:, channels : channels + 2 * STATE]
    step_proj = first_proj[:, channels + 2 * STATE :]
    rates = -jnp.exp(decay_log)

    def per_head(vector):
        return jnp.pad(vector, (0, LANES - heads))[None, :]

    skip = jnp.repeat(skip_scale, HEAD_DIM)[None, :]
    head_of = (
        lax.broadcasted_iota(jnp.int32, (channels, LANES), 0) // HEAD_DIM
        == lax.broadcasted_iota(jnp.int32, (channels, LANES), 1)
    ).astype(f32)
    mixed, input_conv, state_conv, entering = run_scan(
        input_proj, state_proj, step_proj,
        (conv_input, conv_input_bias[None, :], conv_state, conv_state_bias[None, :],
         per_head(step_bias), per_head(rates), skip),
    )
    gate_proj = dot(normed_all, gate_full, rows_dot)
    gate_sig = jax.nn.sigmoid(gate_proj)
    gated = mixed * (gate_proj * gate_sig)
    gate_out_grad = dot(cot_all, out_full, rows_dot)
    sums = lax.psum(
        jnp.stack([jnp.sum(gated * gated, axis=1), jnp.sum(gate_out_grad * gate_gain * gated, axis=1)]), "tensor"
    )
    gate_scale = lax.rsqrt(sums[0] / inner_total + epsilon)[:, None]
    gate_out = (gated * gate_scale * gate_gain).astype(bf16)
    gate_gain_part = jnp.sum(gate_out_grad * gated * gate_scale, axis=0)
    gated_grad = gate_scale * (gate_out_grad * gate_gain) - gated * gate_scale**3 * (sums[1] / inner_total)[:, None]
    mixed_grad = gated_grad * (gate_proj * gate_sig)
    gate_grad = (gated_grad * mixed * (gate_sig * (1.0 + gate_proj * (1.0 - gate_sig)))).astype(bf16)

    out_part = dot(cot_all, gate_out, ((0,), (0,)))
    out_sum = lax.psum_scatter(out_part, "dp", scatter_dimension=0, tiled=True)
    gate_part = dot(normed_all, gate_grad, ((0,), (0,)))
    gate_sum = lax.psum_scatter(gate_part, "dp", scatter_dimension=0, tiled=True)
    branch = lax.psum_scatter(dot(gate_out, out_full, ((1,), (1,))), "tensor", scatter_dimension=0, tiled=True)
    block_output = block_input + branch

    input_back, state_back, step_back, input_sums, state_sums, step_sums = run_scan_back(
        input_proj, state_proj, step_proj, input_conv, state_conv, mixed, entering, mixed_grad,
        (conv_input, conv_state, per_head(step_bias), per_head(rates), skip, head_of),
    )
    state_own = lax.psum_scatter(state_back, "tensor", scatter_dimension=0, tiled=True).astype(bf16)
    state_all = lax.all_gather(state_own, "tensor", axis=0, tiled=True)
    state_share = lax.dynamic_slice_in_dim(state_all, my_index * share, share, 1)
    tail = jnp.concatenate(
        [state_share, step_back[:, :heads], jnp.zeros((state_all.shape[0], LANES - share - heads), bf16)], axis=1
    )
    first_part = dot(normed_all, jnp.concatenate([input_back, tail], axis=1), ((0,), (0,)))
    first_sum = lax.psum_scatter(first_part, "dp", scatter_dimension=0, tiled=True)
    step_full = first_full[:, channels + 2 * STATE :]
    normed_part = dot(gate_grad, gate_full, ((1,), (1,))) + dot(input_back, first_full[:, :channels], ((1,), (1,)))
    normed_part = normed_part + dot(step_back, step_full, ((1,), (1,)))
    normed_grad = lax.psum_scatter(normed_part, "tensor", scatter_dimension=0, tiled=True)
    normed_grad = normed_grad + dot(state_own, first_full[:, channels : channels + 2 * STATE], ((1,), (1,)))

    weighted_grad = normed_grad * norm_gain
    norm_gain_part = jnp.sum(normed_grad * block_input * row_scale, axis=0)
    input_grad = (
        cotangent
        + row_scale * weighted_grad
        - block_input * row_scale**3 * jnp.mean(weighted_grad * block_input, axis=1, keepdims=True)
    )
    state_weight_grad = lax.all_gather(first_sum[:, channels : channels + share], "tensor", axis=1, tiled=True)

    local = jnp.concatenate(
        [
            input_sums[:5].reshape(-1),
            gate_gain_part,
            jnp.sum(input_sums[5].reshape(heads, HEAD_DIM), axis=1),
            step_sums[0, :heads],
            step_sums[1, :heads] * rates,
        ]
    )
    local = lax.psum(local, "dp")
    shared = lax.psum(state_sums[:5], ("dp", "tensor"))
    norm_gain_grad = lax.psum(norm_gain_part, ("dp", "tensor"))
    at = 6 * channels
    return (
        block_output,
        input_grad,
        norm_gain_grad,
        gate_sum,
        first_sum[:, :channels],
        state_weight_grad,
        first_sum[:, channels + share : channels + share + heads],
        local[: 4 * channels].reshape(4, channels),
        local[4 * channels : 5 * channels],
        shared[:4],
        shared[4],
        local[at + heads : at + 2 * heads],
        local[at + 2 * heads : at + 3 * heads],
        local[at : at + heads],
        local[5 * channels : at],
        out_sum.T,
    )


def solution(mesh):
    rows = P(("dp", "tensor"), None)
    both = P("dp", "tensor")
    inner = P("tensor")
    return jax.shard_map(
        shards,
        mesh=mesh,
        in_specs=(
            rows, rows, P(), both, both, P("dp", None), both, P(None, "tensor"), inner, P(), P(), inner, inner,
            inner, inner, P("tensor", "dp"),
        ),
        out_specs=(
            rows, rows, P(), both, both, P("dp", None), both, P(None, "tensor"), inner, P(), P(), inner, inner,
            inner, inner, P("tensor", "dp"),
        ),
        check_vma=False,
    )
```

```python
import jax
import jax.numpy as jnp
from jax import lax
from jax.experimental import pallas as pl
from jax.experimental.pallas import tpu as pltpu
from jax.sharding import PartitionSpec as P

HEAD_DIM = 64
STATE = 128
BLOCK = 256
SEQ = 1024
LANES = 128

epsilon = 1e-05
high = lax.Precision.HIGH
highest = lax.Precision.HIGHEST
f32 = jnp.float32
bf16 = jnp.bfloat16


def dot(left, right, dims, precision=None):
    return lax.dot_general(
        left, right, (dims, ((), ())), precision=precision, preferred_element_type=f32
    )


def sigmoid(v):
    return 1.0 / (1.0 + jnp.exp(-v))


def softplus(v):
    return jnp.maximum(v, 0.0) + jnp.log1p(jnp.exp(-jnp.abs(v)))


def iota(shape, axis):
    return lax.broadcasted_iota(jnp.int32, shape, axis)


def pair_columns(table, pair):
    lane = iota((table.shape[0], LANES), 1)
    return jnp.where(lane < HEAD_DIM, table[:, 2 * pair : 2 * pair + 1], table[:, 2 * pair + 1 : 2 * pair + 2])


def decay_tables(step_rows, step_bias, rates):
    step_size = softplus(step_rows + step_bias)
    earlier = (iota((BLOCK, BLOCK), 0) >= iota((BLOCK, BLOCK), 1)).astype(f32)
    cumulative = dot(earlier, step_size * rates, ((1,), (0,)), highest)
    return step_size, cumulative, jnp.exp(cumulative), jnp.exp(cumulative[BLOCK - 1 : BLOCK, :] - cumulative)


def state_decay(from_start, pair):
    last = from_start[BLOCK - 1 : BLOCK, :]
    row = iota((LANES, STATE), 0)
    return jnp.where(row < HEAD_DIM, last[:, 2 * pair : 2 * pair + 1], last[:, 2 * pair + 1 : 2 * pair + 2])


def shifted_conv(rows_ref, buffer, taps, conv_bias, first):
    @pl.when(first)
    def _():
        buffer[0:8, :] = jnp.zeros((8, buffer.shape[1]), f32)

    @pl.when(jnp.logical_not(first))
    def _():
        buffer[0:8, :] = buffer[BLOCK : BLOCK + 8, :]

    buffer[8 : BLOCK + 8, :] = rows_ref[...]
    total = conv_bias[...] + taps[0:1, :] * buffer[8 : BLOCK + 8, :]
    for tap in range(1, 4):
        total = total + taps[tap : tap + 1, :] * buffer[8 - tap : BLOCK + 8 - tap, :]
    return total


def scan_kernel(
    input_rows, state_rows, step_rows, conv_input, conv_input_bias, conv_state, conv_state_bias,
    step_bias, rates, skip, mixed, input_conv, state_conv, entering, input_buffer, state_buffer, carried,
):
    first = pl.program_id(0) == 0
    pairs = input_rows.shape[1] // LANES

    @pl.when(first)
    def _():
        carried[...] = jnp.zeros(carried.shape, f32)

    input_conv[...] = shifted_conv(input_rows, input_buffer, conv_input, conv_input_bias, first)
    state_pre = shifted_conv(state_rows, state_buffer, conv_state, conv_state_bias, first)
    state_conv[...] = state_pre
    state_act = state_pre * sigmoid(state_pre)
    writes, reads = state_act[:, :STATE], state_act[:, STATE:]
    meeting = dot(reads, writes, ((1,), (1,)), high)
    step_size, cumulative, from_start, to_end = decay_tables(step_rows[...], step_bias[...], rates[...])
    cumulative_t = cumulative.T
    causal = iota((BLOCK, BLOCK), 0) >= iota((BLOCK, BLOCK), 1)
    lane = iota((BLOCK, LANES), 1)
    for pair in range(pairs):
        columns = slice(pair * LANES, pair * LANES + LANES)
        pre = input_conv[:, columns]
        inputs = pre * sigmoid(pre)
        weighted = inputs * pair_columns(step_size, pair)
        state_in = carried[pair]
        entering[0, pair] = state_in
        out = dot(reads, state_in, ((1,), (1,)), high) * pair_columns(from_start, pair)
        for side in range(2):
            head = 2 * pair + side
            gap = cumulative[:, head : head + 1] - cumulative_t[head : head + 1, :]
            mixing = jnp.exp(jnp.where(causal, gap, -1e30)) * meeting
            mine = (lane < HEAD_DIM) if side == 0 else (lane >= HEAD_DIM)
            out = out + dot(mixing, jnp.where(mine, weighted, 0.0), ((1,), (0,)), high)
        fresh = dot(weighted * pair_columns(to_end, pair), writes, ((0,), (0,)), high)
        carried[pair] = state_decay(from_start, pair) * state_in + fresh
        mixed[:, columns] = out + skip[:, columns] * inputs


def scan_back_kernel(
    input_rows, state_rows, step_rows, input_conv, state_conv, mixed, entering, mixed_grad,
    conv_input, conv_state, step_bias, rates, skip, head_of,
    input_grad, state_grad, step_grad, input_sums, state_sums, step_sums,
    input_buffer, state_buffer, carried, later, gap_grad, out_products, in_products,
):
    first = pl.program_id(0) == 0
    pairs = input_rows.shape[1] // LANES

    @pl.when(first)
    def _():
        carried[...] = jnp.zeros(carried.shape, f32)
        later[...] = jnp.zeros(later.shape, f32)
        input_sums[...] = jnp.zeros(input_sums.shape, f32)
        state_sums[...] = jnp.zeros(state_sums.shape, f32)
        step_sums[...] = jnp.zeros(step_sums.shape, f32)
        input_buffer[BLOCK : BLOCK + 8, :] = jnp.zeros((8, input_buffer.shape[1]), f32)
        state_buffer[BLOCK : BLOCK + 8, :] = jnp.zeros((8, state_buffer.shape[1]), f32)

    @pl.when(jnp.logical_not(first))
    def _():
        input_buffer[BLOCK : BLOCK + 8, :] = input_buffer[0:8, :]
        state_buffer[BLOCK : BLOCK + 8, :] = state_buffer[0:8, :]

    state_pre = state_conv[...]
    state_sig = sigmoid(state_pre)
    state_act = state_pre * state_sig
    writes, reads = state_act[:, :STATE], state_act[:, STATE:]
    meeting_t = dot(writes, reads, ((1,), (1,)), high)
    step_size, cumulative, from_start, to_end = decay_tables(step_rows[...], step_bias[...], rates[...])
    cumulative_t = cumulative.T
    causal_t = iota((BLOCK, BLOCK), 0) <= iota((BLOCK, BLOCK), 1)
    lane = iota((BLOCK, LANES), 1)
    gap_grad[...] = jnp.zeros(gap_grad.shape, f32)
    writes_grad = jnp.zeros((BLOCK, STATE), f32)
    reads_grad = jnp.zeros((BLOCK, STATE), f32)
    for pair in range(pairs):
        columns = slice(pair * LANES, pair * LANES + LANES)
        pre = input_conv[:, columns]
        sig = sigmoid(pre)
        inputs = pre * sig
        step_pair = pair_columns(step_size, pair)
        weighted = inputs * step_pair
        out_grad = mixed_grad[:, columns]
        skip_product = out_grad * inputs
        input_sums[5:6, columns] += jnp.sum(skip_product, axis=0, keepdims=True)
        end_pair = pair_columns(to_end, pair)
        leaving_grad = carried[pair]
        weighted_grad = dot(writes, leaving_grad, ((1,), (1,)), high) * end_pair
        for side in range(2):
            head = 2 * pair + side
            gap = cumulative_t[head : head + 1, :] - cumulative[:, head : head + 1]
            within = jnp.exp(jnp.where(causal_t, gap, -1e30))
            mine = (lane < HEAD_DIM) if side == 0 else (lane >= HEAD_DIM)
            own_grad = jnp.where(mine, out_grad, 0.0)
            weighted_grad = weighted_grad + dot(within * meeting_t, own_grad, ((1,), (0,)), high)
            gap_grad[...] += within * dot(weighted, own_grad, ((1,), (1,)), high)
        start_grad = out_grad * pair_columns(from_start, pair)
        reads_grad = reads_grad + dot(start_grad, entering[0, pair], ((1,), (0,)), high)
        writes_grad = writes_grad + dot(weighted * end_pair, leaving_grad, ((1,), (0,)), high)
        carried[pair] = state_decay(from_start, pair) * leaving_grad + dot(start_grad, reads, ((0,), (0,)), high)
        out_products[:, columns] = out_grad * mixed[:, columns] - skip[:, columns] * skip_product
        in_products[:, columns] = inputs * weighted_grad
        inputs_grad = skip[:, columns] * out_grad + step_pair * weighted_grad
        input_buffer[0:BLOCK, columns] = inputs_grad * (sig * (1.0 + pre * (1.0 - sig)))
    reads_grad = reads_grad + dot(gap_grad[...], writes, ((0,), (0,)), high)
    writes_grad = writes_grad + dot(gap_grad[...], reads, ((1,), (0,)), high)
    state_slope = state_sig * (1.0 + state_pre * (1.0 - state_sig))
    state_buffer[0:BLOCK, 0:STATE] = writes_grad * state_slope[:, :STATE]
    state_buffer[0:BLOCK, STATE : 2 * STATE] = reads_grad * state_slope[:, STATE:]

    for buffer, rows, taps, sums, result in (
        (input_buffer, input_rows, conv_input, input_sums, input_grad),
        (state_buffer, state_rows, conv_state, state_sums, state_grad),
    ):
        raw = rows[...]
        total = jnp.zeros(raw.shape, f32)
        for tap in range(4):
            ahead = buffer[tap : tap + BLOCK, :]
            total = total + taps[tap : tap + 1, :] * ahead
            sums[tap : tap + 1, :] += jnp.sum(ahead * raw, axis=0, keepdims=True)
        sums[4:5, :] += jnp.sum(buffer[0:BLOCK, :], axis=0, keepdims=True)
        result[...] = total.astype(result.dtype)

    out_head = dot(out_products[...], head_of[...], ((1,), (0,)), high)
    in_head = dot(in_products[...], head_of[...], ((1,), (0,)), high)
    upper = (iota((BLOCK, BLOCK), 0) <= iota((BLOCK, BLOCK), 1)).astype(f32)
    decay_grad = dot(upper, out_head - step_size * in_head, ((1,), (0,)), highest) + later[0:1, :]
    later[0:1, :] = decay_grad[0:1, :]
    step_sig = sigmoid(step_rows[...] + step_bias[...])
    step_back = (rates[...] * decay_grad + in_head) * step_sig
    step_grad[...] = step_back.astype(step_grad.dtype)
    step_sums[0:1, :] += jnp.sum(step_back, axis=0, keepdims=True)
    step_sums[1:2, :] += jnp.sum(step_size * decay_grad, axis=0, keepdims=True)


def whole(array):
    zeros = (0,) * array.ndim
    return pl.BlockSpec(array.shape, lambda k: zeros)


params = pltpu.CompilerParams(dimension_semantics=("arbitrary",), vmem_limit_bytes=48 * 1024 * 1024)


def run_scan(input_rows, state_rows, step_rows, consts):
    rows, channels = input_rows.shape
    blocks, pairs = rows // BLOCK, channels // LANES

    def tokens(width):
        return pl.BlockSpec((BLOCK, width), lambda k: (k, 0))

    return pl.pallas_call(
        scan_kernel,
        grid=(blocks,),
        in_specs=[tokens(channels), tokens(2 * STATE), tokens(LANES)] + [whole(c) for c in consts],
        out_specs=[
            tokens(channels),
            tokens(channels),
            tokens(2 * STATE),
            pl.BlockSpec((1, pairs, LANES, STATE), lambda k: (k, 0, 0, 0)),
        ],
        out_shape=[
            jax.ShapeDtypeStruct((rows, channels), f32),
            jax.ShapeDtypeStruct((rows, channels), f32),
            jax.ShapeDtypeStruct((rows, 2 * STATE), f32),
            jax.ShapeDtypeStruct((blocks, pairs, LANES, STATE), f32),
        ],
        scratch_shapes=[
            pltpu.VMEM((BLOCK + 8, channels), f32),
            pltpu.VMEM((BLOCK + 8, 2 * STATE), f32),
            pltpu.VMEM((pairs, LANES, STATE), f32),
        ],
        compiler_params=params,
        cost_estimate=pl.CostEstimate(flops=18 * 10**9, bytes_accessed=13 * 2**20, transcendentals=0),
        name="scan",
    )(input_rows, state_rows, step_rows, *consts)


def run_scan_back(input_rows, state_rows, step_rows, input_conv, state_conv, mixed, entering, mixed_grad, consts):
    rows, channels = input_rows.shape
    blocks, pairs = rows // BLOCK, channels // LANES

    def tokens(width):
        return pl.BlockSpec((BLOCK, width), lambda k: (blocks - 1 - k, 0))

    def fixed(height, width):
        return pl.BlockSpec((height, width), lambda k: (0, 0))

    return pl.pallas_call(
        scan_back_kernel,
        grid=(blocks,),
        in_specs=[
            tokens(channels), tokens(2 * STATE), tokens(LANES), tokens(channels), tokens(2 * STATE), tokens(channels),
            pl.BlockSpec((1, pairs, LANES, STATE), lambda k: (blocks - 1 - k, 0, 0, 0)),
            tokens(channels),
        ] + [whole(c) for c in consts],
        out_specs=[
            tokens(channels), tokens(2 * STATE), tokens(LANES),
            fixed(8, channels), fixed(8, 2 * STATE), fixed(8, LANES),
        ],
        out_shape=[
            jax.ShapeDtypeStruct((rows, channels), bf16),
            jax.ShapeDtypeStruct((rows, 2 * STATE), f32),
            jax.ShapeDtypeStruct((rows, LANES), bf16),
            jax.ShapeDtypeStruct((8, channels), f32),
            jax.ShapeDtypeStruct((8, 2 * STATE), f32),
            jax.ShapeDtypeStruct((8, LANES), f32),
        ],
        scratch_shapes=[
            pltpu.VMEM((BLOCK + 8, channels), f32),
            pltpu.VMEM((BLOCK + 8, 2 * STATE), f32),
            pltpu.VMEM((pairs, LANES, STATE), f32),
            pltpu.VMEM((8, LANES), f32),
            pltpu.VMEM((BLOCK, BLOCK), f32),
            pltpu.VMEM((BLOCK, channels), f32),
            pltpu.VMEM((BLOCK, channels), f32),
        ],
        compiler_params=params,
        cost_estimate=pl.CostEstimate(flops=30 * 10**9, bytes_accessed=20 * 2**20, transcendentals=0),
        name="scan_back",
    )(input_rows, state_rows, step_rows, input_conv, state_conv, mixed, entering, mixed_grad, *consts)


def cycle(count):
    return list(range(0, count, 2)) + list(range(count - 1, 0, -2))


class Ring:
    def __init__(self):
        self.count = lax.axis_size("dp")
        order = cycle(self.count)
        self.up = [(order[i], order[(i + 1) % self.count]) for i in range(self.count)]
        self.down = [(b, a) for a, b in self.up]
        me = lax.axis_index("dp")
        self.place = jnp.where(me % 2 == 0, me // 2, self.count - 1 - me // 2)

    def owner(self, offset):
        place = (self.place + offset + self.count) % self.count
        return jnp.where(place < self.count // 2, 2 * place, 2 * (self.count - 1 - place) + 1)

    def gather(self, shard):
        rows, width = shard.shape
        half, cut = self.count // 2, rows // 2
        whole_array = jnp.zeros((rows * self.count, width), shard.dtype)

        def put(array, piece, offset, skip=0):
            return lax.dynamic_update_slice(array, piece, (self.owner(offset) * rows + skip, 0))

        whole_array = put(whole_array, shard, 0)
        from_below = from_above = shard
        for step in range(1, half):
            from_below = lax.ppermute(from_below, "dp", self.up)
            from_above = lax.ppermute(from_above, "dp", self.down)
            whole_array = put(whole_array, from_below, -step)
            whole_array = put(whole_array, from_above, step)
        last_below = lax.ppermute(from_below[:cut], "dp", self.up)
        last_above = lax.ppermute(from_above[cut:], "dp", self.down)
        whole_array = put(whole_array, last_below, half)
        whole_array = put(whole_array, last_above, half, cut)
        return whole_array, from_below

    def scatter(self, part, scale):
        half = self.count // 2

        def send(rows, pairs):
            return lax.ppermute((rows * scale).astype(jnp.float16), "dp", pairs)

        far = part(self.owner(half))
        cut = far.shape[0] // 2
        up, down = send(far[:cut], self.up), send(far[cut:], self.down)
        back = 1.0 / scale
        for step in range(half - 1, -1, -1):
            above, below = part(self.owner(step)), None
            if step > 0:
                below = part(self.owner(-step))
            got_up, got_down = up.astype(f32) * back, down.astype(f32) * back
            if step == half - 1:
                got_up = jnp.pad(got_up, ((0, above.shape[0] - cut), (0, 0)))
                got_down = jnp.pad(got_down, ((cut, 0), (0, 0)))
            if step == 0:
                return above + got_up + got_down
            up, down = send(above + got_up, self.up), send(below + got_down, self.down)


def across(array, bit):
    count = lax.axis_size("tensor")
    return lax.ppermute(array, "tensor", [(i, i ^ bit) for i in range(count)])


def tensor_gather(shard, me):
    rows = shard.shape[0]
    far = across(shard, 2)
    whole_array = jnp.zeros((rows * lax.axis_size("tensor"), shard.shape[1]), shard.dtype)
    for bits, piece in ((0, shard), (1, across(shard, 1)), (2, far), (3, across(far, 1))):
        whole_array = lax.dynamic_update_slice(whole_array, piece, ((me ^ bits) * rows, 0))
    return whole_array


def tensor_scatter(part, me, narrow):
    for_far = across(part(me ^ 3), 1)
    for_me = across(part(me ^ 1), 1)
    far = part(me ^ 2) + for_far
    if narrow:
        top = jnp.maximum(jnp.max(jnp.abs(far), axis=1), 1e-30)
        got = across((far * (1.0 / top)[:, None]).astype(jnp.float16), 2)
        got = got.astype(f32) * across(top, 2)[:, None]
    else:
        got = across(far, 2)
    return part(me) + for_me + got


def largest(values, axis):
    count = lax.axis_size(axis)
    bit = 1
    while bit < count:
        values = jnp.maximum(values, lax.ppermute(values, axis, [(i, i ^ bit) for i in range(count)]))
        bit *= 2
    return values


def shards(
    block_input, cotangent, norm_gain, gate_weight, input_weight, state_weight, step_weight, conv_input,
    conv_input_bias, conv_state, conv_state_bias, step_bias, decay_log, skip_scale, gate_gain, out_weight,
):
    group_count = lax.axis_size("tensor")
    me = lax.axis_index("tensor")
    ring = Ring()
    local_rows = block_input.shape[0]
    weight_rows = gate_weight.shape[0]
    channels = gate_gain.shape[0]
    heads = step_bias.shape[0]
    inner_total = channels * group_count
    share = 2 * STATE // group_count
    tokens = local_rows * group_count
    fold = LANES // share
    rows_dot = ((1,), (0,))

    state_mine = lax.dynamic_slice_in_dim(state_weight, me * share, share, 1)
    first_weight = jnp.concatenate(
        [input_weight, state_mine, jnp.pad(step_weight, ((0, 0), (0, LANES - share - heads)))], axis=1
    ).astype(bf16)
    gate_low = gate_weight.astype(bf16)
    out_low = out_weight.T.astype(bf16)
    first_full, mark = ring.gather(first_weight)
    gate_low, mark = lax.optimization_barrier((gate_low, mark))
    gate_full, mark = ring.gather(gate_low)
    out_low, mark = lax.optimization_barrier((out_low, mark))
    out_full, mark = ring.gather(out_low)

    row_scale = lax.rsqrt(jnp.mean(block_input * block_input, axis=1, keepdims=True) + epsilon)
    normed_all = tensor_gather((block_input * row_scale * norm_gain).astype(bf16), me)
    cot_all = tensor_gather(cotangent.astype(bf16), me)
    normed_t = normed_all.T
    cot_t = cot_all.T
    token_bound = float(tokens * ring.count)

    input_full, tail_full = first_full[:, :channels], first_full[:, channels:]
    tail_proj = dot(normed_all, tail_full, rows_dot)
    step_proj = jnp.pad(tail_proj[:, share : share + heads], ((0, 0), (0, LANES - heads)))
    state_mine = tail_proj[:, :share].reshape(fold, tokens // fold, share).transpose(1, 0, 2).reshape(tokens // fold, LANES)
    far = across(state_mine, 2)
    same_x, same_core, diagonal = across(state_mine, 1), far, across(far, 1)
    right_core = me % 2 == 1
    near = (jnp.where(right_core, same_x, state_mine), jnp.where(right_core, state_mine, same_x))
    away = (jnp.where(right_core, diagonal, same_core), jnp.where(right_core, same_core, diagonal))
    right_chip = me // 2 == 1
    state_parts = [jnp.where(right_chip, away[i], near[i]) for i in range(2)]
    state_parts += [jnp.where(right_chip, near[i], away[i]) for i in range(2)]
    state_proj = jnp.concatenate(
        [jnp.concatenate([p[:, i * share : (i + 1) * share] for p in state_parts], axis=1) for i in range(fold)], axis=0
    )
    input_proj = dot(normed_all, input_full, rows_dot)
    rates = -jnp.exp(decay_log)

    def per_head(vector):
        return jnp.pad(vector, (0, LANES - heads))[None, :]

    skip = jnp.repeat(skip_scale, HEAD_DIM)[None, :]
    head_of = (
        lax.broadcasted_iota(jnp.int32, (channels, LANES), 0) // HEAD_DIM
        == lax.broadcasted_iota(jnp.int32, (channels, LANES), 1)
    ).astype(f32)
    mixed, input_conv, state_conv, entering = run_scan(
        input_proj, state_proj, step_proj,
        (conv_input, conv_input_bias[None, :], conv_state, conv_state_bias[None, :],
         per_head(step_bias), per_head(rates), skip),
    )
    gate_proj = dot(normed_all, gate_full, rows_dot)
    gate_sig = jax.nn.sigmoid(gate_proj)
    gated = mixed * (gate_proj * gate_sig)
    gate_out_grad = dot(cot_all, out_full, rows_dot)
    sums = jnp.stack([jnp.sum(gated * gated, axis=1), jnp.sum(gate_out_grad * gate_gain * gated, axis=1)])
    sums = sums + across(sums, 1) + (across(sums, 2) + across(sums, 3))
    gate_scale = lax.rsqrt(sums[0] / inner_total + epsilon)[:, None]
    gate_out = (gated * gate_scale * gate_gain).astype(bf16)
    gate_gain_part = jnp.sum(gate_out_grad * gated * gate_scale, axis=0)
    gated_grad = gate_scale * (gate_out_grad * gate_gain) - gated * gate_scale**3 * (sums[1] / inner_total)[:, None]
    mixed_grad = gated_grad * (gate_proj * gate_sig)
    gate_grad = (gated_grad * mixed * (gate_sig * (1.0 + gate_proj * (1.0 - gate_sig)))).astype(bf16)

    def bound(left, right):
        tops = jnp.stack([jnp.max(jnp.abs(left)).astype(f32), jnp.max(jnp.abs(right)).astype(f32)])
        tops = largest(jnp.broadcast_to(tops[:, None], (2, LANES)), "dp")[:, 0]
        return 32768.0 / jnp.maximum(token_bound * tops[0] * tops[1], 1e-30)

    def chunk(array_t, index):
        return lax.dynamic_slice_in_dim(array_t, index * weight_rows, weight_rows, 0)

    out_sum = ring.scatter(lambda i: dot(chunk(cot_t, i), gate_out, rows_dot), bound(cot_all, gate_out))
    gate_sum = ring.scatter(lambda i: dot(chunk(normed_t, i), gate_grad, rows_dot), bound(normed_all, gate_grad))

    def token_rows(array, index):
        return lax.dynamic_slice_in_dim(array, index * local_rows, local_rows, 0)

    branch = tensor_scatter(lambda i: dot(token_rows(gate_out, i), out_full, ((1,), (1,))), me, True)
    block_output = block_input + branch

    input_back, state_back, step_back, input_sums, state_sums, step_sums = run_scan_back(
        input_proj, state_proj, step_proj, input_conv, state_conv, mixed, entering, mixed_grad,
        (conv_input, conv_state, per_head(step_bias), per_head(rates), skip, head_of),
    )

    def state_columns(index):
        mine = lax.dynamic_slice_in_dim(state_back, index * share, share, 1)
        return jnp.concatenate([mine[i * (tokens // fold) : (i + 1) * (tokens // fold)] for i in range(fold)], axis=1)

    state_share = tensor_scatter(state_columns, me, False).astype(bf16)
    state_share = jnp.concatenate([state_share[:, i * share : (i + 1) * share] for i in range(fold)], axis=0)
    tail = jnp.concatenate(
        [state_share, step_back[:, :heads], jnp.zeros((tokens, LANES - share - heads), bf16)], axis=1
    )
    input_sum = ring.scatter(lambda i: dot(chunk(normed_t, i), input_back, rows_dot), bound(normed_all, input_back))
    tail_sum = ring.scatter(lambda i: dot(chunk(normed_t, i), tail, rows_dot), bound(normed_all, tail))

    def normed_rows(index):
        part = dot(token_rows(gate_grad, index), gate_full, ((1,), (1,)))
        part = part + dot(token_rows(input_back, index), input_full, ((1,), (1,)))
        return part + dot(token_rows(tail, index), tail_full, ((1,), (1,)))

    normed_grad = tensor_scatter(normed_rows, me, True)

    weighted_grad = normed_grad * norm_gain
    norm_gain_part = jnp.sum(normed_grad * block_input * row_scale, axis=0)
    input_grad = (
        cotangent
        + row_scale * weighted_grad
        - block_input * row_scale**3 * jnp.mean(weighted_grad * block_input, axis=1, keepdims=True)
    )
    state_weight_grad = lax.all_gather(tail_sum[:, :share], "tensor", axis=1, tiled=True)

    local = jnp.concatenate(
        [
            input_sums[:5].reshape(-1),
            gate_gain_part,
            jnp.sum(input_sums[5].reshape(heads, HEAD_DIM), axis=1),
            step_sums[0, :heads],
            step_sums[1, :heads] * rates,
        ]
    )
    local = lax.psum(local, "dp")
    shared = lax.psum(state_sums[:5], ("dp", "tensor"))
    norm_gain_grad = lax.psum(norm_gain_part, ("dp", "tensor"))
    at = 6 * channels
    return (
        block_output,
        input_grad,
        norm_gain_grad,
        gate_sum,
        input_sum,
        state_weight_grad,
        tail_sum[:, share : share + heads],
        local[: 4 * channels].reshape(4, channels),
        local[4 * channels : 5 * channels],
        shared[:4],
        shared[4],
        local[at + heads : at + 2 * heads],
        local[at + 2 * heads : at + 3 * heads],
        local[at : at + heads],
        local[5 * channels : at],
        out_sum.T,
    )


def solution(mesh):
    rows = P(("dp", "tensor"), None)
    both = P("dp", "tensor")
    inner = P("tensor")
    return jax.shard_map(
        shards,
        mesh=mesh,
        in_specs=(
            rows, rows, P(), both, both, P("dp", None), both, P(None, "tensor"), inner, P(), P(), inner, inner,
            inner, inner, P("tensor", "dp"),
        ),
        out_specs=(
            rows, rows, P(), both, both, P("dp", None), both, P(None, "tensor"), inner, P(), P(), inner, inner,
            inner, inner, P("tensor", "dp"),
        ),
        check_vma=False,
    )
```

```python
import jax
import jax.numpy as jnp
from jax import lax
from jax.experimental import pallas as pl
from jax.experimental.pallas import tpu as pltpu
from jax.sharding import PartitionSpec as P

HEAD_DIM = 64
STATE = 128
BLOCK = 256
SEQ = 1024
LANES = 128

epsilon = 1e-05
high = lax.Precision.HIGH
highest = lax.Precision.HIGHEST
f32 = jnp.float32
bf16 = jnp.bfloat16


def dot(left, right, dims, precision=None):
    return lax.dot_general(
        left, right, (dims, ((), ())), precision=precision, preferred_element_type=f32
    )


def sigmoid(v):
    return 1.0 / (1.0 + jnp.exp(-v))


def softplus(v):
    return jnp.maximum(v, 0.0) + jnp.log1p(jnp.exp(-jnp.abs(v)))


def iota(shape, axis):
    return lax.broadcasted_iota(jnp.int32, shape, axis)


def pair_columns(table, pair):
    lane = iota((table.shape[0], LANES), 1)
    return jnp.where(lane < HEAD_DIM, table[:, 2 * pair : 2 * pair + 1], table[:, 2 * pair + 1 : 2 * pair + 2])


def decay_tables(step_rows, step_bias, rates):
    step_size = softplus(step_rows + step_bias)
    earlier = (iota((BLOCK, BLOCK), 0) >= iota((BLOCK, BLOCK), 1)).astype(f32)
    cumulative = dot(earlier, step_size * rates, ((1,), (0,)), highest)
    return step_size, cumulative, jnp.exp(cumulative), jnp.exp(cumulative[BLOCK - 1 : BLOCK, :] - cumulative)


def state_decay(from_start, pair):
    last = from_start[BLOCK - 1 : BLOCK, :]
    row = iota((LANES, STATE), 0)
    return jnp.where(row < HEAD_DIM, last[:, 2 * pair : 2 * pair + 1], last[:, 2 * pair + 1 : 2 * pair + 2])


def shifted_conv(rows_ref, before, buffer, taps, conv_bias, first):
    @pl.when(first)
    def _():
        buffer[0:8, :] = before[...]

    @pl.when(jnp.logical_not(first))
    def _():
        buffer[0:8, :] = buffer[BLOCK : BLOCK + 8, :]

    buffer[8 : BLOCK + 8, :] = rows_ref[...]
    total = conv_bias[...] + taps[0:1, :] * buffer[8 : BLOCK + 8, :]
    for tap in range(1, 4):
        total = total + taps[tap : tap + 1, :] * buffer[8 - tap : BLOCK + 8 - tap, :]
    return total


def scan_kernel(
    input_rows, state_rows, step_rows, input_before, state_before, state_entering,
    conv_input, conv_input_bias, conv_state, conv_state_bias, step_bias, rates, skip,
    mixed, input_conv, state_conv, entering, carried, input_buffer, state_buffer,
):
    first = pl.program_id(0) == 0
    pairs = input_rows.shape[1] // LANES

    @pl.when(first)
    def _():
        carried[...] = state_entering[...]

    input_conv[...] = shifted_conv(input_rows, input_before, input_buffer, conv_input, conv_input_bias, first)
    state_pre = shifted_conv(state_rows, state_before, state_buffer, conv_state, conv_state_bias, first)
    state_conv[...] = state_pre
    state_act = state_pre * sigmoid(state_pre)
    writes, reads = state_act[:, :STATE], state_act[:, STATE:]
    meeting = dot(reads, writes, ((1,), (1,)), high)
    step_size, cumulative, from_start, to_end = decay_tables(step_rows[...], step_bias[...], rates[...])
    cumulative_t = cumulative.T
    causal = iota((BLOCK, BLOCK), 0) >= iota((BLOCK, BLOCK), 1)
    lane = iota((BLOCK, LANES), 1)
    for pair in range(pairs):
        columns = slice(pair * LANES, pair * LANES + LANES)
        pre = input_conv[:, columns]
        inputs = pre * sigmoid(pre)
        weighted = inputs * pair_columns(step_size, pair)
        state_in = carried[pair]
        entering[0, pair] = state_in
        out = dot(reads, state_in, ((1,), (1,)), high) * pair_columns(from_start, pair)
        for side in range(2):
            head = 2 * pair + side
            gap = cumulative[:, head : head + 1] - cumulative_t[head : head + 1, :]
            mixing = jnp.exp(jnp.where(causal, gap, -1e30)) * meeting
            mine = (lane < HEAD_DIM) if side == 0 else (lane >= HEAD_DIM)
            out = out + dot(mixing, jnp.where(mine, weighted, 0.0), ((1,), (0,)), high)
        fresh = dot(weighted * pair_columns(to_end, pair), writes, ((0,), (0,)), high)
        carried[pair] = state_decay(from_start, pair) * state_in + fresh
        mixed[:, columns] = out + skip[:, columns] * inputs


def scan_back_kernel(
    input_rows, state_rows, step_rows, input_conv, state_conv, mixed, entering, mixed_grad,
    input_after, state_after, state_leaving, decay_after,
    conv_input, conv_state, step_bias, rates, skip, head_of,
    input_grad, state_grad, step_grad, input_sums, state_sums, step_sums, input_first, state_first, carried, later,
    input_buffer, state_buffer, gap_grad, out_products, in_products,
):
    first = pl.program_id(0) == 0
    pairs = input_rows.shape[1] // LANES

    @pl.when(first)
    def _():
        carried[...] = state_leaving[...]
        later[...] = decay_after[...]
        input_sums[...] = jnp.zeros(input_sums.shape, f32)
        state_sums[...] = jnp.zeros(state_sums.shape, f32)
        step_sums[...] = jnp.zeros(step_sums.shape, f32)
        input_buffer[BLOCK : BLOCK + 8, :] = input_after[...]
        state_buffer[BLOCK : BLOCK + 8, :] = state_after[...]

    @pl.when(jnp.logical_not(first))
    def _():
        input_buffer[BLOCK : BLOCK + 8, :] = input_buffer[0:8, :]
        state_buffer[BLOCK : BLOCK + 8, :] = state_buffer[0:8, :]

    state_pre = state_conv[...]
    state_sig = sigmoid(state_pre)
    state_act = state_pre * state_sig
    writes, reads = state_act[:, :STATE], state_act[:, STATE:]
    meeting_t = dot(writes, reads, ((1,), (1,)), high)
    step_size, cumulative, from_start, to_end = decay_tables(step_rows[...], step_bias[...], rates[...])
    cumulative_t = cumulative.T
    causal_t = iota((BLOCK, BLOCK), 0) <= iota((BLOCK, BLOCK), 1)
    lane = iota((BLOCK, LANES), 1)
    gap_grad[...] = jnp.zeros(gap_grad.shape, f32)
    writes_grad = jnp.zeros((BLOCK, STATE), f32)
    reads_grad = jnp.zeros((BLOCK, STATE), f32)
    for pair in range(pairs):
        columns = slice(pair * LANES, pair * LANES + LANES)
        pre = input_conv[:, columns]
        sig = sigmoid(pre)
        inputs = pre * sig
        step_pair = pair_columns(step_size, pair)
        weighted = inputs * step_pair
        out_grad = mixed_grad[:, columns]
        skip_product = out_grad * inputs
        input_sums[5:6, columns] += jnp.sum(skip_product, axis=0, keepdims=True)
        end_pair = pair_columns(to_end, pair)
        leaving_grad = carried[pair]
        weighted_grad = dot(writes, leaving_grad, ((1,), (1,)), high) * end_pair
        for side in range(2):
            head = 2 * pair + side
            gap = cumulative_t[head : head + 1, :] - cumulative[:, head : head + 1]
            within = jnp.exp(jnp.where(causal_t, gap, -1e30))
            mine = (lane < HEAD_DIM) if side == 0 else (lane >= HEAD_DIM)
            own_grad = jnp.where(mine, out_grad, 0.0)
            weighted_grad = weighted_grad + dot(within * meeting_t, own_grad, ((1,), (0,)), high)
            gap_grad[...] += within * dot(weighted, own_grad, ((1,), (1,)), high)
        start_grad = out_grad * pair_columns(from_start, pair)
        reads_grad = reads_grad + dot(start_grad, entering[0, pair], ((1,), (0,)), high)
        writes_grad = writes_grad + dot(weighted * end_pair, leaving_grad, ((1,), (0,)), high)
        carried[pair] = state_decay(from_start, pair) * leaving_grad + dot(start_grad, reads, ((0,), (0,)), high)
        out_products[:, columns] = out_grad * mixed[:, columns] - skip[:, columns] * skip_product
        in_products[:, columns] = inputs * weighted_grad
        inputs_grad = skip[:, columns] * out_grad + step_pair * weighted_grad
        input_buffer[0:BLOCK, columns] = inputs_grad * (sig * (1.0 + pre * (1.0 - sig)))
    reads_grad = reads_grad + dot(gap_grad[...], writes, ((0,), (0,)), high)
    writes_grad = writes_grad + dot(gap_grad[...], reads, ((1,), (0,)), high)
    state_slope = state_sig * (1.0 + state_pre * (1.0 - state_sig))
    state_buffer[0:BLOCK, 0:STATE] = writes_grad * state_slope[:, :STATE]
    state_buffer[0:BLOCK, STATE : 2 * STATE] = reads_grad * state_slope[:, STATE:]

    for buffer, rows, taps, sums, result in (
        (input_buffer, input_rows, conv_input, input_sums, input_grad),
        (state_buffer, state_rows, conv_state, state_sums, state_grad),
    ):
        raw = rows[...]
        total = jnp.zeros(raw.shape, f32)
        for tap in range(4):
            ahead = buffer[tap : tap + BLOCK, :]
            total = total + taps[tap : tap + 1, :] * ahead
            sums[tap : tap + 1, :] += jnp.sum(ahead * raw, axis=0, keepdims=True)
        sums[4:5, :] += jnp.sum(buffer[0:BLOCK, :], axis=0, keepdims=True)
        result[...] = total.astype(result.dtype)
    input_first[...] = input_buffer[0:8, :]
    state_first[...] = state_buffer[0:8, :]

    out_head = dot(out_products[...], head_of[...], ((1,), (0,)), high)
    in_head = dot(in_products[...], head_of[...], ((1,), (0,)), high)
    upper = (iota((BLOCK, BLOCK), 0) <= iota((BLOCK, BLOCK), 1)).astype(f32)
    decay_grad = dot(upper, out_head - step_size * in_head, ((1,), (0,)), highest) + later[0:1, :]
    later[0:1, :] = decay_grad[0:1, :]
    step_sig = sigmoid(step_rows[...] + step_bias[...])
    step_back = (rates[...] * decay_grad + in_head) * step_sig
    step_grad[...] = step_back.astype(step_grad.dtype)
    step_sums[0:1, :] += jnp.sum(step_back, axis=0, keepdims=True)
    step_sums[1:2, :] += jnp.sum(step_size * decay_grad, axis=0, keepdims=True)


def whole(array):
    zeros = (0,) * array.ndim
    return pl.BlockSpec(array.shape, lambda k: zeros)


params = pltpu.CompilerParams(dimension_semantics=("arbitrary",), vmem_limit_bytes=48 * 1024 * 1024)


def run_scan(start, span, input_rows, state_rows, step_rows, state_entering, consts):
    channels = input_rows.shape[1]
    pairs = channels // LANES
    rows = span * BLOCK
    edge = start * BLOCK // 8 - 1

    def tokens(width):
        return pl.BlockSpec((BLOCK, width), lambda k: (start + k, 0))

    def results(width):
        return pl.BlockSpec((BLOCK, width), lambda k: (k, 0))

    if start == 0:
        before = (jnp.zeros((8, channels), f32), jnp.zeros((8, 2 * STATE), f32))
        before_specs = [whole(c) for c in before]
    else:
        before = (input_rows, state_rows)
        before_specs = [pl.BlockSpec((8, c.shape[1]), lambda k: (edge, 0)) for c in before]
    return pl.pallas_call(
        scan_kernel,
        grid=(span,),
        in_specs=[tokens(channels), tokens(2 * STATE), tokens(LANES)] + before_specs + [whole(state_entering)]
        + [whole(c) for c in consts],
        out_specs=[
            results(channels), results(channels), results(2 * STATE),
            pl.BlockSpec((1, pairs, LANES, STATE), lambda k: (k, 0, 0, 0)), whole(state_entering),
        ],
        out_shape=[
            jax.ShapeDtypeStruct((rows, channels), f32),
            jax.ShapeDtypeStruct((rows, channels), f32),
            jax.ShapeDtypeStruct((rows, 2 * STATE), f32),
            jax.ShapeDtypeStruct((span, pairs, LANES, STATE), f32),
            jax.ShapeDtypeStruct((pairs, LANES, STATE), f32),
        ],
        scratch_shapes=[pltpu.VMEM((BLOCK + 8, channels), f32), pltpu.VMEM((BLOCK + 8, 2 * STATE), f32)],
        compiler_params=params,
        cost_estimate=pl.CostEstimate(flops=5 * span * 10**9, bytes_accessed=3 * span * 2**20, transcendentals=0),
        name="scan",
    )(input_rows, state_rows, step_rows, *before, state_entering, *consts)


def run_scan_back(start, span, projections, kept, at, mixed_grad, carry, consts):
    channels = mixed_grad.shape[1]
    pairs = channels // LANES
    rows = span * BLOCK

    def tokens(width):
        return pl.BlockSpec((BLOCK, width), lambda k: (start + span - 1 - k, 0))

    def own(width, first=0):
        return pl.BlockSpec((BLOCK, width), lambda k: (first + span - 1 - k, 0))

    def shape(*dims):
        return jax.ShapeDtypeStruct(dims, f32)

    sums = [shape(8, channels), shape(8, 2 * STATE), shape(8, LANES)]
    ends = [jax.ShapeDtypeStruct(c.shape, f32) for c in carry]
    return pl.pallas_call(
        scan_back_kernel,
        grid=(span,),
        in_specs=[
            tokens(channels), tokens(2 * STATE), tokens(LANES), own(channels, at),
            own(2 * STATE, at), own(channels, at),
            pl.BlockSpec((1, pairs, LANES, STATE), lambda k: (at + span - 1 - k, 0, 0, 0)), tokens(channels),
        ] + [whole(c) for c in carry] + [whole(c) for c in consts],
        out_specs=[own(channels), own(2 * STATE), own(LANES)] + [whole(c) for c in sums + ends],
        out_shape=[
            jax.ShapeDtypeStruct((rows, channels), bf16), shape(rows, 2 * STATE),
            jax.ShapeDtypeStruct((rows, LANES), bf16),
        ] + sums + ends,
        scratch_shapes=[
            pltpu.VMEM((BLOCK + 8, channels), f32), pltpu.VMEM((BLOCK + 8, 2 * STATE), f32),
            pltpu.VMEM((BLOCK, BLOCK), f32), pltpu.VMEM((BLOCK, channels), f32), pltpu.VMEM((BLOCK, channels), f32),
        ],
        compiler_params=params,
        cost_estimate=pl.CostEstimate(flops=8 * span * 10**9, bytes_accessed=5 * span * 2**20, transcendentals=0),
        name="scan_back",
    )(*projections, *kept, mixed_grad, *carry, *consts)


def gate_kernel(mixed, gate_proj, out_grad, scales, gain, gate_out, gate_grad, mixed_grad, gain_sum, top):
    @pl.when(pl.program_id(0) == 0)
    def _():
        gain_sum[...] = jnp.zeros(gain_sum.shape, f32)
        top[...] = jnp.zeros(top.shape, f32)

    proj, rows_mixed, grad = gate_proj[...], mixed[...], out_grad[...]
    sig = sigmoid(proj)
    act = proj * sig
    gated = rows_mixed * act
    scale, pull = scales[:, 0:1], scales[:, 1:2]
    scaled = gated * scale
    gate_out[...] = (scaled * gain[...]).astype(bf16)
    gain_sum[0:1, :] += jnp.sum(grad * scaled, axis=0, keepdims=True)
    gated_grad = scale * (grad * gain[...]) - gated * pull
    mixed_grad[...] = gated_grad * act
    back = gated_grad * rows_mixed * (sig * (1.0 + proj * (1.0 - sig)))
    gate_grad[...] = back.astype(bf16)
    top[0:1, :] = jnp.maximum(top[0:1, :], jnp.max(jnp.abs(back), axis=0, keepdims=True))


def run_gate(mixed, gate_proj, out_grad, scales, gain):
    rows, channels = mixed.shape
    tokens = pl.BlockSpec((BLOCK, channels), lambda k: (k, 0))
    small = jax.ShapeDtypeStruct((8, channels), f32)
    return pl.pallas_call(
        gate_kernel,
        grid=(rows // BLOCK,),
        in_specs=[tokens, tokens, tokens, pl.BlockSpec((BLOCK, 2), lambda k: (k, 0)), whole(gain)],
        out_specs=[tokens, tokens, tokens, whole(small), whole(small)],
        out_shape=[
            jax.ShapeDtypeStruct((rows, channels), bf16), jax.ShapeDtypeStruct((rows, channels), bf16),
            jax.ShapeDtypeStruct((rows, channels), f32), small, small,
        ],
        compiler_params=params,
        cost_estimate=pl.CostEstimate(flops=10**8, bytes_accessed=16 * 2**20, transcendentals=0),
        name="gate",
    )(mixed, gate_proj, out_grad, scales, gain)


def assemble_kernel(sizes, places, *refs):
    pieces, result, sems = refs[:-2], refs[-2], refs[-1]
    copies = []
    for i, (piece, size) in enumerate(zip(pieces, sizes)):
        spot = result.at[pl.ds(pl.multiple_of(places[i], 16), size), :]
        copies.append(pltpu.make_async_copy(piece, spot, sems.at[i]))
        copies[-1].start()
    for copy in copies:
        copy.wait()


def assemble(pieces, places, rows):
    sizes = tuple(p.shape[0] for p in pieces)
    anywhere = pl.BlockSpec(memory_space=pl.ANY)
    return pl.pallas_call(
        lambda *refs: assemble_kernel(sizes, *refs),
        grid_spec=pltpu.PrefetchScalarGridSpec(
            num_scalar_prefetch=1, grid=(1,), in_specs=[anywhere] * len(pieces), out_specs=anywhere,
            scratch_shapes=[pltpu.SemaphoreType.DMA((len(pieces),))],
        ),
        out_shape=jax.ShapeDtypeStruct((rows, pieces[0].shape[1]), pieces[0].dtype),
        compiler_params=params,
        name="assemble",
    )(jnp.stack(places).astype(jnp.int32), *pieces)


def cycle(count):
    return list(range(0, count, 2)) + list(range(count - 1, 0, -2))


class Ring:
    def __init__(self):
        self.count = lax.axis_size("dp")
        order = cycle(self.count)
        self.up = [(order[i], order[(i + 1) % self.count]) for i in range(self.count)]
        self.down = [(b, a) for a, b in self.up]
        me = lax.axis_index("dp")
        self.place = jnp.where(me % 2 == 0, me // 2, self.count - 1 - me // 2)

    def owner(self, offset):
        place = (self.place + offset + self.count) % self.count
        return jnp.where(place < self.count // 2, 2 * place, 2 * (self.count - 1 - place) + 1)

    def gather(self, shards_in):
        rows = shards_in[0].shape[0]
        half = self.count // 2
        cut = (rows // 2 + 15) // 16 * 16
        held = [[(s, 0, 0)] for s in shards_in]
        below, above = list(shards_in), list(shards_in)
        for step in range(1, half):
            below = [lax.ppermute(b, "dp", self.up) for b in below]
            above = [lax.ppermute(a, "dp", self.down) for a in above]
            for pieces, b, a in zip(held, below, above):
                pieces += [(b, -step, 0), (a, step, 0)]
            yield below + above
        last_below = [lax.ppermute(b[:cut], "dp", self.up) for b in below]
        last_above = [lax.ppermute(a[cut:], "dp", self.down) for a in above]
        yield last_below + last_above
        for pieces, b, a in zip(held, last_below, last_above):
            pieces += [(b, half, 0), (a, half, cut)]
        return [
            assemble([p for p, _, _ in pieces], [self.owner(o) * rows + skip for _, o, skip in pieces], rows * self.count)
            for pieces in held
        ]


class Scatter:
    def __init__(self, ring, part, scale):
        self.ring, self.part, self.scale = ring, part, scale
        self.step = ring.count // 2
        self.cut = None

    def send(self, up, down):
        if self.scale is not None:
            up, down = ((rows * self.scale).astype(jnp.float16) for rows in (up, down))
        self.sent = (up, down)

    def go(self, marks):
        flat, tree = jax.tree.flatten((self.sent, marks))
        sent, marks = jax.tree.unflatten(tree, lax.optimization_barrier(flat))
        self.got = (lax.ppermute(sent[0], "dp", self.ring.up), lax.ppermute(sent[1], "dp", self.ring.down))
        return marks

    def add(self):
        if self.cut is None:
            far = self.part(self.ring.owner(self.step))
            self.cut = (far.shape[0] // 2 + 15) // 16 * 16
            self.send(far[: self.cut], far[self.cut :])
            return None
        up, down = self.got
        if self.scale is not None:
            up, down = (rows.astype(f32) * (1.0 / self.scale) for rows in (up, down))
        if self.step == self.ring.count // 2:
            rest = down.shape[0]
            up, down = jnp.pad(up, ((0, rest), (0, 0))), jnp.pad(down, ((self.cut, 0), (0, 0)))
        self.step -= 1
        if self.step == 0:
            return self.part(self.ring.owner(0)) + up + down
        self.send(self.part(self.ring.owner(self.step)) + up, self.part(self.ring.owner(-self.step)) + down)
        return None


def finish(generator):
    while True:
        try:
            next(generator)
        except StopIteration as stop:
            return stop.value


def fence(*arrays):
    flat, tree = jax.tree.flatten(arrays)
    return jax.tree.unflatten(tree, lax.optimization_barrier(flat))


def everyone(values, axis, combine):
    count = lax.axis_size(axis)
    terms = [values]
    for other in range(1, count):
        terms.append(lax.ppermute(values, axis, [(i, i ^ other) for i in range(count)]))
    while len(terms) > 1:
        terms = [combine(terms[i], terms[i + 1]) for i in range(0, len(terms), 2)]
    return terms[0]


def across(array, bit):
    count = lax.axis_size("tensor")
    return lax.ppermute(array, "tensor", [(i, i ^ bit) for i in range(count)])


def tensor_gather(shard, me):
    rows = shard.shape[0]
    far = across(shard, 2)
    whole_array = jnp.zeros((rows * lax.axis_size("tensor"), shard.shape[1]), shard.dtype)
    for bits, piece in ((0, shard), (1, across(shard, 1)), (2, far), (3, across(far, 1))):
        whole_array = lax.dynamic_update_slice(whole_array, piece, ((me ^ bits) * rows, 0))
    return whole_array


class TensorScatter:
    def __init__(self, part, me, narrow):
        self.part, self.me, self.narrow = part, me, narrow

    def cores(self):
        self.for_far = across(self.part(self.me ^ 3), 1)
        self.for_me = across(self.part(self.me ^ 1), 1)

    def chips(self):
        far = self.part(self.me ^ 2) + self.for_far
        if self.narrow:
            top = jnp.maximum(jnp.max(jnp.abs(far), axis=1), 1e-30)
            low = (far * (1.0 / top)[:, None]).astype(jnp.float16)
            self.got = (across(low, 2), across(top, 2))
        else:
            self.got = (across(far, 2),)

    def total(self):
        got = self.got[0]
        if self.narrow:
            got = got.astype(f32) * self.got[1][:, None]
        return self.part(self.me) + self.for_me + got


def shards(
    block_input, cotangent, norm_gain, gate_weight, input_weight, state_weight, step_weight, conv_input,
    conv_input_bias, conv_state, conv_state_bias, step_bias, decay_log, skip_scale, gate_gain, out_weight,
):
    group_count = lax.axis_size("tensor")
    me = lax.axis_index("tensor")
    ring = Ring()
    local_rows = block_input.shape[0]
    weight_rows = gate_weight.shape[0]
    channels = gate_gain.shape[0]
    heads = step_bias.shape[0]
    inner_total = channels * group_count
    share = 2 * STATE // group_count
    tokens = local_rows * group_count
    fold = LANES // share
    rows_dot = ((1,), (0,))

    blocks = tokens // BLOCK

    state_mine = lax.dynamic_slice_in_dim(state_weight, me * share, share, 1)
    first_weight = jnp.concatenate(
        [input_weight, state_mine, jnp.pad(step_weight, ((0, 0), (0, LANES - share - heads)))], axis=1
    ).astype(bf16)
    first_ring = ring.gather([first_weight])
    next(first_ring)
    row_scale = lax.rsqrt(jnp.mean(block_input * block_input, axis=1, keepdims=True) + epsilon)
    normed_all = tensor_gather((block_input * row_scale * norm_gain).astype(bf16), me)
    mark = next(first_ring)
    for _ in range(ring.count // 2 - 3):
        mark = next(first_ring)
    cot_low, gate_low, out_low, mark = fence(
        cotangent.astype(bf16), gate_weight.astype(bf16), out_weight.T.astype(bf16), mark
    )
    cot_all = lax.all_gather(cot_low, "tensor", axis=0, tiled=True)
    cot_top = everyone(jnp.full((8, LANES), jnp.max(jnp.abs(cotangent))), "dp", jnp.maximum)[0, 0]
    (first_full,) = finish(first_ring)
    second_ring = ring.gather([gate_low, out_low])
    arrived = next(second_ring)
    normed_t = normed_all.T
    cot_t = cot_all.T

    input_full, tail_full = first_full[:, :channels], first_full[:, channels:]
    tail_proj = dot(normed_all, tail_full, rows_dot)
    step_proj = jnp.pad(tail_proj[:, share : share + heads], ((0, 0), (0, LANES - heads)))
    state_mine = tail_proj[:, :share].reshape(fold, tokens // fold, share).transpose(1, 0, 2).reshape(tokens // fold, LANES)
    far = across(state_mine, 2)
    same_x, same_core, diagonal = across(state_mine, 1), far, across(far, 1)
    right_core = me % 2 == 1
    near = (jnp.where(right_core, same_x, state_mine), jnp.where(right_core, state_mine, same_x))
    away = (jnp.where(right_core, diagonal, same_core), jnp.where(right_core, same_core, diagonal))
    right_chip = me // 2 == 1
    state_parts = [jnp.where(right_chip, away[i], near[i]) for i in range(2)]
    state_parts += [jnp.where(right_chip, near[i], away[i]) for i in range(2)]
    state_proj = jnp.concatenate(
        [jnp.concatenate([p[:, i * share : (i + 1) * share] for p in state_parts], axis=1) for i in range(fold)], axis=0
    )
    input_proj = dot(normed_all, input_full, rows_dot)
    rates = -jnp.exp(decay_log)

    def per_head(vector):
        return jnp.pad(vector, (0, LANES - heads))[None, :]

    skip = jnp.repeat(skip_scale, HEAD_DIM)[None, :]
    head_of = (
        lax.broadcasted_iota(jnp.int32, (channels, LANES), 0) // HEAD_DIM
        == lax.broadcasted_iota(jnp.int32, (channels, LANES), 1)
    ).astype(f32)
    scan_consts = (
        conv_input, conv_input_bias[None, :], conv_state, conv_state_bias[None, :], per_head(step_bias),
        per_head(rates), skip,
    )
    carried = jnp.zeros((channels // LANES, LANES, STATE), f32)
    span = 2
    scanned = []
    for start in range(0, blocks, span):
        carried, arrived = fence(carried, arrived)
        scanned.append(run_scan(start, span, input_proj, state_proj, step_proj, carried, scan_consts))
        carried = scanned[-1][4]
        if start + span < blocks:
            arrived = next(second_ring)
    gate_full, out_full = finish(second_ring)
    mixed = jnp.concatenate([block[0] for block in scanned], axis=0)

    gate_proj = dot(normed_all, gate_full, rows_dot)
    gated = mixed * (gate_proj * jax.nn.sigmoid(gate_proj))
    gate_out_grad = dot(cot_all, out_full, rows_dot)
    sums = jnp.stack([jnp.sum(gated * gated, axis=1), jnp.sum(gate_out_grad * gate_gain * gated, axis=1)])
    sums = everyone(sums, "tensor", jnp.add)
    gate_scale = lax.rsqrt(sums[0] / inner_total + epsilon)
    scales = jnp.stack([gate_scale, gate_scale**3 * (sums[1] / inner_total)], axis=1)
    gate_out, gate_grad, mixed_grad, gain_sum, gate_top = run_gate(
        mixed, gate_proj, gate_out_grad, scales, gate_gain[None, :]
    )

    token_bound = float(tokens * ring.count)
    normed_bound = token_bound * float(block_input.shape[1]) ** 0.5 * jnp.max(jnp.abs(norm_gain))
    out_bound = token_bound * float(inner_total) ** 0.5 * jnp.max(jnp.abs(gate_gain))

    def scale_for(limit):
        return 32768.0 / jnp.maximum(limit, 1e-30)

    def dp_top(values):
        return everyone(jnp.full((8, LANES), jnp.max(values).astype(f32)), "dp", jnp.maximum)[0, 0]

    def chunk(array_t, index):
        return lax.dynamic_slice_in_dim(array_t, index * weight_rows, weight_rows, 0)

    def token_rows(array, index):
        return lax.dynamic_slice_in_dim(array, index * local_rows, local_rows, 0)

    out_ring = Scatter(ring, lambda i: dot(chunk(cot_t, i), gate_out, rows_dot), scale_for(out_bound * cot_top))
    gate_ring = Scatter(
        ring, lambda i: dot(chunk(normed_t, i), gate_grad, rows_dot), scale_for(normed_bound * dp_top(gate_top))
    )
    branch = TensorScatter(lambda i: dot(token_rows(gate_out, i), out_full, ((1,), (1,))), me, True)

    back_consts = (conv_input, conv_state, per_head(step_bias), per_head(rates), skip, head_of)
    carry = (
        jnp.zeros((8, channels), f32), jnp.zeros((8, 2 * STATE), f32),
        jnp.zeros((channels // LANES, LANES, STATE), f32), jnp.zeros((8, LANES), f32),
    )
    done = []
    out_sum = gate_sum = None
    for turn in range(blocks):
        if out_sum is None:
            out_sum = out_ring.add()
            if out_sum is None:
                carry = out_ring.go(carry)
        if turn > 0:
            gate_ring.add()
            carry = gate_ring.go(carry)
        if turn == 1:
            branch.cores()
        if turn == 2:
            branch.chips()
        start = blocks - 1 - turn
        kept = scanned[start // span]
        kept = [kept[1], kept[2], kept[0], kept[3]]
        result = run_scan_back(
            start, 1, (input_proj, state_proj, step_proj), kept, start % span, mixed_grad, carry, back_consts
        )
        done.insert(0, result)
        carry = tuple(result[6:])
    while out_sum is None:
        out_sum = out_ring.add()
        if out_sum is None:
            out_ring.go(())
    while gate_sum is None:
        gate_sum = gate_ring.add()
        if gate_sum is None:
            gate_ring.go(())
    block_output = block_input + branch.total()
    input_back, state_back, step_back = (jnp.concatenate([d[i] for d in done], axis=0) for i in range(3))
    input_sums, state_sums, step_sums = (sum(d[i] for d in done) for i in range(3, 6))

    def state_columns(index):
        mine = lax.dynamic_slice_in_dim(state_back, index * share, share, 1)
        return jnp.concatenate([mine[i * (tokens // fold) : (i + 1) * (tokens // fold)] for i in range(fold)], axis=1)

    state_exchange = TensorScatter(state_columns, me, False)
    state_exchange.cores()
    state_exchange.chips()
    input_ring = Scatter(
        ring, lambda i: dot(chunk(normed_t, i), input_back, rows_dot),
        scale_for(normed_bound * dp_top(jnp.abs(input_back))),
    )
    input_ring.add()
    input_ring.go(())
    state_share = state_exchange.total().astype(bf16)
    state_share = jnp.concatenate([state_share[:, i * share : (i + 1) * share] for i in range(fold)], axis=0)
    tail = jnp.concatenate(
        [state_share, step_back[:, :heads], jnp.zeros((tokens, LANES - share - heads), bf16)], axis=1
    )

    def normed_rows(index):
        part = dot(token_rows(gate_grad, index), gate_full, ((1,), (1,)))
        part = part + dot(token_rows(input_back, index), input_full, ((1,), (1,)))
        return part + dot(token_rows(tail, index), tail_full, ((1,), (1,)))

    normed_exchange = TensorScatter(normed_rows, me, True)
    normed_exchange.cores()
    normed_exchange.chips()
    tail_ring = Scatter(ring, lambda i: dot(chunk(normed_t, i), tail, rows_dot), None)
    input_sum = tail_sum = None
    tail_ring.add()
    tail_ring.go(())
    while tail_sum is None:
        input_sum = input_ring.add()
        tail_sum = tail_ring.add()
        if tail_sum is None:
            input_ring.go(())
            tail_ring.go(())
    normed_grad = normed_exchange.total()

    weighted_grad = normed_grad * norm_gain
    norm_gain_part = jnp.sum(normed_grad * block_input * row_scale, axis=0)
    input_grad = (
        cotangent
        + row_scale * weighted_grad
        - block_input * row_scale**3 * jnp.mean(weighted_grad * block_input, axis=1, keepdims=True)
    )
    state_weight_grad = lax.all_gather(tail_sum[:, :share], "tensor", axis=1, tiled=True)

    local = jnp.concatenate(
        [
            input_sums[:5].reshape(-1),
            gain_sum[0],
            jnp.sum(input_sums[5].reshape(heads, HEAD_DIM), axis=1),
            step_sums[0, :heads],
            step_sums[1, :heads] * rates,
        ]
    )
    packed = jnp.concatenate([local, state_sums[:5].reshape(-1)])
    packed = jnp.pad(packed, (0, -packed.shape[0] % (8 * LANES))).reshape(-1, LANES)
    packed = everyone(packed, "dp", jnp.add).reshape(-1)
    local, shared = packed[: local.shape[0]], packed[local.shape[0] :][: 10 * STATE]
    shared = everyone(shared.reshape(-1, LANES), "tensor", jnp.add).reshape(5, 2 * STATE)
    norm_gain_grad = everyone(norm_gain_part.reshape(-1, LANES), "tensor", jnp.add)
    norm_gain_grad = everyone(norm_gain_grad, "dp", jnp.add).reshape(-1)
    at = 6 * channels
    return (
        block_output,
        input_grad,
        norm_gain_grad,
        gate_sum,
        input_sum,
        state_weight_grad,
        tail_sum[:, share : share + heads],
        local[: 4 * channels].reshape(4, channels),
        local[4 * channels : 5 * channels],
        shared[:4],
        shared[4],
        local[at + heads : at + 2 * heads],
        local[at + 2 * heads : at + 3 * heads],
        local[at : at + heads],
        local[5 * channels : at],
        out_sum.T,
    )


def solution(mesh):
    rows = P(("dp", "tensor"), None)
    both = P("dp", "tensor")
    inner = P("tensor")
    return jax.shard_map(
        shards,
        mesh=mesh,
        in_specs=(
            rows, rows, P(), both, both, P("dp", None), both, P(None, "tensor"), inner, P(), P(), inner, inner,
            inner, inner, P("tensor", "dp"),
        ),
        out_specs=(
            rows, rows, P(), both, both, P("dp", None), both, P(None, "tensor"), inner, P(), P(), inner, inner,
            inner, inner, P("tensor", "dp"),
        ),
        check_vma=False,
    )
```

```python
import jax
import jax.numpy as jnp
from jax import lax
from jax.experimental import pallas as pl
from jax.experimental.pallas import tpu as pltpu
from jax.sharding import PartitionSpec as P

HEAD_DIM = 64
STATE = 128
BLOCK = 256
SEQ = 1024
LANES = 128

epsilon = 1e-05
high = lax.Precision.HIGH
highest = lax.Precision.HIGHEST
f32 = jnp.float32
bf16 = jnp.bfloat16


def dot(left, right, dims, precision=None):
    return lax.dot_general(
        left, right, (dims, ((), ())), precision=precision, preferred_element_type=f32
    )


def sigmoid(v):
    return 1.0 / (1.0 + jnp.exp(-v))


def softplus(v):
    return jnp.maximum(v, 0.0) + jnp.log1p(jnp.exp(-jnp.abs(v)))


def iota(shape, axis):
    return lax.broadcasted_iota(jnp.int32, shape, axis)


def pair_columns(table, pair):
    lane = iota((table.shape[0], LANES), 1)
    return jnp.where(lane < HEAD_DIM, table[:, 2 * pair : 2 * pair + 1], table[:, 2 * pair + 1 : 2 * pair + 2])


def decay_tables(step_rows, step_bias, rates):
    step_size = softplus(step_rows + step_bias)
    earlier = (iota((BLOCK, BLOCK), 0) >= iota((BLOCK, BLOCK), 1)).astype(f32)
    cumulative = dot(earlier, step_size * rates, ((1,), (0,)), highest)
    return step_size, cumulative, jnp.exp(cumulative), jnp.exp(cumulative[BLOCK - 1 : BLOCK, :] - cumulative)


def state_decay(from_start, pair):
    last = from_start[BLOCK - 1 : BLOCK, :]
    row = iota((LANES, STATE), 0)
    return jnp.where(row < HEAD_DIM, last[:, 2 * pair : 2 * pair + 1], last[:, 2 * pair + 1 : 2 * pair + 2])


def shifted_conv(rows_ref, before, buffer, taps, conv_bias, first):
    @pl.when(first)
    def _():
        buffer[0:8, :] = before[...]

    @pl.when(jnp.logical_not(first))
    def _():
        buffer[0:8, :] = buffer[BLOCK : BLOCK + 8, :]

    buffer[8 : BLOCK + 8, :] = rows_ref[...]
    total = conv_bias[...] + taps[0:1, :] * buffer[8 : BLOCK + 8, :]
    for tap in range(1, 4):
        total = total + taps[tap : tap + 1, :] * buffer[8 - tap : BLOCK + 8 - tap, :]
    return total


def scan_kernel(
    input_rows, state_rows, step_rows, input_before, state_before, state_entering,
    conv_input, conv_input_bias, conv_state, conv_state_bias, step_bias, rates, skip,
    mixed, input_conv, state_conv, entering, carried, input_buffer, state_buffer,
):
    first = pl.program_id(0) == 0
    pairs = input_rows.shape[1] // LANES

    @pl.when(first)
    def _():
        carried[...] = state_entering[...]

    input_conv[...] = shifted_conv(input_rows, input_before, input_buffer, conv_input, conv_input_bias, first)
    state_pre = shifted_conv(state_rows, state_before, state_buffer, conv_state, conv_state_bias, first)
    state_conv[...] = state_pre
    state_act = state_pre * sigmoid(state_pre)
    writes, reads = state_act[:, :STATE], state_act[:, STATE:]
    meeting = dot(reads, writes, ((1,), (1,)), high)
    step_size, cumulative, from_start, to_end = decay_tables(step_rows[...], step_bias[...], rates[...])
    cumulative_t = cumulative.T
    causal = iota((BLOCK, BLOCK), 0) >= iota((BLOCK, BLOCK), 1)
    lane = iota((BLOCK, LANES), 1)
    for pair in range(pairs):
        columns = slice(pair * LANES, pair * LANES + LANES)
        pre = input_conv[:, columns]
        inputs = pre * sigmoid(pre)
        weighted = inputs * pair_columns(step_size, pair)
        state_in = carried[pair]
        entering[0, pair] = state_in
        out = dot(reads, state_in, ((1,), (1,)), high) * pair_columns(from_start, pair)
        for side in range(2):
            head = 2 * pair + side
            gap = cumulative[:, head : head + 1] - cumulative_t[head : head + 1, :]
            mixing = jnp.exp(jnp.where(causal, gap, -1e30)) * meeting
            mine = (lane < HEAD_DIM) if side == 0 else (lane >= HEAD_DIM)
            out = out + dot(mixing, jnp.where(mine, weighted, 0.0), ((1,), (0,)), high)
        fresh = dot(weighted * pair_columns(to_end, pair), writes, ((0,), (0,)), high)
        carried[pair] = state_decay(from_start, pair) * state_in + fresh
        mixed[:, columns] = out + skip[:, columns] * inputs


def scan_back_kernel(
    input_rows, state_rows, step_rows, input_conv, state_conv, mixed, entering, mixed_grad,
    input_after, state_after, state_leaving, decay_after,
    conv_input, conv_state, step_bias, rates, skip, head_of,
    input_grad, state_grad, step_grad, input_sums, state_sums, step_sums, input_first, state_first, carried, later,
    input_buffer, state_buffer, gap_grad, out_products, in_products,
):
    first = pl.program_id(0) == 0
    pairs = input_rows.shape[1] // LANES

    @pl.when(first)
    def _():
        carried[...] = state_leaving[...]
        later[...] = decay_after[...]
        input_sums[...] = jnp.zeros(input_sums.shape, f32)
        state_sums[...] = jnp.zeros(state_sums.shape, f32)
        step_sums[...] = jnp.zeros(step_sums.shape, f32)
        input_buffer[BLOCK : BLOCK + 8, :] = input_after[...]
        state_buffer[BLOCK : BLOCK + 8, :] = state_after[...]

    @pl.when(jnp.logical_not(first))
    def _():
        input_buffer[BLOCK : BLOCK + 8, :] = input_buffer[0:8, :]
        state_buffer[BLOCK : BLOCK + 8, :] = state_buffer[0:8, :]

    state_pre = state_conv[...]
    state_sig = sigmoid(state_pre)
    state_act = state_pre * state_sig
    writes, reads = state_act[:, :STATE], state_act[:, STATE:]
    meeting_t = dot(writes, reads, ((1,), (1,)), high)
    step_size, cumulative, from_start, to_end = decay_tables(step_rows[...], step_bias[...], rates[...])
    cumulative_t = cumulative.T
    causal_t = iota((BLOCK, BLOCK), 0) <= iota((BLOCK, BLOCK), 1)
    lane = iota((BLOCK, LANES), 1)
    gap_grad[...] = jnp.zeros(gap_grad.shape, f32)
    writes_grad = jnp.zeros((BLOCK, STATE), f32)
    reads_grad = jnp.zeros((BLOCK, STATE), f32)
    for pair in range(pairs):
        columns = slice(pair * LANES, pair * LANES + LANES)
        pre = input_conv[:, columns]
        sig = sigmoid(pre)
        inputs = pre * sig
        step_pair = pair_columns(step_size, pair)
        weighted = inputs * step_pair
        out_grad = mixed_grad[:, columns]
        skip_product = out_grad * inputs
        input_sums[5:6, columns] += jnp.sum(skip_product, axis=0, keepdims=True)
        end_pair = pair_columns(to_end, pair)
        leaving_grad = carried[pair]
        weighted_grad = dot(writes, leaving_grad, ((1,), (1,)), high) * end_pair
        for side in range(2):
            head = 2 * pair + side
            gap = cumulative_t[head : head + 1, :] - cumulative[:, head : head + 1]
            within = jnp.exp(jnp.where(causal_t, gap, -1e30))
            mine = (lane < HEAD_DIM) if side == 0 else (lane >= HEAD_DIM)
            own_grad = jnp.where(mine, out_grad, 0.0)
            weighted_grad = weighted_grad + dot(within * meeting_t, own_grad, ((1,), (0,)), high)
            gap_grad[...] += within * dot(weighted, own_grad, ((1,), (1,)), high)
        start_grad = out_grad * pair_columns(from_start, pair)
        reads_grad = reads_grad + dot(start_grad, entering[0, pair], ((1,), (0,)), high)
        writes_grad = writes_grad + dot(weighted * end_pair, leaving_grad, ((1,), (0,)), high)
        carried[pair] = state_decay(from_start, pair) * leaving_grad + dot(start_grad, reads, ((0,), (0,)), high)
        out_products[:, columns] = out_grad * mixed[:, columns] - skip[:, columns] * skip_product
        in_products[:, columns] = inputs * weighted_grad
        inputs_grad = skip[:, columns] * out_grad + step_pair * weighted_grad
        input_buffer[0:BLOCK, columns] = inputs_grad * (sig * (1.0 + pre * (1.0 - sig)))
    reads_grad = reads_grad + dot(gap_grad[...], writes, ((0,), (0,)), high)
    writes_grad = writes_grad + dot(gap_grad[...], reads, ((1,), (0,)), high)
    state_slope = state_sig * (1.0 + state_pre * (1.0 - state_sig))
    state_buffer[0:BLOCK, 0:STATE] = writes_grad * state_slope[:, :STATE]
    state_buffer[0:BLOCK, STATE : 2 * STATE] = reads_grad * state_slope[:, STATE:]

    for buffer, rows, taps, sums, result in (
        (input_buffer, input_rows, conv_input, input_sums, input_grad),
        (state_buffer, state_rows, conv_state, state_sums, state_grad),
    ):
        raw = rows[...]
        total = jnp.zeros(raw.shape, f32)
        for tap in range(4):
            ahead = buffer[tap : tap + BLOCK, :]
            total = total + taps[tap : tap + 1, :] * ahead
            sums[tap : tap + 1, :] += jnp.sum(ahead * raw, axis=0, keepdims=True)
        sums[4:5, :] += jnp.sum(buffer[0:BLOCK, :], axis=0, keepdims=True)
        result[...] = total.astype(result.dtype)
    input_first[...] = input_buffer[0:8, :]
    state_first[...] = state_buffer[0:8, :]

    out_head = dot(out_products[...], head_of[...], ((1,), (0,)), high)
    in_head = dot(in_products[...], head_of[...], ((1,), (0,)), high)
    upper = (iota((BLOCK, BLOCK), 0) <= iota((BLOCK, BLOCK), 1)).astype(f32)
    decay_grad = dot(upper, out_head - step_size * in_head, ((1,), (0,)), highest) + later[0:1, :]
    later[0:1, :] = decay_grad[0:1, :]
    step_sig = sigmoid(step_rows[...] + step_bias[...])
    step_back = (rates[...] * decay_grad + in_head) * step_sig
    step_grad[...] = step_back.astype(step_grad.dtype)
    step_sums[0:1, :] += jnp.sum(step_back, axis=0, keepdims=True)
    step_sums[1:2, :] += jnp.sum(step_size * decay_grad, axis=0, keepdims=True)


def whole(array):
    zeros = (0,) * array.ndim
    return pl.BlockSpec(array.shape, lambda k: zeros)


params = pltpu.CompilerParams(dimension_semantics=("arbitrary",), vmem_limit_bytes=48 * 1024 * 1024)


def run_scan(start, span, input_rows, state_rows, step_rows, state_entering, consts):
    channels = input_rows.shape[1]
    pairs = channels // LANES
    rows = span * BLOCK
    edge = start * BLOCK // 8 - 1

    def tokens(width):
        return pl.BlockSpec((BLOCK, width), lambda k: (start + k, 0))

    def results(width):
        return pl.BlockSpec((BLOCK, width), lambda k: (k, 0))

    if start == 0:
        before = (jnp.zeros((8, channels), f32), jnp.zeros((8, 2 * STATE), f32))
        before_specs = [whole(c) for c in before]
    else:
        before = (input_rows, state_rows)
        before_specs = [pl.BlockSpec((8, c.shape[1]), lambda k: (edge, 0)) for c in before]
    return pl.pallas_call(
        scan_kernel,
        grid=(span,),
        in_specs=[tokens(channels), tokens(2 * STATE), tokens(LANES)] + before_specs + [whole(state_entering)]
        + [whole(c) for c in consts],
        out_specs=[
            results(channels), results(channels), results(2 * STATE),
            pl.BlockSpec((1, pairs, LANES, STATE), lambda k: (k, 0, 0, 0)), whole(state_entering),
        ],
        out_shape=[
            jax.ShapeDtypeStruct((rows, channels), f32),
            jax.ShapeDtypeStruct((rows, channels), f32),
            jax.ShapeDtypeStruct((rows, 2 * STATE), f32),
            jax.ShapeDtypeStruct((span, pairs, LANES, STATE), f32),
            jax.ShapeDtypeStruct((pairs, LANES, STATE), f32),
        ],
        scratch_shapes=[pltpu.VMEM((BLOCK + 8, channels), f32), pltpu.VMEM((BLOCK + 8, 2 * STATE), f32)],
        compiler_params=params,
        cost_estimate=pl.CostEstimate(flops=5 * span * 10**9, bytes_accessed=3 * span * 2**20, transcendentals=0),
        name="scan",
    )(input_rows, state_rows, step_rows, *before, state_entering, *consts)


def run_scan_back(start, span, projections, kept, at, mixed_grad, carry, consts):
    channels = mixed_grad.shape[1]
    pairs = channels // LANES
    rows = span * BLOCK

    def tokens(width):
        return pl.BlockSpec((BLOCK, width), lambda k: (start + span - 1 - k, 0))

    def own(width, first=0):
        return pl.BlockSpec((BLOCK, width), lambda k: (first + span - 1 - k, 0))

    def shape(*dims):
        return jax.ShapeDtypeStruct(dims, f32)

    sums = [shape(8, channels), shape(8, 2 * STATE), shape(8, LANES)]
    ends = [jax.ShapeDtypeStruct(c.shape, f32) for c in carry]
    return pl.pallas_call(
        scan_back_kernel,
        grid=(span,),
        in_specs=[
            tokens(channels), tokens(2 * STATE), tokens(LANES), own(channels, at),
            own(2 * STATE, at), own(channels, at),
            pl.BlockSpec((1, pairs, LANES, STATE), lambda k: (at + span - 1 - k, 0, 0, 0)), tokens(channels),
        ] + [whole(c) for c in carry] + [whole(c) for c in consts],
        out_specs=[own(channels), own(2 * STATE), own(LANES)] + [whole(c) for c in sums + ends],
        out_shape=[
            jax.ShapeDtypeStruct((rows, channels), bf16), shape(rows, 2 * STATE),
            jax.ShapeDtypeStruct((rows, LANES), bf16),
        ] + sums + ends,
        scratch_shapes=[
            pltpu.VMEM((BLOCK + 8, channels), f32), pltpu.VMEM((BLOCK + 8, 2 * STATE), f32),
            pltpu.VMEM((BLOCK, BLOCK), f32), pltpu.VMEM((BLOCK, channels), f32), pltpu.VMEM((BLOCK, channels), f32),
        ],
        compiler_params=params,
        cost_estimate=pl.CostEstimate(flops=8 * span * 10**9, bytes_accessed=5 * span * 2**20, transcendentals=0),
        name="scan_back",
    )(*projections, *kept, mixed_grad, *carry, *consts)


def gate_kernel(mixed, gate_proj, out_grad, scales, gain, gate_out, gate_grad, mixed_grad, gain_sum):
    @pl.when(pl.program_id(0) == 0)
    def _():
        gain_sum[...] = jnp.zeros(gain_sum.shape, f32)

    proj, rows_mixed, grad = gate_proj[...], mixed[...], out_grad[...]
    sig = sigmoid(proj)
    act = proj * sig
    gated = rows_mixed * act
    scale, pull = scales[:, 0:1], scales[:, 1:2]
    scaled = gated * scale
    gate_out[...] = (scaled * gain[...]).astype(bf16)
    gain_sum[0:1, :] += jnp.sum(grad * scaled, axis=0, keepdims=True)
    gated_grad = scale * (grad * gain[...]) - gated * pull
    mixed_grad[...] = gated_grad * act
    back = gated_grad * rows_mixed * (sig * (1.0 + proj * (1.0 - sig)))
    gate_grad[...] = back.astype(bf16)


def run_gate(mixed, gate_proj, out_grad, scales, gain):
    rows, channels = mixed.shape
    tokens = pl.BlockSpec((BLOCK, channels), lambda k: (k, 0))
    small = jax.ShapeDtypeStruct((8, channels), f32)
    return pl.pallas_call(
        gate_kernel,
        grid=(rows // BLOCK,),
        in_specs=[tokens, tokens, tokens, pl.BlockSpec((BLOCK, 2), lambda k: (k, 0)), whole(gain)],
        out_specs=[tokens, tokens, tokens, whole(small)],
        out_shape=[
            jax.ShapeDtypeStruct((rows, channels), bf16), jax.ShapeDtypeStruct((rows, channels), bf16),
            jax.ShapeDtypeStruct((rows, channels), f32), small,
        ],
        compiler_params=params,
        cost_estimate=pl.CostEstimate(flops=10**8, bytes_accessed=16 * 2**20, transcendentals=0),
        name="gate",
    )(mixed, gate_proj, out_grad, scales, gain)


def assemble_kernel(sizes, places, *refs):
    pieces, result, sems = refs[:-2], refs[-2], refs[-1]
    copies = []
    for i, (piece, size) in enumerate(zip(pieces, sizes)):
        spot = result.at[pl.ds(pl.multiple_of(places[i], 16), size), :]
        copies.append(pltpu.make_async_copy(piece, spot, sems.at[i]))
        copies[-1].start()
    for copy in copies:
        copy.wait()


def assemble(pieces, places, rows):
    sizes = tuple(p.shape[0] for p in pieces)
    anywhere = pl.BlockSpec(memory_space=pl.ANY)
    return pl.pallas_call(
        lambda *refs: assemble_kernel(sizes, *refs),
        grid_spec=pltpu.PrefetchScalarGridSpec(
            num_scalar_prefetch=1, grid=(1,), in_specs=[anywhere] * len(pieces), out_specs=anywhere,
            scratch_shapes=[pltpu.SemaphoreType.DMA((len(pieces),))],
        ),
        out_shape=jax.ShapeDtypeStruct((rows, pieces[0].shape[1]), pieces[0].dtype),
        compiler_params=params,
        name="assemble",
    )(jnp.stack(places).astype(jnp.int32), *pieces)


def partial_kernel(count, steps, places, *refs):
    lefts, rights, (result, top) = refs[:count], refs[count : 2 * count], refs[2 * count :]
    owners, rows = result.shape[0], result.shape[1]
    for i in range(count):

        @pl.when(pl.program_id(0) // steps == i)
        def _():
            product = dot(lefts[i][...], rights[i][...], ((1,), (0,)))
            for owner in range(owners):
                own = product[owner * rows : (owner + 1) * rows]
                result[places[owner]] = own
                top[places[owner]] = jnp.broadcast_to(jnp.max(jnp.abs(own), axis=0, keepdims=True), top.shape[1:])


def partials(ring, lefts, rights):
    width, tile = rights[0].shape[1], 2 * LANES
    steps, count = width // tile, len(lefts)
    rows = lefts[0].shape[0] // ring.count
    order = cycle(ring.count)
    places = [(order.index(i) - ring.place + ring.count) % ring.count for i in range(ring.count)]

    def column(i):
        return lambda n, _: (0, jnp.clip(n - i * steps, 0, steps - 1))

    def fixed(n, _):
        return (0, 0)

    return pl.pallas_call(
        lambda *refs: partial_kernel(count, steps, *refs),
        grid_spec=pltpu.PrefetchScalarGridSpec(
            num_scalar_prefetch=1, grid=(count * steps,),
            in_specs=[pl.BlockSpec(left.shape, fixed) for left in lefts]
            + [pl.BlockSpec((right.shape[0], tile), column(i)) for i, right in enumerate(rights)],
            out_specs=[
                pl.BlockSpec((ring.count, rows, tile), lambda n, _: (0, 0, n)),
                pl.BlockSpec((ring.count, 8, tile), lambda n, _: (0, 0, n)),
            ],
        ),
        out_shape=[
            jax.ShapeDtypeStruct((ring.count, rows, count * width), f32),
            jax.ShapeDtypeStruct((ring.count, 8, count * width), f32),
        ],
        compiler_params=params,
        cost_estimate=pl.CostEstimate(flops=count * 4 * 10**9, bytes_accessed=count * 9 * 2**20, transcendentals=0),
        name="partials",
    )(jnp.stack(places).astype(jnp.int32), *lefts, *rights)


def cycle(count):
    return list(range(0, count, 2)) + list(range(count - 1, 0, -2))


class Ring:
    def __init__(self):
        self.count = lax.axis_size("dp")
        order = cycle(self.count)
        self.up = [(order[i], order[(i + 1) % self.count]) for i in range(self.count)]
        self.down = [(b, a) for a, b in self.up]
        me = lax.axis_index("dp")
        self.place = jnp.where(me % 2 == 0, me // 2, self.count - 1 - me // 2)

    def owner(self, offset):
        place = (self.place + offset + self.count) % self.count
        return jnp.where(place < self.count // 2, 2 * place, 2 * (self.count - 1 - place) + 1)


def middle(rows):
    return (rows // 2 + 15) // 16 * 16


class Gather:
    def __init__(self, ring, shard):
        self.ring, self.shard, self.step = ring, shard, 0
        self.held = [(shard, 0, 0)]
        self.last = (shard, shard)

    def hop(self):
        self.step += 1
        half, cut = self.ring.count // 2, middle(self.shard.shape[0])
        up, down = self.last
        offsets = ((-self.step, 0), (self.step, 0))
        if self.step == half:
            up, down = up[:cut], down[cut:]
            offsets = ((half, 0), (half, cut))
        self.last = (lax.ppermute(up, "dp", self.ring.up), lax.ppermute(down, "dp", self.ring.down))
        self.held += [(piece, *offset) for piece, offset in zip(self.last, offsets)]

    def after(self, *marks):
        self.last, marks = fence(self.last, marks)
        self.held[-2:] = [(piece, *old[1:]) for piece, old in zip(self.last, self.held[-2:])]
        return marks if len(marks) > 1 else marks[0]

    def result(self):
        rows = self.shard.shape[0]
        pieces = [piece for piece, _, _ in self.held]
        places = [self.ring.owner(offset) * rows + skip for _, offset, skip in self.held]
        return assemble(pieces, places, rows * self.ring.count)


def encode(rows, limit):
    power = jnp.ceil(jnp.log2(jnp.maximum(limit, 1e-30)))
    scaled = rows * jnp.exp2(15.0 - power)
    return jnp.concatenate([scaled, jnp.broadcast_to(power, (16, rows.shape[1]))], axis=0).astype(jnp.float16)


def decode(payload):
    power = payload[-16:-15].astype(f32)
    return payload[:-16].astype(f32) * jnp.exp2(power - 15.0), jnp.exp2(power)


class Scatter:
    def __init__(self, ring, parts, tops):
        self.ring, self.parts, self.tops = ring, parts, tops
        self.step = ring.count // 2
        self.cut = middle(parts.shape[1])
        far, top = parts[self.step], tops[self.step, 0:1]
        self.send = (encode(far[: self.cut], top), encode(far[self.cut :], top))

    def hop(self):
        self.got = (lax.ppermute(self.send[0], "dp", self.ring.up), lax.ppermute(self.send[1], "dp", self.ring.down))

    def before(self, *marks):
        self.send, marks = fence(self.send, marks)
        return marks if len(marks) > 1 else marks[0]

    def add(self):
        first = self.step == self.ring.count // 2
        (up, up_top), (down, down_top) = (decode(g) for g in self.got)
        if first:
            rest = down.shape[0]
            up, down = jnp.pad(up, ((0, rest), (0, 0))), jnp.pad(down, ((self.cut, 0), (0, 0)))
        self.step -= 1
        if self.step == 0:
            return self.parts[0] + up + down
        above, below = self.step, self.ring.count - self.step
        self.send = (
            encode(self.parts[above] + up, self.tops[above, 0:1] + up_top),
            encode(self.parts[below] + down, self.tops[below, 0:1] + down_top),
        )
        return None


def fence(*arrays):
    flat, tree = jax.tree.flatten(arrays)
    return jax.tree.unflatten(tree, lax.optimization_barrier(flat))


def across(array, bit, axis="tensor"):
    count = lax.axis_size(axis)
    return lax.ppermute(array, axis, [(i, i ^ bit) for i in range(count)])


def cube_sum(array, axis):
    bit = 1
    while bit < lax.axis_size(axis):
        array = array + across(array, bit, axis)
        bit *= 2
    return array


def shards(
    block_input, cotangent, norm_gain, gate_weight, input_weight, state_weight, step_weight, conv_input,
    conv_input_bias, conv_state, conv_state_bias, step_bias, decay_log, skip_scale, gate_gain, out_weight,
):
    group_count = lax.axis_size("tensor")
    me = lax.axis_index("tensor")
    ring = Ring()
    half = ring.count // 2
    local_rows = block_input.shape[0]
    channels = gate_gain.shape[0]
    heads = step_bias.shape[0]
    inner_total = channels * group_count
    share = 2 * STATE // group_count
    tokens = local_rows * group_count
    blocks = tokens // BLOCK
    fold = LANES // share
    folded = tokens // fold
    rows_dot = ((1,), (0,))
    back_dot = ((1,), (1,))

    state_mine = lax.dynamic_slice_in_dim(state_weight, me * share, share, 1)
    first = Gather(
        ring,
        jnp.concatenate(
            [input_weight, state_mine, jnp.pad(step_weight, ((0, 0), (0, LANES - share - heads)))], axis=1
        ).astype(bf16),
    )
    first.hop()
    row_scale = lax.rsqrt(jnp.mean(block_input * block_input, axis=1, keepdims=True) + epsilon)
    normed = (block_input * row_scale * norm_gain).astype(bf16)
    far = across(normed, 2)
    normed_pieces = (normed, across(normed, 1), far, across(far, 1))
    normed_all = assemble(normed_pieces, [(me ^ bits) * local_rows for bits in range(4)], tokens)
    second_weight = jnp.concatenate([gate_weight, out_weight.T], axis=1).astype(bf16)
    for _ in range(half - 2):
        first.hop()
    second_weight, cot_low = first.after(second_weight, cotangent.astype(bf16))
    first.hop()
    second = Gather(ring, second_weight)
    second.hop()
    cot_all = lax.all_gather(cot_low, "tensor", axis=0, tiled=True)
    first_full = first.result()

    input_full, tail_full = first_full[:, :channels], first_full[:, channels:]
    tail_proj = dot(normed_all, tail_full, rows_dot)
    step_proj = jnp.pad(tail_proj[:, share : share + heads], ((0, 0), (0, LANES - heads)))
    state_mine = jnp.concatenate([tail_proj[i * folded : (i + 1) * folded, :share] for i in range(fold)], axis=1)
    far = across(state_mine, 2)
    same_x, same_core, diagonal = across(state_mine, 1), far, across(far, 1)
    right_core = me % 2 == 1
    near = (jnp.where(right_core, same_x, state_mine), jnp.where(right_core, state_mine, same_x))
    away = (jnp.where(right_core, diagonal, same_core), jnp.where(right_core, same_core, diagonal))
    right_chip = me // 2 == 1
    state_parts = [jnp.where(right_chip, away[i], near[i]) for i in range(2)]
    state_parts += [jnp.where(right_chip, near[i], away[i]) for i in range(2)]
    state_proj = jnp.concatenate(
        [jnp.concatenate([p[:, i * share : (i + 1) * share] for p in state_parts], axis=1) for i in range(fold)], axis=0
    )
    input_proj = dot(normed_all, input_full, rows_dot)
    rates = -jnp.exp(decay_log)

    def per_head(vector):
        return jnp.pad(vector, (0, LANES - heads))[None, :]

    skip = jnp.repeat(skip_scale, HEAD_DIM)[None, :]
    head_of = (
        lax.broadcasted_iota(jnp.int32, (channels, LANES), 0) // HEAD_DIM
        == lax.broadcasted_iota(jnp.int32, (channels, LANES), 1)
    ).astype(f32)
    scan_consts = (
        conv_input, conv_input_bias[None, :], conv_state, conv_state_bias[None, :], per_head(step_bias),
        per_head(rates), skip,
    )
    carried = jnp.zeros((channels // LANES, LANES, STATE), f32)
    span = 2
    scanned = []
    input_proj = second.after(input_proj)
    for start in range(0, blocks, span):
        if second.step < half - 1:
            second.hop()
        scanned.append(run_scan(start, span, input_proj, state_proj, step_proj, carried, scan_consts))
        carried = second.after(scanned[-1][4])
    while second.step < half:
        second.hop()
    second_full = second.result()
    gate_full, out_full = second_full[:, :channels], second_full[:, channels:]
    mixed = jnp.concatenate([block[0] for block in scanned], axis=0)

    gate_proj = dot(normed_all, gate_full, rows_dot)
    gated = mixed * (gate_proj * jax.nn.sigmoid(gate_proj))
    gate_out_grad = dot(cot_all, out_full, rows_dot)
    sums = jnp.stack([jnp.sum(gated * gated, axis=1), jnp.sum(gate_out_grad * gate_gain * gated, axis=1)])
    sums = (sums + across(sums, 1)) + (across(sums, 2) + across(sums, 3))
    gate_scale = lax.rsqrt(sums[0] / inner_total + epsilon)
    scales = jnp.stack([gate_scale, gate_scale**3 * (sums[1] / inner_total)], axis=1)
    gate_out, gate_grad, mixed_grad, gain_sum = run_gate(mixed, gate_proj, gate_out_grad, scales, gate_gain[None, :])

    normed_t = normed_all.T
    pair_ring = Scatter(ring, *partials(ring, (cot_all.T, normed_t), (gate_out, gate_grad)))
    branch_part = dot(gate_out, out_full, back_dot)
    back_consts = (conv_input, conv_state, per_head(step_bias), per_head(rates), skip, head_of)
    carry = (
        jnp.zeros((8, channels), f32), jnp.zeros((8, 2 * STATE), f32),
        jnp.zeros((channels // LANES, LANES, STATE), f32), jnp.zeros((8, LANES), f32),
    )
    done = []
    pair_sum = None
    for turn in range(blocks):
        if turn > 0 and pair_sum is None:
            pair_sum = pair_ring.add()
        if turn == 0:
            carry, branch_part = pair_ring.before(carry, branch_part)
        elif pair_sum is None:
            carry = pair_ring.before(carry)
        if pair_sum is None:
            pair_ring.hop()
        start = blocks - 1 - turn
        kept = scanned[start // span]
        kept = [kept[1], kept[2], kept[0], kept[3]]
        result = run_scan_back(
            start, 1, (input_proj, state_proj, step_proj), kept, start % span, mixed_grad, carry, back_consts
        )
        done.insert(0, result)
        carry = tuple(result[6:])
    branch = lax.psum_scatter(branch_part, "tensor", scatter_dimension=0, tiled=True)
    block_output = block_input + branch
    while pair_sum is None:
        pair_sum = pair_ring.add()
        if pair_sum is None:
            pair_ring.hop()
    input_back, state_back, step_back = (jnp.concatenate([d[i] for d in done], axis=0) for i in range(3))
    input_sums, state_sums, step_sums = (sum(d[i] for d in done) for i in range(3, 6))

    def state_columns(index):
        mine = lax.dynamic_slice_in_dim(state_back, index * share, share, 1)
        return jnp.concatenate([mine[i * folded : (i + 1) * folded] for i in range(fold)], axis=1)

    for_far = across(state_columns(me ^ 3), 1)
    for_me = across(state_columns(me ^ 1), 1)
    from_far = across(state_columns(me ^ 2) + for_far, 2)
    input_ring = Scatter(ring, *partials(ring, (normed_t,), (input_back,)))
    state_share = (state_columns(me) + for_me + from_far).astype(bf16)
    state_share = jnp.concatenate([state_share[:, i * share : (i + 1) * share] for i in range(fold)], axis=0)
    tail = jnp.concatenate(
        [state_share, step_back[:, :heads], jnp.zeros((tokens, LANES - share - heads), bf16)], axis=1
    )
    tail_sum = lax.psum_scatter(dot(normed_t, tail, rows_dot), "dp", scatter_dimension=0, tiled=True)

    def normed_rows(index):
        gate_rows, input_rows, tail_rows = (
            lax.dynamic_slice_in_dim(array, index * local_rows, local_rows, 0)
            for array in (gate_grad, input_back, tail)
        )
        part = dot(gate_rows, gate_full, back_dot) + dot(input_rows, input_full, back_dot)
        return part + dot(tail_rows, tail_full, back_dot)

    input_ring.hop()
    for_far = across(normed_rows(me ^ 3), 1)
    for_me = across(normed_rows(me ^ 1), 1)
    input_ring.add()
    input_ring.hop()
    for_far = normed_rows(me ^ 2) + for_far
    from_far = across(encode(for_far, jnp.max(jnp.abs(for_far), axis=0, keepdims=True)), 2)
    normed_grad = normed_rows(me) + for_me
    input_sum = None
    while input_sum is None:
        input_sum = input_ring.add()
        if input_sum is None:
            input_ring.hop()
    normed_grad = normed_grad + decode(from_far)[0]

    weighted_grad = normed_grad * norm_gain
    norm_gain_part = jnp.sum(normed_grad * block_input * row_scale, axis=0)
    input_grad = (
        cotangent
        + row_scale * weighted_grad
        - block_input * row_scale**3 * jnp.mean(weighted_grad * block_input, axis=1, keepdims=True)
    )
    state_grad = lax.all_gather(tail_sum[:, :share], "tensor", axis=1, tiled=True)

    shared = jnp.concatenate([norm_gain_part, state_sums[:5].reshape(-1)])
    local = jnp.concatenate(
        [
            input_sums[:5].reshape(-1),
            gain_sum[0],
            jnp.sum(input_sums[5].reshape(heads, HEAD_DIM), axis=1),
            step_sums[0, :heads],
            step_sums[1, :heads] * rates,
        ]
    )
    packed = jnp.concatenate([shared, local])
    packed = jnp.pad(packed, (0, -packed.shape[0] % (8 * LANES))).reshape(-1, LANES)
    packed = cube_sum(packed, "dp")
    local = packed.reshape(-1)[shared.shape[0] :]
    shared = cube_sum(packed[: -(-shared.shape[0] // (8 * LANES)) * 8], "tensor").reshape(-1)
    width = block_input.shape[1]
    state_sum = shared[width : width + 10 * STATE].reshape(5, 2 * STATE)
    at = 6 * channels
    return (
        block_output,
        input_grad,
        shared[:width],
        pair_sum[:, channels:],
        input_sum,
        state_grad,
        tail_sum[:, share : share + heads],
        local[: 4 * channels].reshape(4, channels),
        local[4 * channels : 5 * channels],
        state_sum[:4],
        state_sum[4],
        local[at + heads : at + 2 * heads],
        local[at + 2 * heads : at + 3 * heads],
        local[at : at + heads],
        local[5 * channels : at],
        pair_sum[:, :channels].T,
    )


def solution(mesh):
    rows = P(("dp", "tensor"), None)
    both = P("dp", "tensor")
    inner = P("tensor")
    return jax.shard_map(
        shards,
        mesh=mesh,
        in_specs=(
            rows, rows, P(), both, both, P("dp", None), both, P(None, "tensor"), inner, P(), P(), inner, inner,
            inner, inner, P("tensor", "dp"),
        ),
        out_specs=(
            rows, rows, P(), both, both, P("dp", None), both, P(None, "tensor"), inner, P(), P(), inner, inner,
            inner, inner, P("tensor", "dp"),
        ),
        check_vma=False,
    )
```

```python
import jax
import jax.numpy as jnp
from jax import lax
from jax.experimental import pallas as pl
from jax.experimental.pallas import tpu as pltpu
from jax.sharding import PartitionSpec as P

HEAD_DIM = 64
STATE = 128
BLOCK = 256
SEQ = 1024
LANES = 128

epsilon = 1e-05
high = lax.Precision.HIGH
highest = lax.Precision.HIGHEST
f32 = jnp.float32
bf16 = jnp.bfloat16


def dot(left, right, dims, precision=None):
    return lax.dot_general(
        left, right, (dims, ((), ())), precision=precision, preferred_element_type=f32
    )


def sigmoid(v):
    return 1.0 / (1.0 + jnp.exp(-v))


def softplus(v):
    return jnp.maximum(v, 0.0) + jnp.log1p(jnp.exp(-jnp.abs(v)))


def iota(shape, axis):
    return lax.broadcasted_iota(jnp.int32, shape, axis)


def pair_columns(table, pair):
    lane = iota((table.shape[0], LANES), 1)
    return jnp.where(lane < HEAD_DIM, table[:, 2 * pair : 2 * pair + 1], table[:, 2 * pair + 1 : 2 * pair + 2])


def decay_tables(step_rows, step_bias, rates):
    step_size = softplus(step_rows + step_bias)
    earlier = (iota((BLOCK, BLOCK), 0) >= iota((BLOCK, BLOCK), 1)).astype(f32)
    cumulative = dot(earlier, step_size * rates, ((1,), (0,)), highest)
    return step_size, cumulative, jnp.exp(cumulative), jnp.exp(cumulative[BLOCK - 1 : BLOCK, :] - cumulative)


def state_decay(from_start, pair):
    last = from_start[BLOCK - 1 : BLOCK, :]
    row = iota((LANES, STATE), 0)
    return jnp.where(row < HEAD_DIM, last[:, 2 * pair : 2 * pair + 1], last[:, 2 * pair + 1 : 2 * pair + 2])


def shifted_conv(rows_ref, before, buffer, taps, conv_bias, first):
    @pl.when(first)
    def _():
        buffer[0:8, :] = before[...]

    @pl.when(jnp.logical_not(first))
    def _():
        buffer[0:8, :] = buffer[BLOCK : BLOCK + 8, :]

    buffer[8 : BLOCK + 8, :] = rows_ref[...]
    total = conv_bias[...] + taps[0:1, :] * buffer[8 : BLOCK + 8, :]
    for tap in range(1, 4):
        total = total + taps[tap : tap + 1, :] * buffer[8 - tap : BLOCK + 8 - tap, :]
    return total


def scan_kernel(
    input_rows, state_rows, step_rows, input_before, state_before, state_entering,
    conv_input, conv_input_bias, conv_state, conv_state_bias, step_bias, rates, skip,
    mixed, input_conv, state_conv, entering, carried, input_buffer, state_buffer,
):
    first = pl.program_id(0) == 0
    pairs = input_rows.shape[1] // LANES

    @pl.when(first)
    def _():
        carried[...] = state_entering[...]

    input_conv[...] = shifted_conv(input_rows, input_before, input_buffer, conv_input, conv_input_bias, first)
    state_pre = shifted_conv(state_rows, state_before, state_buffer, conv_state, conv_state_bias, first)
    state_conv[...] = state_pre
    state_act = state_pre * sigmoid(state_pre)
    writes, reads = state_act[:, :STATE], state_act[:, STATE:]
    meeting = dot(reads, writes, ((1,), (1,)), high)
    step_size, cumulative, from_start, to_end = decay_tables(step_rows[...], step_bias[...], rates[...])
    cumulative_t = cumulative.T
    causal = iota((BLOCK, BLOCK), 0) >= iota((BLOCK, BLOCK), 1)
    lane = iota((BLOCK, LANES), 1)
    for pair in range(pairs):
        columns = slice(pair * LANES, pair * LANES + LANES)
        pre = input_conv[:, columns]
        inputs = pre * sigmoid(pre)
        weighted = inputs * pair_columns(step_size, pair)
        state_in = carried[pair]
        entering[0, pair] = state_in
        out = dot(reads, state_in, ((1,), (1,)), high) * pair_columns(from_start, pair)
        for side in range(2):
            head = 2 * pair + side
            gap = cumulative[:, head : head + 1] - cumulative_t[head : head + 1, :]
            mixing = jnp.exp(jnp.where(causal, gap, -1e30)) * meeting
            mine = (lane < HEAD_DIM) if side == 0 else (lane >= HEAD_DIM)
            out = out + dot(mixing, jnp.where(mine, weighted, 0.0), ((1,), (0,)), high)
        fresh = dot(weighted * pair_columns(to_end, pair), writes, ((0,), (0,)), high)
        carried[pair] = state_decay(from_start, pair) * state_in + fresh
        mixed[:, columns] = out + skip[:, columns] * inputs


def scan_back_kernel(
    input_rows, state_rows, step_rows, input_conv, state_conv, mixed, entering, mixed_grad,
    input_after, state_after, state_leaving, decay_after,
    conv_input, conv_state, step_bias, rates, skip, head_of,
    input_grad, state_grad, step_grad, input_sums, state_sums, step_sums, input_first, state_first, carried, later,
    input_buffer, state_buffer, gap_grad, out_products, in_products,
):
    first = pl.program_id(0) == 0
    pairs = input_rows.shape[1] // LANES

    @pl.when(first)
    def _():
        carried[...] = state_leaving[...]
        later[...] = decay_after[...]
        input_sums[...] = jnp.zeros(input_sums.shape, f32)
        state_sums[...] = jnp.zeros(state_sums.shape, f32)
        step_sums[...] = jnp.zeros(step_sums.shape, f32)
        input_buffer[BLOCK : BLOCK + 8, :] = input_after[...]
        state_buffer[BLOCK : BLOCK + 8, :] = state_after[...]

    @pl.when(jnp.logical_not(first))
    def _():
        input_buffer[BLOCK : BLOCK + 8, :] = input_buffer[0:8, :]
        state_buffer[BLOCK : BLOCK + 8, :] = state_buffer[0:8, :]

    state_pre = state_conv[...]
    state_sig = sigmoid(state_pre)
    state_act = state_pre * state_sig
    writes, reads = state_act[:, :STATE], state_act[:, STATE:]
    meeting_t = dot(writes, reads, ((1,), (1,)), high)
    step_size, cumulative, from_start, to_end = decay_tables(step_rows[...], step_bias[...], rates[...])
    cumulative_t = cumulative.T
    causal_t = iota((BLOCK, BLOCK), 0) <= iota((BLOCK, BLOCK), 1)
    lane = iota((BLOCK, LANES), 1)
    gap_grad[...] = jnp.zeros(gap_grad.shape, f32)
    writes_grad = jnp.zeros((BLOCK, STATE), f32)
    reads_grad = jnp.zeros((BLOCK, STATE), f32)
    for pair in range(pairs):
        columns = slice(pair * LANES, pair * LANES + LANES)
        pre = input_conv[:, columns]
        sig = sigmoid(pre)
        inputs = pre * sig
        step_pair = pair_columns(step_size, pair)
        weighted = inputs * step_pair
        out_grad = mixed_grad[:, columns]
        skip_product = out_grad * inputs
        input_sums[5:6, columns] += jnp.sum(skip_product, axis=0, keepdims=True)
        end_pair = pair_columns(to_end, pair)
        leaving_grad = carried[pair]
        weighted_grad = dot(writes, leaving_grad, ((1,), (1,)), high) * end_pair
        for side in range(2):
            head = 2 * pair + side
            gap = cumulative_t[head : head + 1, :] - cumulative[:, head : head + 1]
            within = jnp.exp(jnp.where(causal_t, gap, -1e30))
            mine = (lane < HEAD_DIM) if side == 0 else (lane >= HEAD_DIM)
            own_grad = jnp.where(mine, out_grad, 0.0)
            weighted_grad = weighted_grad + dot(within * meeting_t, own_grad, ((1,), (0,)), high)
            gap_grad[...] += within * dot(weighted, own_grad, ((1,), (1,)), high)
        start_grad = out_grad * pair_columns(from_start, pair)
        reads_grad = reads_grad + dot(start_grad, entering[0, pair], ((1,), (0,)), high)
        writes_grad = writes_grad + dot(weighted * end_pair, leaving_grad, ((1,), (0,)), high)
        carried[pair] = state_decay(from_start, pair) * leaving_grad + dot(start_grad, reads, ((0,), (0,)), high)
        out_products[:, columns] = out_grad * mixed[:, columns] - skip[:, columns] * skip_product
        in_products[:, columns] = inputs * weighted_grad
        inputs_grad = skip[:, columns] * out_grad + step_pair * weighted_grad
        input_buffer[0:BLOCK, columns] = inputs_grad * (sig * (1.0 + pre * (1.0 - sig)))
    reads_grad = reads_grad + dot(gap_grad[...], writes, ((0,), (0,)), high)
    writes_grad = writes_grad + dot(gap_grad[...], reads, ((1,), (0,)), high)
    state_slope = state_sig * (1.0 + state_pre * (1.0 - state_sig))
    state_buffer[0:BLOCK, 0:STATE] = writes_grad * state_slope[:, :STATE]
    state_buffer[0:BLOCK, STATE : 2 * STATE] = reads_grad * state_slope[:, STATE:]

    for buffer, rows, taps, sums, result in (
        (input_buffer, input_rows, conv_input, input_sums, input_grad),
        (state_buffer, state_rows, conv_state, state_sums, state_grad),
    ):
        raw = rows[...]
        total = jnp.zeros(raw.shape, f32)
        for tap in range(4):
            ahead = buffer[tap : tap + BLOCK, :]
            total = total + taps[tap : tap + 1, :] * ahead
            sums[tap : tap + 1, :] += jnp.sum(ahead * raw, axis=0, keepdims=True)
        sums[4:5, :] += jnp.sum(buffer[0:BLOCK, :], axis=0, keepdims=True)
        result[...] = total.astype(result.dtype)
    input_first[...] = input_buffer[0:8, :]
    state_first[...] = state_buffer[0:8, :]

    out_head = dot(out_products[...], head_of[...], ((1,), (0,)), high)
    in_head = dot(in_products[...], head_of[...], ((1,), (0,)), high)
    upper = (iota((BLOCK, BLOCK), 0) <= iota((BLOCK, BLOCK), 1)).astype(f32)
    decay_grad = dot(upper, out_head - step_size * in_head, ((1,), (0,)), highest) + later[0:1, :]
    later[0:1, :] = decay_grad[0:1, :]
    step_sig = sigmoid(step_rows[...] + step_bias[...])
    step_back = (rates[...] * decay_grad + in_head) * step_sig
    step_grad[...] = step_back.astype(step_grad.dtype)
    step_sums[0:1, :] += jnp.sum(step_back, axis=0, keepdims=True)
    step_sums[1:2, :] += jnp.sum(step_size * decay_grad, axis=0, keepdims=True)


def whole(array):
    zeros = (0,) * array.ndim
    return pl.BlockSpec(array.shape, lambda k: zeros)


params = pltpu.CompilerParams(dimension_semantics=("arbitrary",), vmem_limit_bytes=48 * 1024 * 1024)


little = pl.CostEstimate(flops=10**6, bytes_accessed=2**16, transcendentals=0)


def run_scan(start, span, input_rows, state_rows, step_rows, state_entering, consts):
    channels = input_rows.shape[1]
    pairs = channels // LANES
    rows = span * BLOCK
    edge = start * BLOCK // 8 - 1

    def tokens(width):
        return pl.BlockSpec((BLOCK, width), lambda k: (start + k, 0))

    def results(width):
        return pl.BlockSpec((BLOCK, width), lambda k: (k, 0))

    if start == 0:
        before = (jnp.zeros((8, channels), f32), jnp.zeros((8, 2 * STATE), f32))
        before_specs = [whole(c) for c in before]
    else:
        before = (input_rows, state_rows)
        before_specs = [pl.BlockSpec((8, c.shape[1]), lambda k: (edge, 0)) for c in before]
    return pl.pallas_call(
        scan_kernel,
        grid=(span,),
        in_specs=[tokens(channels), tokens(2 * STATE), tokens(LANES)] + before_specs + [whole(state_entering)]
        + [whole(c) for c in consts],
        out_specs=[
            results(channels), results(channels), results(2 * STATE),
            pl.BlockSpec((1, pairs, LANES, STATE), lambda k: (k, 0, 0, 0)), whole(state_entering),
        ],
        out_shape=[
            jax.ShapeDtypeStruct((rows, channels), f32),
            jax.ShapeDtypeStruct((rows, channels), f32),
            jax.ShapeDtypeStruct((rows, 2 * STATE), f32),
            jax.ShapeDtypeStruct((span, pairs, LANES, STATE), f32),
            jax.ShapeDtypeStruct((pairs, LANES, STATE), f32),
        ],
        scratch_shapes=[pltpu.VMEM((BLOCK + 8, channels), f32), pltpu.VMEM((BLOCK + 8, 2 * STATE), f32)],
        compiler_params=params,
        cost_estimate=little,
        name="scan",
    )(input_rows, state_rows, step_rows, *before, state_entering, *consts)


def run_scan_back(start, span, projections, kept, at, mixed_grad, carry, consts):
    channels = mixed_grad.shape[1]
    pairs = channels // LANES
    rows = span * BLOCK

    def tokens(width):
        return pl.BlockSpec((BLOCK, width), lambda k: (start + span - 1 - k, 0))

    def own(width, first=0):
        return pl.BlockSpec((BLOCK, width), lambda k: (first + span - 1 - k, 0))

    def shape(*dims):
        return jax.ShapeDtypeStruct(dims, f32)

    sums = [shape(8, channels), shape(8, 2 * STATE), shape(8, LANES)]
    ends = [jax.ShapeDtypeStruct(c.shape, f32) for c in carry]
    return pl.pallas_call(
        scan_back_kernel,
        grid=(span,),
        in_specs=[
            tokens(channels), tokens(2 * STATE), tokens(LANES), own(channels, at),
            own(2 * STATE, at), own(channels, at),
            pl.BlockSpec((1, pairs, LANES, STATE), lambda k: (at + span - 1 - k, 0, 0, 0)), tokens(channels),
        ] + [whole(c) for c in carry] + [whole(c) for c in consts],
        out_specs=[own(channels), own(2 * STATE), own(LANES)] + [whole(c) for c in sums + ends],
        out_shape=[
            jax.ShapeDtypeStruct((rows, channels), bf16), shape(rows, 2 * STATE),
            jax.ShapeDtypeStruct((rows, LANES), bf16),
        ] + sums + ends,
        scratch_shapes=[
            pltpu.VMEM((BLOCK + 8, channels), f32), pltpu.VMEM((BLOCK + 8, 2 * STATE), f32),
            pltpu.VMEM((BLOCK, BLOCK), f32), pltpu.VMEM((BLOCK, channels), f32), pltpu.VMEM((BLOCK, channels), f32),
        ],
        compiler_params=params,
        cost_estimate=little,
        name="scan_back",
    )(*projections, *kept, mixed_grad, *carry, *consts)


def gate_kernel(mixed, gate_proj, out_grad, scales, gain, gate_out, gate_grad, mixed_grad, gain_sum):
    @pl.when(pl.program_id(0) == 0)
    def _():
        gain_sum[...] = jnp.zeros(gain_sum.shape, f32)

    proj, rows_mixed, grad = gate_proj[...], mixed[...], out_grad[...]
    sig = sigmoid(proj)
    act = proj * sig
    gated = rows_mixed * act
    scale, pull = scales[:, 0:1], scales[:, 1:2]
    scaled = gated * scale
    gate_out[...] = (scaled * gain[...]).astype(bf16)
    gain_sum[0:1, :] += jnp.sum(grad * scaled, axis=0, keepdims=True)
    gated_grad = scale * (grad * gain[...]) - gated * pull
    mixed_grad[...] = gated_grad * act
    back = gated_grad * rows_mixed * (sig * (1.0 + proj * (1.0 - sig)))
    gate_grad[...] = back.astype(bf16)


def run_gate(mixed, gate_proj, out_grad, scales, gain):
    rows, channels = mixed.shape
    tokens = pl.BlockSpec((BLOCK, channels), lambda k: (k, 0))
    small = jax.ShapeDtypeStruct((8, channels), f32)
    return pl.pallas_call(
        gate_kernel,
        grid=(rows // BLOCK,),
        in_specs=[tokens, tokens, tokens, pl.BlockSpec((BLOCK, 2), lambda k: (k, 0)), whole(gain)],
        out_specs=[tokens, tokens, tokens, whole(small)],
        out_shape=[
            jax.ShapeDtypeStruct((rows, channels), bf16), jax.ShapeDtypeStruct((rows, channels), bf16),
            jax.ShapeDtypeStruct((rows, channels), f32), small,
        ],
        compiler_params=params,
        cost_estimate=little,
        name="gate",
    )(mixed, gate_proj, out_grad, scales, gain)


def assemble_kernel(places, *refs):
    result = refs[-1]
    for i, piece in enumerate(refs[:-1]):
        result[pl.ds(pl.multiple_of(places[i], 16), piece.shape[0]), :] = piece[...]


def assemble(pieces, places, rows):
    def fixed(n, _):
        return (0, 0)

    width = pieces[0].shape[1]
    return pl.pallas_call(
        assemble_kernel,
        grid_spec=pltpu.PrefetchScalarGridSpec(
            num_scalar_prefetch=1, grid=(1,), in_specs=[pl.BlockSpec(piece.shape, fixed) for piece in pieces],
            out_specs=pl.BlockSpec((rows, width), fixed),
        ),
        out_shape=jax.ShapeDtypeStruct((rows, width), pieces[0].dtype),
        compiler_params=params,
        cost_estimate=little,
        name="assemble",
    )(jnp.stack(places).astype(jnp.int32), *pieces)


def partial_kernel(count, steps, places, *refs):
    lefts, rights, (result, top) = refs[:count], refs[count : 2 * count], refs[2 * count :]
    owners, rows = result.shape[0], result.shape[1]
    for i in range(count):

        @pl.when(pl.program_id(0) // steps == i)
        def _():
            product = dot(lefts[i][...], rights[i][...], ((1,), (0,)))
            for owner in range(owners):
                own = product[owner * rows : (owner + 1) * rows]
                result[places[owner]] = own
                top[places[owner]] = jnp.broadcast_to(jnp.max(jnp.abs(own), axis=0, keepdims=True), top.shape[1:])


def partials(ring, lefts, rights):
    width = rights[0].shape[1]
    tile = min(width, 2 * LANES)
    steps, count = width // tile, len(lefts)
    rows = lefts[0].shape[0] // ring.count
    order = cycle(ring.count)
    places = [(order.index(i) - ring.place + ring.count) % ring.count for i in range(ring.count)]

    def column(i):
        return lambda n, _: (0, jnp.clip(n - i * steps, 0, steps - 1))

    def fixed(n, _):
        return (0, 0)

    return pl.pallas_call(
        lambda *refs: partial_kernel(count, steps, *refs),
        grid_spec=pltpu.PrefetchScalarGridSpec(
            num_scalar_prefetch=1, grid=(count * steps,),
            in_specs=[pl.BlockSpec(left.shape, fixed) for left in lefts]
            + [pl.BlockSpec((right.shape[0], tile), column(i)) for i, right in enumerate(rights)],
            out_specs=[
                pl.BlockSpec((ring.count, rows, tile), lambda n, _: (0, 0, n)),
                pl.BlockSpec((ring.count, 8, tile), lambda n, _: (0, 0, n)),
            ],
        ),
        out_shape=[
            jax.ShapeDtypeStruct((ring.count, rows, count * width), f32),
            jax.ShapeDtypeStruct((ring.count, 8, count * width), f32),
        ],
        compiler_params=params,
        cost_estimate=little,
        name="partials",
    )(jnp.stack(places).astype(jnp.int32), *lefts, *rights)


def normed_kernel(places, gate_rows, input_rows, tail_rows, gate_tile, input_tile, tail_tile, result):
    product = dot(gate_rows[...], gate_tile[...], ((1,), (1,)))
    product = product + dot(input_rows[...], input_tile[...], ((1,), (1,)))
    product = product + dot(tail_rows[...], tail_tile[...], ((1,), (1,)))
    rows = result.shape[1]
    for owner in range(result.shape[0]):
        result[places[owner]] = product[owner * rows : (owner + 1) * rows]


def normed_parts(me, gate_grad, input_back, tail, second_full, first_full):
    count = lax.axis_size("tensor")
    tokens, channels = gate_grad.shape
    width, tile = first_full.shape[0], 2 * LANES
    places = jnp.stack([i ^ me for i in range(count)]).astype(jnp.int32)

    def fixed(n, _):
        return (0, 0)

    return pl.pallas_call(
        normed_kernel,
        grid_spec=pltpu.PrefetchScalarGridSpec(
            num_scalar_prefetch=1, grid=(width // tile,),
            in_specs=[
                pl.BlockSpec((tokens, channels), fixed), pl.BlockSpec((tokens, channels), fixed),
                pl.BlockSpec((tokens, LANES), fixed), pl.BlockSpec((tile, channels), lambda n, _: (n, 0)),
                pl.BlockSpec((tile, channels), lambda n, _: (n, 0)),
                pl.BlockSpec((tile, LANES), lambda n, _: (n, channels // LANES)),
            ],
            out_specs=pl.BlockSpec((count, tokens // count, tile), lambda n, _: (0, 0, n)),
        ),
        out_shape=jax.ShapeDtypeStruct((count, tokens // count, width), f32),
        compiler_params=params,
        cost_estimate=little,
        name="normed_parts",
    )(places, gate_grad, input_back, tail, second_full, first_full, first_full)


def cycle(count):
    return list(range(0, count, 2)) + list(range(count - 1, 0, -2))


class Ring:
    def __init__(self):
        self.count = lax.axis_size("dp")
        order = cycle(self.count)
        self.up = [(order[i], order[(i + 1) % self.count]) for i in range(self.count)]
        self.down = [(b, a) for a, b in self.up]
        me = lax.axis_index("dp")
        self.place = jnp.where(me % 2 == 0, me // 2, self.count - 1 - me // 2)

    def owner(self, offset):
        place = (self.place + offset + self.count) % self.count
        return jnp.where(place < self.count // 2, 2 * place, 2 * (self.count - 1 - place) + 1)


def middle(rows):
    return (rows // 2 + 15) // 16 * 16


class Gather:
    def __init__(self, ring, shard):
        self.ring, self.shard, self.step = ring, shard, 0
        self.held = [(shard, 0, 0)]
        self.last = (shard, shard)

    def hop(self):
        self.step += 1
        half, cut = self.ring.count // 2, middle(self.shard.shape[0])
        up, down = self.last
        offsets = ((-self.step, 0), (self.step, 0))
        if self.step == half:
            up, down = up[:cut], down[cut:]
            offsets = ((half, 0), (half, cut))
        self.last = (lax.ppermute(up, "dp", self.ring.up), lax.ppermute(down, "dp", self.ring.down))
        self.held += [(piece, *offset) for piece, offset in zip(self.last, offsets)]

    def after(self, *marks):
        self.last, marks = fence(self.last, marks)
        self.held[-2:] = [(piece, *old[1:]) for piece, old in zip(self.last, self.held[-2:])]
        return marks if len(marks) > 1 else marks[0]

    def result(self):
        rows = self.shard.shape[0]
        pieces = [piece for piece, _, _ in self.held]
        places = [self.ring.owner(offset) * rows + skip for _, offset, skip in self.held]
        return assemble(pieces, places, rows * self.ring.count)


def encode(rows, limit):
    power = jnp.ceil(jnp.log2(jnp.maximum(limit, 1e-30)))
    scaled = rows * jnp.exp2(15.0 - power)
    return jnp.concatenate([scaled, jnp.broadcast_to(power, (16, rows.shape[1]))], axis=0).astype(jnp.float16)


def decode(payload):
    power = payload[-16:-15].astype(f32)
    return payload[:-16].astype(f32) * jnp.exp2(power - 15.0), jnp.exp2(power)


class Scatter:
    def __init__(self, ring, parts, tops):
        self.ring, self.parts, self.tops = ring, parts, tops
        self.step = ring.count // 2
        self.cut = middle(parts.shape[1])
        far, top = parts[self.step], tops[self.step, 0:1]
        self.send = (encode(far[: self.cut], top), encode(far[self.cut :], top))

    def hop(self):
        self.got = (lax.ppermute(self.send[0], "dp", self.ring.up), lax.ppermute(self.send[1], "dp", self.ring.down))

    def after(self, *marks):
        self.got, marks = fence(self.got, marks)
        return marks if len(marks) > 1 else marks[0]

    def before(self, *marks):
        self.send, marks = fence(self.send, marks)
        return marks if len(marks) > 1 else marks[0]

    def add(self):
        first = self.step == self.ring.count // 2
        (up, up_top), (down, down_top) = (decode(g) for g in self.got)
        if first:
            rest = down.shape[0]
            up, down = jnp.pad(up, ((0, rest), (0, 0))), jnp.pad(down, ((self.cut, 0), (0, 0)))
        self.step -= 1
        if self.step == 0:
            return self.parts[0] + up + down
        above, below = self.step, self.ring.count - self.step
        self.send = (
            encode(self.parts[above] + up, self.tops[above, 0:1] + up_top),
            encode(self.parts[below] + down, self.tops[below, 0:1] + down_top),
        )
        return None


def fence(*arrays):
    flat, tree = jax.tree.flatten(arrays)
    return jax.tree.unflatten(tree, lax.optimization_barrier(flat))


def across(array, bit, axis="tensor"):
    count = lax.axis_size(axis)
    return lax.ppermute(array, axis, [(i, i ^ bit) for i in range(count)])


def cube_sum(array, axis):
    bit = 1
    while bit < lax.axis_size(axis):
        array = array + across(array, bit, axis)
        bit *= 2
    return array


def shards(
    block_input, cotangent, norm_gain, gate_weight, input_weight, state_weight, step_weight, conv_input,
    conv_input_bias, conv_state, conv_state_bias, step_bias, decay_log, skip_scale, gate_gain, out_weight,
):
    group_count = lax.axis_size("tensor")
    me = lax.axis_index("tensor")
    ring = Ring()
    half = ring.count // 2
    local_rows = block_input.shape[0]
    channels = gate_gain.shape[0]
    heads = step_bias.shape[0]
    inner_total = channels * group_count
    share = 2 * STATE // group_count
    tokens = local_rows * group_count
    blocks = tokens // BLOCK
    fold = LANES // share
    folded = tokens // fold
    rows_dot = ((1,), (0,))
    back_dot = ((1,), (1,))

    state_mine = lax.dynamic_slice_in_dim(state_weight, me * share, share, 1)
    first = Gather(
        ring,
        jnp.concatenate(
            [input_weight, state_mine, jnp.pad(step_weight, ((0, 0), (0, LANES - share - heads)))], axis=1
        ).astype(bf16),
    )
    first.hop()
    row_scale = lax.rsqrt(jnp.mean(block_input * block_input, axis=1, keepdims=True) + epsilon)
    normed = (block_input * row_scale * norm_gain).astype(bf16)
    far = across(normed, 2)
    normed_pieces = (normed, across(normed, 1), far, across(far, 1))
    normed_all = assemble(normed_pieces, [(me ^ bits) * local_rows for bits in range(4)], tokens)
    second_weight = jnp.concatenate([gate_weight, out_weight.T], axis=1).astype(bf16)
    for _ in range(half - 2):
        first.hop()
    second_weight, cot_low = first.after(second_weight, cotangent.astype(bf16))
    first.hop()
    second = Gather(ring, second_weight)
    second.hop()
    cot_all = lax.all_gather(cot_low, "tensor", axis=0, tiled=True)
    first_full = first.result()

    input_full, tail_full = first_full[:, :channels], first_full[:, channels:]
    tail_proj = dot(normed_all, tail_full, rows_dot)
    step_proj = jnp.pad(tail_proj[:, share : share + heads], ((0, 0), (0, LANES - heads)))
    state_mine = jnp.concatenate([tail_proj[i * folded : (i + 1) * folded, :share] for i in range(fold)], axis=1)
    far = across(state_mine, 2)
    same_x, same_core, diagonal = across(state_mine, 1), far, across(far, 1)
    right_core = me % 2 == 1
    near = (jnp.where(right_core, same_x, state_mine), jnp.where(right_core, state_mine, same_x))
    away = (jnp.where(right_core, diagonal, same_core), jnp.where(right_core, same_core, diagonal))
    right_chip = me // 2 == 1
    state_parts = [jnp.where(right_chip, away[i], near[i]) for i in range(2)]
    state_parts += [jnp.where(right_chip, near[i], away[i]) for i in range(2)]
    state_proj = jnp.concatenate(
        [jnp.concatenate([p[:, i * share : (i + 1) * share] for p in state_parts], axis=1) for i in range(fold)], axis=0
    )
    input_proj = dot(normed_all, input_full, rows_dot)
    rates = -jnp.exp(decay_log)

    def per_head(vector):
        return jnp.pad(vector, (0, LANES - heads))[None, :]

    skip = jnp.repeat(skip_scale, HEAD_DIM)[None, :]
    head_of = (
        lax.broadcasted_iota(jnp.int32, (channels, LANES), 0) // HEAD_DIM
        == lax.broadcasted_iota(jnp.int32, (channels, LANES), 1)
    ).astype(f32)
    scan_consts = (
        conv_input, conv_input_bias[None, :], conv_state, conv_state_bias[None, :], per_head(step_bias),
        per_head(rates), skip,
    )
    carried = jnp.zeros((channels // LANES, LANES, STATE), f32)
    span = 2
    scanned = []
    input_proj = second.after(input_proj)
    for start in range(0, blocks, span):
        if second.step < half - 1:
            second.hop()
        scanned.append(run_scan(start, span, input_proj, state_proj, step_proj, carried, scan_consts))
        carried = second.after(scanned[-1][4])
    while second.step < half:
        second.hop()
    second_full = second.result()
    gate_full, out_full = second_full[:, :channels], second_full[:, channels:]
    mixed = jnp.concatenate([block[0] for block in scanned], axis=0)

    gate_proj = dot(normed_all, gate_full, rows_dot)
    gated = mixed * (gate_proj * jax.nn.sigmoid(gate_proj))
    gate_out_grad = dot(cot_all, out_full, rows_dot)
    sums = jnp.stack([jnp.sum(gated * gated, axis=1), jnp.sum(gate_out_grad * gate_gain * gated, axis=1)])
    sums = (sums + across(sums, 1)) + (across(sums, 2) + across(sums, 3))
    gate_scale = lax.rsqrt(sums[0] / inner_total + epsilon)
    scales = jnp.stack([gate_scale, gate_scale**3 * (sums[1] / inner_total)], axis=1)
    gate_out, gate_grad, mixed_grad, gain_sum = run_gate(mixed, gate_proj, gate_out_grad, scales, gate_gain[None, :])

    normed_t = normed_all.T
    pair_ring = Scatter(ring, *partials(ring, (cot_all.T, normed_t), (gate_out, gate_grad)))
    back_consts = (conv_input, conv_state, per_head(step_bias), per_head(rates), skip, head_of)
    carry = (
        jnp.zeros((8, channels), f32), jnp.zeros((8, 2 * STATE), f32),
        jnp.zeros((channels // LANES, LANES, STATE), f32), jnp.zeros((8, LANES), f32),
    )
    done = []
    pair_sum = None
    for turn in range(blocks):
        if turn > 0 and pair_sum is None:
            pair_sum = pair_ring.add()
        if pair_sum is None:
            carry = pair_ring.before(carry)
        if pair_sum is None:
            pair_ring.hop()
        start = blocks - 1 - turn
        kept = scanned[start // span]
        kept = [kept[1], kept[2], kept[0], kept[3]]
        result = run_scan_back(
            start, 1, (input_proj, state_proj, step_proj), kept, start % span, mixed_grad, carry, back_consts
        )
        done.insert(0, result)
        carry = tuple(result[6:])
        if turn == 0:
            branch_part = dot(fence(gate_out, carry)[0], out_full, back_dot)
            carry, branch_part = fence(carry, branch_part)
            branch = lax.psum_scatter(branch_part, "tensor", scatter_dimension=0, tiled=True)
    if pair_sum is None:
        done, branch = pair_ring.after(done, branch)
    block_output = block_input + branch
    while pair_sum is None:
        pair_sum = pair_ring.add()
        if pair_sum is None:
            pair_ring.hop()
    input_back, state_back, step_back = (jnp.concatenate([d[i] for d in done], axis=0) for i in range(3))
    input_sums, state_sums, step_sums = (sum(d[i] for d in done) for i in range(3, 6))

    def state_columns(index):
        mine = lax.dynamic_slice_in_dim(state_back, index * share, share, 1)
        return jnp.concatenate([mine[i * folded : (i + 1) * folded] for i in range(fold)], axis=1)

    for_far, for_me = across(state_columns(me ^ 3), 1), across(state_columns(me ^ 1), 1)
    input_ring = Scatter(ring, *partials(ring, (normed_t,), (input_back,)))
    for_far, for_me = input_ring.before(for_far, for_me)
    input_ring.hop()
    from_far = across(state_columns(me ^ 2) + for_far, 2)
    state_share = (state_columns(me) + for_me + from_far).astype(bf16)
    state_share = jnp.concatenate([state_share[:, i * share : (i + 1) * share] for i in range(fold)], axis=0)
    tail = jnp.concatenate(
        [state_share, step_back[:, :heads], jnp.zeros((tokens, LANES - share - heads), bf16)], axis=1
    )
    parts = normed_parts(me, gate_grad, input_back, tail, second_full, first_full)
    parts = input_ring.after(parts)
    tail_ring = Scatter(ring, *partials(ring, (normed_t,), (tail,)))
    input_ring.add()
    input_ring.send, tail_ring.send, parts = fence(input_ring.send, tail_ring.send, parts)
    input_ring.hop()
    tail_ring.hop()
    for_far, for_me = across(parts[3], 1), across(parts[1], 1)
    for_far = parts[2] + for_far
    sent = encode(for_far, jnp.max(jnp.abs(for_far), axis=0, keepdims=True))
    input_ring.got, tail_ring.got, sent = fence(input_ring.got, tail_ring.got, sent)
    from_far = across(sent, 2)
    input_sum = tail_sum = None
    while input_sum is None:
        input_sum = input_ring.add()
        tail_ring.add()
        if input_sum is None:
            input_ring.send, tail_ring.send = fence(input_ring.send, tail_ring.send)
            input_ring.hop()
        tail_ring.hop()
        if input_sum is None:
            input_ring.got, tail_ring.got = fence(input_ring.got, tail_ring.got)
    tail_sum = tail_ring.add()
    normed_grad = parts[0] + for_me + decode(from_far)[0]

    weighted_grad = normed_grad * norm_gain
    norm_gain_part = jnp.sum(normed_grad * block_input * row_scale, axis=0)
    input_grad = (
        cotangent
        + row_scale * weighted_grad
        - block_input * row_scale**3 * jnp.mean(weighted_grad * block_input, axis=1, keepdims=True)
    )
    shared = jnp.concatenate([norm_gain_part, state_sums[:5].reshape(-1)])
    local = jnp.concatenate(
        [
            input_sums[:5].reshape(-1),
            gain_sum[0],
            jnp.sum(input_sums[5].reshape(heads, HEAD_DIM), axis=1),
            step_sums[0, :heads],
            step_sums[1, :heads] * rates,
        ]
    )
    packed = jnp.concatenate([shared, local])
    packed = jnp.pad(packed, (0, -packed.shape[0] % (8 * LANES))).reshape(-1, LANES)
    packed = cube_sum(packed, "dp")
    local = packed.reshape(-1)[shared.shape[0] :]
    spread = [jnp.where(me == i, tail_sum[:, :share], 0.0) for i in range(group_count)]
    spread = jnp.concatenate(
        [jnp.concatenate(spread[i : i + fold], axis=1) for i in range(0, group_count, fold)]
        + [packed[: -(-shared.shape[0] // (8 * LANES)) * 8]], axis=0
    )
    spread = cube_sum(spread, "tensor")
    rows = tail_sum.shape[0]
    state_grad = jnp.concatenate([spread[i * rows : (i + 1) * rows] for i in range(group_count // fold)], axis=1)
    shared = spread[rows * group_count // fold :].reshape(-1)
    width = block_input.shape[1]
    state_sum = shared[width : width + 10 * STATE].reshape(5, 2 * STATE)
    at = 6 * channels
    return (
        block_output,
        input_grad,
        shared[:width],
        pair_sum[:, channels:],
        input_sum,
        state_grad,
        tail_sum[:, share : share + heads],
        local[: 4 * channels].reshape(4, channels),
        local[4 * channels : 5 * channels],
        state_sum[:4],
        state_sum[4],
        local[at + heads : at + 2 * heads],
        local[at + 2 * heads : at + 3 * heads],
        local[at : at + heads],
        local[5 * channels : at],
        pair_sum[:, :channels].T,
    )


def solution(mesh):
    rows = P(("dp", "tensor"), None)
    both = P("dp", "tensor")
    inner = P("tensor")
    return jax.shard_map(
        shards,
        mesh=mesh,
        in_specs=(
            rows, rows, P(), both, both, P("dp", None), both, P(None, "tensor"), inner, P(), P(), inner, inner,
            inner, inner, P("tensor", "dp"),
        ),
        out_specs=(
            rows, rows, P(), both, both, P("dp", None), both, P(None, "tensor"), inner, P(), P(), inner, inner,
            inner, inner, P("tensor", "dp"),
        ),
        check_vma=False,
    )
```

```python
import jax
import jax.numpy as jnp
from jax import lax
from jax.experimental import pallas as pl
from jax.experimental.pallas import tpu as pltpu
from jax.sharding import PartitionSpec as P

HEAD_DIM = 64
STATE = 128
BLOCK = 256
SEQ = 1024
LANES = 128

LIM_SCAN = 20
LIM_SCAN_BACK = 24
LIM_GATE = 20
LIM_ASSEMBLE = 24
LIM_PARTIALS = 32
LIM_NORMED_PARTS = 32

epsilon = 1e-05
high = lax.Precision.HIGH
highest = lax.Precision.HIGHEST
f32 = jnp.float32
bf16 = jnp.bfloat16


def dot(left, right, dims, precision=None):
    return lax.dot_general(
        left, right, (dims, ((), ())), precision=precision, preferred_element_type=f32
    )


def sigmoid(v):
    return 1.0 / (1.0 + jnp.exp(-v))


def softplus(v):
    return jnp.maximum(v, 0.0) + jnp.log1p(jnp.exp(-jnp.abs(v)))


def iota(shape, axis):
    return lax.broadcasted_iota(jnp.int32, shape, axis)


def pair_columns(table, pair):
    lane = iota((table.shape[0], LANES), 1)
    return jnp.where(lane < HEAD_DIM, table[:, 2 * pair : 2 * pair + 1], table[:, 2 * pair + 1 : 2 * pair + 2])


def decay_tables(step_rows, step_bias, rates):
    step_size = softplus(step_rows + step_bias)
    earlier = (iota((BLOCK, BLOCK), 0) >= iota((BLOCK, BLOCK), 1)).astype(f32)
    cumulative = dot(earlier, step_size * rates, ((1,), (0,)), highest)
    return step_size, cumulative, jnp.exp(cumulative), jnp.exp(cumulative[BLOCK - 1 : BLOCK, :] - cumulative)


def state_decay(from_start, pair):
    last = from_start[BLOCK - 1 : BLOCK, :]
    row = iota((LANES, STATE), 0)
    return jnp.where(row < HEAD_DIM, last[:, 2 * pair : 2 * pair + 1], last[:, 2 * pair + 1 : 2 * pair + 2])


def shifted_conv(rows_ref, before, buffer, taps, conv_bias, first):
    @pl.when(first)
    def _():
        buffer[0:8, :] = before[...]

    @pl.when(jnp.logical_not(first))
    def _():
        buffer[0:8, :] = buffer[BLOCK : BLOCK + 8, :]

    buffer[8 : BLOCK + 8, :] = rows_ref[...]
    total = conv_bias[...] + taps[0:1, :] * buffer[8 : BLOCK + 8, :]
    for tap in range(1, 4):
        total = total + taps[tap : tap + 1, :] * buffer[8 - tap : BLOCK + 8 - tap, :]
    return total


def scan_kernel(
    input_rows, state_rows, step_rows, input_before, state_before, state_entering,
    conv_input, conv_input_bias, conv_state, conv_state_bias, step_bias, rates, skip,
    mixed, input_conv, state_conv, entering, carried, input_buffer, state_buffer,
):
    first = pl.program_id(0) == 0
    pairs = input_rows.shape[1] // LANES

    @pl.when(first)
    def _():
        carried[...] = state_entering[...]

    input_conv[...] = shifted_conv(input_rows, input_before, input_buffer, conv_input, conv_input_bias, first)
    state_pre = shifted_conv(state_rows, state_before, state_buffer, conv_state, conv_state_bias, first)
    state_conv[...] = state_pre
    state_act = state_pre * sigmoid(state_pre)
    writes, reads = state_act[:, :STATE], state_act[:, STATE:]
    meeting = dot(reads, writes, ((1,), (1,)), high)
    step_size, cumulative, from_start, to_end = decay_tables(step_rows[...], step_bias[...], rates[...])
    cumulative_t = cumulative.T
    causal = iota((BLOCK, BLOCK), 0) >= iota((BLOCK, BLOCK), 1)
    lane = iota((BLOCK, LANES), 1)
    for pair in range(pairs):
        columns = slice(pair * LANES, pair * LANES + LANES)
        pre = input_conv[:, columns]
        inputs = pre * sigmoid(pre)
        weighted = inputs * pair_columns(step_size, pair)
        state_in = carried[pair]
        entering[0, pair] = state_in
        out = dot(reads, state_in, ((1,), (1,)), high) * pair_columns(from_start, pair)
        for side in range(2):
            head = 2 * pair + side
            gap = cumulative[:, head : head + 1] - cumulative_t[head : head + 1, :]
            mixing = jnp.exp(jnp.where(causal, gap, -1e30)) * meeting
            mine = (lane < HEAD_DIM) if side == 0 else (lane >= HEAD_DIM)
            out = out + dot(mixing, jnp.where(mine, weighted, 0.0), ((1,), (0,)), high)
        fresh = dot(weighted * pair_columns(to_end, pair), writes, ((0,), (0,)), high)
        carried[pair] = state_decay(from_start, pair) * state_in + fresh
        mixed[:, columns] = out + skip[:, columns] * inputs


def scan_back_kernel(
    input_rows, state_rows, step_rows, input_conv, state_conv, mixed, entering, mixed_grad,
    input_after, state_after, state_leaving, decay_after,
    conv_input, conv_state, step_bias, rates, skip, head_of,
    input_grad, state_grad, step_grad, input_sums, state_sums, step_sums, input_first, state_first, carried, later,
    input_buffer, state_buffer, gap_grad, out_products, in_products,
):
    first = pl.program_id(0) == 0
    pairs = input_rows.shape[1] // LANES

    @pl.when(first)
    def _():
        carried[...] = state_leaving[...]
        later[...] = decay_after[...]
        input_sums[...] = jnp.zeros(input_sums.shape, f32)
        state_sums[...] = jnp.zeros(state_sums.shape, f32)
        step_sums[...] = jnp.zeros(step_sums.shape, f32)
        input_buffer[BLOCK : BLOCK + 8, :] = input_after[...]
        state_buffer[BLOCK : BLOCK + 8, :] = state_after[...]

    @pl.when(jnp.logical_not(first))
    def _():
        input_buffer[BLOCK : BLOCK + 8, :] = input_buffer[0:8, :]
        state_buffer[BLOCK : BLOCK + 8, :] = state_buffer[0:8, :]

    state_pre = state_conv[...]
    state_sig = sigmoid(state_pre)
    state_act = state_pre * state_sig
    writes, reads = state_act[:, :STATE], state_act[:, STATE:]
    meeting_t = dot(writes, reads, ((1,), (1,)), high)
    step_size, cumulative, from_start, to_end = decay_tables(step_rows[...], step_bias[...], rates[...])
    cumulative_t = cumulative.T
    causal_t = iota((BLOCK, BLOCK), 0) <= iota((BLOCK, BLOCK), 1)
    lane = iota((BLOCK, LANES), 1)
    gap_grad[...] = jnp.zeros(gap_grad.shape, f32)
    writes_grad = jnp.zeros((BLOCK, STATE), f32)
    reads_grad = jnp.zeros((BLOCK, STATE), f32)
    for pair in range(pairs):
        columns = slice(pair * LANES, pair * LANES + LANES)
        pre = input_conv[:, columns]
        sig = sigmoid(pre)
        inputs = pre * sig
        step_pair = pair_columns(step_size, pair)
        weighted = inputs * step_pair
        out_grad = mixed_grad[:, columns]
        skip_product = out_grad * inputs
        input_sums[5:6, columns] += jnp.sum(skip_product, axis=0, keepdims=True)
        end_pair = pair_columns(to_end, pair)
        leaving_grad = carried[pair]
        weighted_grad = dot(writes, leaving_grad, ((1,), (1,)), high) * end_pair
        for side in range(2):
            head = 2 * pair + side
            gap = cumulative_t[head : head + 1, :] - cumulative[:, head : head + 1]
            within = jnp.exp(jnp.where(causal_t, gap, -1e30))
            mine = (lane < HEAD_DIM) if side == 0 else (lane >= HEAD_DIM)
            own_grad = jnp.where(mine, out_grad, 0.0)
            weighted_grad = weighted_grad + dot(within * meeting_t, own_grad, ((1,), (0,)), high)
            gap_grad[...] += within * dot(weighted, own_grad, ((1,), (1,)), high)
        start_grad = out_grad * pair_columns(from_start, pair)
        reads_grad = reads_grad + dot(start_grad, entering[0, pair], ((1,), (0,)), high)
        writes_grad = writes_grad + dot(weighted * end_pair, leaving_grad, ((1,), (0,)), high)
        carried[pair] = state_decay(from_start, pair) * leaving_grad + dot(start_grad, reads, ((0,), (0,)), high)
        out_products[:, columns] = out_grad * mixed[:, columns] - skip[:, columns] * skip_product
        in_products[:, columns] = inputs * weighted_grad
        inputs_grad = skip[:, columns] * out_grad + step_pair * weighted_grad
        input_buffer[0:BLOCK, columns] = inputs_grad * (sig * (1.0 + pre * (1.0 - sig)))
    reads_grad = reads_grad + dot(gap_grad[...], writes, ((0,), (0,)), high)
    writes_grad = writes_grad + dot(gap_grad[...], reads, ((1,), (0,)), high)
    state_slope = state_sig * (1.0 + state_pre * (1.0 - state_sig))
    state_buffer[0:BLOCK, 0:STATE] = writes_grad * state_slope[:, :STATE]
    state_buffer[0:BLOCK, STATE : 2 * STATE] = reads_grad * state_slope[:, STATE:]

    for buffer, rows, taps, sums, result in (
        (input_buffer, input_rows, conv_input, input_sums, input_grad),
        (state_buffer, state_rows, conv_state, state_sums, state_grad),
    ):
        raw = rows[...]
        total = jnp.zeros(raw.shape, f32)
        for tap in range(4):
            ahead = buffer[tap : tap + BLOCK, :]
            total = total + taps[tap : tap + 1, :] * ahead
            sums[tap : tap + 1, :] += jnp.sum(ahead * raw, axis=0, keepdims=True)
        sums[4:5, :] += jnp.sum(buffer[0:BLOCK, :], axis=0, keepdims=True)
        result[...] = total.astype(result.dtype)
    input_first[...] = input_buffer[0:8, :]
    state_first[...] = state_buffer[0:8, :]

    out_head = dot(out_products[...], head_of[...], ((1,), (0,)), high)
    in_head = dot(in_products[...], head_of[...], ((1,), (0,)), high)
    upper = (iota((BLOCK, BLOCK), 0) <= iota((BLOCK, BLOCK), 1)).astype(f32)
    decay_grad = dot(upper, out_head - step_size * in_head, ((1,), (0,)), highest) + later[0:1, :]
    later[0:1, :] = decay_grad[0:1, :]
    step_sig = sigmoid(step_rows[...] + step_bias[...])
    step_back = (rates[...] * decay_grad + in_head) * step_sig
    step_grad[...] = step_back.astype(step_grad.dtype)
    step_sums[0:1, :] += jnp.sum(step_back, axis=0, keepdims=True)
    step_sums[1:2, :] += jnp.sum(step_size * decay_grad, axis=0, keepdims=True)


def whole(array):
    zeros = (0,) * array.ndim
    return pl.BlockSpec(array.shape, lambda k: zeros)


def params(mebibytes):
    return pltpu.CompilerParams(dimension_semantics=("arbitrary",), vmem_limit_bytes=mebibytes * 1024 * 1024)


little = pl.CostEstimate(flops=10**6, bytes_accessed=2**16, transcendentals=0)


def run_scan(start, span, input_rows, state_rows, step_rows, state_entering, consts):
    channels = input_rows.shape[1]
    pairs = channels // LANES
    rows = span * BLOCK
    edge = start * BLOCK // 8 - 1

    def tokens(width):
        return pl.BlockSpec((BLOCK, width), lambda k: (start + k, 0))

    def results(width):
        return pl.BlockSpec((BLOCK, width), lambda k: (k, 0))

    if start == 0:
        before = (jnp.zeros((8, channels), f32), jnp.zeros((8, 2 * STATE), f32))
        before_specs = [whole(c) for c in before]
    else:
        before = (input_rows, state_rows)
        before_specs = [pl.BlockSpec((8, c.shape[1]), lambda k: (edge, 0)) for c in before]
    return pl.pallas_call(
        scan_kernel,
        grid=(span,),
        in_specs=[tokens(channels), tokens(2 * STATE), tokens(LANES)] + before_specs + [whole(state_entering)]
        + [whole(c) for c in consts],
        out_specs=[
            results(channels), results(channels), results(2 * STATE),
            pl.BlockSpec((1, pairs, LANES, STATE), lambda k: (k, 0, 0, 0)), whole(state_entering),
        ],
        out_shape=[
            jax.ShapeDtypeStruct((rows, channels), f32),
            jax.ShapeDtypeStruct((rows, channels), f32),
            jax.ShapeDtypeStruct((rows, 2 * STATE), f32),
            jax.ShapeDtypeStruct((span, pairs, LANES, STATE), f32),
            jax.ShapeDtypeStruct((pairs, LANES, STATE), f32),
        ],
        scratch_shapes=[pltpu.VMEM((BLOCK + 8, channels), f32), pltpu.VMEM((BLOCK + 8, 2 * STATE), f32)],
        compiler_params=params(LIM_SCAN),
        cost_estimate=little,
        name="scan",
    )(input_rows, state_rows, step_rows, *before, state_entering, *consts)


def run_scan_back(start, span, projections, kept, at, mixed_grad, carry, consts):
    channels = mixed_grad.shape[1]
    pairs = channels // LANES
    rows = span * BLOCK

    def tokens(width):
        return pl.BlockSpec((BLOCK, width), lambda k: (start + span - 1 - k, 0))

    def own(width, first=0):
        return pl.BlockSpec((BLOCK, width), lambda k: (first + span - 1 - k, 0))

    def shape(*dims):
        return jax.ShapeDtypeStruct(dims, f32)

    sums = [shape(8, channels), shape(8, 2 * STATE), shape(8, LANES)]
    ends = [jax.ShapeDtypeStruct(c.shape, f32) for c in carry]
    return pl.pallas_call(
        scan_back_kernel,
        grid=(span,),
        in_specs=[
            tokens(channels), tokens(2 * STATE), tokens(LANES), own(channels, at),
            own(2 * STATE, at), own(channels, at),
            pl.BlockSpec((1, pairs, LANES, STATE), lambda k: (at + span - 1 - k, 0, 0, 0)), tokens(channels),
        ] + [whole(c) for c in carry] + [whole(c) for c in consts],
        out_specs=[own(channels), own(2 * STATE), own(LANES)] + [whole(c) for c in sums + ends],
        out_shape=[
            jax.ShapeDtypeStruct((rows, channels), bf16), shape(rows, 2 * STATE),
            jax.ShapeDtypeStruct((rows, LANES), bf16),
        ] + sums + ends,
        scratch_shapes=[
            pltpu.VMEM((BLOCK + 8, channels), f32), pltpu.VMEM((BLOCK + 8, 2 * STATE), f32),
            pltpu.VMEM((BLOCK, BLOCK), f32), pltpu.VMEM((BLOCK, channels), f32), pltpu.VMEM((BLOCK, channels), f32),
        ],
        compiler_params=params(LIM_SCAN_BACK),
        cost_estimate=little,
        name="scan_back",
    )(*projections, *kept, mixed_grad, *carry, *consts)


def gate_kernel(mixed, gate_proj, out_grad, scales, gain, gate_out, gate_grad, mixed_grad, gain_sum):
    @pl.when(pl.program_id(0) == 0)
    def _():
        gain_sum[...] = jnp.zeros(gain_sum.shape, f32)

    proj, rows_mixed, grad = gate_proj[...], mixed[...], out_grad[...]
    sig = sigmoid(proj)
    act = proj * sig
    gated = rows_mixed * act
    scale, pull = scales[:, 0:1], scales[:, 1:2]
    scaled = gated * scale
    gate_out[...] = (scaled * gain[...]).astype(bf16)
    gain_sum[0:1, :] += jnp.sum(grad * scaled, axis=0, keepdims=True)
    gated_grad = scale * (grad * gain[...]) - gated * pull
    mixed_grad[...] = gated_grad * act
    back = gated_grad * rows_mixed * (sig * (1.0 + proj * (1.0 - sig)))
    gate_grad[...] = back.astype(bf16)


def run_gate(mixed, gate_proj, out_grad, scales, gain):
    rows, channels = mixed.shape
    tokens = pl.BlockSpec((BLOCK, channels), lambda k: (k, 0))
    small = jax.ShapeDtypeStruct((8, channels), f32)
    return pl.pallas_call(
        gate_kernel,
        grid=(rows // BLOCK,),
        in_specs=[tokens, tokens, tokens, pl.BlockSpec((BLOCK, 2), lambda k: (k, 0)), whole(gain)],
        out_specs=[tokens, tokens, tokens, whole(small)],
        out_shape=[
            jax.ShapeDtypeStruct((rows, channels), bf16), jax.ShapeDtypeStruct((rows, channels), bf16),
            jax.ShapeDtypeStruct((rows, channels), f32), small,
        ],
        compiler_params=params(LIM_GATE),
        cost_estimate=little,
        name="gate",
    )(mixed, gate_proj, out_grad, scales, gain)


def assemble_kernel(places, *refs):
    result = refs[-1]
    for i, piece in enumerate(refs[:-1]):
        result[pl.ds(pl.multiple_of(places[i], 16), piece.shape[0]), :] = piece[...]


def assemble(pieces, places, rows):
    def fixed(n, _):
        return (0, 0)

    width = pieces[0].shape[1]
    return pl.pallas_call(
        assemble_kernel,
        grid_spec=pltpu.PrefetchScalarGridSpec(
            num_scalar_prefetch=1, grid=(1,), in_specs=[pl.BlockSpec(piece.shape, fixed) for piece in pieces],
            out_specs=pl.BlockSpec((rows, width), fixed),
        ),
        out_shape=jax.ShapeDtypeStruct((rows, width), pieces[0].dtype),
        compiler_params=params(LIM_ASSEMBLE),
        cost_estimate=little,
        name="assemble",
    )(jnp.stack(places).astype(jnp.int32), *pieces)


def partial_kernel(count, steps, places, *refs):
    lefts, rights, result = refs[:count], refs[count : 2 * count], refs[2 * count]
    owners, rows = result.shape[0], result.shape[1] - 16
    for i in range(count):

        @pl.when(pl.program_id(0) // steps == i)
        def _():
            product = dot(lefts[i][...], rights[i][...], ((1,), (0,)))
            for owner in range(owners):
                own = product[owner * rows : (owner + 1) * rows]
                result[places[owner], 0:rows, :] = own
                top = jnp.max(jnp.abs(own), axis=0, keepdims=True)
                result[places[owner], rows : rows + 16, :] = jnp.broadcast_to(top, (16, own.shape[1]))


def partials(ring, lefts, rights):
    width = rights[0].shape[1]
    tile = min(width, 2 * LANES)
    steps, count = width // tile, len(lefts)
    rows = lefts[0].shape[0] // ring.count
    order = cycle(ring.count)
    places = [(order.index(i) - ring.place + ring.count) % ring.count for i in range(ring.count)]

    def column(i):
        return lambda n, _: (0, jnp.clip(n - i * steps, 0, steps - 1))

    def fixed(n, _):
        return (0, 0)

    return pl.pallas_call(
        lambda *refs: partial_kernel(count, steps, *refs),
        grid_spec=pltpu.PrefetchScalarGridSpec(
            num_scalar_prefetch=1, grid=(count * steps,),
            in_specs=[pl.BlockSpec(left.shape, fixed) for left in lefts]
            + [pl.BlockSpec((right.shape[0], tile), column(i)) for i, right in enumerate(rights)],
            out_specs=pl.BlockSpec((ring.count, rows + 16, tile), lambda n, _: (0, 0, n)),
        ),
        out_shape=jax.ShapeDtypeStruct((ring.count, rows + 16, count * width), f32),
        compiler_params=params(LIM_PARTIALS),
        cost_estimate=little,
        name="partials",
    )(jnp.stack(places).astype(jnp.int32), *lefts, *rights)


def normed_kernel(places, gate_rows, input_rows, tail_rows, gate_tile, input_tile, tail_tile, *refs):
    results, product = refs[:-1], refs[-1]
    total = dot(gate_rows[...], gate_tile[...], ((1,), (1,)))
    total = total + dot(input_rows[...], input_tile[...], ((1,), (1,)))
    product[...] = total + dot(tail_rows[...], tail_tile[...], ((1,), (1,)))
    rows = results[0].shape[0]
    for i, result in enumerate(results):
        result[...] = product[pl.ds(pl.multiple_of(places[i] * rows, 16), rows), :]


def normed_parts(me, gate_grad, input_back, tail, second_full, first_full):
    count = lax.axis_size("tensor")
    tokens, channels = gate_grad.shape
    width, tile = first_full.shape[0], 2 * LANES
    places = jnp.stack([i ^ me for i in range(count)]).astype(jnp.int32)

    def fixed(n, _):
        return (0, 0)

    return pl.pallas_call(
        normed_kernel,
        grid_spec=pltpu.PrefetchScalarGridSpec(
            num_scalar_prefetch=1, grid=(width // tile,),
            in_specs=[
                pl.BlockSpec((tokens, channels), fixed), pl.BlockSpec((tokens, channels), fixed),
                pl.BlockSpec((tokens, LANES), fixed), pl.BlockSpec((tile, channels), lambda n, _: (n, 0)),
                pl.BlockSpec((tile, channels), lambda n, _: (n, 0)),
                pl.BlockSpec((tile, LANES), lambda n, _: (n, channels // LANES)),
            ],
            out_specs=[pl.BlockSpec((tokens // count, tile), lambda n, _: (0, n))] * count,
            scratch_shapes=[pltpu.VMEM((tokens, tile), f32)],
        ),
        out_shape=[jax.ShapeDtypeStruct((tokens // count, width), f32)] * count,
        compiler_params=params(LIM_NORMED_PARTS),
        cost_estimate=little,
        name="normed_parts",
    )(places, gate_grad, input_back, tail, second_full, first_full, first_full)


def cycle(count):
    return list(range(0, count, 2)) + list(range(count - 1, 0, -2))


class Ring:
    def __init__(self):
        self.count = lax.axis_size("dp")
        order = cycle(self.count)
        self.up = [(order[i], order[(i + 1) % self.count]) for i in range(self.count)]
        self.down = [(b, a) for a, b in self.up]
        me = lax.axis_index("dp")
        self.place = jnp.where(me % 2 == 0, me // 2, self.count - 1 - me // 2)

    def owner(self, offset):
        place = (self.place + offset + self.count) % self.count
        return jnp.where(place < self.count // 2, 2 * place, 2 * (self.count - 1 - place) + 1)


def middle(rows):
    return (rows // 2 + 15) // 16 * 16


class Gather:
    def __init__(self, ring, shard):
        self.ring, self.shard, self.step = ring, shard, 0
        self.held = [(shard, 0, 0)]
        self.last = (shard, shard)

    def hop(self):
        self.step += 1
        half, cut = self.ring.count // 2, middle(self.shard.shape[0])
        up, down = self.last
        offsets = ((-self.step, 0), (self.step, 0))
        if self.step == half:
            up, down = up[:cut], down[cut:]
            offsets = ((half, 0), (half, cut))
        self.last = (lax.ppermute(up, "dp", self.ring.up), lax.ppermute(down, "dp", self.ring.down))
        self.held += [(piece, *offset) for piece, offset in zip(self.last, offsets)]

    def after(self, *marks):
        self.last, marks = fence(self.last, marks)
        self.held[-2:] = [(piece, *old[1:]) for piece, old in zip(self.last, self.held[-2:])]
        return marks if len(marks) > 1 else marks[0]

    def result(self):
        rows = self.shard.shape[0]
        pieces = [piece for piece, _, _ in self.held]
        places = [self.ring.owner(offset) * rows + skip for _, offset, skip in self.held]
        return assemble(pieces, places, rows * self.ring.count)


def encode(rows, limit):
    power = jnp.ceil(jnp.log2(jnp.maximum(limit, 1e-30)))
    ours = lax.broadcasted_iota(jnp.int32, rows.shape, 0) < rows.shape[0] - 16
    return jnp.where(ours, rows * jnp.exp2(15.0 - power), power).astype(jnp.float16)


def decode(payload):
    power = payload[-16:-15].astype(f32)
    return payload.astype(f32) * jnp.exp2(power - 15.0), jnp.exp2(power)


class Scatter:
    def __init__(self, ring, parts):
        self.ring, self.parts = ring, parts
        self.step = ring.count // 2
        self.rows = parts.shape[1] - 16
        self.cut = middle(self.rows)
        far, top = parts[self.step], parts[self.step, -16:-15]
        upper = jnp.concatenate([far[: self.cut], far[-16:]], axis=0)
        self.send = (encode(upper, top), encode(far[self.cut :], top))

    def hop(self):
        self.got = (lax.ppermute(self.send[0], "dp", self.ring.up), lax.ppermute(self.send[1], "dp", self.ring.down))

    def after(self, *marks):
        self.got, marks = fence(self.got, marks)
        return marks if len(marks) > 1 else marks[0]

    def before(self, *marks):
        self.send, marks = fence(self.send, marks)
        return marks if len(marks) > 1 else marks[0]

    def add(self):
        first = self.step == self.ring.count // 2
        (up, up_top), (down, down_top) = (decode(g) for g in self.got)
        if first:
            up, down = jnp.pad(up, ((0, self.rows - self.cut), (0, 0))), jnp.pad(down, ((self.cut, 0), (0, 0)))
            upper = lax.broadcasted_iota(jnp.int32, up.shape, 0) < self.cut
            up = jnp.where(upper, up, 0.0)
        self.step -= 1
        if self.step == 0:
            return (self.parts[0] + up + down)[: self.rows]
        above, below = self.parts[self.step], self.parts[self.ring.count - self.step]
        self.send = (
            encode(above + up, above[-16:-15] + up_top),
            encode(below + down, below[-16:-15] + down_top),
        )
        return None


def fence(*arrays):
    flat, tree = jax.tree.flatten(arrays)
    return jax.tree.unflatten(tree, lax.optimization_barrier(flat))


def across(array, bit, axis="tensor"):
    count = lax.axis_size(axis)
    return lax.ppermute(array, axis, [(i, i ^ bit) for i in range(count)])


def cube_sum(array, axis):
    bit = 1
    while bit < lax.axis_size(axis):
        array = array + across(array, bit, axis)
        bit *= 2
    return array


def shards(
    block_input, cotangent, norm_gain, gate_weight, input_weight, state_weight, step_weight, conv_input,
    conv_input_bias, conv_state, conv_state_bias, step_bias, decay_log, skip_scale, gate_gain, out_weight,
):
    group_count = lax.axis_size("tensor")
    me = lax.axis_index("tensor")
    ring = Ring()
    half = ring.count // 2
    local_rows = block_input.shape[0]
    channels = gate_gain.shape[0]
    heads = step_bias.shape[0]
    inner_total = channels * group_count
    share = 2 * STATE // group_count
    tokens = local_rows * group_count
    blocks = tokens // BLOCK
    fold = LANES // share
    folded = tokens // fold
    rows_dot = ((1,), (0,))
    back_dot = ((1,), (1,))

    state_mine = lax.dynamic_slice_in_dim(state_weight, me * share, share, 1)
    first = Gather(
        ring,
        jnp.concatenate(
            [input_weight, state_mine, jnp.pad(step_weight, ((0, 0), (0, LANES - share - heads)))], axis=1
        ).astype(bf16),
    )
    first.hop()
    row_scale = lax.rsqrt(jnp.mean(block_input * block_input, axis=1, keepdims=True) + epsilon)
    normed = (block_input * row_scale * norm_gain).astype(bf16)
    far = across(normed, 2)
    normed_pieces = (normed, across(normed, 1), far, across(far, 1))
    normed_all = assemble(normed_pieces, [(me ^ bits) * local_rows for bits in range(4)], tokens)
    second_weight = jnp.concatenate([gate_weight, out_weight.T], axis=1).astype(bf16)
    for _ in range(half - 2):
        first.hop()
    second_weight, cot_low = first.after(second_weight, cotangent.astype(bf16))
    first.hop()
    second = Gather(ring, second_weight)
    second.hop()
    cot_all = lax.all_gather(cot_low, "tensor", axis=0, tiled=True)
    first_full = second.after(first.result())
    second.hop()

    input_full, tail_full = first_full[:, :channels], first_full[:, channels:]
    tail_proj = dot(normed_all, tail_full, rows_dot)
    step_proj = jnp.pad(tail_proj[:, share : share + heads], ((0, 0), (0, LANES - heads)))
    state_mine = jnp.concatenate([tail_proj[i * folded : (i + 1) * folded, :share] for i in range(fold)], axis=1)
    far = across(state_mine, 2)
    same_x, same_core, diagonal = across(state_mine, 1), far, across(far, 1)
    right_core = me % 2 == 1
    near = (jnp.where(right_core, same_x, state_mine), jnp.where(right_core, state_mine, same_x))
    away = (jnp.where(right_core, diagonal, same_core), jnp.where(right_core, same_core, diagonal))
    right_chip = me // 2 == 1
    state_parts = [jnp.where(right_chip, away[i], near[i]) for i in range(2)]
    state_parts += [jnp.where(right_chip, near[i], away[i]) for i in range(2)]
    state_proj = jnp.concatenate(
        [jnp.concatenate([p[:, i * share : (i + 1) * share] for p in state_parts], axis=1) for i in range(fold)], axis=0
    )
    input_proj = dot(normed_all, input_full, rows_dot)
    rates = -jnp.exp(decay_log)

    def per_head(vector):
        return jnp.pad(vector, (0, LANES - heads))[None, :]

    skip = jnp.repeat(skip_scale, HEAD_DIM)[None, :]
    head_of = (
        lax.broadcasted_iota(jnp.int32, (channels, LANES), 0) // HEAD_DIM
        == lax.broadcasted_iota(jnp.int32, (channels, LANES), 1)
    ).astype(f32)
    scan_consts = (
        conv_input, conv_input_bias[None, :], conv_state, conv_state_bias[None, :], per_head(step_bias),
        per_head(rates), skip,
    )
    carried = jnp.zeros((channels // LANES, LANES, STATE), f32)
    span = 2
    scanned = []
    input_proj = second.after(input_proj)
    second.hop()
    for start in range(0, blocks, span):
        scanned.append(run_scan(start, span, input_proj, state_proj, step_proj, carried, scan_consts))
        carried = scanned[-1][4]
        if second.step < half - 1:
            carried = second.after(carried)
            second.hop()
    while second.step < half:
        second.hop()
    second_full = second.result()
    gate_full, out_full = second_full[:, :channels], second_full[:, channels:]
    mixed = jnp.concatenate([block[0] for block in scanned], axis=0)

    gate_proj = dot(normed_all, gate_full, rows_dot)
    gated = mixed * (gate_proj * jax.nn.sigmoid(gate_proj))
    gate_out_grad = dot(cot_all, out_full, rows_dot)
    sums = jnp.stack([jnp.sum(gated * gated, axis=1), jnp.sum(gate_out_grad * gate_gain * gated, axis=1)])
    sums = (sums + across(sums, 1)) + (across(sums, 2) + across(sums, 3))
    gate_scale = lax.rsqrt(sums[0] / inner_total + epsilon)
    scales = jnp.stack([gate_scale, gate_scale**3 * (sums[1] / inner_total)], axis=1)
    gate_out, gate_grad, mixed_grad, gain_sum = run_gate(mixed, gate_proj, gate_out_grad, scales, gate_gain[None, :])

    normed_t = normed_all.T
    pair_ring = Scatter(ring, partials(ring, (cot_all.T, normed_t), (gate_out, gate_grad)))
    back_consts = (conv_input, conv_state, per_head(step_bias), per_head(rates), skip, head_of)
    carry = (
        jnp.zeros((8, channels), f32), jnp.zeros((8, 2 * STATE), f32),
        jnp.zeros((channels // LANES, LANES, STATE), f32), jnp.zeros((8, LANES), f32),
    )
    done = []
    pair_sum = None
    for turn in range(blocks):
        if turn == 1:
            carry, late_out = pair_ring.after(carry, gate_out)
            branch_part = dot(late_out, out_full, back_dot)
            branch = lax.psum_scatter(branch_part, "tensor", scatter_dimension=0, tiled=True)
        if turn > 0 and pair_sum is None:
            pair_sum = pair_ring.add()
        if turn == 1:
            carry, branch_part = fence(carry, branch_part)
        if pair_sum is None:
            carry = pair_ring.before(carry)
        if pair_sum is None:
            pair_ring.hop()
        start = blocks - 1 - turn
        kept = scanned[start // span]
        kept = [kept[1], kept[2], kept[0], kept[3]]
        result = run_scan_back(
            start, 1, (input_proj, state_proj, step_proj), kept, start % span, mixed_grad, carry, back_consts
        )
        done.insert(0, result)
        carry = tuple(result[6:])
    if pair_sum is None:
        done, branch = pair_ring.after(done, branch)
    block_output = block_input + branch
    while pair_sum is None:
        pair_sum = pair_ring.add()
        if pair_sum is None:
            pair_ring.hop()
    input_back, state_back, step_back = (jnp.concatenate([d[i] for d in done], axis=0) for i in range(3))
    input_sums, state_sums, step_sums = (sum(d[i] for d in done) for i in range(3, 6))

    def state_columns(index):
        mine = lax.dynamic_slice_in_dim(state_back, index * share, share, 1)
        return jnp.concatenate([mine[i * folded : (i + 1) * folded] for i in range(fold)], axis=1)

    for_far, for_me = across(state_columns(me ^ 3), 1), across(state_columns(me ^ 1), 1)
    input_ring = Scatter(ring, partials(ring, (normed_t,), (input_back,)))
    for_far, for_me = input_ring.before(for_far, for_me)
    input_ring.hop()
    from_far = across(state_columns(me ^ 2) + for_far, 2)
    from_far = input_ring.after(from_far)
    input_ring.add()
    state_share = (state_columns(me) + for_me + from_far).astype(bf16)
    state_share = input_ring.before(state_share)
    input_ring.hop()
    state_share = jnp.concatenate([state_share[:, i * share : (i + 1) * share] for i in range(fold)], axis=0)
    tail = jnp.concatenate(
        [state_share, step_back[:, :heads], jnp.zeros((tokens, LANES - share - heads), bf16)], axis=1
    )
    parts = normed_parts(me, gate_grad, input_back, tail, second_full, first_full)
    tail_ring = Scatter(ring, partials(ring, (normed_t,), (tail,)))
    parts, tail_ring.send = input_ring.after(parts, tail_ring.send)
    for_far, for_me = across(parts[3], 1), across(parts[1], 1)
    input_ring.add()
    input_ring.send, tail_ring.send, for_far, for_me = fence(input_ring.send, tail_ring.send, for_far, for_me)
    input_ring.hop()
    tail_ring.hop()
    sent = parts[2] + for_far
    sent = jnp.concatenate([sent, jnp.zeros((16, sent.shape[1]), f32)], axis=0)
    from_far = across(encode(sent, jnp.max(jnp.abs(sent), axis=0, keepdims=True)), 2)
    input_sum = tail_sum = None
    while input_sum is None:
        input_ring.got, tail_ring.got = fence(input_ring.got, tail_ring.got)
        input_sum = input_ring.add()
        tail_ring.add()
        if input_sum is None:
            input_ring.send, tail_ring.send = fence(input_ring.send, tail_ring.send)
            input_ring.hop()
        tail_ring.hop()
    while tail_sum is None:
        tail_sum = tail_ring.add()
        if tail_sum is None:
            tail_ring.hop()
    normed_grad = parts[0] + for_me + decode(from_far)[0][:local_rows]

    weighted_grad = normed_grad * norm_gain
    norm_gain_part = jnp.sum(normed_grad * block_input * row_scale, axis=0)
    input_grad = (
        cotangent
        + row_scale * weighted_grad
        - block_input * row_scale**3 * jnp.mean(weighted_grad * block_input, axis=1, keepdims=True)
    )
    shared = jnp.concatenate([norm_gain_part, state_sums[:5].reshape(-1)])
    local = jnp.concatenate(
        [
            input_sums[:5].reshape(-1),
            gain_sum[0],
            jnp.sum(input_sums[5].reshape(heads, HEAD_DIM), axis=1),
            step_sums[0, :heads],
            step_sums[1, :heads] * rates,
        ]
    )
    packed = jnp.concatenate([shared, local])
    packed = jnp.pad(packed, (0, -packed.shape[0] % (8 * LANES))).reshape(-1, LANES)
    packed = cube_sum(packed, "dp")
    local = packed.reshape(-1)[shared.shape[0] :]
    spread = [jnp.where(me == i, tail_sum[:, :share], 0.0) for i in range(group_count)]
    spread = jnp.concatenate(
        [jnp.concatenate(spread[i : i + fold], axis=1) for i in range(0, group_count, fold)], axis=0
    )
    spread = cube_sum(spread, "tensor")
    rows = tail_sum.shape[0]
    state_grad = jnp.concatenate([spread[i * rows : (i + 1) * rows] for i in range(group_count // fold)], axis=1)
    shared = cube_sum(packed[: -(-shared.shape[0] // (8 * LANES)) * 8], "tensor").reshape(-1)
    width = block_input.shape[1]
    state_sum = shared[width : width + 10 * STATE].reshape(5, 2 * STATE)
    at = 6 * channels
    return (
        block_output,
        input_grad,
        shared[:width],
        pair_sum[:, channels:],
        input_sum,
        state_grad,
        tail_sum[:, share : share + heads],
        local[: 4 * channels].reshape(4, channels),
        local[4 * channels : 5 * channels],
        state_sum[:4],
        state_sum[4],
        local[at + heads : at + 2 * heads],
        local[at + 2 * heads : at + 3 * heads],
        local[at : at + heads],
        local[5 * channels : at],
        pair_sum[:, :channels].T,
    )


def solution(mesh):
    rows = P(("dp", "tensor"), None)
    both = P("dp", "tensor")
    inner = P("tensor")
    return jax.shard_map(
        shards,
        mesh=mesh,
        in_specs=(
            rows, rows, P(), both, both, P("dp", None), both, P(None, "tensor"), inner, P(), P(), inner, inner,
            inner, inner, P("tensor", "dp"),
        ),
        out_specs=(
            rows, rows, P(), both, both, P("dp", None), both, P(None, "tensor"), inner, P(), P(), inner, inner,
            inner, inner, P("tensor", "dp"),
        ),
        check_vma=False,
    )
```

```python
import jax
import jax.numpy as jnp
from jax import lax
from jax.experimental import pallas as pl
from jax.experimental.pallas import tpu as pltpu
from jax.sharding import PartitionSpec as P

HEAD_DIM = 64
STATE = 128
BLOCK = 256
SEQ = 1024
LANES = 128

LIM_SCAN = 61
LIM_SCAN_BACK = 61
LIM_GATE = 61
LIM_ASSEMBLE = 61
LIM_PARTIALS = 61
LIM_NORMED_PARTS = 61

epsilon = 1e-05
high = lax.Precision.HIGH
highest = lax.Precision.HIGHEST
f32 = jnp.float32
bf16 = jnp.bfloat16


def dot(left, right, dims, precision=None):
    return lax.dot_general(
        left, right, (dims, ((), ())), precision=precision, preferred_element_type=f32
    )


def sigmoid(v):
    return 1.0 / (1.0 + jnp.exp(-v))


def softplus(v):
    return jnp.maximum(v, 0.0) + jnp.log1p(jnp.exp(-jnp.abs(v)))


def iota(shape, axis):
    return lax.broadcasted_iota(jnp.int32, shape, axis)


def pair_columns(table, pair):
    lane = iota((table.shape[0], LANES), 1)
    return jnp.where(lane < HEAD_DIM, table[:, 2 * pair : 2 * pair + 1], table[:, 2 * pair + 1 : 2 * pair + 2])


def decay_tables(step_rows, step_bias, rates):
    step_size = softplus(step_rows + step_bias)
    earlier = (iota((BLOCK, BLOCK), 0) >= iota((BLOCK, BLOCK), 1)).astype(f32)
    cumulative = dot(earlier, step_size * rates, ((1,), (0,)), highest)
    return step_size, cumulative, jnp.exp(cumulative), jnp.exp(cumulative[BLOCK - 1 : BLOCK, :] - cumulative)


def state_decay(from_start, pair):
    last = from_start[BLOCK - 1 : BLOCK, :]
    row = iota((LANES, STATE), 0)
    return jnp.where(row < HEAD_DIM, last[:, 2 * pair : 2 * pair + 1], last[:, 2 * pair + 1 : 2 * pair + 2])


def shifted_conv(rows_ref, before, buffer, taps, conv_bias, first):
    @pl.when(first)
    def _():
        buffer[0:8, :] = before[...]

    @pl.when(jnp.logical_not(first))
    def _():
        buffer[0:8, :] = buffer[BLOCK : BLOCK + 8, :]

    buffer[8 : BLOCK + 8, :] = rows_ref[...]
    total = conv_bias[...] + taps[0:1, :] * buffer[8 : BLOCK + 8, :]
    for tap in range(1, 4):
        total = total + taps[tap : tap + 1, :] * buffer[8 - tap : BLOCK + 8 - tap, :]
    return total


def scan_kernel(
    input_rows, state_rows, step_rows, input_before, state_before, state_entering,
    conv_input, conv_input_bias, conv_state, conv_state_bias, step_bias, rates, skip,
    mixed, input_conv, state_conv, entering, carried, input_buffer, state_buffer,
):
    first = pl.program_id(0) == 0
    pairs = input_rows.shape[1] // LANES

    @pl.when(first)
    def _():
        carried[...] = state_entering[...]

    input_conv[...] = shifted_conv(input_rows, input_before, input_buffer, conv_input, conv_input_bias, first)
    state_pre = shifted_conv(state_rows, state_before, state_buffer, conv_state, conv_state_bias, first)
    state_conv[...] = state_pre
    state_act = state_pre * sigmoid(state_pre)
    writes, reads = state_act[:, :STATE], state_act[:, STATE:]
    meeting = dot(reads, writes, ((1,), (1,)), high)
    step_size, cumulative, from_start, to_end = decay_tables(step_rows[...], step_bias[...], rates[...])
    cumulative_t = cumulative.T
    causal = iota((BLOCK, BLOCK), 0) >= iota((BLOCK, BLOCK), 1)
    lane = iota((BLOCK, LANES), 1)
    for pair in range(pairs):
        columns = slice(pair * LANES, pair * LANES + LANES)
        pre = input_conv[:, columns]
        inputs = pre * sigmoid(pre)
        weighted = inputs * pair_columns(step_size, pair)
        state_in = carried[pair]
        entering[0, pair] = state_in
        out = dot(reads, state_in, ((1,), (1,)), high) * pair_columns(from_start, pair)
        for side in range(2):
            head = 2 * pair + side
            gap = cumulative[:, head : head + 1] - cumulative_t[head : head + 1, :]
            mixing = jnp.exp(jnp.where(causal, gap, -1e30)) * meeting
            mine = (lane < HEAD_DIM) if side == 0 else (lane >= HEAD_DIM)
            out = out + dot(mixing, jnp.where(mine, weighted, 0.0), ((1,), (0,)), high)
        fresh = dot(weighted * pair_columns(to_end, pair), writes, ((0,), (0,)), high)
        carried[pair] = state_decay(from_start, pair) * state_in + fresh
        mixed[:, columns] = out + skip[:, columns] * inputs


def scan_back_kernel(
    input_rows, state_rows, step_rows, input_conv, state_conv, mixed, entering, mixed_grad,
    input_after, state_after, state_leaving, decay_after,
    conv_input, conv_state, step_bias, rates, skip, head_of,
    input_grad, state_grad, step_grad, input_sums, state_sums, step_sums, input_first, state_first, carried, later,
    input_buffer, state_buffer, gap_grad, out_products, in_products,
):
    first = pl.program_id(0) == 0
    pairs = input_rows.shape[1] // LANES

    @pl.when(first)
    def _():
        carried[...] = state_leaving[...]
        later[...] = decay_after[...]
        input_sums[...] = jnp.zeros(input_sums.shape, f32)
        state_sums[...] = jnp.zeros(state_sums.shape, f32)
        step_sums[...] = jnp.zeros(step_sums.shape, f32)
        input_buffer[BLOCK : BLOCK + 8, :] = input_after[...]
        state_buffer[BLOCK : BLOCK + 8, :] = state_after[...]

    @pl.when(jnp.logical_not(first))
    def _():
        input_buffer[BLOCK : BLOCK + 8, :] = input_buffer[0:8, :]
        state_buffer[BLOCK : BLOCK + 8, :] = state_buffer[0:8, :]

    state_pre = state_conv[...]
    state_sig = sigmoid(state_pre)
    state_act = state_pre * state_sig
    writes, reads = state_act[:, :STATE], state_act[:, STATE:]
    meeting_t = dot(writes, reads, ((1,), (1,)), high)
    step_size, cumulative, from_start, to_end = decay_tables(step_rows[...], step_bias[...], rates[...])
    cumulative_t = cumulative.T
    causal_t = iota((BLOCK, BLOCK), 0) <= iota((BLOCK, BLOCK), 1)
    lane = iota((BLOCK, LANES), 1)
    gap_grad[...] = jnp.zeros(gap_grad.shape, f32)
    writes_grad = jnp.zeros((BLOCK, STATE), f32)
    reads_grad = jnp.zeros((BLOCK, STATE), f32)
    for pair in range(pairs):
        columns = slice(pair * LANES, pair * LANES + LANES)
        pre = input_conv[:, columns]
        sig = sigmoid(pre)
        inputs = pre * sig
        step_pair = pair_columns(step_size, pair)
        weighted = inputs * step_pair
        out_grad = mixed_grad[:, columns]
        skip_product = out_grad * inputs
        input_sums[5:6, columns] += jnp.sum(skip_product, axis=0, keepdims=True)
        end_pair = pair_columns(to_end, pair)
        leaving_grad = carried[pair]
        weighted_grad = dot(writes, leaving_grad, ((1,), (1,)), high) * end_pair
        for side in range(2):
            head = 2 * pair + side
            gap = cumulative_t[head : head + 1, :] - cumulative[:, head : head + 1]
            within = jnp.exp(jnp.where(causal_t, gap, -1e30))
            mine = (lane < HEAD_DIM) if side == 0 else (lane >= HEAD_DIM)
            own_grad = jnp.where(mine, out_grad, 0.0)
            weighted_grad = weighted_grad + dot(within * meeting_t, own_grad, ((1,), (0,)), high)
            gap_grad[...] += within * dot(weighted, own_grad, ((1,), (1,)), high)
        start_grad = out_grad * pair_columns(from_start, pair)
        reads_grad = reads_grad + dot(start_grad, entering[0, pair], ((1,), (0,)), high)
        writes_grad = writes_grad + dot(weighted * end_pair, leaving_grad, ((1,), (0,)), high)
        carried[pair] = state_decay(from_start, pair) * leaving_grad + dot(start_grad, reads, ((0,), (0,)), high)
        out_products[:, columns] = out_grad * mixed[:, columns] - skip[:, columns] * skip_product
        in_products[:, columns] = inputs * weighted_grad
        inputs_grad = skip[:, columns] * out_grad + step_pair * weighted_grad
        input_buffer[0:BLOCK, columns] = inputs_grad * (sig * (1.0 + pre * (1.0 - sig)))
    reads_grad = reads_grad + dot(gap_grad[...], writes, ((0,), (0,)), high)
    writes_grad = writes_grad + dot(gap_grad[...], reads, ((1,), (0,)), high)
    state_slope = state_sig * (1.0 + state_pre * (1.0 - state_sig))
    state_buffer[0:BLOCK, 0:STATE] = writes_grad * state_slope[:, :STATE]
    state_buffer[0:BLOCK, STATE : 2 * STATE] = reads_grad * state_slope[:, STATE:]

    for buffer, rows, taps, sums, result in (
        (input_buffer, input_rows, conv_input, input_sums, input_grad),
        (state_buffer, state_rows, conv_state, state_sums, state_grad),
    ):
        raw = rows[...]
        total = jnp.zeros(raw.shape, f32)
        for tap in range(4):
            ahead = buffer[tap : tap + BLOCK, :]
            total = total + taps[tap : tap + 1, :] * ahead
            sums[tap : tap + 1, :] += jnp.sum(ahead * raw, axis=0, keepdims=True)
        sums[4:5, :] += jnp.sum(buffer[0:BLOCK, :], axis=0, keepdims=True)
        result[...] = total.astype(result.dtype)
    input_first[...] = input_buffer[0:8, :]
    state_first[...] = state_buffer[0:8, :]

    out_head = dot(out_products[...], head_of[...], ((1,), (0,)), high)
    in_head = dot(in_products[...], head_of[...], ((1,), (0,)), high)
    upper = (iota((BLOCK, BLOCK), 0) <= iota((BLOCK, BLOCK), 1)).astype(f32)
    decay_grad = dot(upper, out_head - step_size * in_head, ((1,), (0,)), highest) + later[0:1, :]
    later[0:1, :] = decay_grad[0:1, :]
    step_sig = sigmoid(step_rows[...] + step_bias[...])
    step_back = (rates[...] * decay_grad + in_head) * step_sig
    step_grad[...] = step_back.astype(step_grad.dtype)
    step_sums[0:1, :] += jnp.sum(step_back, axis=0, keepdims=True)
    step_sums[1:2, :] += jnp.sum(step_size * decay_grad, axis=0, keepdims=True)


def whole(array):
    zeros = (0,) * array.ndim
    return pl.BlockSpec(array.shape, lambda k: zeros)


def params(mebibytes):
    return pltpu.CompilerParams(dimension_semantics=("arbitrary",), vmem_limit_bytes=mebibytes * 1024 * 1024)


little = pl.CostEstimate(flops=10**6, bytes_accessed=2**16, transcendentals=0)


def run_scan(start, span, input_rows, state_rows, step_rows, state_entering, consts):
    channels = input_rows.shape[1]
    pairs = channels // LANES
    rows = span * BLOCK
    edge = start * BLOCK // 8 - 1

    def tokens(width):
        return pl.BlockSpec((BLOCK, width), lambda k: (start + k, 0))

    def results(width):
        return pl.BlockSpec((BLOCK, width), lambda k: (k, 0))

    if start == 0:
        before = (jnp.zeros((8, channels), f32), jnp.zeros((8, 2 * STATE), f32))
        before_specs = [whole(c) for c in before]
    else:
        before = (input_rows, state_rows)
        before_specs = [pl.BlockSpec((8, c.shape[1]), lambda k: (edge, 0)) for c in before]
    return pl.pallas_call(
        scan_kernel,
        grid=(span,),
        in_specs=[tokens(channels), tokens(2 * STATE), tokens(LANES)] + before_specs + [whole(state_entering)]
        + [whole(c) for c in consts],
        out_specs=[
            results(channels), results(channels), results(2 * STATE),
            pl.BlockSpec((1, pairs, LANES, STATE), lambda k: (k, 0, 0, 0)), whole(state_entering),
        ],
        out_shape=[
            jax.ShapeDtypeStruct((rows, channels), f32),
            jax.ShapeDtypeStruct((rows, channels), f32),
            jax.ShapeDtypeStruct((rows, 2 * STATE), f32),
            jax.ShapeDtypeStruct((span, pairs, LANES, STATE), f32),
            jax.ShapeDtypeStruct((pairs, LANES, STATE), f32),
        ],
        scratch_shapes=[pltpu.VMEM((BLOCK + 8, channels), f32), pltpu.VMEM((BLOCK + 8, 2 * STATE), f32)],
        compiler_params=params(LIM_SCAN),
        cost_estimate=little,
        name="scan",
    )(input_rows, state_rows, step_rows, *before, state_entering, *consts)


def run_scan_back(start, span, projections, kept, at, mixed_grad, carry, consts):
    channels = mixed_grad.shape[1]
    pairs = channels // LANES
    rows = span * BLOCK

    def tokens(width):
        return pl.BlockSpec((BLOCK, width), lambda k: (start + span - 1 - k, 0))

    def own(width, first=0):
        return pl.BlockSpec((BLOCK, width), lambda k: (first + span - 1 - k, 0))

    def shape(*dims):
        return jax.ShapeDtypeStruct(dims, f32)

    sums = [shape(8, channels), shape(8, 2 * STATE), shape(8, LANES)]
    ends = [jax.ShapeDtypeStruct(c.shape, f32) for c in carry]
    return pl.pallas_call(
        scan_back_kernel,
        grid=(span,),
        in_specs=[
            tokens(channels), tokens(2 * STATE), tokens(LANES), own(channels, at),
            own(2 * STATE, at), own(channels, at),
            pl.BlockSpec((1, pairs, LANES, STATE), lambda k: (at + span - 1 - k, 0, 0, 0)), tokens(channels),
        ] + [whole(c) for c in carry] + [whole(c) for c in consts],
        out_specs=[own(channels), own(2 * STATE), own(LANES)] + [whole(c) for c in sums + ends],
        out_shape=[
            jax.ShapeDtypeStruct((rows, channels), bf16), shape(rows, 2 * STATE),
            jax.ShapeDtypeStruct((rows, LANES), bf16),
        ] + sums + ends,
        scratch_shapes=[
            pltpu.VMEM((BLOCK + 8, channels), f32), pltpu.VMEM((BLOCK + 8, 2 * STATE), f32),
            pltpu.VMEM((BLOCK, BLOCK), f32), pltpu.VMEM((BLOCK, channels), f32), pltpu.VMEM((BLOCK, channels), f32),
        ],
        compiler_params=params(LIM_SCAN_BACK),
        cost_estimate=little,
        name="scan_back",
    )(*projections, *kept, mixed_grad, *carry, *consts)


def gate_kernel(mixed, gate_proj, out_grad, scales, gain, gate_out, gate_grad, mixed_grad, gain_sum):
    @pl.when(pl.program_id(0) == 0)
    def _():
        gain_sum[...] = jnp.zeros(gain_sum.shape, f32)

    proj, rows_mixed, grad = gate_proj[...], mixed[...], out_grad[...]
    sig = sigmoid(proj)
    act = proj * sig
    gated = rows_mixed * act
    scale, pull = scales[:, 0:1], scales[:, 1:2]
    scaled = gated * scale
    gate_out[...] = (scaled * gain[...]).astype(bf16)
    gain_sum[0:1, :] += jnp.sum(grad * scaled, axis=0, keepdims=True)
    gated_grad = scale * (grad * gain[...]) - gated * pull
    mixed_grad[...] = gated_grad * act
    back = gated_grad * rows_mixed * (sig * (1.0 + proj * (1.0 - sig)))
    gate_grad[...] = back.astype(bf16)


def run_gate(mixed, gate_proj, out_grad, scales, gain):
    rows, channels = mixed.shape
    tokens = pl.BlockSpec((BLOCK, channels), lambda k: (k, 0))
    small = jax.ShapeDtypeStruct((8, channels), f32)
    return pl.pallas_call(
        gate_kernel,
        grid=(rows // BLOCK,),
        in_specs=[tokens, tokens, tokens, pl.BlockSpec((BLOCK, 2), lambda k: (k, 0)), whole(gain)],
        out_specs=[tokens, tokens, tokens, whole(small)],
        out_shape=[
            jax.ShapeDtypeStruct((rows, channels), bf16), jax.ShapeDtypeStruct((rows, channels), bf16),
            jax.ShapeDtypeStruct((rows, channels), f32), small,
        ],
        compiler_params=params(LIM_GATE),
        cost_estimate=little,
        name="gate",
    )(mixed, gate_proj, out_grad, scales, gain)


def assemble_kernel(places, *refs):
    result = refs[-1]
    for i, piece in enumerate(refs[:-1]):
        result[pl.ds(pl.multiple_of(places[i], 16), piece.shape[0]), :] = piece[...]


def assemble(pieces, places, rows):
    def fixed(n, _):
        return (0, 0)

    width = pieces[0].shape[1]
    return pl.pallas_call(
        assemble_kernel,
        grid_spec=pltpu.PrefetchScalarGridSpec(
            num_scalar_prefetch=1, grid=(1,), in_specs=[pl.BlockSpec(piece.shape, fixed) for piece in pieces],
            out_specs=pl.BlockSpec((rows, width), fixed),
        ),
        out_shape=jax.ShapeDtypeStruct((rows, width), pieces[0].dtype),
        compiler_params=params(LIM_ASSEMBLE),
        cost_estimate=little,
        name="assemble",
    )(jnp.stack(places).astype(jnp.int32), *pieces)


def partial_kernel(count, steps, places, *refs):
    lefts, rights, result = refs[:count], refs[count : 2 * count], refs[2 * count]
    owners, rows = result.shape[0], result.shape[1] - 16
    for i in range(count):

        @pl.when(pl.program_id(0) // steps == i)
        def _():
            product = dot(lefts[i][...], rights[i][...], ((1,), (0,)))
            for owner in range(owners):
                own = product[owner * rows : (owner + 1) * rows]
                result[places[owner], 0:rows, :] = own
                top = jnp.max(jnp.abs(own), axis=0, keepdims=True)
                result[places[owner], rows : rows + 16, :] = jnp.broadcast_to(top, (16, own.shape[1]))


def partials(ring, lefts, rights):
    width = rights[0].shape[1]
    tile = min(width, 2 * LANES)
    steps, count = width // tile, len(lefts)
    rows = lefts[0].shape[0] // ring.count
    order = cycle(ring.count)
    places = [(order.index(i) - ring.place + ring.count) % ring.count for i in range(ring.count)]

    def column(i):
        return lambda n, _: (0, jnp.clip(n - i * steps, 0, steps - 1))

    def fixed(n, _):
        return (0, 0)

    return pl.pallas_call(
        lambda *refs: partial_kernel(count, steps, *refs),
        grid_spec=pltpu.PrefetchScalarGridSpec(
            num_scalar_prefetch=1, grid=(count * steps,),
            in_specs=[pl.BlockSpec(left.shape, fixed) for left in lefts]
            + [pl.BlockSpec((right.shape[0], tile), column(i)) for i, right in enumerate(rights)],
            out_specs=pl.BlockSpec((ring.count, rows + 16, tile), lambda n, _: (0, 0, n)),
        ),
        out_shape=jax.ShapeDtypeStruct((ring.count, rows + 16, count * width), f32),
        compiler_params=params(LIM_PARTIALS),
        cost_estimate=little,
        name="partials",
    )(jnp.stack(places).astype(jnp.int32), *lefts, *rights)


def normed_kernel(places, gate_rows, input_rows, tail_rows, gate_tile, input_tile, tail_tile, *refs):
    results, product = refs[:-1], refs[-1]
    total = dot(gate_rows[...], gate_tile[...], ((1,), (1,)))
    total = total + dot(input_rows[...], input_tile[...], ((1,), (1,)))
    product[...] = total + dot(tail_rows[...], tail_tile[...], ((1,), (1,)))
    rows = results[0].shape[0]
    for i, result in enumerate(results):
        result[...] = product[pl.ds(pl.multiple_of(places[i] * rows, 16), rows), :]


def normed_parts(me, gate_grad, input_back, tail, second_full, first_full):
    count = lax.axis_size("tensor")
    tokens, channels = gate_grad.shape
    width, tile = first_full.shape[0], 2 * LANES
    places = jnp.stack([i ^ me for i in range(count)]).astype(jnp.int32)

    def fixed(n, _):
        return (0, 0)

    return pl.pallas_call(
        normed_kernel,
        grid_spec=pltpu.PrefetchScalarGridSpec(
            num_scalar_prefetch=1, grid=(width // tile,),
            in_specs=[
                pl.BlockSpec((tokens, channels), fixed), pl.BlockSpec((tokens, channels), fixed),
                pl.BlockSpec((tokens, LANES), fixed), pl.BlockSpec((tile, channels), lambda n, _: (n, 0)),
                pl.BlockSpec((tile, channels), lambda n, _: (n, 0)),
                pl.BlockSpec((tile, LANES), lambda n, _: (n, channels // LANES)),
            ],
            out_specs=[pl.BlockSpec((tokens // count, tile), lambda n, _: (0, n))] * count,
            scratch_shapes=[pltpu.VMEM((tokens, tile), f32)],
        ),
        out_shape=[jax.ShapeDtypeStruct((tokens // count, width), f32)] * count,
        compiler_params=params(LIM_NORMED_PARTS),
        cost_estimate=little,
        name="normed_parts",
    )(places, gate_grad, input_back, tail, second_full, first_full, first_full)


def cycle(count):
    return list(range(0, count, 2)) + list(range(count - 1, 0, -2))


class Ring:
    def __init__(self):
        self.count = lax.axis_size("dp")
        order = cycle(self.count)
        self.up = [(order[i], order[(i + 1) % self.count]) for i in range(self.count)]
        self.down = [(b, a) for a, b in self.up]
        me = lax.axis_index("dp")
        self.place = jnp.where(me % 2 == 0, me // 2, self.count - 1 - me // 2)

    def owner(self, offset):
        place = (self.place + offset + self.count) % self.count
        return jnp.where(place < self.count // 2, 2 * place, 2 * (self.count - 1 - place) + 1)


def middle(rows):
    return (rows // 2 + 15) // 16 * 16


class Gather:
    def __init__(self, ring, shard):
        self.ring, self.shard, self.step = ring, shard, 0
        self.held = [(shard, 0, 0)]
        self.last = (shard, shard)

    def hop(self):
        self.step += 1
        half, cut = self.ring.count // 2, middle(self.shard.shape[0])
        up, down = self.last
        offsets = ((-self.step, 0), (self.step, 0))
        if self.step == half:
            up, down = up[:cut], down[cut:]
            offsets = ((half, 0), (half, cut))
        self.last = (lax.ppermute(up, "dp", self.ring.up), lax.ppermute(down, "dp", self.ring.down))
        self.held += [(piece, *offset) for piece, offset in zip(self.last, offsets)]

    def after(self, *marks):
        self.last, marks = fence(self.last, marks)
        self.held[-2:] = [(piece, *old[1:]) for piece, old in zip(self.last, self.held[-2:])]
        return marks if len(marks) > 1 else marks[0]

    def result(self):
        rows = self.shard.shape[0]
        pieces = [piece for piece, _, _ in self.held]
        places = [self.ring.owner(offset) * rows + skip for _, offset, skip in self.held]
        return assemble(pieces, places, rows * self.ring.count)


def encode(rows, limit):
    power = jnp.ceil(jnp.log2(jnp.maximum(limit, 1e-30)))
    ours = lax.broadcasted_iota(jnp.int32, rows.shape, 0) < rows.shape[0] - 16
    return jnp.where(ours, rows * jnp.exp2(15.0 - power), power).astype(jnp.float16)


def decode(payload):
    power = payload[-16:-15].astype(f32)
    return payload.astype(f32) * jnp.exp2(power - 15.0), jnp.exp2(power)


class Scatter:
    def __init__(self, ring, parts):
        self.ring, self.parts = ring, parts
        self.step = ring.count // 2
        self.rows = parts.shape[1] - 16
        self.cut = middle(self.rows)
        far, top = parts[self.step], parts[self.step, -16:-15]
        upper = jnp.concatenate([far[: self.cut], far[-16:]], axis=0)
        self.send = (encode(upper, top), encode(far[self.cut :], top))

    def hop(self):
        self.got = (lax.ppermute(self.send[0], "dp", self.ring.up), lax.ppermute(self.send[1], "dp", self.ring.down))

    def after(self, *marks):
        self.got, marks = fence(self.got, marks)
        return marks if len(marks) > 1 else marks[0]

    def before(self, *marks):
        self.send, marks = fence(self.send, marks)
        return marks if len(marks) > 1 else marks[0]

    def add(self):
        first = self.step == self.ring.count // 2
        (up, up_top), (down, down_top) = (decode(g) for g in self.got)
        if first:
            up, down = jnp.pad(up, ((0, self.rows - self.cut), (0, 0))), jnp.pad(down, ((self.cut, 0), (0, 0)))
            upper = lax.broadcasted_iota(jnp.int32, up.shape, 0) < self.cut
            up = jnp.where(upper, up, 0.0)
        self.step -= 1
        if self.step == 0:
            return (self.parts[0] + up + down)[: self.rows]
        above, below = self.parts[self.step], self.parts[self.ring.count - self.step]
        self.send = (
            encode(above + up, above[-16:-15] + up_top),
            encode(below + down, below[-16:-15] + down_top),
        )
        return None


def fence(*arrays):
    flat, tree = jax.tree.flatten(arrays)
    return jax.tree.unflatten(tree, lax.optimization_barrier(flat))


def across(array, bit, axis="tensor"):
    count = lax.axis_size(axis)
    return lax.ppermute(array, axis, [(i, i ^ bit) for i in range(count)])


def cube_sum(array, axis):
    bit = 1
    while bit < lax.axis_size(axis):
        array = array + across(array, bit, axis)
        bit *= 2
    return array


def shards(
    block_input, cotangent, norm_gain, gate_weight, input_weight, state_weight, step_weight, conv_input,
    conv_input_bias, conv_state, conv_state_bias, step_bias, decay_log, skip_scale, gate_gain, out_weight,
):
    group_count = lax.axis_size("tensor")
    me = lax.axis_index("tensor")
    ring = Ring()
    half = ring.count // 2
    local_rows = block_input.shape[0]
    channels = gate_gain.shape[0]
    heads = step_bias.shape[0]
    inner_total = channels * group_count
    share = 2 * STATE // group_count
    tokens = local_rows * group_count
    blocks = tokens // BLOCK
    fold = LANES // share
    folded = tokens // fold
    rows_dot = ((1,), (0,))
    back_dot = ((1,), (1,))

    state_mine = lax.dynamic_slice_in_dim(state_weight, me * share, share, 1)
    first = Gather(
        ring,
        jnp.concatenate(
            [input_weight, state_mine, jnp.pad(step_weight, ((0, 0), (0, LANES - share - heads)))], axis=1
        ).astype(bf16),
    )
    first.hop()
    row_scale = lax.rsqrt(jnp.mean(block_input * block_input, axis=1, keepdims=True) + epsilon)
    normed = (block_input * row_scale * norm_gain).astype(bf16)
    second_weight = jnp.concatenate([gate_weight, out_weight.T], axis=1).astype(bf16)
    normed = first.after(normed)
    first.hop()
    far, near = across(normed, 2), across(normed, 1)
    for _ in range(half - 3):
        first.hop()
    far, near, second_weight, cot_low = first.after(far, near, second_weight, cotangent.astype(bf16))
    first.hop()
    normed_pieces = (normed, near, far, across(far, 1))
    normed_all = assemble(normed_pieces, [(me ^ bits) * local_rows for bits in range(4)], tokens)
    second = Gather(ring, second_weight)
    second.hop()
    cot_all = lax.all_gather(cot_low, "tensor", axis=0, tiled=True)
    first_full = second.after(first.result())
    second.hop()

    input_full, tail_full = first_full[:, :channels], first_full[:, channels:]
    tail_proj = dot(normed_all, tail_full, rows_dot)
    step_proj = jnp.pad(tail_proj[:, share : share + heads], ((0, 0), (0, LANES - heads)))
    state_mine = jnp.concatenate([tail_proj[i * folded : (i + 1) * folded, :share] for i in range(fold)], axis=1)
    far = across(state_mine, 2)
    same_x, same_core, diagonal = across(state_mine, 1), far, across(far, 1)
    right_core = me % 2 == 1
    near = (jnp.where(right_core, same_x, state_mine), jnp.where(right_core, state_mine, same_x))
    away = (jnp.where(right_core, diagonal, same_core), jnp.where(right_core, same_core, diagonal))
    right_chip = me // 2 == 1
    state_parts = [jnp.where(right_chip, away[i], near[i]) for i in range(2)]
    state_parts += [jnp.where(right_chip, near[i], away[i]) for i in range(2)]
    state_proj = jnp.concatenate(
        [jnp.concatenate([p[:, i * share : (i + 1) * share] for p in state_parts], axis=1) for i in range(fold)], axis=0
    )
    input_proj = dot(normed_all, input_full, rows_dot)
    rates = -jnp.exp(decay_log)

    def per_head(vector):
        return jnp.pad(vector, (0, LANES - heads))[None, :]

    skip = jnp.repeat(skip_scale, HEAD_DIM)[None, :]
    head_of = (
        lax.broadcasted_iota(jnp.int32, (channels, LANES), 0) // HEAD_DIM
        == lax.broadcasted_iota(jnp.int32, (channels, LANES), 1)
    ).astype(f32)
    scan_consts = (
        conv_input, conv_input_bias[None, :], conv_state, conv_state_bias[None, :], per_head(step_bias),
        per_head(rates), skip,
    )
    carried = jnp.zeros((channels // LANES, LANES, STATE), f32)
    span = 2
    scanned = []
    input_proj = second.after(input_proj)
    second.hop()
    for start in range(0, blocks, span):
        scanned.append(run_scan(start, span, input_proj, state_proj, step_proj, carried, scan_consts))
        carried = scanned[-1][4]
        if second.step < half - 1:
            carried = second.after(carried)
            second.hop()
    while second.step < half:
        second.hop()
    second_full = second.result()
    gate_full, out_full = second_full[:, :channels], second_full[:, channels:]
    mixed = jnp.concatenate([block[0] for block in scanned], axis=0)

    gate_proj = dot(normed_all, gate_full, rows_dot)
    gated = mixed * (gate_proj * jax.nn.sigmoid(gate_proj))
    gate_out_grad = dot(cot_all, out_full, rows_dot)
    sums = jnp.stack([jnp.sum(gated * gated, axis=1), jnp.sum(gate_out_grad * gate_gain * gated, axis=1)])
    sums = (sums + across(sums, 1)) + (across(sums, 2) + across(sums, 3))
    gate_scale = lax.rsqrt(sums[0] / inner_total + epsilon)
    scales = jnp.stack([gate_scale, gate_scale**3 * (sums[1] / inner_total)], axis=1)
    gate_out, gate_grad, mixed_grad, gain_sum = run_gate(mixed, gate_proj, gate_out_grad, scales, gate_gain[None, :])

    normed_t = normed_all.T
    pair_ring = Scatter(ring, partials(ring, (cot_all.T, normed_t), (gate_out, gate_grad)))
    back_consts = (conv_input, conv_state, per_head(step_bias), per_head(rates), skip, head_of)
    carry = (
        jnp.zeros((8, channels), f32), jnp.zeros((8, 2 * STATE), f32),
        jnp.zeros((channels // LANES, LANES, STATE), f32), jnp.zeros((8, LANES), f32),
    )
    done = []
    pair_sum = None
    for turn in range(blocks):
        if turn == 1:
            carry, late_out = pair_ring.after(carry, gate_out)
            branch_part = dot(late_out, out_full, back_dot)
            branch = lax.psum_scatter(branch_part, "tensor", scatter_dimension=0, tiled=True)
        if turn > 0 and pair_sum is None:
            pair_sum = pair_ring.add()
        if turn == 1:
            carry, branch_part = fence(carry, branch_part)
        if pair_sum is None:
            carry = pair_ring.before(carry)
        if pair_sum is None:
            pair_ring.hop()
        start = blocks - 1 - turn
        kept = scanned[start // span]
        kept = [kept[1], kept[2], kept[0], kept[3]]
        result = run_scan_back(
            start, 1, (input_proj, state_proj, step_proj), kept, start % span, mixed_grad, carry, back_consts
        )
        done.insert(0, result)
        carry = tuple(result[6:])
    if pair_sum is None:
        done, branch = pair_ring.after(done, branch)
    block_output = block_input + branch
    while pair_sum is None:
        pair_sum = pair_ring.add()
        if pair_sum is None:
            pair_ring.hop()
    input_back, state_back, step_back = (jnp.concatenate([d[i] for d in done], axis=0) for i in range(3))
    input_sums, state_sums, step_sums = (sum(d[i] for d in done) for i in range(3, 6))

    packed = jnp.concatenate(
        [
            state_sums[:5].reshape(-1),
            input_sums[:5].reshape(-1),
            gain_sum[0],
            jnp.sum(input_sums[5].reshape(heads, HEAD_DIM), axis=1),
            step_sums[0, :heads],
            step_sums[1, :heads] * rates,
        ]
    )
    packed = jnp.pad(packed, (0, -packed.shape[0] % LANES)).reshape(-1, LANES)

    def state_columns(index):
        mine = lax.dynamic_slice_in_dim(state_back, index * share, share, 1)
        return jnp.concatenate([mine[i * folded : (i + 1) * folded] for i in range(fold)], axis=1)

    for_far, for_me = across(state_columns(me ^ 3), 1), across(state_columns(me ^ 1), 1)
    input_ring = Scatter(ring, partials(ring, (normed_t,), (input_back,)))
    for_far, for_me, packed = input_ring.before(for_far, for_me, packed)
    input_ring.hop()
    from_far = across(state_columns(me ^ 2) + for_far, 2)
    from_far = input_ring.after(from_far)
    input_ring.add()
    state_share = (state_columns(me) + for_me + from_far).astype(bf16)
    state_share = input_ring.before(state_share)
    input_ring.hop()
    state_share = jnp.concatenate([state_share[:, i * share : (i + 1) * share] for i in range(fold)], axis=0)
    tail = jnp.concatenate(
        [state_share, step_back[:, :heads], jnp.zeros((tokens, LANES - share - heads), bf16)], axis=1
    )
    parts = normed_parts(me, gate_grad, input_back, tail, second_full, first_full)
    tail_ring = Scatter(ring, partials(ring, (normed_t,), (tail,)))
    parts, tail_ring.send = input_ring.after(parts, tail_ring.send)
    for_far, for_me = across(parts[3], 1), across(parts[1], 1)
    input_ring.add()
    input_ring.send, tail_ring.send, for_far, for_me = fence(input_ring.send, tail_ring.send, for_far, for_me)
    input_ring.hop()
    tail_ring.hop()
    sent = parts[2] + for_far
    sent = jnp.concatenate([sent, jnp.zeros((16, sent.shape[1]), f32)], axis=0)
    from_far = across(encode(sent, jnp.max(jnp.abs(sent), axis=0, keepdims=True)), 2)
    input_sum = tail_sum = None
    while input_sum is None:
        input_ring.got, tail_ring.got = fence(input_ring.got, tail_ring.got)
        input_sum = input_ring.add()
        tail_ring.add()
        if input_sum is None:
            input_ring.send, tail_ring.send = fence(input_ring.send, tail_ring.send)
            input_ring.hop()
        tail_ring.hop()
    while tail_sum is None:
        tail_sum = tail_ring.add()
        if tail_sum is None:
            tail_ring.hop()
    normed_grad = parts[0] + for_me + decode(from_far)[0][:local_rows]

    weighted_grad = normed_grad * norm_gain
    norm_gain_part = jnp.sum(normed_grad * block_input * row_scale, axis=0)
    input_grad = (
        cotangent
        + row_scale * weighted_grad
        - block_input * row_scale**3 * jnp.mean(weighted_grad * block_input, axis=1, keepdims=True)
    )
    packed = cube_sum(jnp.concatenate([norm_gain_part.reshape(-1, LANES), packed], axis=0), "dp")
    shared_rows = norm_gain_part.shape[0] // LANES + 10 * STATE // LANES
    local = packed[shared_rows:].reshape(-1)
    spread = [jnp.where(me == i, tail_sum[:, :share], 0.0) for i in range(group_count)]
    spread = jnp.concatenate(
        [jnp.concatenate(spread[i : i + fold], axis=1) for i in range(0, group_count, fold)], axis=0
    )
    spread = cube_sum(spread, "tensor")
    rows = tail_sum.shape[0]
    state_grad = jnp.concatenate([spread[i * rows : (i + 1) * rows] for i in range(group_count // fold)], axis=1)
    shared = cube_sum(packed[:shared_rows], "tensor").reshape(-1)
    width = block_input.shape[1]
    state_sum = shared[width : width + 10 * STATE].reshape(5, 2 * STATE)
    at = 6 * channels
    return (
        block_output,
        input_grad,
        shared[:width],
        pair_sum[:, channels:],
        input_sum,
        state_grad,
        tail_sum[:, share : share + heads],
        local[: 4 * channels].reshape(4, channels),
        local[4 * channels : 5 * channels],
        state_sum[:4],
        state_sum[4],
        local[at + heads : at + 2 * heads],
        local[at + 2 * heads : at + 3 * heads],
        local[at : at + heads],
        local[5 * channels : at],
        pair_sum[:, :channels].T,
    )


def solution(mesh):
    rows = P(("dp", "tensor"), None)
    both = P("dp", "tensor")
    inner = P("tensor")
    return jax.shard_map(
        shards,
        mesh=mesh,
        in_specs=(
            rows, rows, P(), both, both, P("dp", None), both, P(None, "tensor"), inner, P(), P(), inner, inner,
            inner, inner, P("tensor", "dp"),
        ),
        out_specs=(
            rows, rows, P(), both, both, P("dp", None), both, P(None, "tensor"), inner, P(), P(), inner, inner,
            inner, inner, P("tensor", "dp"),
        ),
        check_vma=False,
    )
```

```python
import jax
import jax.numpy as jnp
from jax import lax
from jax.experimental import pallas as pl
from jax.experimental.pallas import tpu as pltpu
from jax.sharding import PartitionSpec as P

HEAD_DIM = 64
STATE = 128
BLOCK = 256
SEQ = 1024
LANES = 128

LIM_SCAN = 61
LIM_SCAN_BACK = 61
LIM_GATE = 61
LIM_ASSEMBLE = 61
LIM_PARTIALS = 61
LIM_NORMED_PARTS = 61

epsilon = 1e-05
high = lax.Precision.HIGH
highest = lax.Precision.HIGHEST
f32 = jnp.float32
bf16 = jnp.bfloat16


def dot(left, right, dims, precision=None):
    return lax.dot_general(
        left, right, (dims, ((), ())), precision=precision, preferred_element_type=f32
    )


def sigmoid(v):
    return 1.0 / (1.0 + jnp.exp(-v))


def softplus(v):
    return jnp.maximum(v, 0.0) + jnp.log1p(jnp.exp(-jnp.abs(v)))


def iota(shape, axis):
    return lax.broadcasted_iota(jnp.int32, shape, axis)


def pair_columns(table, pair):
    lane = iota((table.shape[0], LANES), 1)
    return jnp.where(lane < HEAD_DIM, table[:, 2 * pair : 2 * pair + 1], table[:, 2 * pair + 1 : 2 * pair + 2])


def decay_tables(step_rows, step_bias, rates):
    step_size = softplus(step_rows + step_bias)
    earlier = (iota((BLOCK, BLOCK), 0) >= iota((BLOCK, BLOCK), 1)).astype(f32)
    cumulative = dot(earlier, step_size * rates, ((1,), (0,)), highest)
    return step_size, cumulative, jnp.exp(cumulative), jnp.exp(cumulative[BLOCK - 1 : BLOCK, :] - cumulative)


def state_decay(from_start, pair):
    last = from_start[BLOCK - 1 : BLOCK, :]
    row = iota((LANES, STATE), 0)
    return jnp.where(row < HEAD_DIM, last[:, 2 * pair : 2 * pair + 1], last[:, 2 * pair + 1 : 2 * pair + 2])


def shifted_conv(rows_ref, before, buffer, taps, conv_bias, first):
    @pl.when(first)
    def _():
        buffer[0:8, :] = before[...]

    @pl.when(jnp.logical_not(first))
    def _():
        buffer[0:8, :] = buffer[BLOCK : BLOCK + 8, :]

    buffer[8 : BLOCK + 8, :] = rows_ref[...]
    total = conv_bias[...] + taps[0:1, :] * buffer[8 : BLOCK + 8, :]
    for tap in range(1, 4):
        total = total + taps[tap : tap + 1, :] * buffer[8 - tap : BLOCK + 8 - tap, :]
    return total


def scan_kernel(
    input_rows, state_rows, step_rows, input_before, state_before, state_entering,
    conv_input, conv_input_bias, conv_state, conv_state_bias, step_bias, rates, skip,
    mixed, input_conv, state_conv, entering, carried, input_buffer, state_buffer,
):
    first = pl.program_id(0) == 0
    pairs = input_rows.shape[1] // LANES

    @pl.when(first)
    def _():
        carried[...] = state_entering[...]

    input_conv[...] = shifted_conv(input_rows, input_before, input_buffer, conv_input, conv_input_bias, first)
    state_pre = shifted_conv(state_rows, state_before, state_buffer, conv_state, conv_state_bias, first)
    state_conv[...] = state_pre
    state_act = state_pre * sigmoid(state_pre)
    writes, reads = state_act[:, :STATE], state_act[:, STATE:]
    meeting = dot(reads, writes, ((1,), (1,)), high)
    step_size, cumulative, from_start, to_end = decay_tables(step_rows[...], step_bias[...], rates[...])
    cumulative_t = cumulative.T
    causal = iota((BLOCK, BLOCK), 0) >= iota((BLOCK, BLOCK), 1)
    lane = iota((BLOCK, LANES), 1)
    for pair in range(pairs):
        columns = slice(pair * LANES, pair * LANES + LANES)
        pre = input_conv[:, columns]
        inputs = pre * sigmoid(pre)
        weighted = inputs * pair_columns(step_size, pair)
        state_in = carried[pair]
        entering[0, pair] = state_in
        out = dot(reads, state_in, ((1,), (1,)), high) * pair_columns(from_start, pair)
        for side in range(2):
            head = 2 * pair + side
            gap = cumulative[:, head : head + 1] - cumulative_t[head : head + 1, :]
            mixing = jnp.exp(jnp.where(causal, gap, -1e30)) * meeting
            mine = (lane < HEAD_DIM) if side == 0 else (lane >= HEAD_DIM)
            out = out + dot(mixing, jnp.where(mine, weighted, 0.0), ((1,), (0,)), high)
        fresh = dot(weighted * pair_columns(to_end, pair), writes, ((0,), (0,)), high)
        carried[pair] = state_decay(from_start, pair) * state_in + fresh
        mixed[:, columns] = out + skip[:, columns] * inputs


def scan_back_kernel(
    input_rows, state_rows, step_rows, input_conv, state_conv, mixed, entering, mixed_grad,
    input_after, state_after, state_leaving, decay_after,
    conv_input, conv_state, step_bias, rates, skip, head_of,
    input_grad, state_grad, step_grad, input_sums, state_sums, step_sums, input_first, state_first, carried, later,
    input_buffer, state_buffer, gap_grad, out_products, in_products,
):
    first = pl.program_id(0) == 0
    pairs = input_rows.shape[1] // LANES

    @pl.when(first)
    def _():
        carried[...] = state_leaving[...]
        later[...] = decay_after[...]
        input_sums[...] = jnp.zeros(input_sums.shape, f32)
        state_sums[...] = jnp.zeros(state_sums.shape, f32)
        step_sums[...] = jnp.zeros(step_sums.shape, f32)
        input_buffer[BLOCK : BLOCK + 8, :] = input_after[...]
        state_buffer[BLOCK : BLOCK + 8, :] = state_after[...]

    @pl.when(jnp.logical_not(first))
    def _():
        input_buffer[BLOCK : BLOCK + 8, :] = input_buffer[0:8, :]
        state_buffer[BLOCK : BLOCK + 8, :] = state_buffer[0:8, :]

    state_pre = state_conv[...]
    state_sig = sigmoid(state_pre)
    state_act = state_pre * state_sig
    writes, reads = state_act[:, :STATE], state_act[:, STATE:]
    meeting_t = dot(writes, reads, ((1,), (1,)), high)
    step_size, cumulative, from_start, to_end = decay_tables(step_rows[...], step_bias[...], rates[...])
    cumulative_t = cumulative.T
    causal_t = iota((BLOCK, BLOCK), 0) <= iota((BLOCK, BLOCK), 1)
    lane = iota((BLOCK, LANES), 1)
    gap_grad[...] = jnp.zeros(gap_grad.shape, f32)
    writes_grad = jnp.zeros((BLOCK, STATE), f32)
    reads_grad = jnp.zeros((BLOCK, STATE), f32)
    for pair in range(pairs):
        columns = slice(pair * LANES, pair * LANES + LANES)
        pre = input_conv[:, columns]
        sig = sigmoid(pre)
        inputs = pre * sig
        step_pair = pair_columns(step_size, pair)
        weighted = inputs * step_pair
        out_grad = mixed_grad[:, columns]
        skip_product = out_grad * inputs
        input_sums[5:6, columns] += jnp.sum(skip_product, axis=0, keepdims=True)
        end_pair = pair_columns(to_end, pair)
        leaving_grad = carried[pair]
        weighted_grad = dot(writes, leaving_grad, ((1,), (1,)), high) * end_pair
        for side in range(2):
            head = 2 * pair + side
            gap = cumulative_t[head : head + 1, :] - cumulative[:, head : head + 1]
            within = jnp.exp(jnp.where(causal_t, gap, -1e30))
            mine = (lane < HEAD_DIM) if side == 0 else (lane >= HEAD_DIM)
            own_grad = jnp.where(mine, out_grad, 0.0)
            weighted_grad = weighted_grad + dot(within * meeting_t, own_grad, ((1,), (0,)), high)
            gap_grad[...] += within * dot(weighted, own_grad, ((1,), (1,)), high)
        start_grad = out_grad * pair_columns(from_start, pair)
        reads_grad = reads_grad + dot(start_grad, entering[0, pair], ((1,), (0,)), high)
        writes_grad = writes_grad + dot(weighted * end_pair, leaving_grad, ((1,), (0,)), high)
        carried[pair] = state_decay(from_start, pair) * leaving_grad + dot(start_grad, reads, ((0,), (0,)), high)
        out_products[:, columns] = out_grad * mixed[:, columns] - skip[:, columns] * skip_product
        in_products[:, columns] = inputs * weighted_grad
        inputs_grad = skip[:, columns] * out_grad + step_pair * weighted_grad
        input_buffer[0:BLOCK, columns] = inputs_grad * (sig * (1.0 + pre * (1.0 - sig)))
    reads_grad = reads_grad + dot(gap_grad[...], writes, ((0,), (0,)), high)
    writes_grad = writes_grad + dot(gap_grad[...], reads, ((1,), (0,)), high)
    state_slope = state_sig * (1.0 + state_pre * (1.0 - state_sig))
    state_buffer[0:BLOCK, 0:STATE] = writes_grad * state_slope[:, :STATE]
    state_buffer[0:BLOCK, STATE : 2 * STATE] = reads_grad * state_slope[:, STATE:]

    for buffer, rows, taps, sums, result in (
        (input_buffer, input_rows, conv_input, input_sums, input_grad),
        (state_buffer, state_rows, conv_state, state_sums, state_grad),
    ):
        raw = rows[...]
        total = jnp.zeros(raw.shape, f32)
        for tap in range(4):
            ahead = buffer[tap : tap + BLOCK, :]
            total = total + taps[tap : tap + 1, :] * ahead
            sums[tap : tap + 1, :] += jnp.sum(ahead * raw, axis=0, keepdims=True)
        sums[4:5, :] += jnp.sum(buffer[0:BLOCK, :], axis=0, keepdims=True)
        result[...] = total.astype(result.dtype)
    input_first[...] = input_buffer[0:8, :]
    state_first[...] = state_buffer[0:8, :]

    out_head = dot(out_products[...], head_of[...], ((1,), (0,)), high)
    in_head = dot(in_products[...], head_of[...], ((1,), (0,)), high)
    upper = (iota((BLOCK, BLOCK), 0) <= iota((BLOCK, BLOCK), 1)).astype(f32)
    decay_grad = dot(upper, out_head - step_size * in_head, ((1,), (0,)), highest) + later[0:1, :]
    later[0:1, :] = decay_grad[0:1, :]
    step_sig = sigmoid(step_rows[...] + step_bias[...])
    step_back = (rates[...] * decay_grad + in_head) * step_sig
    step_grad[...] = step_back.astype(step_grad.dtype)
    step_sums[0:1, :] += jnp.sum(step_back, axis=0, keepdims=True)
    step_sums[1:2, :] += jnp.sum(step_size * decay_grad, axis=0, keepdims=True)


def whole(array):
    zeros = (0,) * array.ndim
    return pl.BlockSpec(array.shape, lambda k: zeros)


def params(mebibytes):
    return pltpu.CompilerParams(dimension_semantics=("arbitrary",), vmem_limit_bytes=mebibytes * 1024 * 1024)


little = pl.CostEstimate(flops=10**6, bytes_accessed=2**16, transcendentals=0)


def run_scan(start, span, input_rows, state_rows, step_rows, state_entering, consts):
    channels = input_rows.shape[1]
    pairs = channels // LANES
    rows = span * BLOCK
    edge = start * BLOCK // 8 - 1

    def tokens(width):
        return pl.BlockSpec((BLOCK, width), lambda k: (start + k, 0))

    def results(width):
        return pl.BlockSpec((BLOCK, width), lambda k: (k, 0))

    if start == 0:
        before = (jnp.zeros((8, channels), f32), jnp.zeros((8, 2 * STATE), f32))
        before_specs = [whole(c) for c in before]
    else:
        before = (input_rows, state_rows)
        before_specs = [pl.BlockSpec((8, c.shape[1]), lambda k: (edge, 0)) for c in before]
    return pl.pallas_call(
        scan_kernel,
        grid=(span,),
        in_specs=[tokens(channels), tokens(2 * STATE), tokens(LANES)] + before_specs + [whole(state_entering)]
        + [whole(c) for c in consts],
        out_specs=[
            results(channels), results(channels), results(2 * STATE),
            pl.BlockSpec((1, pairs, LANES, STATE), lambda k: (k, 0, 0, 0)), whole(state_entering),
        ],
        out_shape=[
            jax.ShapeDtypeStruct((rows, channels), f32),
            jax.ShapeDtypeStruct((rows, channels), f32),
            jax.ShapeDtypeStruct((rows, 2 * STATE), f32),
            jax.ShapeDtypeStruct((span, pairs, LANES, STATE), f32),
            jax.ShapeDtypeStruct((pairs, LANES, STATE), f32),
        ],
        scratch_shapes=[pltpu.VMEM((BLOCK + 8, channels), f32), pltpu.VMEM((BLOCK + 8, 2 * STATE), f32)],
        compiler_params=params(LIM_SCAN),
        cost_estimate=little,
        name="scan",
    )(input_rows, state_rows, step_rows, *before, state_entering, *consts)


def run_scan_back(start, span, projections, kept, at, mixed_grad, carry, consts):
    channels = mixed_grad.shape[1]
    pairs = channels // LANES
    rows = span * BLOCK

    def tokens(width):
        return pl.BlockSpec((BLOCK, width), lambda k: (start + span - 1 - k, 0))

    def own(width, first=0):
        return pl.BlockSpec((BLOCK, width), lambda k: (first + span - 1 - k, 0))

    def shape(*dims):
        return jax.ShapeDtypeStruct(dims, f32)

    sums = [shape(8, channels), shape(8, 2 * STATE), shape(8, LANES)]
    ends = [jax.ShapeDtypeStruct(c.shape, f32) for c in carry]
    return pl.pallas_call(
        scan_back_kernel,
        grid=(span,),
        in_specs=[
            tokens(channels), tokens(2 * STATE), tokens(LANES), own(channels, at),
            own(2 * STATE, at), own(channels, at),
            pl.BlockSpec((1, pairs, LANES, STATE), lambda k: (at + span - 1 - k, 0, 0, 0)), tokens(channels),
        ] + [whole(c) for c in carry] + [whole(c) for c in consts],
        out_specs=[own(channels), own(2 * STATE), own(LANES)] + [whole(c) for c in sums + ends],
        out_shape=[
            jax.ShapeDtypeStruct((rows, channels), bf16), shape(rows, 2 * STATE),
            jax.ShapeDtypeStruct((rows, LANES), bf16),
        ] + sums + ends,
        scratch_shapes=[
            pltpu.VMEM((BLOCK + 8, channels), f32), pltpu.VMEM((BLOCK + 8, 2 * STATE), f32),
            pltpu.VMEM((BLOCK, BLOCK), f32), pltpu.VMEM((BLOCK, channels), f32), pltpu.VMEM((BLOCK, channels), f32),
        ],
        compiler_params=params(LIM_SCAN_BACK),
        cost_estimate=little,
        name="scan_back",
    )(*projections, *kept, mixed_grad, *carry, *consts)


def gate_kernel(mixed, gate_proj, out_grad, scales, gain, gate_out, gate_grad, mixed_grad, gain_sum):
    @pl.when(pl.program_id(0) == 0)
    def _():
        gain_sum[...] = jnp.zeros(gain_sum.shape, f32)

    proj, rows_mixed, grad = gate_proj[...], mixed[...], out_grad[...]
    sig = sigmoid(proj)
    act = proj * sig
    gated = rows_mixed * act
    scale, pull = scales[:, 0:1], scales[:, 1:2]
    scaled = gated * scale
    gate_out[...] = (scaled * gain[...]).astype(bf16)
    gain_sum[0:1, :] += jnp.sum(grad * scaled, axis=0, keepdims=True)
    gated_grad = scale * (grad * gain[...]) - gated * pull
    mixed_grad[...] = gated_grad * act
    back = gated_grad * rows_mixed * (sig * (1.0 + proj * (1.0 - sig)))
    gate_grad[...] = back.astype(bf16)


def run_gate(mixed, gate_proj, out_grad, scales, gain):
    rows, channels = mixed.shape
    tokens = pl.BlockSpec((BLOCK, channels), lambda k: (k, 0))
    small = jax.ShapeDtypeStruct((8, channels), f32)
    return pl.pallas_call(
        gate_kernel,
        grid=(rows // BLOCK,),
        in_specs=[tokens, tokens, tokens, pl.BlockSpec((BLOCK, 2), lambda k: (k, 0)), whole(gain)],
        out_specs=[tokens, tokens, tokens, whole(small)],
        out_shape=[
            jax.ShapeDtypeStruct((rows, channels), bf16), jax.ShapeDtypeStruct((rows, channels), bf16),
            jax.ShapeDtypeStruct((rows, channels), f32), small,
        ],
        compiler_params=params(LIM_GATE),
        cost_estimate=little,
        name="gate",
    )(mixed, gate_proj, out_grad, scales, gain)


def assemble_kernel(places, *refs):
    result = refs[-1]
    for i, piece in enumerate(refs[:-1]):
        result[pl.ds(pl.multiple_of(places[i], 16), piece.shape[0]), :] = piece[...]


def assemble(pieces, places, rows):
    def fixed(n, _):
        return (0, 0)

    width = pieces[0].shape[1]
    return pl.pallas_call(
        assemble_kernel,
        grid_spec=pltpu.PrefetchScalarGridSpec(
            num_scalar_prefetch=1, grid=(1,), in_specs=[pl.BlockSpec(piece.shape, fixed) for piece in pieces],
            out_specs=pl.BlockSpec((rows, width), fixed),
        ),
        out_shape=jax.ShapeDtypeStruct((rows, width), pieces[0].dtype),
        compiler_params=params(LIM_ASSEMBLE),
        cost_estimate=little,
        name="assemble",
    )(jnp.stack(places).astype(jnp.int32), *pieces)


def partial_kernel(count, steps, places, *refs):
    lefts, rights, result = refs[:count], refs[count : 2 * count], refs[2 * count]
    owners, rows = result.shape[0], result.shape[1] - 16
    for i in range(count):

        @pl.when(pl.program_id(0) // steps == i)
        def _():
            product = dot(lefts[i][...], rights[i][...], ((1,), (0,)))
            for owner in range(owners):
                own = product[owner * rows : (owner + 1) * rows]
                result[places[owner], 0:rows, :] = own
                top = jnp.max(jnp.abs(own), axis=0, keepdims=True)
                result[places[owner], rows : rows + 16, :] = jnp.broadcast_to(top, (16, own.shape[1]))


def partials(ring, lefts, rights):
    width = rights[0].shape[1]
    tile = 2 * LANES if width % (2 * LANES) == 0 else LANES
    steps, count = width // tile, len(lefts)
    rows = lefts[0].shape[0] // ring.count
    order = cycle(ring.count)
    places = [(order.index(i) - ring.place + ring.count) % ring.count for i in range(ring.count)]

    def column(i):
        return lambda n, _: (0, jnp.clip(n - i * steps, 0, steps - 1))

    def fixed(n, _):
        return (0, 0)

    return pl.pallas_call(
        lambda *refs: partial_kernel(count, steps, *refs),
        grid_spec=pltpu.PrefetchScalarGridSpec(
            num_scalar_prefetch=1, grid=(count * steps,),
            in_specs=[pl.BlockSpec(left.shape, fixed) for left in lefts]
            + [pl.BlockSpec((right.shape[0], tile), column(i)) for i, right in enumerate(rights)],
            out_specs=pl.BlockSpec((ring.count, rows + 16, tile), lambda n, _: (0, 0, n)),
        ),
        out_shape=jax.ShapeDtypeStruct((ring.count, rows + 16, count * width), f32),
        compiler_params=params(LIM_PARTIALS),
        cost_estimate=little,
        name="partials",
    )(jnp.stack(places).astype(jnp.int32), *lefts, *rights)


def normed_kernel(places, gate_rows, input_rows, gate_tile, input_tile, *refs):
    results, product = refs[:-1], refs[-1]
    total = dot(gate_rows[...], gate_tile[...], ((1,), (1,)))
    product[...] = total + dot(input_rows[...], input_tile[...], ((1,), (1,)))
    rows = results[0].shape[0]
    for i, result in enumerate(results):
        result[...] = product[pl.ds(pl.multiple_of(places[i] * rows, 16), rows), :]


def normed_parts(me, gate_grad, input_back, second_full, first_full):
    count = lax.axis_size("tensor")
    tokens, channels = gate_grad.shape
    width, tile = first_full.shape[0], 2 * LANES
    places = jnp.stack([i ^ me for i in range(count)]).astype(jnp.int32)

    def fixed(n, _):
        return (0, 0)

    return pl.pallas_call(
        normed_kernel,
        grid_spec=pltpu.PrefetchScalarGridSpec(
            num_scalar_prefetch=1, grid=(width // tile,),
            in_specs=[
                pl.BlockSpec((tokens, channels), fixed), pl.BlockSpec((tokens, channels), fixed),
                pl.BlockSpec((tile, channels), lambda n, _: (n, 0)), pl.BlockSpec((tile, channels), lambda n, _: (n, 0)),
            ],
            out_specs=[pl.BlockSpec((tokens // count, tile), lambda n, _: (0, n))] * count,
            scratch_shapes=[pltpu.VMEM((tokens, tile), f32)],
        ),
        out_shape=[jax.ShapeDtypeStruct((tokens // count, width), f32)] * count,
        compiler_params=params(LIM_NORMED_PARTS),
        cost_estimate=little,
        name="normed_parts",
    )(places, gate_grad, input_back, second_full, first_full)


def cycle(count):
    return list(range(0, count, 2)) + list(range(count - 1, 0, -2))


class Ring:
    def __init__(self):
        self.count = lax.axis_size("dp")
        order = cycle(self.count)
        self.up = [(order[i], order[(i + 1) % self.count]) for i in range(self.count)]
        self.down = [(b, a) for a, b in self.up]
        me = lax.axis_index("dp")
        self.place = jnp.where(me % 2 == 0, me // 2, self.count - 1 - me // 2)

    def owner(self, offset):
        place = (self.place + offset + self.count) % self.count
        return jnp.where(place < self.count // 2, 2 * place, 2 * (self.count - 1 - place) + 1)


def middle(rows):
    return (rows // 2 + 15) // 16 * 16


class Gather:
    def __init__(self, ring, shard):
        self.ring, self.shard, self.step = ring, shard, 0
        self.held = [(shard, 0, 0)]
        self.last = (shard, shard)

    def hop(self):
        self.step += 1
        half, cut = self.ring.count // 2, middle(self.shard.shape[0])
        up, down = self.last
        offsets = ((-self.step, 0), (self.step, 0))
        if self.step == half:
            up, down = up[:cut], down[cut:]
            offsets = ((half, 0), (half, cut))
        self.last = (lax.ppermute(up, "dp", self.ring.up), lax.ppermute(down, "dp", self.ring.down))
        self.held += [(piece, *offset) for piece, offset in zip(self.last, offsets)]

    def after(self, *marks):
        self.last, marks = fence(self.last, marks)
        self.held[-2:] = [(piece, *old[1:]) for piece, old in zip(self.last, self.held[-2:])]
        return marks if len(marks) > 1 else marks[0]

    def result(self):
        rows = self.shard.shape[0]
        pieces = [piece for piece, _, _ in self.held]
        places = [self.ring.owner(offset) * rows + skip for _, offset, skip in self.held]
        return assemble(pieces, places, rows * self.ring.count)


def encode(rows, limit):
    power = jnp.ceil(jnp.log2(jnp.maximum(limit, 1e-30)))
    ours = lax.broadcasted_iota(jnp.int32, rows.shape, 0) < rows.shape[0] - 16
    return jnp.where(ours, rows * jnp.exp2(15.0 - power), power).astype(jnp.float16)


def decode(payload):
    power = payload[-16:-15].astype(f32)
    return payload.astype(f32) * jnp.exp2(power - 15.0), jnp.exp2(power)


class Scatter:
    def __init__(self, ring, parts):
        self.ring, self.parts = ring, parts
        self.step = ring.count // 2
        self.rows = parts.shape[1] - 16
        self.cut = middle(self.rows)
        far, top = parts[self.step], parts[self.step, -16:-15]
        upper = jnp.concatenate([far[: self.cut], far[-16:]], axis=0)
        self.send = (encode(upper, top), encode(far[self.cut :], top))

    def hop(self):
        self.send = fence(*self.send)
        self.got = (lax.ppermute(self.send[0], "dp", self.ring.up), lax.ppermute(self.send[1], "dp", self.ring.down))

    def after(self, *marks):
        self.got, marks = fence(self.got, marks)
        return marks if len(marks) > 1 else marks[0]

    def before(self, *marks):
        self.send, marks = fence(self.send, marks)
        return marks if len(marks) > 1 else marks[0]

    def add(self):
        first = self.step == self.ring.count // 2
        self.got = fence(*self.got)
        (up, up_top), (down, down_top) = (decode(g) for g in self.got)
        if first:
            up, down = jnp.pad(up, ((0, self.rows - self.cut), (0, 0))), jnp.pad(down, ((self.cut, 0), (0, 0)))
            upper = lax.broadcasted_iota(jnp.int32, up.shape, 0) < self.cut
            up = jnp.where(upper, up, 0.0)
        self.step -= 1
        if self.step == 0:
            return (self.parts[0] + up + down)[: self.rows]
        above, below = self.parts[self.step], self.parts[self.ring.count - self.step]
        self.send = (
            encode(above + up, above[-16:-15] + up_top),
            encode(below + down, below[-16:-15] + down_top),
        )
        return None


def fence(*arrays):
    flat, tree = jax.tree.flatten(arrays)
    return jax.tree.unflatten(tree, lax.optimization_barrier(flat))


def across(array, bit, axis="tensor"):
    count = lax.axis_size(axis)
    return lax.ppermute(array, axis, [(i, i ^ bit) for i in range(count)])


def group_sum(array, axis, first, count):
    terms = [array] + [across(array, first * other, axis) for other in range(1, count)]
    while len(terms) > 1:
        terms = [terms[i] + terms[i + 1] for i in range(0, len(terms), 2)]
    return terms[0]


def cube_sum(array, axis):
    bit = 1
    while bit < lax.axis_size(axis):
        array = array + across(array, bit, axis)
        bit *= 2
    return array


def shards(
    block_input, cotangent, norm_gain, gate_weight, input_weight, state_weight, step_weight, conv_input,
    conv_input_bias, conv_state, conv_state_bias, step_bias, decay_log, skip_scale, gate_gain, out_weight,
):
    group_count = lax.axis_size("tensor")
    me = lax.axis_index("tensor")
    ring = Ring()
    half = ring.count // 2
    local_rows = block_input.shape[0]
    channels = gate_gain.shape[0]
    heads = step_bias.shape[0]
    inner_total = channels * group_count
    share = 2 * STATE // group_count
    tokens = local_rows * group_count
    blocks = tokens // BLOCK
    fold = LANES // share
    folded = tokens // fold
    rows_dot = ((1,), (0,))
    back_dot = ((1,), (1,))

    state_mine = lax.dynamic_slice_in_dim(state_weight, me * share, share, 1)
    first = Gather(
        ring,
        jnp.concatenate(
            [input_weight, state_mine, jnp.pad(step_weight, ((0, 0), (0, LANES - share - heads)))], axis=1
        ).astype(bf16),
    )
    first.hop()
    row_scale = lax.rsqrt(jnp.mean(block_input * block_input, axis=1, keepdims=True) + epsilon)
    normed = (block_input * row_scale * norm_gain).astype(bf16)
    second_weight = jnp.concatenate([gate_weight, out_weight.T], axis=1).astype(bf16)
    rates = -jnp.exp(decay_log)

    def per_head(vector):
        return jnp.pad(vector, (0, LANES - heads))[None, :]

    skip = jnp.repeat(skip_scale, HEAD_DIM)[None, :]
    head_of = (
        lax.broadcasted_iota(jnp.int32, (channels, LANES), 0) // HEAD_DIM
        == lax.broadcasted_iota(jnp.int32, (channels, LANES), 1)
    ).astype(f32)
    scan_consts = (
        conv_input, conv_input_bias[None, :], conv_state, conv_state_bias[None, :], per_head(step_bias),
        per_head(rates), skip,
    )
    back_consts = (conv_input, conv_state, per_head(step_bias), per_head(rates), skip, head_of)
    carried = jnp.zeros((channels // LANES, LANES, STATE), f32)
    carry = (jnp.zeros((8, channels), f32), jnp.zeros((8, 2 * STATE), f32), carried, jnp.zeros((8, LANES), f32))
    gain = gate_gain[None, :]
    normed, scan_consts, back_consts, carried, carry, gain = first.after(
        normed, scan_consts, back_consts, carried, carry, gain
    )
    first.hop()
    far, near = across(normed, 2), across(normed, 1)
    for _ in range(half - 3):
        first.hop()
    far, near, second_weight, cot_low = first.after(far, near, second_weight, cotangent.astype(bf16))
    first.hop()
    normed_pieces = (normed, near, far, across(far, 1))
    normed_all = assemble(normed_pieces, [(me ^ bits) * local_rows for bits in range(4)], tokens)
    second = Gather(ring, second_weight)
    second.hop()
    cot_all = lax.all_gather(cot_low, "tensor", axis=0, tiled=True)
    first_full, normed_all = second.after(first.result(), normed_all)
    second.hop()

    input_full, tail_full = first_full[:, :channels], first_full[:, channels:]
    tail_proj = dot(normed_all, tail_full, rows_dot)
    step_proj = jnp.pad(tail_proj[:, share : share + heads], ((0, 0), (0, LANES - heads)))
    state_mine = jnp.concatenate([tail_proj[i * folded : (i + 1) * folded, :share] for i in range(fold)], axis=1)
    far = across(state_mine, 2)
    same_x, same_core, diagonal = across(state_mine, 1), far, across(far, 1)
    right_core = me % 2 == 1
    near = (jnp.where(right_core, same_x, state_mine), jnp.where(right_core, state_mine, same_x))
    away = (jnp.where(right_core, diagonal, same_core), jnp.where(right_core, same_core, diagonal))
    right_chip = me // 2 == 1
    state_parts = [jnp.where(right_chip, away[i], near[i]) for i in range(2)]
    state_parts += [jnp.where(right_chip, near[i], away[i]) for i in range(2)]
    state_proj = jnp.concatenate(
        [jnp.concatenate([p[:, i * share : (i + 1) * share] for p in state_parts], axis=1) for i in range(fold)], axis=0
    )
    input_proj = dot(normed_all, input_full, rows_dot)
    span = 2
    scanned = []
    input_proj, tail_proj = second.after(input_proj, tail_proj)
    second.hop()
    for start in range(0, blocks, span):
        scanned.append(run_scan(start, span, input_proj, state_proj, step_proj, carried, scan_consts))
        carried = scanned[-1][4]
        if second.step < half:
            carried = second.after(carried)
            second.hop()
    while second.step < half:
        second.hop()
    second_full = second.result()
    gate_full, out_full = second_full[:, :channels], second_full[:, channels:]
    mixed = jnp.concatenate([block[0] for block in scanned], axis=0)

    gate_proj = dot(normed_all, gate_full, rows_dot)
    gated = mixed * (gate_proj * jax.nn.sigmoid(gate_proj))
    gate_out_grad = dot(cot_all, out_full, rows_dot)
    sums = jnp.stack([jnp.sum(gated * gated, axis=1), jnp.sum(gate_out_grad * gate_gain * gated, axis=1)])
    sums = (sums + across(sums, 1)) + (across(sums, 2) + across(sums, 3))
    gate_scale = lax.rsqrt(sums[0] / inner_total + epsilon)
    scales = jnp.stack([gate_scale, gate_scale**3 * (sums[1] / inner_total)], axis=1)
    gate_out, gate_grad, mixed_grad, gain_sum = run_gate(mixed, gate_proj, gate_out_grad, scales, gain)

    normed_t = normed_all.T
    pair_ring = Scatter(ring, partials(ring, (cot_all.T, normed_t), (gate_out, gate_grad)))
    done = []
    for turn in range(blocks // span):
        if turn == 0:
            carry, late_out = pair_ring.before(carry, gate_out)
            pair_ring.hop()
            branch_part = dot(late_out, out_full, back_dot)
            branch = lax.psum_scatter(branch_part, "tensor", scatter_dimension=0, tiled=True)
            carry, branch_part = fence(carry, branch_part)
        else:
            carry = pair_ring.after(carry)
            pair_ring.add()
            carry = pair_ring.before(carry)
            pair_ring.hop()
        start = blocks - span * (turn + 1)
        kept = scanned[start // span]
        kept = [kept[1], kept[2], kept[0], kept[3]]
        result = run_scan_back(
            start, span, (input_proj, state_proj, step_proj), kept, 0, mixed_grad, carry, back_consts
        )
        done.insert(0, result)
        carry = tuple(result[6:])
    done = pair_ring.after(done)
    pair_ring.add()
    done = pair_ring.before(done)
    pair_ring.hop()
    input_back, state_back, step_back = (jnp.concatenate([d[i] for d in done], axis=0) for i in range(3))
    input_sums, state_sums, step_sums = (sum(d[i] for d in done) for i in range(3, 6))

    packed = jnp.concatenate(
        [
            state_sums[:5].reshape(-1),
            input_sums[:5].reshape(-1),
            gain_sum[0],
            jnp.sum(input_sums[5].reshape(heads, HEAD_DIM), axis=1),
            step_sums[0, :heads],
            step_sums[1, :heads] * rates,
        ]
    )
    packed = jnp.pad(packed, (0, -packed.shape[0] % LANES)).reshape(-1, LANES)

    def state_columns(index):
        mine = lax.dynamic_slice_in_dim(state_back, index * share, share, 1)
        return jnp.concatenate([mine[i * folded : (i + 1) * folded] for i in range(fold)], axis=1)

    for_far, for_me = across(state_columns(me ^ 3), 1), across(state_columns(me ^ 1), 1)
    packed, for_far, for_me, input_back = fence(packed, for_far, for_me, input_back)
    far = state_columns(me ^ 2) + for_far
    far, input_back = fence(far, input_back)
    from_far = across(far, 2)
    parts = normed_parts(me, gate_grad, input_back, second_full, first_full)
    from_far, branch, *parts = pair_ring.after(from_far, branch, *parts)
    block_output = block_input + branch
    pair_ring.add()
    from_far = pair_ring.before(from_far)
    pair_ring.hop()
    state_share = (state_columns(me) + for_me + from_far).astype(bf16)
    state_share = jnp.concatenate([state_share[:, i * share : (i + 1) * share] for i in range(fold)], axis=0)
    tail = jnp.concatenate(
        [state_share, step_back[:, :heads], jnp.zeros((tokens, LANES - share - heads), bf16)], axis=1
    )

    def whole_part(bits):
        rows = lax.dynamic_slice_in_dim(tail, (me ^ bits) * local_rows, local_rows, 0)
        return parts[bits] + dot(rows, tail_full, back_dot)

    for_far, for_me = across(whole_part(3), 1), across(whole_part(1), 1)
    input_ring = Scatter(ring, partials(ring, (normed_t,), (jnp.concatenate([input_back, tail], axis=1),)))
    for_far, for_me, pair_ring.got = input_ring.before(for_far, for_me, pair_ring.got)
    input_ring.hop()
    pair_sum = pair_ring.add()
    while pair_sum is None:
        pair_ring.hop()
        pair_sum = pair_ring.add()
    sent = whole_part(2) + for_far
    sent = jnp.concatenate([sent, jnp.zeros((16, sent.shape[1]), f32)], axis=0)
    from_far = across(encode(sent, jnp.max(jnp.abs(sent), axis=0, keepdims=True)), 2)
    packed = cube_sum(packed, "dp")
    input_sum = input_ring.add()
    while input_sum is None:
        input_ring.hop()
        if input_ring.step == 2:
            from_far = input_ring.after(from_far)
        input_sum = input_ring.add()
    normed_grad = whole_part(0) + for_me + decode(from_far)[0][:local_rows]
    tail_sum = input_sum[:, channels:]

    weighted_grad = normed_grad * norm_gain
    norm_gain_part = jnp.sum(normed_grad * block_input * row_scale, axis=0)
    input_grad = (
        cotangent
        + row_scale * weighted_grad
        - block_input * row_scale**3 * jnp.mean(weighted_grad * block_input, axis=1, keepdims=True)
    )
    local = packed[10 * STATE // LANES :].reshape(-1)
    spread = [jnp.where(me == i, tail_sum[:, :share], 0.0) for i in range(group_count)]
    spread = jnp.concatenate(
        [jnp.concatenate(spread[i : i + fold], axis=1) for i in range(0, group_count, fold)], axis=0
    )
    spread = cube_sum(spread, "tensor")
    rows = tail_sum.shape[0]
    state_grad = jnp.concatenate([spread[i * rows : (i + 1) * rows] for i in range(group_count // fold)], axis=1)
    shared = group_sum(norm_gain_part.reshape(-1, LANES), "tensor", 1, 4)
    shared = group_sum(group_sum(shared, "dp", 2, ring.count // 2), "dp", 1, 2).reshape(-1)
    state_sum = cube_sum(packed[: 10 * STATE // LANES], "tensor").reshape(5, 2 * STATE)
    at = 6 * channels
    return (
        block_output,
        input_grad,
        shared,
        pair_sum[:, channels:],
        input_sum[:, :channels],
        state_grad,
        tail_sum[:, share : share + heads],
        local[: 4 * channels].reshape(4, channels),
        local[4 * channels : 5 * channels],
        state_sum[:4],
        state_sum[4],
        local[at + heads : at + 2 * heads],
        local[at + 2 * heads : at + 3 * heads],
        local[at : at + heads],
        local[5 * channels : at],
        pair_sum[:, :channels].T,
    )


def solution(mesh):
    rows = P(("dp", "tensor"), None)
    both = P("dp", "tensor")
    inner = P("tensor")
    return jax.shard_map(
        shards,
        mesh=mesh,
        in_specs=(
            rows, rows, P(), both, both, P("dp", None), both, P(None, "tensor"), inner, P(), P(), inner, inner,
            inner, inner, P("tensor", "dp"),
        ),
        out_specs=(
            rows, rows, P(), both, both, P("dp", None), both, P(None, "tensor"), inner, P(), P(), inner, inner,
            inner, inner, P("tensor", "dp"),
        ),
        check_vma=False,
    )
```

```python
import jax
import jax.numpy as jnp
from jax import lax
from jax.experimental import pallas as pl
from jax.experimental.pallas import tpu as pltpu
from jax.sharding import PartitionSpec as P

HEAD_DIM = 64
STATE = 128
BLOCK = 256
SEQ = 1024
LANES = 128

LIM_SCAN = 61
LIM_SCAN_BACK = 61
LIM_NORMED_PARTS = 61

epsilon = 1e-05
high = lax.Precision.HIGH
highest = lax.Precision.HIGHEST
f32 = jnp.float32
bf16 = jnp.bfloat16


def dot(left, right, dims, precision=None):
    return lax.dot_general(
        left, right, (dims, ((), ())), precision=precision, preferred_element_type=f32
    )


def sigmoid(v):
    return 1.0 / (1.0 + jnp.exp(-v))


def softplus(v):
    return jnp.maximum(v, 0.0) + jnp.log1p(jnp.exp(-jnp.abs(v)))


def iota(shape, axis):
    return lax.broadcasted_iota(jnp.int32, shape, axis)


def pair_columns(table, pair):
    lane = iota((table.shape[0], LANES), 1)
    return jnp.where(lane < HEAD_DIM, table[:, 2 * pair : 2 * pair + 1], table[:, 2 * pair + 1 : 2 * pair + 2])


def decay_tables(step_rows, step_bias, rates):
    step_size = softplus(step_rows + step_bias)
    earlier = (iota((BLOCK, BLOCK), 0) >= iota((BLOCK, BLOCK), 1)).astype(f32)
    cumulative = dot(earlier, step_size * rates, ((1,), (0,)), highest)
    return step_size, cumulative, jnp.exp(cumulative), jnp.exp(cumulative[BLOCK - 1 : BLOCK, :] - cumulative)


def state_decay(from_start, pair):
    last = from_start[BLOCK - 1 : BLOCK, :]
    row = iota((LANES, STATE), 0)
    return jnp.where(row < HEAD_DIM, last[:, 2 * pair : 2 * pair + 1], last[:, 2 * pair + 1 : 2 * pair + 2])


def shifted_conv(rows_ref, before, buffer, taps, conv_bias, first):
    @pl.when(first)
    def _():
        buffer[0:8, :] = before[...]

    @pl.when(jnp.logical_not(first))
    def _():
        buffer[0:8, :] = buffer[BLOCK : BLOCK + 8, :]

    buffer[8 : BLOCK + 8, :] = rows_ref[...]
    total = conv_bias[...] + taps[0:1, :] * buffer[8 : BLOCK + 8, :]
    for tap in range(1, 4):
        total = total + taps[tap : tap + 1, :] * buffer[8 - tap : BLOCK + 8 - tap, :]
    return total


def scan_kernel(
    input_rows, state_rows, step_rows, input_before, state_before, state_entering,
    conv_input, conv_input_bias, conv_state, conv_state_bias, step_bias, rates, skip,
    mixed, input_conv, state_conv, entering, carried, input_buffer, state_buffer,
):
    first = pl.program_id(0) == 0
    pairs = input_rows.shape[1] // LANES

    @pl.when(first)
    def _():
        carried[...] = state_entering[...]

    input_conv[...] = shifted_conv(input_rows, input_before, input_buffer, conv_input, conv_input_bias, first)
    state_pre = shifted_conv(state_rows, state_before, state_buffer, conv_state, conv_state_bias, first)
    state_conv[...] = state_pre
    state_act = state_pre * sigmoid(state_pre)
    writes, reads = state_act[:, :STATE], state_act[:, STATE:]
    meeting = dot(reads, writes, ((1,), (1,)), high)
    step_size, cumulative, from_start, to_end = decay_tables(step_rows[...], step_bias[...], rates[...])
    cumulative_t = cumulative.T
    causal = iota((BLOCK, BLOCK), 0) >= iota((BLOCK, BLOCK), 1)
    lane = iota((BLOCK, LANES), 1)
    for pair in range(pairs):
        columns = slice(pair * LANES, pair * LANES + LANES)
        pre = input_conv[:, columns]
        inputs = pre * sigmoid(pre)
        weighted = inputs * pair_columns(step_size, pair)
        state_in = carried[pair]
        entering[0, pair] = state_in
        out = dot(reads, state_in, ((1,), (1,)), high) * pair_columns(from_start, pair)
        for side in range(2):
            head = 2 * pair + side
            gap = cumulative[:, head : head + 1] - cumulative_t[head : head + 1, :]
            mixing = jnp.exp(jnp.where(causal, gap, -1e30)) * meeting
            mine = (lane < HEAD_DIM) if side == 0 else (lane >= HEAD_DIM)
            out = out + dot(mixing, jnp.where(mine, weighted, 0.0), ((1,), (0,)), high)
        fresh = dot(weighted * pair_columns(to_end, pair), writes, ((0,), (0,)), high)
        carried[pair] = state_decay(from_start, pair) * state_in + fresh
        mixed[:, columns] = out + skip[:, columns] * inputs


def scan_back_kernel(
    input_rows, state_rows, step_rows, input_conv, state_conv, mixed, entering, mixed_grad,
    input_after, state_after, state_leaving, decay_after,
    conv_input, conv_state, step_bias, rates, skip, head_of,
    input_grad, state_grad, step_grad, input_sums, state_sums, step_sums, input_first, state_first, carried, later,
    input_buffer, state_buffer, gap_grad, out_products, in_products,
):
    first = pl.program_id(0) == 0
    pairs = input_rows.shape[1] // LANES

    @pl.when(first)
    def _():
        carried[...] = state_leaving[...]
        later[...] = decay_after[...]
        input_sums[...] = jnp.zeros(input_sums.shape, f32)
        state_sums[...] = jnp.zeros(state_sums.shape, f32)
        step_sums[...] = jnp.zeros(step_sums.shape, f32)
        input_buffer[BLOCK : BLOCK + 8, :] = input_after[...]
        state_buffer[BLOCK : BLOCK + 8, :] = state_after[...]

    @pl.when(jnp.logical_not(first))
    def _():
        input_buffer[BLOCK : BLOCK + 8, :] = input_buffer[0:8, :]
        state_buffer[BLOCK : BLOCK + 8, :] = state_buffer[0:8, :]

    state_pre = state_conv[...]
    state_sig = sigmoid(state_pre)
    state_act = state_pre * state_sig
    writes, reads = state_act[:, :STATE], state_act[:, STATE:]
    meeting_t = dot(writes, reads, ((1,), (1,)), high)
    step_size, cumulative, from_start, to_end = decay_tables(step_rows[...], step_bias[...], rates[...])
    cumulative_t = cumulative.T
    causal_t = iota((BLOCK, BLOCK), 0) <= iota((BLOCK, BLOCK), 1)
    lane = iota((BLOCK, LANES), 1)
    gap_grad[...] = jnp.zeros(gap_grad.shape, f32)
    writes_grad = jnp.zeros((BLOCK, STATE), f32)
    reads_grad = jnp.zeros((BLOCK, STATE), f32)
    for pair in range(pairs):
        columns = slice(pair * LANES, pair * LANES + LANES)
        pre = input_conv[:, columns]
        sig = sigmoid(pre)
        inputs = pre * sig
        step_pair = pair_columns(step_size, pair)
        weighted = inputs * step_pair
        out_grad = mixed_grad[:, columns]
        skip_product = out_grad * inputs
        input_sums[5:6, columns] += jnp.sum(skip_product, axis=0, keepdims=True)
        end_pair = pair_columns(to_end, pair)
        leaving_grad = carried[pair]
        weighted_grad = dot(writes, leaving_grad, ((1,), (1,)), high) * end_pair
        for side in range(2):
            head = 2 * pair + side
            gap = cumulative_t[head : head + 1, :] - cumulative[:, head : head + 1]
            within = jnp.exp(jnp.where(causal_t, gap, -1e30))
            mine = (lane < HEAD_DIM) if side == 0 else (lane >= HEAD_DIM)
            own_grad = jnp.where(mine, out_grad, 0.0)
            weighted_grad = weighted_grad + dot(within * meeting_t, own_grad, ((1,), (0,)), high)
            gap_grad[...] += within * dot(weighted, own_grad, ((1,), (1,)), high)
        start_grad = out_grad * pair_columns(from_start, pair)
        reads_grad = reads_grad + dot(start_grad, entering[0, pair], ((1,), (0,)), high)
        writes_grad = writes_grad + dot(weighted * end_pair, leaving_grad, ((1,), (0,)), high)
        carried[pair] = state_decay(from_start, pair) * leaving_grad + dot(start_grad, reads, ((0,), (0,)), high)
        out_products[:, columns] = out_grad * mixed[:, columns] - skip[:, columns] * skip_product
        in_products[:, columns] = inputs * weighted_grad
        inputs_grad = skip[:, columns] * out_grad + step_pair * weighted_grad
        input_buffer[0:BLOCK, columns] = inputs_grad * (sig * (1.0 + pre * (1.0 - sig)))
    reads_grad = reads_grad + dot(gap_grad[...], writes, ((0,), (0,)), high)
    writes_grad = writes_grad + dot(gap_grad[...], reads, ((1,), (0,)), high)
    state_slope = state_sig * (1.0 + state_pre * (1.0 - state_sig))
    state_buffer[0:BLOCK, 0:STATE] = writes_grad * state_slope[:, :STATE]
    state_buffer[0:BLOCK, STATE : 2 * STATE] = reads_grad * state_slope[:, STATE:]

    for buffer, rows, taps, sums, result in (
        (input_buffer, input_rows, conv_input, input_sums, input_grad),
        (state_buffer, state_rows, conv_state, state_sums, state_grad),
    ):
        raw = rows[...]
        total = jnp.zeros(raw.shape, f32)
        for tap in range(4):
            ahead = buffer[tap : tap + BLOCK, :]
            total = total + taps[tap : tap + 1, :] * ahead
            sums[tap : tap + 1, :] += jnp.sum(ahead * raw, axis=0, keepdims=True)
        sums[4:5, :] += jnp.sum(buffer[0:BLOCK, :], axis=0, keepdims=True)
        result[...] = total.astype(result.dtype)
    input_first[...] = input_buffer[0:8, :]
    state_first[...] = state_buffer[0:8, :]

    out_head = dot(out_products[...], head_of[...], ((1,), (0,)), high)
    in_head = dot(in_products[...], head_of[...], ((1,), (0,)), high)
    upper = (iota((BLOCK, BLOCK), 0) <= iota((BLOCK, BLOCK), 1)).astype(f32)
    decay_grad = dot(upper, out_head - step_size * in_head, ((1,), (0,)), highest) + later[0:1, :]
    later[0:1, :] = decay_grad[0:1, :]
    step_sig = sigmoid(step_rows[...] + step_bias[...])
    step_back = (rates[...] * decay_grad + in_head) * step_sig
    step_grad[...] = step_back.astype(step_grad.dtype)
    step_sums[0:1, :] += jnp.sum(step_back, axis=0, keepdims=True)
    step_sums[1:2, :] += jnp.sum(step_size * decay_grad, axis=0, keepdims=True)


def whole(array):
    zeros = (0,) * array.ndim
    return pl.BlockSpec(array.shape, lambda k: zeros)


def params(mebibytes):
    return pltpu.CompilerParams(dimension_semantics=("arbitrary",), vmem_limit_bytes=mebibytes * 1024 * 1024)


little = pl.CostEstimate(flops=10**6, bytes_accessed=2**16, transcendentals=0)


def run_scan(start, span, input_rows, state_rows, step_rows, state_entering, consts):
    channels = input_rows.shape[1]
    pairs = channels // LANES
    rows = span * BLOCK
    edge = start * BLOCK // 8 - 1

    def tokens(width):
        return pl.BlockSpec((BLOCK, width), lambda k: (start + k, 0))

    def results(width):
        return pl.BlockSpec((BLOCK, width), lambda k: (k, 0))

    if start == 0:
        before = (jnp.zeros((8, channels), f32), jnp.zeros((8, 2 * STATE), f32))
        before_specs = [whole(c) for c in before]
    else:
        before = (input_rows, state_rows)
        before_specs = [pl.BlockSpec((8, c.shape[1]), lambda k: (edge, 0)) for c in before]
    return pl.pallas_call(
        scan_kernel,
        grid=(span,),
        in_specs=[tokens(channels), tokens(2 * STATE), tokens(LANES)] + before_specs + [whole(state_entering)]
        + [whole(c) for c in consts],
        out_specs=[
            results(channels), results(channels), results(2 * STATE),
            pl.BlockSpec((1, pairs, LANES, STATE), lambda k: (k, 0, 0, 0)), whole(state_entering),
        ],
        out_shape=[
            jax.ShapeDtypeStruct((rows, channels), f32),
            jax.ShapeDtypeStruct((rows, channels), f32),
            jax.ShapeDtypeStruct((rows, 2 * STATE), f32),
            jax.ShapeDtypeStruct((span, pairs, LANES, STATE), f32),
            jax.ShapeDtypeStruct((pairs, LANES, STATE), f32),
        ],
        scratch_shapes=[pltpu.VMEM((BLOCK + 8, channels), f32), pltpu.VMEM((BLOCK + 8, 2 * STATE), f32)],
        compiler_params=params(LIM_SCAN),
        cost_estimate=little,
        name="scan",
    )(input_rows, state_rows, step_rows, *before, state_entering, *consts)


def run_scan_back(start, span, projections, kept, at, mixed_grad, carry, consts):
    channels = mixed_grad.shape[1]
    pairs = channels // LANES
    rows = span * BLOCK

    def tokens(width):
        return pl.BlockSpec((BLOCK, width), lambda k: (start + span - 1 - k, 0))

    def own(width, first=0):
        return pl.BlockSpec((BLOCK, width), lambda k: (first + span - 1 - k, 0))

    def shape(*dims):
        return jax.ShapeDtypeStruct(dims, f32)

    sums = [shape(8, channels), shape(8, 2 * STATE), shape(8, LANES)]
    ends = [jax.ShapeDtypeStruct(c.shape, f32) for c in carry]
    return pl.pallas_call(
        scan_back_kernel,
        grid=(span,),
        in_specs=[
            tokens(channels), tokens(2 * STATE), tokens(LANES), own(channels, at),
            own(2 * STATE, at), own(channels, at),
            pl.BlockSpec((1, pairs, LANES, STATE), lambda k: (at + span - 1 - k, 0, 0, 0)), tokens(channels),
        ] + [whole(c) for c in carry] + [whole(c) for c in consts],
        out_specs=[own(channels), own(2 * STATE), own(LANES)] + [whole(c) for c in sums + ends],
        out_shape=[
            jax.ShapeDtypeStruct((rows, channels), bf16), shape(rows, 2 * STATE),
            jax.ShapeDtypeStruct((rows, LANES), bf16),
        ] + sums + ends,
        scratch_shapes=[
            pltpu.VMEM((BLOCK + 8, channels), f32), pltpu.VMEM((BLOCK + 8, 2 * STATE), f32),
            pltpu.VMEM((BLOCK, BLOCK), f32), pltpu.VMEM((BLOCK, channels), f32), pltpu.VMEM((BLOCK, channels), f32),
        ],
        compiler_params=params(LIM_SCAN_BACK),
        cost_estimate=little,
        name="scan_back",
    )(*projections, *kept, mixed_grad, *carry, *consts)


def fixed_block(*shape):
    zeros = (0,) * len(shape)
    return pl.BlockSpec(shape, lambda n, *_: zeros)


def call(kernel, places, steps, operands, in_specs, out_specs, out_shape, name, scratch=()):
    return pl.pallas_call(
        kernel,
        grid_spec=pltpu.PrefetchScalarGridSpec(
            num_scalar_prefetch=1, grid=(steps,), in_specs=in_specs, out_specs=out_specs, scratch_shapes=list(scratch)
        ),
        out_shape=out_shape,
        compiler_params=params(61),
        cost_estimate=little,
        name=name,
    )(jnp.stack(places).astype(jnp.int32), *operands)


def lay(places, pieces, result, first=0):
    for i, piece in enumerate(pieces):
        result[pl.ds(pl.multiple_of(places[first + i], 16), piece.shape[0]), :] = piece[...]


TILE = 256


def tile_columns(ref, n, first=0):
    return ref[:, pl.ds(pl.multiple_of(n * TILE + first, LANES), TILE)]


def first_project(weights, weight_places, tokens, token_places, channels):
    count = len(weights)
    depth, width = tokens[0].shape[1], weights[0].shape[1]
    rows = tokens[0].shape[0] * len(tokens)

    def kernel(places, *refs):
        pieces, (normed, full, input_proj, tail_proj) = refs[:-4], refs[-4:]
        n = pl.program_id(0)

        @pl.when(n == 0)
        def _():
            lay(places, pieces[:count], full)
            lay(places, pieces[count:], normed, count)
            tail_proj[...] = dot(normed[...], full[:, channels:], ((1,), (0,)))

        input_proj[...] = dot(normed[...], tile_columns(full, n), ((1,), (0,)))

    return call(
        kernel, weight_places + token_places, channels // TILE, (*weights, *tokens),
        [fixed_block(*piece.shape) for piece in (*weights, *tokens)],
        [
            fixed_block(rows, depth), fixed_block(depth, width), pl.BlockSpec((rows, TILE), lambda n, _: (0, n)),
            fixed_block(rows, width - channels),
        ],
        [
            jax.ShapeDtypeStruct((rows, depth), bf16), jax.ShapeDtypeStruct((depth, width), bf16),
            jax.ShapeDtypeStruct((rows, channels), f32), jax.ShapeDtypeStruct((rows, width - channels), f32),
        ],
        "first_project",
    )


def second_project(weights, places, normed, cot, mixed, gain):
    count, halves = len(weights), len(mixed)
    width = weights[0].shape[1]
    rows, depth = normed.shape
    channels = width // 2
    part_rows = mixed[0].shape[0]

    def kernel(places, *refs):
        pieces, (normed_ref, cot_ref, gain_ref), mixed_refs = refs[:count], refs[count : count + 3], refs[count + 3 : -4]
        full, gate_proj, out_grad, sums = refs[-4:]
        n = pl.program_id(0)

        @pl.when(n == 0)
        def _():
            lay(places, pieces, full)
            sums[...] = jnp.zeros(sums.shape, f32)

        gate_proj[...] = dot(normed_ref[...], tile_columns(full, n), ((1,), (0,)))
        out_grad[...] = dot(cot_ref[...], tile_columns(full, n, channels), ((1,), (0,)))
        ones = jnp.ones((8, TILE), f32)
        for i in range(halves):
            at = slice(i * part_rows, (i + 1) * part_rows)
            proj = gate_proj[at, :]
            gated = mixed_refs[i][...] * (proj * sigmoid(proj))
            pulled = out_grad[at, :] * gain_ref[...] * gated
            sums[0:8, at] += dot(ones, gated * gated, ((1,), (1,)), highest)
            sums[8:16, at] += dot(ones, pulled, ((1,), (1,)), highest)

    tile = pl.BlockSpec((rows, TILE), lambda n, _: (0, n))
    return call(
        kernel, places, channels // TILE, (*weights, normed, cot, gain, *mixed),
        [fixed_block(*piece.shape) for piece in (*weights, normed, cot)]
        + [pl.BlockSpec((1, TILE), lambda n, _: (0, n))]
        + [pl.BlockSpec((part_rows, TILE), lambda n, _: (0, n)) for _ in mixed],
        [fixed_block(depth, width), tile, tile, fixed_block(16, rows)],
        [
            jax.ShapeDtypeStruct((depth, width), bf16), jax.ShapeDtypeStruct((rows, channels), f32),
            jax.ShapeDtypeStruct((rows, channels), f32), jax.ShapeDtypeStruct((16, rows), f32),
        ],
        "second_project",
    )


def store_shares(places, product, result, columns):
    owners, rows = result.shape[-3], result.shape[-2] - 16
    for owner in range(owners):
        own = product[owner * rows : (owner + 1) * rows]
        result[places[owner], 0:rows, columns] = own
        top = jnp.max(jnp.abs(own), axis=0, keepdims=True)
        result[places[owner], rows : rows + 16, columns] = jnp.broadcast_to(top, (16, own.shape[1]))


def gate_step(ring, sums, gain, mixed, gate_proj, out_grad, cot_t, normed_t, inner_total):
    rows, channels = gate_proj.shape
    halves, part_rows = len(mixed), mixed[0].shape[0]
    share = cot_t.shape[0] // ring.count

    def kernel(places, *refs):
        sums_ref, gain_ref, proj_ref, grad_ref, cot_ref, normed_ref = refs[:6]
        mixed_refs, (gate_out, gate_grad, mixed_grad, gain_sum, result) = refs[6 : 6 + halves], refs[6 + halves :]
        gain_sum[...] = jnp.zeros(gain_sum.shape, f32)
        scale_row = lax.rsqrt(sums_ref[0:8, :] / inner_total + epsilon)
        pull_row = scale_row * scale_row * scale_row * (sums_ref[8:16, :] / inner_total)
        scales, pulls = scale_row.T, pull_row.T
        for i in range(halves):
            at = slice(i * part_rows, (i + 1) * part_rows)
            proj, rows_mixed, grad = proj_ref[at, :], mixed_refs[i][...], grad_ref[at, :]
            sig = sigmoid(proj)
            act = proj * sig
            gated = rows_mixed * act
            scale = scales[at, 0:1]
            scaled = gated * scale
            gate_out[at, :] = (scaled * gain_ref[...]).astype(bf16)
            gain_sum[0:1, :] += jnp.sum(grad * scaled, axis=0, keepdims=True)
            gated_grad = scale * (grad * gain_ref[...]) - gated * pulls[at, 0:1]
            mixed_grad[at, :] = gated_grad * act
            gate_grad[at, :] = (gated_grad * rows_mixed * (sig * (1.0 + proj * (1.0 - sig)))).astype(bf16)
        everything = slice(0, TILE)
        store_shares(places, dot(cot_ref[...], gate_out[...], ((1,), (0,))), result.at[0], everything)
        store_shares(places, dot(normed_ref[...], gate_grad[...], ((1,), (0,))), result.at[1], everything)

    tile = pl.BlockSpec((rows, TILE), lambda n, _: (0, n))
    return call(
        kernel, ring.places(), channels // TILE, (sums, gain, gate_proj, out_grad, cot_t, normed_t, *mixed),
        [
            fixed_block(16, rows), pl.BlockSpec((1, TILE), lambda n, _: (0, n)), tile, tile,
            fixed_block(*cot_t.shape), fixed_block(*normed_t.shape),
        ] + [pl.BlockSpec((part_rows, TILE), lambda n, _: (0, n)) for _ in mixed],
        [
            tile, tile, tile, pl.BlockSpec((8, TILE), lambda n, _: (0, n)),
            pl.BlockSpec((2, ring.count, share + 16, TILE), lambda n, _: (0, 0, 0, n)),
        ],
        [
            jax.ShapeDtypeStruct((rows, channels), bf16), jax.ShapeDtypeStruct((rows, channels), bf16),
            jax.ShapeDtypeStruct((rows, channels), f32), jax.ShapeDtypeStruct((8, channels), f32),
            jax.ShapeDtypeStruct((2, ring.count, share + 16, channels), f32),
        ],
        "gate_step",
    )


def partials(ring, normed_t, input_back, tail):
    rows, channels = input_back.shape
    share = normed_t.shape[0] // ring.count
    steps = channels // TILE

    def kernel(places, left, right, tail_ref, result):
        n = pl.program_id(0)

        @pl.when(n == 0)
        def _():
            product = dot(left[...], tail_ref[...], ((1,), (0,)))
            store_shares(places, product, result.at[0], slice(channels, channels + LANES))

        product = dot(left[...], right[...], ((1,), (0,)))
        store_shares(places, product, result.at[0], pl.ds(pl.multiple_of(n * TILE, LANES), TILE))

    shape = (1, ring.count, share + 16, channels + LANES)
    return call(
        kernel, ring.places(), steps, (normed_t, input_back, tail),
        [fixed_block(*normed_t.shape), pl.BlockSpec((rows, TILE), lambda n, _: (0, n)), fixed_block(rows, LANES)],
        fixed_block(*shape), jax.ShapeDtypeStruct(shape, f32), "partials",
    )


def branch_product(gate_out, second_full):
    rows, channels = gate_out.shape
    width = second_full.shape[0]

    def kernel(places, left, right, result):
        result[...] = dot(left[...], right[...], ((1,), (1,)))

    return call(
        kernel, [jnp.int32(0)], width // TILE, (gate_out, second_full),
        [fixed_block(rows, channels), pl.BlockSpec((TILE, channels), lambda n, _: (n, 1))],
        pl.BlockSpec((rows, TILE), lambda n, _: (0, n)), jax.ShapeDtypeStruct((rows, width), f32), "branch_product",
    )


def normed_kernel(places, gate_rows, input_rows, gate_tile, input_tile, *refs):
    results, product = refs[:-1], refs[-1]
    total = dot(gate_rows[...], gate_tile[...], ((1,), (1,)))
    product[...] = total + dot(input_rows[...], input_tile[...], ((1,), (1,)))
    rows = results[0].shape[0]
    for i, result in enumerate(results):
        result[...] = product[pl.ds(pl.multiple_of(places[i] * rows, 16), rows), :]


def normed_parts(me, gate_grad, input_back, second_full, first_full):
    count = lax.axis_size("tensor")
    tokens, channels = gate_grad.shape
    width, tile = first_full.shape[0], 2 * LANES
    places = jnp.stack([i ^ me for i in range(count)]).astype(jnp.int32)

    def fixed(n, _):
        return (0, 0)

    return pl.pallas_call(
        normed_kernel,
        grid_spec=pltpu.PrefetchScalarGridSpec(
            num_scalar_prefetch=1, grid=(width // tile,),
            in_specs=[
                pl.BlockSpec((tokens, channels), fixed), pl.BlockSpec((tokens, channels), fixed),
                pl.BlockSpec((tile, channels), lambda n, _: (n, 0)), pl.BlockSpec((tile, channels), lambda n, _: (n, 0)),
            ],
            out_specs=[pl.BlockSpec((tokens // count, tile), lambda n, _: (0, n))] * count,
            scratch_shapes=[pltpu.VMEM((tokens, tile), f32)],
        ),
        out_shape=[jax.ShapeDtypeStruct((tokens // count, width), f32)] * count,
        compiler_params=params(LIM_NORMED_PARTS),
        cost_estimate=little,
        name="normed_parts",
    )(places, gate_grad, input_back, second_full, first_full)


def cycle(count):
    return list(range(0, count, 2)) + list(range(count - 1, 0, -2))


class Ring:
    def __init__(self):
        self.count = lax.axis_size("dp")
        order = cycle(self.count)
        self.up = [(order[i], order[(i + 1) % self.count]) for i in range(self.count)]
        self.down = [(b, a) for a, b in self.up]
        me = lax.axis_index("dp")
        self.place = jnp.where(me % 2 == 0, me // 2, self.count - 1 - me // 2)

    def places(self):
        order = cycle(self.count)
        return [(order.index(i) - self.place + self.count) % self.count for i in range(self.count)]

    def owner(self, offset):
        place = (self.place + offset + self.count) % self.count
        return jnp.where(place < self.count // 2, 2 * place, 2 * (self.count - 1 - place) + 1)


def middle(rows):
    return (rows // 2 + 15) // 16 * 16


class Gather:
    def __init__(self, ring, shard):
        self.ring, self.shard, self.step = ring, shard, 0
        self.held = [(shard, 0, 0)]
        self.last = (shard, shard)

    def hop(self):
        self.step += 1
        half, cut = self.ring.count // 2, middle(self.shard.shape[0])
        up, down = self.last
        offsets = ((-self.step, 0), (self.step, 0))
        if self.step == half:
            up, down = up[:cut], down[cut:]
            offsets = ((half, 0), (half, cut))
        self.last = (lax.ppermute(up, "dp", self.ring.up), lax.ppermute(down, "dp", self.ring.down))
        self.held += [(piece, *offset) for piece, offset in zip(self.last, offsets)]

    def after(self, *marks):
        self.last, marks = fence(self.last, marks)
        self.held[-2:] = [(piece, *old[1:]) for piece, old in zip(self.last, self.held[-2:])]
        return marks if len(marks) > 1 else marks[0]

    def pieces(self):
        rows = self.shard.shape[0]
        places = [self.ring.owner(offset) * rows + skip for _, offset, skip in self.held]
        return [piece for piece, _, _ in self.held], places


def encode(rows, limit):
    power = jnp.ceil(jnp.log2(jnp.maximum(limit, 1e-30)))
    ours = lax.broadcasted_iota(jnp.int32, rows.shape, 1) < rows.shape[1] - 16
    return jnp.where(ours, rows * jnp.exp2(15.0 - power), power).astype(jnp.float16)


def decode(payload):
    power = payload[:, -16:-15].astype(f32)
    return payload.astype(f32) * jnp.exp2(power - 15.0), jnp.exp2(power)


class Scatter:
    def __init__(self, ring, parts):
        self.ring, self.parts = ring, parts
        self.step = ring.count // 2
        self.rows = parts.shape[2] - 16
        self.cut = middle(self.rows)
        far = parts[:, self.step]
        top = far[:, -16:-15]
        upper = jnp.concatenate([far[:, : self.cut], far[:, -16:]], axis=1)
        self.send = (encode(upper, top), encode(far[:, self.cut :], top))

    def hop(self):
        self.send = fence(*self.send)
        self.got = (lax.ppermute(self.send[0], "dp", self.ring.up), lax.ppermute(self.send[1], "dp", self.ring.down))

    def after(self, *marks):
        self.got, marks = fence(self.got, marks)
        return marks if len(marks) > 1 else marks[0]

    def before(self, *marks):
        self.send, marks = fence(self.send, marks)
        return marks if len(marks) > 1 else marks[0]

    def add(self):
        first = self.step == self.ring.count // 2
        self.got = fence(*self.got)
        (up, up_top), (down, down_top) = (decode(g) for g in self.got)
        if first:
            up = jnp.pad(up, ((0, 0), (0, self.rows - self.cut), (0, 0)))
            down = jnp.pad(down, ((0, 0), (self.cut, 0), (0, 0)))
            up = jnp.where(lax.broadcasted_iota(jnp.int32, up.shape, 1) < self.cut, up, 0.0)
        self.step -= 1
        if self.step == 0:
            return (self.parts[:, 0] + up + down)[:, : self.rows]
        above, below = self.parts[:, self.step], self.parts[:, self.ring.count - self.step]
        self.send = (
            encode(above + up, above[:, -16:-15] + up_top),
            encode(below + down, below[:, -16:-15] + down_top),
        )
        return None


def fence(*arrays):
    flat, tree = jax.tree.flatten(arrays)
    return jax.tree.unflatten(tree, lax.optimization_barrier(flat))


def across(array, bit, axis="tensor"):
    count = lax.axis_size(axis)
    return lax.ppermute(array, axis, [(i, i ^ bit) for i in range(count)])


def group_sum(array, axis, first, count):
    terms = [array] + [across(array, first * other, axis) for other in range(1, count)]
    while len(terms) > 1:
        terms = [terms[i] + terms[i + 1] for i in range(0, len(terms), 2)]
    return terms[0]


def cube_sum(array, axis):
    bit = 1
    while bit < lax.axis_size(axis):
        array = array + across(array, bit, axis)
        bit *= 2
    return array


def shards(
    block_input, cotangent, norm_gain, gate_weight, input_weight, state_weight, step_weight, conv_input,
    conv_input_bias, conv_state, conv_state_bias, step_bias, decay_log, skip_scale, gate_gain, out_weight,
):
    group_count = lax.axis_size("tensor")
    me = lax.axis_index("tensor")
    ring = Ring()
    half = ring.count // 2
    local_rows = block_input.shape[0]
    channels = gate_gain.shape[0]
    heads = step_bias.shape[0]
    inner_total = channels * group_count
    share = 2 * STATE // group_count
    tokens = local_rows * group_count
    blocks = tokens // BLOCK
    fold = LANES // share
    folded = tokens // fold
    rows_dot = ((1,), (0,))
    back_dot = ((1,), (1,))

    state_mine = lax.dynamic_slice_in_dim(state_weight, me * share, share, 1)
    first = Gather(
        ring,
        jnp.concatenate(
            [input_weight, state_mine, jnp.pad(step_weight, ((0, 0), (0, LANES - share - heads)))], axis=1
        ).astype(bf16),
    )
    first.hop()
    row_scale = lax.rsqrt(jnp.mean(block_input * block_input, axis=1, keepdims=True) + epsilon)
    normed = (block_input * row_scale * norm_gain).astype(bf16)
    second_weight = jnp.concatenate([gate_weight, out_weight.T], axis=1).astype(bf16)
    rates = -jnp.exp(decay_log)

    def per_head(vector):
        return jnp.pad(vector, (0, LANES - heads))[None, :]

    skip = jnp.repeat(skip_scale, HEAD_DIM)[None, :]
    head_of = (
        lax.broadcasted_iota(jnp.int32, (channels, LANES), 0) // HEAD_DIM
        == lax.broadcasted_iota(jnp.int32, (channels, LANES), 1)
    ).astype(f32)
    scan_consts = (
        conv_input, conv_input_bias[None, :], conv_state, conv_state_bias[None, :], per_head(step_bias),
        per_head(rates), skip,
    )
    back_consts = (conv_input, conv_state, per_head(step_bias), per_head(rates), skip, head_of)
    carried = jnp.zeros((channels // LANES, LANES, STATE), f32)
    carry = (jnp.zeros((8, channels), f32), jnp.zeros((8, 2 * STATE), f32), carried, jnp.zeros((8, LANES), f32))
    gain = gate_gain[None, :]
    normed, scan_consts, back_consts, carried, carry, gain = first.after(
        normed, scan_consts, back_consts, carried, carry, gain
    )
    first.hop()
    far, near = across(normed, 2), across(normed, 1)
    for _ in range(half - 3):
        first.hop()
    far, near, second_weight, cot_low = first.after(far, near, second_weight, cotangent.astype(bf16))
    first.hop()
    normed_pieces = (normed, near, far, across(far, 1))
    second = Gather(ring, second_weight)
    second.hop()
    cot_all = lax.all_gather(cot_low, "tensor", axis=0, tiled=True)
    pieces, places = first.pieces()
    pieces = second.after(pieces)
    second.hop()
    normed_all, first_full, input_proj, tail_proj = first_project(
        pieces, places, normed_pieces, [(me ^ bits) * local_rows for bits in range(4)], channels
    )
    tail_full = first_full[:, channels:]
    step_proj = jnp.pad(tail_proj[:, share : share + heads], ((0, 0), (0, LANES - heads)))
    state_mine = jnp.concatenate([tail_proj[i * folded : (i + 1) * folded, :share] for i in range(fold)], axis=1)
    far = across(state_mine, 2)
    same_x, same_core, diagonal = across(state_mine, 1), far, across(far, 1)
    right_core = me % 2 == 1
    near = (jnp.where(right_core, same_x, state_mine), jnp.where(right_core, state_mine, same_x))
    away = (jnp.where(right_core, diagonal, same_core), jnp.where(right_core, same_core, diagonal))
    right_chip = me // 2 == 1
    state_parts = [jnp.where(right_chip, away[i], near[i]) for i in range(2)]
    state_parts += [jnp.where(right_chip, near[i], away[i]) for i in range(2)]
    state_proj = jnp.concatenate(
        [jnp.concatenate([p[:, i * share : (i + 1) * share] for p in state_parts], axis=1) for i in range(fold)], axis=0
    )
    span = 2
    scanned = []
    input_proj, tail_proj = second.after(input_proj, tail_proj)
    second.hop()
    for start in range(0, blocks, span):
        scanned.append(run_scan(start, span, input_proj, state_proj, step_proj, carried, scan_consts))
        carried = scanned[-1][4]
        if second.step < half:
            carried = second.after(carried)
            second.hop()
    while second.step < half:
        second.hop()
    mixed = [block[0] for block in scanned]
    pieces, places = second.pieces()
    second_full, gate_proj, gate_out_grad, sums = second_project(pieces, places, normed_all, cot_all, mixed, gain)
    sums = (sums + across(sums, 1)) + (across(sums, 2) + across(sums, 3))
    normed_t = normed_all.T
    gate_out, gate_grad, mixed_grad, gain_sum, pair_parts = gate_step(
        ring, sums, gain, mixed, gate_proj, gate_out_grad, cot_all.T, normed_t, float(inner_total)
    )
    pair_ring = Scatter(ring, pair_parts)
    done = []
    for turn in range(blocks // span):
        if turn == 0:
            carry, late_out = pair_ring.before(carry, gate_out)
            pair_ring.hop()
            branch_part = branch_product(late_out, second_full)
            branch = lax.psum_scatter(branch_part, "tensor", scatter_dimension=0, tiled=True)
            carry, branch_part = fence(carry, branch_part)
        else:
            carry = pair_ring.after(carry)
            pair_ring.add()
            carry = pair_ring.before(carry)
            pair_ring.hop()
        start = blocks - span * (turn + 1)
        kept = scanned[start // span]
        kept = [kept[1], kept[2], kept[0], kept[3]]
        result = run_scan_back(
            start, span, (input_proj, state_proj, step_proj), kept, 0, mixed_grad, carry, back_consts
        )
        done.insert(0, result)
        carry = tuple(result[6:])
    done = pair_ring.after(done)
    pair_ring.add()
    done = pair_ring.before(done)
    pair_ring.hop()
    input_back, state_back, step_back = (jnp.concatenate([d[i] for d in done], axis=0) for i in range(3))
    input_sums, state_sums, step_sums = (sum(d[i] for d in done) for i in range(3, 6))

    packed = jnp.concatenate(
        [
            state_sums[:5].reshape(-1),
            input_sums[:5].reshape(-1),
            gain_sum[0],
            jnp.sum(input_sums[5].reshape(heads, HEAD_DIM), axis=1),
            step_sums[0, :heads],
            step_sums[1, :heads] * rates,
        ]
    )
    packed = jnp.pad(packed, (0, -packed.shape[0] % LANES)).reshape(-1, LANES)

    def state_columns(index):
        mine = lax.dynamic_slice_in_dim(state_back, index * share, share, 1)
        return jnp.concatenate([mine[i * folded : (i + 1) * folded] for i in range(fold)], axis=1)

    for_far, for_me = across(state_columns(me ^ 3), 1), across(state_columns(me ^ 1), 1)
    packed, for_far, for_me, input_back = fence(packed, for_far, for_me, input_back)
    far = state_columns(me ^ 2) + for_far
    far, input_back = fence(far, input_back)
    from_far = across(far, 2)
    parts = normed_parts(me, gate_grad, input_back, second_full, first_full)
    from_far, branch, *parts = pair_ring.after(from_far, branch, *parts)
    block_output = block_input + branch
    pair_ring.add()
    from_far = pair_ring.before(from_far)
    pair_ring.hop()
    state_share = (state_columns(me) + for_me + from_far).astype(bf16)
    state_share = jnp.concatenate([state_share[:, i * share : (i + 1) * share] for i in range(fold)], axis=0)
    tail = jnp.concatenate(
        [state_share, step_back[:, :heads], jnp.zeros((tokens, LANES - share - heads), bf16)], axis=1
    )

    def whole_part(bits):
        rows = lax.dynamic_slice_in_dim(tail, (me ^ bits) * local_rows, local_rows, 0)
        return parts[bits] + dot(rows, tail_full, back_dot)

    for_far, for_me = across(whole_part(3), 1), across(whole_part(1), 1)
    input_ring = Scatter(ring, partials(ring, normed_t, input_back, tail))
    for_far, for_me, pair_ring.got = input_ring.before(for_far, for_me, pair_ring.got)
    input_ring.hop()
    pair_sum = pair_ring.add()
    while pair_sum is None:
        pair_ring.hop()
        pair_sum = pair_ring.add()
    sent = whole_part(2) + for_far
    sent = jnp.pad(sent, ((0, 16), (0, 0)))[None]
    from_far = across(encode(sent, jnp.max(jnp.abs(sent), axis=1, keepdims=True)), 2)
    input_sum = input_ring.add()
    while input_sum is None:
        input_ring.hop()
        if input_ring.step == 2:
            from_far = input_ring.after(from_far)
        input_sum = input_ring.add()
    normed_grad = whole_part(0) + for_me + decode(from_far)[0][0, :local_rows]
    input_sum = input_sum[0]
    tail_sum = input_sum[:, channels:]

    weighted_grad = normed_grad * norm_gain
    norm_gain_part = jnp.sum(normed_grad * block_input * row_scale, axis=0)
    input_grad = (
        cotangent
        + row_scale * weighted_grad
        - block_input * row_scale**3 * jnp.mean(weighted_grad * block_input, axis=1, keepdims=True)
    )
    state_rows = 10 * STATE // LANES
    shared = jnp.concatenate([norm_gain_part.reshape(-1, LANES), packed[:state_rows]], axis=0)
    shared = group_sum(shared, "tensor", 1, group_count)
    packed = jnp.concatenate([shared, packed[state_rows:]], axis=0)
    packed = group_sum(group_sum(packed, "dp", 2, half), "dp", 1, 2)
    local = packed[shared.shape[0] :].reshape(-1)
    norm_gain_grad = packed[: shared.shape[0] - state_rows].reshape(-1)
    state_sum = packed[shared.shape[0] - state_rows : shared.shape[0]].reshape(5, 2 * STATE)
    spread = [jnp.where(me == i, tail_sum[:, :share], 0.0) for i in range(group_count)]
    spread = jnp.concatenate(
        [jnp.concatenate(spread[i : i + fold], axis=1) for i in range(0, group_count, fold)], axis=0
    )
    spread = cube_sum(spread, "tensor")
    rows = tail_sum.shape[0]
    state_grad = jnp.concatenate([spread[i * rows : (i + 1) * rows] for i in range(group_count // fold)], axis=1)
    at = 6 * channels
    return (
        block_output,
        input_grad,
        norm_gain_grad,
        pair_sum[1],
        input_sum[:, :channels],
        state_grad,
        tail_sum[:, share : share + heads],
        local[: 4 * channels].reshape(4, channels),
        local[4 * channels : 5 * channels],
        state_sum[:4],
        state_sum[4],
        local[at + heads : at + 2 * heads],
        local[at + 2 * heads : at + 3 * heads],
        local[at : at + heads],
        local[5 * channels : at],
        pair_sum[0].T,
    )


def solution(mesh):
    rows = P(("dp", "tensor"), None)
    both = P("dp", "tensor")
    inner = P("tensor")
    return jax.shard_map(
        shards,
        mesh=mesh,
        in_specs=(
            rows, rows, P(), both, both, P("dp", None), both, P(None, "tensor"), inner, P(), P(), inner, inner,
            inner, inner, P("tensor", "dp"),
        ),
        out_specs=(
            rows, rows, P(), both, both, P("dp", None), both, P(None, "tensor"), inner, P(), P(), inner, inner,
            inner, inner, P("tensor", "dp"),
        ),
        check_vma=False,
    )
```

```python
import jax
import jax.numpy as jnp
from jax import lax
from jax.experimental import pallas as pl
from jax.experimental.pallas import tpu as pltpu
from jax.sharding import PartitionSpec as P

HEAD_DIM = 64
STATE = 128
BLOCK = 256
SEQ = 1024
LANES = 128

LIM_SCAN = 61
LIM_SCAN_BACK = 61
LIM_NORMED_PARTS = 61

epsilon = 1e-05
high = lax.Precision.HIGH
highest = lax.Precision.HIGHEST
f32 = jnp.float32
bf16 = jnp.bfloat16


def dot(left, right, dims, precision=None):
    return lax.dot_general(
        left, right, (dims, ((), ())), precision=precision, preferred_element_type=f32
    )


def sigmoid(v):
    return 1.0 / (1.0 + jnp.exp(-v))


def softplus(v):
    return jnp.maximum(v, 0.0) + jnp.log1p(jnp.exp(-jnp.abs(v)))


def iota(shape, axis):
    return lax.broadcasted_iota(jnp.int32, shape, axis)


def pair_columns(table, pair):
    lane = iota((table.shape[0], LANES), 1)
    return jnp.where(lane < HEAD_DIM, table[:, 2 * pair : 2 * pair + 1], table[:, 2 * pair + 1 : 2 * pair + 2])


def decay_tables(step_rows, step_bias, rates):
    step_size = softplus(step_rows + step_bias)
    earlier = (iota((BLOCK, BLOCK), 0) >= iota((BLOCK, BLOCK), 1)).astype(f32)
    cumulative = dot(earlier, step_size * rates, ((1,), (0,)), highest)
    return step_size, cumulative, jnp.exp(cumulative), jnp.exp(cumulative[BLOCK - 1 : BLOCK, :] - cumulative)


def state_decay(from_start, pair):
    last = from_start[BLOCK - 1 : BLOCK, :]
    row = iota((LANES, STATE), 0)
    return jnp.where(row < HEAD_DIM, last[:, 2 * pair : 2 * pair + 1], last[:, 2 * pair + 1 : 2 * pair + 2])


def shifted_conv(rows_ref, before, buffer, taps, conv_bias, first):
    @pl.when(first)
    def _():
        buffer[0:8, :] = before[...]

    @pl.when(jnp.logical_not(first))
    def _():
        buffer[0:8, :] = buffer[BLOCK : BLOCK + 8, :]

    buffer[8 : BLOCK + 8, :] = rows_ref[...]
    total = conv_bias[...] + taps[0:1, :] * buffer[8 : BLOCK + 8, :]
    for tap in range(1, 4):
        total = total + taps[tap : tap + 1, :] * buffer[8 - tap : BLOCK + 8 - tap, :]
    return total


def scan_kernel(
    input_rows, state_rows, step_rows, input_before, state_before, state_entering,
    conv_input, conv_input_bias, conv_state, conv_state_bias, step_bias, rates, skip,
    mixed, input_conv, state_conv, entering, carried, input_buffer, state_buffer,
):
    first = pl.program_id(0) == 0
    pairs = input_rows.shape[1] // LANES

    @pl.when(first)
    def _():
        carried[...] = state_entering[...]

    input_conv[...] = shifted_conv(input_rows, input_before, input_buffer, conv_input, conv_input_bias, first)
    state_pre = shifted_conv(state_rows, state_before, state_buffer, conv_state, conv_state_bias, first)
    state_conv[...] = state_pre
    state_act = state_pre * sigmoid(state_pre)
    writes, reads = state_act[:, :STATE], state_act[:, STATE:]
    meeting = dot(reads, writes, ((1,), (1,)), high)
    step_size, cumulative, from_start, to_end = decay_tables(step_rows[...], step_bias[...], rates[...])
    cumulative_t = cumulative.T
    causal = iota((BLOCK, BLOCK), 0) >= iota((BLOCK, BLOCK), 1)
    lane = iota((BLOCK, LANES), 1)
    for pair in range(pairs):
        columns = slice(pair * LANES, pair * LANES + LANES)
        pre = input_conv[:, columns]
        inputs = pre * sigmoid(pre)
        weighted = inputs * pair_columns(step_size, pair)
        state_in = carried[pair]
        entering[0, pair] = state_in
        out = dot(reads, state_in, ((1,), (1,)), high) * pair_columns(from_start, pair)
        for side in range(2):
            head = 2 * pair + side
            gap = cumulative[:, head : head + 1] - cumulative_t[head : head + 1, :]
            mixing = jnp.exp(jnp.where(causal, gap, -1e30)) * meeting
            mine = (lane < HEAD_DIM) if side == 0 else (lane >= HEAD_DIM)
            out = out + dot(mixing, jnp.where(mine, weighted, 0.0), ((1,), (0,)), high)
        fresh = dot(weighted * pair_columns(to_end, pair), writes, ((0,), (0,)), high)
        carried[pair] = state_decay(from_start, pair) * state_in + fresh
        mixed[:, columns] = out + skip[:, columns] * inputs


def scan_back_kernel(
    input_rows, state_rows, step_rows, input_conv, state_conv, mixed, entering, mixed_grad,
    input_after, state_after, state_leaving, decay_after,
    conv_input, conv_state, step_bias, rates, skip, head_of,
    input_grad, state_grad, step_grad, input_sums, state_sums, step_sums, input_first, state_first, carried, later,
    input_buffer, state_buffer, gap_grad, out_products, in_products,
):
    first = pl.program_id(0) == 0
    pairs = input_rows.shape[1] // LANES

    @pl.when(first)
    def _():
        carried[...] = state_leaving[...]
        later[...] = decay_after[...]
        input_sums[...] = jnp.zeros(input_sums.shape, f32)
        state_sums[...] = jnp.zeros(state_sums.shape, f32)
        step_sums[...] = jnp.zeros(step_sums.shape, f32)
        input_buffer[BLOCK : BLOCK + 8, :] = input_after[...]
        state_buffer[BLOCK : BLOCK + 8, :] = state_after[...]

    @pl.when(jnp.logical_not(first))
    def _():
        input_buffer[BLOCK : BLOCK + 8, :] = input_buffer[0:8, :]
        state_buffer[BLOCK : BLOCK + 8, :] = state_buffer[0:8, :]

    state_pre = state_conv[...]
    state_sig = sigmoid(state_pre)
    state_act = state_pre * state_sig
    writes, reads = state_act[:, :STATE], state_act[:, STATE:]
    meeting_t = dot(writes, reads, ((1,), (1,)), high)
    step_size, cumulative, from_start, to_end = decay_tables(step_rows[...], step_bias[...], rates[...])
    cumulative_t = cumulative.T
    causal_t = iota((BLOCK, BLOCK), 0) <= iota((BLOCK, BLOCK), 1)
    lane = iota((BLOCK, LANES), 1)
    gap_grad[...] = jnp.zeros(gap_grad.shape, f32)
    writes_grad = jnp.zeros((BLOCK, STATE), f32)
    reads_grad = jnp.zeros((BLOCK, STATE), f32)
    for pair in range(pairs):
        columns = slice(pair * LANES, pair * LANES + LANES)
        pre = input_conv[:, columns]
        sig = sigmoid(pre)
        inputs = pre * sig
        step_pair = pair_columns(step_size, pair)
        weighted = inputs * step_pair
        out_grad = mixed_grad[:, columns]
        skip_product = out_grad * inputs
        input_sums[5:6, columns] += jnp.sum(skip_product, axis=0, keepdims=True)
        end_pair = pair_columns(to_end, pair)
        leaving_grad = carried[pair]
        weighted_grad = dot(writes, leaving_grad, ((1,), (1,)), high) * end_pair
        for side in range(2):
            head = 2 * pair + side
            gap = cumulative_t[head : head + 1, :] - cumulative[:, head : head + 1]
            within = jnp.exp(jnp.where(causal_t, gap, -1e30))
            mine = (lane < HEAD_DIM) if side == 0 else (lane >= HEAD_DIM)
            own_grad = jnp.where(mine, out_grad, 0.0)
            weighted_grad = weighted_grad + dot(within * meeting_t, own_grad, ((1,), (0,)), high)
            gap_grad[...] += within * dot(weighted, own_grad, ((1,), (1,)), high)
        start_grad = out_grad * pair_columns(from_start, pair)
        reads_grad = reads_grad + dot(start_grad, entering[0, pair], ((1,), (0,)), high)
        writes_grad = writes_grad + dot(weighted * end_pair, leaving_grad, ((1,), (0,)), high)
        carried[pair] = state_decay(from_start, pair) * leaving_grad + dot(start_grad, reads, ((0,), (0,)), high)
        out_products[:, columns] = out_grad * mixed[:, columns] - skip[:, columns] * skip_product
        in_products[:, columns] = inputs * weighted_grad
        inputs_grad = skip[:, columns] * out_grad + step_pair * weighted_grad
        input_buffer[0:BLOCK, columns] = inputs_grad * (sig * (1.0 + pre * (1.0 - sig)))
    reads_grad = reads_grad + dot(gap_grad[...], writes, ((0,), (0,)), high)
    writes_grad = writes_grad + dot(gap_grad[...], reads, ((1,), (0,)), high)
    state_slope = state_sig * (1.0 + state_pre * (1.0 - state_sig))
    state_buffer[0:BLOCK, 0:STATE] = writes_grad * state_slope[:, :STATE]
    state_buffer[0:BLOCK, STATE : 2 * STATE] = reads_grad * state_slope[:, STATE:]

    for buffer, rows, taps, sums, result in (
        (input_buffer, input_rows, conv_input, input_sums, input_grad),
        (state_buffer, state_rows, conv_state, state_sums, state_grad),
    ):
        raw = rows[...]
        total = jnp.zeros(raw.shape, f32)
        for tap in range(4):
            ahead = buffer[tap : tap + BLOCK, :]
            total = total + taps[tap : tap + 1, :] * ahead
            sums[tap : tap + 1, :] += jnp.sum(ahead * raw, axis=0, keepdims=True)
        sums[4:5, :] += jnp.sum(buffer[0:BLOCK, :], axis=0, keepdims=True)
        result[...] = total.astype(result.dtype)
    input_first[...] = input_buffer[0:8, :]
    state_first[...] = state_buffer[0:8, :]

    out_head = dot(out_products[...], head_of[...], ((1,), (0,)), high)
    in_head = dot(in_products[...], head_of[...], ((1,), (0,)), high)
    upper = (iota((BLOCK, BLOCK), 0) <= iota((BLOCK, BLOCK), 1)).astype(f32)
    decay_grad = dot(upper, out_head - step_size * in_head, ((1,), (0,)), highest) + later[0:1, :]
    later[0:1, :] = decay_grad[0:1, :]
    step_sig = sigmoid(step_rows[...] + step_bias[...])
    step_back = (rates[...] * decay_grad + in_head) * step_sig
    step_grad[...] = step_back.astype(step_grad.dtype)
    step_sums[0:1, :] += jnp.sum(step_back, axis=0, keepdims=True)
    step_sums[1:2, :] += jnp.sum(step_size * decay_grad, axis=0, keepdims=True)


def whole(array):
    zeros = (0,) * array.ndim
    return pl.BlockSpec(array.shape, lambda k: zeros)


def params(mebibytes):
    return pltpu.CompilerParams(dimension_semantics=("arbitrary",), vmem_limit_bytes=mebibytes * 1024 * 1024)


little = pl.CostEstimate(flops=10**6, bytes_accessed=2**16, transcendentals=0)


def run_scan(start, span, input_rows, state_rows, step_rows, zeros, state_entering, consts):
    channels = input_rows.shape[1]
    pairs = channels // LANES
    rows = span * BLOCK
    edge = start * BLOCK // 8 - 1

    def tokens(width):
        return pl.BlockSpec((BLOCK, width), lambda k: (start + k, 0))

    def results(width):
        return pl.BlockSpec((BLOCK, width), lambda k: (k, 0))

    if start == 0:
        before = zeros
        before_specs = [whole(c) for c in before]
    else:
        before = (input_rows, state_rows)
        before_specs = [pl.BlockSpec((8, c.shape[1]), lambda k: (edge, 0)) for c in before]
    return pl.pallas_call(
        scan_kernel,
        grid=(span,),
        in_specs=[tokens(channels), tokens(2 * STATE), tokens(LANES)] + before_specs + [whole(state_entering)]
        + [whole(c) for c in consts],
        out_specs=[
            results(channels), results(channels), results(2 * STATE),
            pl.BlockSpec((1, pairs, LANES, STATE), lambda k: (k, 0, 0, 0)), whole(state_entering),
        ],
        out_shape=[
            jax.ShapeDtypeStruct((rows, channels), f32),
            jax.ShapeDtypeStruct((rows, channels), f32),
            jax.ShapeDtypeStruct((rows, 2 * STATE), f32),
            jax.ShapeDtypeStruct((span, pairs, LANES, STATE), f32),
            jax.ShapeDtypeStruct((pairs, LANES, STATE), f32),
        ],
        scratch_shapes=[pltpu.VMEM((BLOCK + 8, channels), f32), pltpu.VMEM((BLOCK + 8, 2 * STATE), f32)],
        compiler_params=params(LIM_SCAN),
        cost_estimate=little,
        name="scan",
    )(input_rows, state_rows, step_rows, *before, state_entering, *consts)


def run_scan_back(start, span, projections, kept, at, mixed_grad, carry, consts):
    channels = mixed_grad.shape[1]
    pairs = channels // LANES
    rows = span * BLOCK

    def tokens(width):
        return pl.BlockSpec((BLOCK, width), lambda k: (start + span - 1 - k, 0))

    def own(width, first=0):
        return pl.BlockSpec((BLOCK, width), lambda k: (first + span - 1 - k, 0))

    def shape(*dims):
        return jax.ShapeDtypeStruct(dims, f32)

    sums = [shape(8, channels), shape(8, 2 * STATE), shape(8, LANES)]
    ends = [jax.ShapeDtypeStruct(c.shape, f32) for c in carry]
    return pl.pallas_call(
        scan_back_kernel,
        grid=(span,),
        in_specs=[
            tokens(channels), tokens(2 * STATE), tokens(LANES), own(channels, at),
            own(2 * STATE, at), own(channels, at),
            pl.BlockSpec((1, pairs, LANES, STATE), lambda k: (at + span - 1 - k, 0, 0, 0)), tokens(channels),
        ] + [whole(c) for c in carry] + [whole(c) for c in consts],
        out_specs=[own(channels), own(2 * STATE), own(LANES)] + [whole(c) for c in sums + ends],
        out_shape=[
            jax.ShapeDtypeStruct((rows, channels), bf16), shape(rows, 2 * STATE),
            jax.ShapeDtypeStruct((rows, LANES), bf16),
        ] + sums + ends,
        scratch_shapes=[
            pltpu.VMEM((BLOCK + 8, channels), f32), pltpu.VMEM((BLOCK + 8, 2 * STATE), f32),
            pltpu.VMEM((BLOCK, BLOCK), f32), pltpu.VMEM((BLOCK, channels), f32), pltpu.VMEM((BLOCK, channels), f32),
        ],
        compiler_params=params(LIM_SCAN_BACK),
        cost_estimate=little,
        name="scan_back",
    )(*projections, *kept, mixed_grad, *carry, *consts)


def fixed_block(*shape):
    zeros = (0,) * len(shape)
    return pl.BlockSpec(shape, lambda n, *_: zeros)


def call(kernel, places, steps, operands, in_specs, out_specs, out_shape, name, scratch=()):
    return pl.pallas_call(
        kernel,
        grid_spec=pltpu.PrefetchScalarGridSpec(
            num_scalar_prefetch=1, grid=(steps,), in_specs=in_specs, out_specs=out_specs, scratch_shapes=list(scratch)
        ),
        out_shape=out_shape,
        compiler_params=params(61),
        cost_estimate=little,
        name=name,
    )(places, *operands)


def lay(places, pieces, result, first=0):
    for i, piece in enumerate(pieces):
        result[pl.ds(pl.multiple_of(places[first + i], 16), piece.shape[0]), :] = piece[...]


TILE = 256


def tile_columns(ref, n, first=0):
    return ref[:, pl.ds(pl.multiple_of(n * TILE + first, LANES), TILE)]


def first_project(weights, tokens, places, channels):
    count = len(weights)
    depth, width = tokens[0].shape[1], weights[0].shape[1]
    rows = tokens[0].shape[0] * len(tokens)

    def kernel(places, *refs):
        pieces, (normed, full, input_proj, tail_proj) = refs[:-4], refs[-4:]
        n = pl.program_id(0)

        @pl.when(n == 0)
        def _():
            lay(places, pieces[:count], full)
            lay(places, pieces[count:], normed, count)
            tail_proj[...] = dot(normed[...], full[:, channels:], ((1,), (0,)))

        input_proj[...] = dot(normed[...], tile_columns(full, n), ((1,), (0,)))

    return call(
        kernel, places, channels // TILE, (*weights, *tokens),
        [fixed_block(*piece.shape) for piece in (*weights, *tokens)],
        [
            fixed_block(rows, depth), fixed_block(depth, width), pl.BlockSpec((rows, TILE), lambda n, _: (0, n)),
            fixed_block(rows, width - channels),
        ],
        [
            jax.ShapeDtypeStruct((rows, depth), bf16), jax.ShapeDtypeStruct((depth, width), bf16),
            jax.ShapeDtypeStruct((rows, channels), f32), jax.ShapeDtypeStruct((rows, width - channels), f32),
        ],
        "first_project",
    )


def second_project(weights, places, normed, cot, mixed, gain):
    count, halves = len(weights), len(mixed)
    width = weights[0].shape[1]
    rows, depth = normed.shape
    channels = width // 2
    part_rows = mixed[0].shape[0]

    def kernel(places, *refs):
        pieces, (normed_ref, cot_ref, gain_ref), mixed_refs = refs[:count], refs[count : count + 3], refs[count + 3 : -4]
        full, gate_proj, out_grad, sums = refs[-4:]
        n = pl.program_id(0)

        @pl.when(n == 0)
        def _():
            lay(places, pieces, full)
            sums[...] = jnp.zeros(sums.shape, f32)

        gate_proj[...] = dot(normed_ref[...], tile_columns(full, n), ((1,), (0,)))
        out_grad[...] = dot(cot_ref[...], tile_columns(full, n, channels), ((1,), (0,)))
        ones = jnp.ones((8, TILE), f32)
        for i in range(halves):
            at = slice(i * part_rows, (i + 1) * part_rows)
            proj = gate_proj[at, :]
            gated = mixed_refs[i][...] * (proj * sigmoid(proj))
            pulled = out_grad[at, :] * gain_ref[...] * gated
            sums[0:8, at] += dot(ones, gated * gated, ((1,), (1,)), highest)
            sums[8:16, at] += dot(ones, pulled, ((1,), (1,)), highest)

    tile = pl.BlockSpec((rows, TILE), lambda n, _: (0, n))
    return call(
        kernel, places, channels // TILE, (*weights, normed, cot, gain, *mixed),
        [fixed_block(*piece.shape) for piece in (*weights, normed, cot)]
        + [pl.BlockSpec((1, TILE), lambda n, _: (0, n))]
        + [pl.BlockSpec((part_rows, TILE), lambda n, _: (0, n)) for _ in mixed],
        [fixed_block(depth, width), tile, tile, fixed_block(16, rows)],
        [
            jax.ShapeDtypeStruct((depth, width), bf16), jax.ShapeDtypeStruct((rows, channels), f32),
            jax.ShapeDtypeStruct((rows, channels), f32), jax.ShapeDtypeStruct((16, rows), f32),
        ],
        "second_project",
    )


def store_shares(places, product, result, part, columns):
    owners, rows = result.shape[0], result.shape[2] - 16
    for owner in range(owners):
        own = product[owner * rows : (owner + 1) * rows]
        result[places[owner], part, 0:rows, columns] = own
        top = jnp.max(jnp.abs(own), axis=0, keepdims=True)
        result[places[owner], part, rows : rows + 16, columns] = jnp.broadcast_to(top, (16, own.shape[1]))


def gate_step(ring, places, sums, gain, mixed, gate_proj, out_grad, cot_t, normed_t, inner_total):
    rows, channels = gate_proj.shape
    halves, part_rows = len(mixed), mixed[0].shape[0]
    share = cot_t.shape[0] // ring.count

    def kernel(places, *refs):
        sums_ref, gain_ref, proj_ref, grad_ref, cot_ref, normed_ref = refs[:6]
        mixed_refs, (gate_out, gate_grad, mixed_grad, gain_sum, result) = refs[6 : 6 + halves], refs[6 + halves :]
        gain_sum[...] = jnp.zeros(gain_sum.shape, f32)
        scale_row = lax.rsqrt(sums_ref[0:8, :] / inner_total + epsilon)
        pull_row = scale_row * scale_row * scale_row * (sums_ref[8:16, :] / inner_total)
        scales, pulls = scale_row.T, pull_row.T
        for i in range(halves):
            at = slice(i * part_rows, (i + 1) * part_rows)
            proj, rows_mixed, grad = proj_ref[at, :], mixed_refs[i][...], grad_ref[at, :]
            sig = sigmoid(proj)
            act = proj * sig
            gated = rows_mixed * act
            scale = scales[at, 0:1]
            scaled = gated * scale
            gate_out[at, :] = (scaled * gain_ref[...]).astype(bf16)
            gain_sum[0:1, :] += jnp.sum(grad * scaled, axis=0, keepdims=True)
            gated_grad = scale * (grad * gain_ref[...]) - gated * pulls[at, 0:1]
            mixed_grad[at, :] = gated_grad * act
            gate_grad[at, :] = (gated_grad * rows_mixed * (sig * (1.0 + proj * (1.0 - sig)))).astype(bf16)
        everything = slice(0, TILE)
        store_shares(places, dot(cot_ref[...], gate_out[...], ((1,), (0,))), result, 0, everything)
        store_shares(places, dot(normed_ref[...], gate_grad[...], ((1,), (0,))), result, 1, everything)

    tile = pl.BlockSpec((rows, TILE), lambda n, _: (0, n))
    return call(
        kernel, places, channels // TILE, (sums, gain, gate_proj, out_grad, cot_t, normed_t, *mixed),
        [
            fixed_block(16, rows), pl.BlockSpec((1, TILE), lambda n, _: (0, n)), tile, tile,
            fixed_block(*cot_t.shape), fixed_block(*normed_t.shape),
        ] + [pl.BlockSpec((part_rows, TILE), lambda n, _: (0, n)) for _ in mixed],
        [
            tile, tile, tile, pl.BlockSpec((8, TILE), lambda n, _: (0, n)),
            pl.BlockSpec((ring.count, 2, share + 16, TILE), lambda n, _: (0, 0, 0, n)),
        ],
        [
            jax.ShapeDtypeStruct((rows, channels), bf16), jax.ShapeDtypeStruct((rows, channels), bf16),
            jax.ShapeDtypeStruct((rows, channels), f32), jax.ShapeDtypeStruct((8, channels), f32),
            jax.ShapeDtypeStruct((ring.count, 2, share + 16, channels), f32),
        ],
        "gate_step",
    )


def partials(ring, places, normed_t, input_back, tail):
    halves, (part_rows, channels) = len(input_back), input_back[0].shape
    rows = halves * part_rows
    share = normed_t.shape[0] // ring.count

    def kernel(places, left, tail_ref, *refs):
        rights, result = refs[:-1], refs[-1]
        n = pl.program_id(0)

        @pl.when(n == 0)
        def _():
            product = dot(left[...], tail_ref[...], ((1,), (0,)))
            store_shares(places, product, result, 0, slice(channels, channels + LANES))

        product = dot(left[:, 0:part_rows], rights[0][...], ((1,), (0,)))
        for i in range(1, halves):
            product = product + dot(left[:, i * part_rows : (i + 1) * part_rows], rights[i][...], ((1,), (0,)))
        store_shares(places, product, result, 0, pl.ds(pl.multiple_of(n * TILE, LANES), TILE))

    shape = (ring.count, 1, share + 16, channels + LANES)
    return call(
        kernel, places, channels // TILE, (normed_t, tail, *input_back),
        [fixed_block(*normed_t.shape), fixed_block(rows, LANES)]
        + [pl.BlockSpec((part_rows, TILE), lambda n, _: (0, n)) for _ in input_back],
        fixed_block(*shape), jax.ShapeDtypeStruct(shape, f32), "partials",
    )


def branch_product(places, gate_out, second_full):
    rows, channels = gate_out.shape
    width = second_full.shape[0]

    def kernel(places, left, right, result):
        result[...] = dot(left[...], right[...], ((1,), (1,)))

    return call(
        kernel, places, width // TILE, (gate_out, second_full),
        [fixed_block(rows, channels), pl.BlockSpec((TILE, channels), lambda n, _: (n, 1))],
        pl.BlockSpec((rows, TILE), lambda n, _: (0, n)), jax.ShapeDtypeStruct((rows, width), f32), "branch_product",
    )


def normed_kernel(halves, places, gate_rows, gate_tile, input_tile, *refs):
    inputs, results, product = refs[:halves], refs[halves:-1], refs[-1]
    part = inputs[0].shape[0]
    for i, input_rows in enumerate(inputs):
        at = slice(i * part, (i + 1) * part)
        total = dot(gate_rows[at, :], gate_tile[...], ((1,), (1,)))
        product[at, :] = total + dot(input_rows[...], input_tile[...], ((1,), (1,)))
    rows = results[0].shape[0]
    for i, result in enumerate(results):
        result[...] = product[pl.ds(pl.multiple_of(places[i] * rows, 16), rows), :]


def normed_parts(places, gate_grad, input_back, second_full, first_full):
    count = lax.axis_size("tensor")
    tokens, channels = gate_grad.shape
    width, tile = first_full.shape[0], 2 * LANES
    halves = len(input_back)

    def fixed(n, _):
        return (0, 0)

    return pl.pallas_call(
        lambda *refs: normed_kernel(halves, *refs),
        grid_spec=pltpu.PrefetchScalarGridSpec(
            num_scalar_prefetch=1, grid=(width // tile,),
            in_specs=[
                pl.BlockSpec((tokens, channels), fixed),
                pl.BlockSpec((tile, channels), lambda n, _: (n, 0)), pl.BlockSpec((tile, channels), lambda n, _: (n, 0)),
            ] + [pl.BlockSpec(half.shape, fixed) for half in input_back],
            out_specs=[pl.BlockSpec((tokens // count, tile), lambda n, _: (0, n))] * count,
            scratch_shapes=[pltpu.VMEM((tokens, tile), f32)],
        ),
        out_shape=[jax.ShapeDtypeStruct((tokens // count, width), f32)] * count,
        compiler_params=params(LIM_NORMED_PARTS),
        cost_estimate=little,
        name="normed_parts",
    )(places, gate_grad, second_full, first_full, *input_back)


def cycle(count):
    return list(range(0, count, 2)) + list(range(count - 1, 0, -2))


def table(numbers):
    return jnp.stack(numbers).astype(jnp.int32)


class Ring:
    def __init__(self):
        self.count = lax.axis_size("dp")
        order = cycle(self.count)
        self.up = [(order[i], order[(i + 1) % self.count]) for i in range(self.count)]
        self.down = [(b, a) for a, b in self.up]
        me = lax.axis_index("dp")
        self.place = jnp.where(me % 2 == 0, me // 2, self.count - 1 - me // 2)

    def places(self):
        order = cycle(self.count)
        return table([(order.index(i) - self.place + self.count) % self.count for i in range(self.count)])

    def owner(self, offset):
        place = (self.place + offset + self.count) % self.count
        return jnp.where(place < self.count // 2, 2 * place, 2 * (self.count - 1 - place) + 1)


def middle(rows):
    return (rows // 2 + 15) // 16 * 16


class Gather:
    def __init__(self, ring, shard):
        self.ring, self.shard, self.step = ring, shard, 0
        self.held = [(shard, 0, 0)]
        self.last = (shard, shard)

    def hop(self):
        self.step += 1
        half, cut = self.ring.count // 2, middle(self.shard.shape[0])
        up, down = self.last
        offsets = ((-self.step, 0), (self.step, 0))
        if self.step == half:
            up, down = up[:cut], down[cut:]
            offsets = ((half, 0), (half, cut))
        self.last = (lax.ppermute(up, "dp", self.ring.up), lax.ppermute(down, "dp", self.ring.down))
        self.held += [(piece, *offset) for piece, offset in zip(self.last, offsets)]

    def after(self, *marks):
        self.last, marks = fence(self.last, marks)
        self.held[-2:] = [(piece, *old[1:]) for piece, old in zip(self.last, self.held[-2:])]
        return marks if len(marks) > 1 else marks[0]

    def pieces(self):
        return [piece for piece, _, _ in self.held]

    def places(self):
        rows, half = self.shard.shape[0], self.ring.count // 2
        spots = [self.ring.owner(0) * rows]
        for step in range(1, half):
            spots += [self.ring.owner(-step) * rows, self.ring.owner(step) * rows]
        return spots + [self.ring.owner(half) * rows, self.ring.owner(half) * rows + middle(rows)]


def encode(rows, limit):
    power = jnp.ceil(jnp.log2(jnp.maximum(limit, 1e-30)))
    ours = lax.broadcasted_iota(jnp.int32, rows.shape, 1) < rows.shape[1] - 16
    return jnp.where(ours, rows * jnp.exp2(15.0 - power), power).astype(jnp.float16)


def decode(payload):
    power = payload[:, -16:-15].astype(f32)
    return payload.astype(f32) * jnp.exp2(power - 15.0), jnp.exp2(power)


class Scatter:
    def __init__(self, ring, parts):
        self.ring, self.parts = ring, parts
        self.step = ring.count // 2
        self.rows = parts.shape[2] - 16
        self.cut = middle(self.rows)
        far = parts[self.step]
        top = far[:, -16:-15]
        upper = jnp.concatenate([far[:, : self.cut], far[:, -16:]], axis=1)
        self.send = (encode(upper, top), encode(far[:, self.cut :], top))

    def hop(self):
        self.send = fence(*self.send)
        self.got = (lax.ppermute(self.send[0], "dp", self.ring.up), lax.ppermute(self.send[1], "dp", self.ring.down))

    def after(self, *marks):
        self.got, marks = fence(self.got, marks)
        return marks if len(marks) > 1 else marks[0]

    def before(self, *marks):
        self.send, marks = fence(self.send, marks)
        return marks if len(marks) > 1 else marks[0]

    def add(self):
        first = self.step == self.ring.count // 2
        self.got = fence(*self.got)
        (up, up_top), (down, down_top) = (decode(g) for g in self.got)
        if first:
            up = jnp.pad(up, ((0, 0), (0, self.rows - self.cut), (0, 0)))
            down = jnp.pad(down, ((0, 0), (self.cut, 0), (0, 0)))
            up = jnp.where(lax.broadcasted_iota(jnp.int32, up.shape, 1) < self.cut, up, 0.0)
        self.step -= 1
        if self.step == 0:
            return (self.parts[0] + up + down)[:, : self.rows]
        above, below = self.parts[self.step], self.parts[self.ring.count - self.step]
        self.send = (
            encode(above + up, above[:, -16:-15] + up_top),
            encode(below + down, below[:, -16:-15] + down_top),
        )
        return None


def fence(*arrays):
    flat, tree = jax.tree.flatten(arrays)
    return jax.tree.unflatten(tree, lax.optimization_barrier(flat))


def across(array, bit, axis="tensor"):
    count = lax.axis_size(axis)
    return lax.ppermute(array, axis, [(i, i ^ bit) for i in range(count)])


def group_sum(array, axis, first, count):
    terms = [array] + [across(array, first * other, axis) for other in range(1, count)]
    while len(terms) > 1:
        terms = [terms[i] + terms[i + 1] for i in range(0, len(terms), 2)]
    return terms[0]


def cube_sum(array, axis):
    bit = 1
    while bit < lax.axis_size(axis):
        array = array + across(array, bit, axis)
        bit *= 2
    return array


def shards(
    block_input, cotangent, norm_gain, gate_weight, input_weight, state_weight, step_weight, conv_input,
    conv_input_bias, conv_state, conv_state_bias, step_bias, decay_log, skip_scale, gate_gain, out_weight,
):
    group_count = lax.axis_size("tensor")
    me = lax.axis_index("tensor")
    ring = Ring()
    half = ring.count // 2
    local_rows = block_input.shape[0]
    channels = gate_gain.shape[0]
    heads = step_bias.shape[0]
    inner_total = channels * group_count
    share = 2 * STATE // group_count
    tokens = local_rows * group_count
    blocks = tokens // BLOCK
    fold = LANES // share
    folded = tokens // fold
    rows_dot = ((1,), (0,))
    back_dot = ((1,), (1,))

    state_mine = lax.dynamic_slice_in_dim(state_weight, me * share, share, 1)
    first = Gather(
        ring,
        jnp.concatenate(
            [input_weight, state_mine, jnp.pad(step_weight, ((0, 0), (0, LANES - share - heads)))], axis=1
        ).astype(bf16),
    )
    first.hop()
    row_scale = lax.rsqrt(jnp.mean(block_input * block_input, axis=1, keepdims=True) + epsilon)
    normed = (block_input * row_scale * norm_gain).astype(bf16)
    second_weight = jnp.concatenate([gate_weight, out_weight.T], axis=1).astype(bf16)
    rates = -jnp.exp(decay_log)

    def per_head(vector):
        return jnp.pad(vector, (0, LANES - heads))[None, :]

    skip = jnp.repeat(skip_scale, HEAD_DIM)[None, :]
    head_of = (
        lax.broadcasted_iota(jnp.int32, (channels, LANES), 0) // HEAD_DIM
        == lax.broadcasted_iota(jnp.int32, (channels, LANES), 1)
    ).astype(f32)
    scan_consts = (
        conv_input, conv_input_bias[None, :], conv_state, conv_state_bias[None, :], per_head(step_bias),
        per_head(rates), skip,
    )
    back_consts = (conv_input, conv_state, per_head(step_bias), per_head(rates), skip, head_of)
    carried = jnp.zeros((channels // LANES, LANES, STATE), f32)
    carry = (jnp.zeros((8, channels), f32), jnp.zeros((8, 2 * STATE), f32), carried, jnp.zeros((8, LANES), f32))
    gain = gate_gain[None, :]
    shard_places = first.places()
    token_places = [(me ^ bits) * local_rows for bits in range(4)]
    tables = (table(shard_places + token_places), table(shard_places), ring.places(), table([i ^ me for i in range(4)]))
    normed, scan_consts, back_consts, carried, carry, gain, tables = first.after(
        normed, scan_consts, back_consts, carried, carry, gain, tables
    )
    first_places, second_places, share_places, turn_places = tables
    first.hop()
    far, near = across(normed, 2), across(normed, 1)
    for _ in range(half - 3):
        first.hop()
    far, near, second_weight, cot_low = first.after(far, near, second_weight, cotangent.astype(bf16))
    first.hop()
    normed_pieces = (normed, near, far, across(far, 1))
    second = Gather(ring, second_weight)
    second.hop()
    cot_all = lax.all_gather(cot_low, "tensor", axis=0, tiled=True)
    pieces = second.after(first.pieces())
    second.hop()
    normed_all, first_full, input_proj, tail_proj = first_project(pieces, normed_pieces, first_places, channels)
    tail_full = first_full[:, channels:]
    step_proj = jnp.pad(tail_proj[:, share : share + heads], ((0, 0), (0, LANES - heads)))
    state_mine = jnp.concatenate([tail_proj[i * folded : (i + 1) * folded, :share] for i in range(fold)], axis=1)
    far = across(state_mine, 2)
    same_x, same_core, diagonal = across(state_mine, 1), far, across(far, 1)
    right_core = me % 2 == 1
    near = (jnp.where(right_core, same_x, state_mine), jnp.where(right_core, state_mine, same_x))
    away = (jnp.where(right_core, diagonal, same_core), jnp.where(right_core, same_core, diagonal))
    right_chip = me // 2 == 1
    state_parts = [jnp.where(right_chip, away[i], near[i]) for i in range(2)]
    state_parts += [jnp.where(right_chip, near[i], away[i]) for i in range(2)]
    state_proj = jnp.concatenate(
        [jnp.concatenate([p[:, i * share : (i + 1) * share] for p in state_parts], axis=1) for i in range(fold)], axis=0
    )
    span = 2
    scanned = []
    input_proj, tail_proj = second.after(input_proj, tail_proj)
    second.hop()
    normed_t, input_proj = fence(normed_all.T, input_proj)
    for start in range(0, blocks, span):
        scanned.append(run_scan(start, span, input_proj, state_proj, step_proj, carry[:2], carried, scan_consts))
        carried = scanned[-1][4]
        if second.step < half:
            carried = second.after(carried)
            second.hop()
    while second.step < half:
        second.hop()
    mixed = [block[0] for block in scanned]
    second_full, gate_proj, gate_out_grad, sums = second_project(
        second.pieces(), second_places, normed_all, cot_all, mixed, gain
    )
    sums = (sums + across(sums, 1)) + (across(sums, 2) + across(sums, 3))
    gate_out, gate_grad, mixed_grad, gain_sum, pair_parts = gate_step(
        ring, share_places, sums, gain, mixed, gate_proj, gate_out_grad, cot_all.T, normed_t, float(inner_total)
    )
    pair_ring = Scatter(ring, pair_parts)
    done = []
    for turn in range(blocks // span):
        if turn == 0:
            carry, late_out = pair_ring.before(carry, gate_out)
            pair_ring.hop()
            branch_part = branch_product(share_places, late_out, second_full)
            branch = lax.psum_scatter(branch_part, "tensor", scatter_dimension=0, tiled=True)
            carry, branch_part = fence(carry, branch_part)
        else:
            carry = pair_ring.after(carry)
            pair_ring.add()
            carry = pair_ring.before(carry)
            pair_ring.hop()
        start = blocks - span * (turn + 1)
        kept = scanned[start // span]
        kept = [kept[1], kept[2], kept[0], kept[3]]
        result = run_scan_back(
            start, span, (input_proj, state_proj, step_proj), kept, 0, mixed_grad, carry, back_consts
        )
        done.insert(0, result)
        carry = tuple(result[6:])
    done = pair_ring.after(done)
    pair_ring.add()
    done = pair_ring.before(done)
    pair_ring.hop()
    input_back, state_back = [d[0] for d in done], [d[1] for d in done]
    step_back = jnp.concatenate([d[2] for d in done], axis=0)
    input_sums, state_sums, step_sums = (sum(d[i] for d in done) for i in range(3, 6))

    packed = jnp.concatenate(
        [
            state_sums[:5].reshape(-1),
            input_sums[:5].reshape(-1),
            gain_sum[0],
            jnp.sum(input_sums[5].reshape(heads, HEAD_DIM), axis=1),
            step_sums[0, :heads],
            step_sums[1, :heads] * rates,
        ]
    )
    packed = jnp.pad(packed, (0, -packed.shape[0] % LANES)).reshape(-1, LANES)

    def state_columns(index):
        return jnp.concatenate([lax.dynamic_slice_in_dim(rows, index * share, share, 1) for rows in state_back], axis=1)

    for_far, for_me = across(state_columns(me ^ 3), 1), across(state_columns(me ^ 1), 1)
    packed, for_far, for_me, input_back = fence(packed, for_far, for_me, input_back)
    far = state_columns(me ^ 2) + for_far
    far, input_back = fence(far, input_back)
    from_far = across(far, 2)
    parts = normed_parts(turn_places, gate_grad, input_back, second_full, first_full)
    from_far, branch, *parts = pair_ring.after(from_far, branch, *parts)
    block_output = block_input + branch
    pair_ring.add()
    from_far = pair_ring.before(from_far)
    pair_ring.hop()
    state_share = (state_columns(me) + for_me + from_far).astype(bf16)
    state_share = jnp.concatenate([state_share[:, i * share : (i + 1) * share] for i in range(fold)], axis=0)
    tail = jnp.concatenate(
        [state_share, step_back[:, :heads], jnp.zeros((tokens, LANES - share - heads), bf16)], axis=1
    )

    def whole_part(bits):
        rows = lax.dynamic_slice_in_dim(tail, (me ^ bits) * local_rows, local_rows, 0)
        return parts[bits] + dot(rows, tail_full, back_dot)

    for_far, for_me = across(whole_part(3), 1), across(whole_part(1), 1)
    input_parts, pair_ring.got = fence(partials(ring, share_places, normed_t, input_back, tail), pair_ring.got)
    input_ring = Scatter(ring, input_parts)
    for_far, for_me = input_ring.before(for_far, for_me)
    input_ring.hop()
    sent = whole_part(2) + for_far
    sent = jnp.pad(sent, ((0, 16), (0, 0)))[None]
    from_far = across(encode(sent, jnp.max(jnp.abs(sent), axis=1, keepdims=True)), 2)
    input_sum = input_ring.add()
    pair_sum = pair_ring.add()
    while pair_sum is None:
        pair_ring.hop()
        pair_sum = pair_ring.add()
    while input_sum is None:
        input_ring.hop()
        if input_ring.step == 1:
            from_far = input_ring.after(from_far)
        input_sum = input_ring.add()
    normed_grad = whole_part(0) + for_me + decode(from_far)[0][0, :local_rows]
    input_sum = input_sum[0]
    tail_sum = input_sum[:, channels:]

    weighted_grad = normed_grad * norm_gain
    norm_gain_part = jnp.sum(normed_grad * block_input * row_scale, axis=0)
    input_grad = (
        cotangent
        + row_scale * weighted_grad
        - block_input * row_scale**3 * jnp.mean(weighted_grad * block_input, axis=1, keepdims=True)
    )
    state_rows = 10 * STATE // LANES
    shared = jnp.concatenate([norm_gain_part.reshape(-1, LANES), packed[:state_rows]], axis=0)
    shared = group_sum(shared, "tensor", 1, group_count)
    packed = jnp.concatenate([shared, packed[state_rows:]], axis=0)
    packed = group_sum(group_sum(packed, "dp", 2, half), "dp", 1, 2)
    local = packed[shared.shape[0] :].reshape(-1)
    norm_gain_grad = packed[: shared.shape[0] - state_rows].reshape(-1)
    state_sum = packed[shared.shape[0] - state_rows : shared.shape[0]].reshape(5, 2 * STATE)
    spread = [jnp.where(me == i, tail_sum[:, :share], 0.0) for i in range(group_count)]
    spread = jnp.concatenate(
        [jnp.concatenate(spread[i : i + fold], axis=1) for i in range(0, group_count, fold)], axis=0
    )
    spread = cube_sum(spread, "tensor")
    rows = tail_sum.shape[0]
    state_grad = jnp.concatenate([spread[i * rows : (i + 1) * rows] for i in range(group_count // fold)], axis=1)
    at = 6 * channels
    return (
        block_output,
        input_grad,
        norm_gain_grad,
        pair_sum[1],
        input_sum[:, :channels],
        state_grad,
        tail_sum[:, share : share + heads],
        local[: 4 * channels].reshape(4, channels),
        local[4 * channels : 5 * channels],
        state_sum[:4],
        state_sum[4],
        local[at + heads : at + 2 * heads],
        local[at + 2 * heads : at + 3 * heads],
        local[at : at + heads],
        local[5 * channels : at],
        pair_sum[0].T,
    )


def solution(mesh):
    rows = P(("dp", "tensor"), None)
    both = P("dp", "tensor")
    inner = P("tensor")
    return jax.shard_map(
        shards,
        mesh=mesh,
        in_specs=(
            rows, rows, P(), both, both, P("dp", None), both, P(None, "tensor"), inner, P(), P(), inner, inner,
            inner, inner, P("tensor", "dp"),
        ),
        out_specs=(
            rows, rows, P(), both, both, P("dp", None), both, P(None, "tensor"), inner, P(), P(), inner, inner,
            inner, inner, P("tensor", "dp"),
        ),
        check_vma=False,
    )
```

```python
import jax
import jax.numpy as jnp
from jax import lax
from jax.experimental import pallas as pl
from jax.experimental.pallas import tpu as pltpu
from jax.sharding import PartitionSpec as P

HEAD_DIM = 64
STATE = 128
BLOCK = 256
SEQ = 1024
LANES = 128

LIM_SCAN = 61
LIM_SCAN_BACK = 61
LIM_NORMED_PARTS = 61

epsilon = 1e-05
high = lax.Precision.HIGH
highest = lax.Precision.HIGHEST
f32 = jnp.float32
bf16 = jnp.bfloat16


def dot(left, right, dims, precision=None):
    return lax.dot_general(
        left, right, (dims, ((), ())), precision=precision, preferred_element_type=f32
    )


def sigmoid(v):
    return 1.0 / (1.0 + jnp.exp(-v))


def softplus(v):
    return jnp.maximum(v, 0.0) + jnp.log1p(jnp.exp(-jnp.abs(v)))


def iota(shape, axis):
    return lax.broadcasted_iota(jnp.int32, shape, axis)


def split(v):
    high_half = v.astype(bf16).astype(f32)
    return high_half, v - high_half


def packed(mine, first, second):
    return jnp.where(mine, first, pltpu.roll(second, HEAD_DIM, 1)).astype(bf16)


def meet(left, right, mine):
    (left_high, left_low), (right_high, right_low) = left, right
    lefts = [packed(mine, left_high, left_low), jnp.where(mine, left_high, 0.0).astype(bf16)]
    rights = [packed(mine, right_high, right_high), jnp.where(mine, right_low, 0.0).astype(bf16)]
    return dot(jnp.concatenate(lefts, axis=1), jnp.concatenate(rights, axis=1), ((1,), (1,)))


def pair_columns(table, pair):
    lane = iota((table.shape[0], LANES), 1)
    return jnp.where(lane < HEAD_DIM, table[:, 2 * pair : 2 * pair + 1], table[:, 2 * pair + 1 : 2 * pair + 2])


def decay_tables(step_rows, step_bias, rates):
    step_size = softplus(step_rows + step_bias)
    earlier = (iota((BLOCK, BLOCK), 0) >= iota((BLOCK, BLOCK), 1)).astype(f32)
    cumulative = dot(earlier, step_size * rates, ((1,), (0,)), highest)
    return step_size, cumulative, jnp.exp(cumulative), jnp.exp(cumulative[BLOCK - 1 : BLOCK, :] - cumulative)


def state_decay(from_start, pair):
    last = from_start[BLOCK - 1 : BLOCK, :]
    row = iota((LANES, STATE), 0)
    return jnp.where(row < HEAD_DIM, last[:, 2 * pair : 2 * pair + 1], last[:, 2 * pair + 1 : 2 * pair + 2])


def shifted_conv(rows_ref, before, buffer, taps, conv_bias, first):
    @pl.when(first)
    def _():
        buffer[0:8, :] = before[...]

    @pl.when(jnp.logical_not(first))
    def _():
        buffer[0:8, :] = buffer[BLOCK : BLOCK + 8, :]

    buffer[8 : BLOCK + 8, :] = rows_ref[...]
    total = conv_bias[...] + taps[0:1, :] * buffer[8 : BLOCK + 8, :]
    for tap in range(1, 4):
        total = total + taps[tap : tap + 1, :] * buffer[8 - tap : BLOCK + 8 - tap, :]
    return total


def scan_kernel(
    input_rows, state_rows, step_rows, input_before, state_before, state_entering,
    conv_input, conv_input_bias, conv_state, conv_state_bias, step_bias, rates, skip,
    mixed, input_conv, state_conv, entering, carried, input_buffer, state_buffer,
):
    first = pl.program_id(0) == 0
    pairs = input_rows.shape[1] // LANES

    @pl.when(first)
    def _():
        carried[...] = state_entering[...]

    input_conv[...] = shifted_conv(input_rows, input_before, input_buffer, conv_input, conv_input_bias, first)
    state_pre = shifted_conv(state_rows, state_before, state_buffer, conv_state, conv_state_bias, first)
    state_conv[...] = state_pre
    state_act = state_pre * sigmoid(state_pre)
    writes, reads = state_act[:, :STATE], state_act[:, STATE:]
    meeting = dot(reads, writes, ((1,), (1,)), high)
    step_size, cumulative, from_start, to_end = decay_tables(step_rows[...], step_bias[...], rates[...])
    cumulative_t = cumulative.T
    causal = iota((BLOCK, BLOCK), 0) >= iota((BLOCK, BLOCK), 1)
    lane = iota((BLOCK, LANES), 1)
    for pair in range(pairs):
        columns = slice(pair * LANES, pair * LANES + LANES)
        pre = input_conv[:, columns]
        inputs = pre * sigmoid(pre)
        weighted = inputs * pair_columns(step_size, pair)
        state_in = carried[pair]
        entering[0, pair] = state_in
        out = dot(reads, state_in, ((1,), (1,)), high) * pair_columns(from_start, pair)
        for side in range(2):
            head = 2 * pair + side
            gap = cumulative[:, head : head + 1] - cumulative_t[head : head + 1, :]
            mixing = jnp.exp(jnp.where(causal, gap, -1e30)) * meeting
            mine = (lane < HEAD_DIM) if side == 0 else (lane >= HEAD_DIM)
            out = out + dot(mixing, jnp.where(mine, weighted, 0.0), ((1,), (0,)), high)
        fresh = dot(weighted * pair_columns(to_end, pair), writes, ((0,), (0,)), high)
        carried[pair] = state_decay(from_start, pair) * state_in + fresh
        mixed[:, columns] = out + skip[:, columns] * inputs


def scan_back_kernel(
    input_rows, state_rows, step_rows, input_conv, state_conv, mixed, entering, mixed_grad,
    input_after, state_after, state_leaving, decay_after,
    conv_input, conv_state, step_bias, rates, skip, head_of,
    input_grad, state_grad, step_grad, input_sums, state_sums, step_sums, input_first, state_first, carried, later,
    input_buffer, state_buffer, gap_grad, out_products, in_products,
):
    first = pl.program_id(0) == 0
    pairs = input_rows.shape[1] // LANES

    @pl.when(first)
    def _():
        carried[...] = state_leaving[...]
        later[...] = decay_after[...]
        input_sums[...] = jnp.zeros(input_sums.shape, f32)
        state_sums[...] = jnp.zeros(state_sums.shape, f32)
        step_sums[...] = jnp.zeros(step_sums.shape, f32)
        input_buffer[BLOCK : BLOCK + 8, :] = input_after[...]
        state_buffer[BLOCK : BLOCK + 8, :] = state_after[...]

    @pl.when(jnp.logical_not(first))
    def _():
        input_buffer[BLOCK : BLOCK + 8, :] = input_buffer[0:8, :]
        state_buffer[BLOCK : BLOCK + 8, :] = state_buffer[0:8, :]

    state_pre = state_conv[...]
    state_sig = sigmoid(state_pre)
    state_act = state_pre * state_sig
    writes, reads = state_act[:, :STATE], state_act[:, STATE:]
    meeting_t = dot(writes, reads, ((1,), (1,)), high)
    step_size, cumulative, from_start, to_end = decay_tables(step_rows[...], step_bias[...], rates[...])
    cumulative_t = cumulative.T
    causal_t = iota((BLOCK, BLOCK), 0) <= iota((BLOCK, BLOCK), 1)
    lane = iota((BLOCK, LANES), 1)
    gap_grad[...] = jnp.zeros(gap_grad.shape, f32)
    writes_grad = jnp.zeros((BLOCK, STATE), f32)
    reads_grad = jnp.zeros((BLOCK, STATE), f32)
    for pair in range(pairs):
        columns = slice(pair * LANES, pair * LANES + LANES)
        pre = input_conv[:, columns]
        sig = sigmoid(pre)
        inputs = pre * sig
        step_pair = pair_columns(step_size, pair)
        weighted = inputs * step_pair
        out_grad = mixed_grad[:, columns]
        skip_product = out_grad * inputs
        input_sums[5:6, columns] += jnp.sum(skip_product, axis=0, keepdims=True)
        end_pair = pair_columns(to_end, pair)
        leaving_grad = carried[pair]
        weighted_grad = dot(writes, leaving_grad, ((1,), (1,)), high) * end_pair
        grad_halves, weighted_halves = split(out_grad), split(weighted)
        for side in range(2):
            head = 2 * pair + side
            gap = cumulative_t[head : head + 1, :] - cumulative[:, head : head + 1]
            within = jnp.exp(jnp.where(causal_t, gap, -1e30))
            mine = (lane < HEAD_DIM) if side == 0 else (lane >= HEAD_DIM)
            own_grad = jnp.where(mine, out_grad, 0.0)
            weighted_grad = weighted_grad + dot(within * meeting_t, own_grad, ((1,), (0,)), high)
            gap_grad[...] += within * meet(weighted_halves, grad_halves, mine)
        start_grad = out_grad * pair_columns(from_start, pair)
        reads_grad = reads_grad + dot(start_grad, entering[0, pair], ((1,), (0,)), high)
        writes_grad = writes_grad + dot(weighted * end_pair, leaving_grad, ((1,), (0,)), high)
        carried[pair] = state_decay(from_start, pair) * leaving_grad + dot(start_grad, reads, ((0,), (0,)), high)
        out_products[:, columns] = out_grad * mixed[:, columns] - skip[:, columns] * skip_product
        in_products[:, columns] = inputs * weighted_grad
        inputs_grad = skip[:, columns] * out_grad + step_pair * weighted_grad
        input_buffer[0:BLOCK, columns] = inputs_grad * (sig * (1.0 + pre * (1.0 - sig)))
    reads_grad = reads_grad + dot(gap_grad[...], writes, ((0,), (0,)), high)
    writes_grad = writes_grad + dot(gap_grad[...], reads, ((1,), (0,)), high)
    state_slope = state_sig * (1.0 + state_pre * (1.0 - state_sig))
    state_buffer[0:BLOCK, 0:STATE] = writes_grad * state_slope[:, :STATE]
    state_buffer[0:BLOCK, STATE : 2 * STATE] = reads_grad * state_slope[:, STATE:]

    for buffer, rows, taps, sums, result in (
        (input_buffer, input_rows, conv_input, input_sums, input_grad),
        (state_buffer, state_rows, conv_state, state_sums, state_grad),
    ):
        raw = rows[...]
        total = jnp.zeros(raw.shape, f32)
        for tap in range(4):
            ahead = buffer[tap : tap + BLOCK, :]
            total = total + taps[tap : tap + 1, :] * ahead
            sums[tap : tap + 1, :] += jnp.sum(ahead * raw, axis=0, keepdims=True)
        sums[4:5, :] += jnp.sum(buffer[0:BLOCK, :], axis=0, keepdims=True)
        result[...] = total.astype(result.dtype)
    input_first[...] = input_buffer[0:8, :]
    state_first[...] = state_buffer[0:8, :]

    out_head = dot(out_products[...], head_of[...], ((1,), (0,)), high)
    in_head = dot(in_products[...], head_of[...], ((1,), (0,)), high)
    upper = (iota((BLOCK, BLOCK), 0) <= iota((BLOCK, BLOCK), 1)).astype(f32)
    decay_grad = dot(upper, out_head - step_size * in_head, ((1,), (0,)), highest) + later[0:1, :]
    later[0:1, :] = decay_grad[0:1, :]
    step_sig = sigmoid(step_rows[...] + step_bias[...])
    step_back = (rates[...] * decay_grad + in_head) * step_sig
    step_grad[...] = step_back.astype(step_grad.dtype)
    step_sums[0:1, :] += jnp.sum(step_back, axis=0, keepdims=True)
    step_sums[1:2, :] += jnp.sum(step_size * decay_grad, axis=0, keepdims=True)


def whole(array):
    zeros = (0,) * array.ndim
    return pl.BlockSpec(array.shape, lambda k: zeros)


def params(mebibytes):
    return pltpu.CompilerParams(dimension_semantics=("arbitrary",), vmem_limit_bytes=mebibytes * 1024 * 1024)


little = pl.CostEstimate(flops=10**6, bytes_accessed=2**16, transcendentals=0)


def run_scan(start, span, input_rows, state_rows, step_rows, zeros, state_entering, consts):
    channels = input_rows.shape[1]
    pairs = channels // LANES
    rows = span * BLOCK
    edge = start * BLOCK // 8 - 1

    def tokens(width):
        return pl.BlockSpec((BLOCK, width), lambda k: (start + k, 0))

    def results(width):
        return pl.BlockSpec((BLOCK, width), lambda k: (k, 0))

    if start == 0:
        before = zeros
        before_specs = [whole(c) for c in before]
    else:
        before = (input_rows, state_rows)
        before_specs = [pl.BlockSpec((8, c.shape[1]), lambda k: (edge, 0)) for c in before]
    return pl.pallas_call(
        scan_kernel,
        grid=(span,),
        in_specs=[tokens(channels), tokens(2 * STATE), tokens(LANES)] + before_specs + [whole(state_entering)]
        + [whole(c) for c in consts],
        out_specs=[
            results(channels), results(channels), results(2 * STATE),
            pl.BlockSpec((1, pairs, LANES, STATE), lambda k: (k, 0, 0, 0)), whole(state_entering),
        ],
        out_shape=[
            jax.ShapeDtypeStruct((rows, channels), f32),
            jax.ShapeDtypeStruct((rows, channels), f32),
            jax.ShapeDtypeStruct((rows, 2 * STATE), f32),
            jax.ShapeDtypeStruct((span, pairs, LANES, STATE), f32),
            jax.ShapeDtypeStruct((pairs, LANES, STATE), f32),
        ],
        scratch_shapes=[pltpu.VMEM((BLOCK + 8, channels), f32), pltpu.VMEM((BLOCK + 8, 2 * STATE), f32)],
        compiler_params=params(LIM_SCAN),
        cost_estimate=little,
        name="scan",
    )(input_rows, state_rows, step_rows, *before, state_entering, *consts)


def run_scan_back(start, span, projections, kept, at, mixed_grad, carry, consts):
    channels = mixed_grad.shape[1]
    pairs = channels // LANES
    rows = span * BLOCK

    def tokens(width):
        return pl.BlockSpec((BLOCK, width), lambda k: (start + span - 1 - k, 0))

    def own(width, first=0):
        return pl.BlockSpec((BLOCK, width), lambda k: (first + span - 1 - k, 0))

    def shape(*dims):
        return jax.ShapeDtypeStruct(dims, f32)

    sums = [shape(8, channels), shape(8, 2 * STATE), shape(8, LANES)]
    ends = [jax.ShapeDtypeStruct(c.shape, f32) for c in carry]
    return pl.pallas_call(
        scan_back_kernel,
        grid=(span,),
        in_specs=[
            tokens(channels), tokens(2 * STATE), tokens(LANES), own(channels, at),
            own(2 * STATE, at), own(channels, at),
            pl.BlockSpec((1, pairs, LANES, STATE), lambda k: (at + span - 1 - k, 0, 0, 0)), tokens(channels),
        ] + [whole(c) for c in carry] + [whole(c) for c in consts],
        out_specs=[own(channels), own(2 * STATE), own(LANES)] + [whole(c) for c in sums + ends],
        out_shape=[
            jax.ShapeDtypeStruct((rows, channels), bf16), shape(rows, 2 * STATE),
            jax.ShapeDtypeStruct((rows, LANES), bf16),
        ] + sums + ends,
        scratch_shapes=[
            pltpu.VMEM((BLOCK + 8, channels), f32), pltpu.VMEM((BLOCK + 8, 2 * STATE), f32),
            pltpu.VMEM((BLOCK, BLOCK), f32), pltpu.VMEM((BLOCK, channels), f32), pltpu.VMEM((BLOCK, channels), f32),
        ],
        compiler_params=params(LIM_SCAN_BACK),
        cost_estimate=little,
        name="scan_back",
    )(*projections, *kept, mixed_grad, *carry, *consts)


def fixed_block(*shape):
    zeros = (0,) * len(shape)
    return pl.BlockSpec(shape, lambda n, *_: zeros)


def call(kernel, places, steps, operands, in_specs, out_specs, out_shape, name, scratch=()):
    return pl.pallas_call(
        kernel,
        grid_spec=pltpu.PrefetchScalarGridSpec(
            num_scalar_prefetch=1, grid=(steps,), in_specs=in_specs, out_specs=out_specs, scratch_shapes=list(scratch)
        ),
        out_shape=out_shape,
        compiler_params=params(61),
        cost_estimate=little,
        name=name,
    )(places, *operands)


def lay(places, pieces, result, first=0):
    for i, piece in enumerate(pieces):
        result[pl.ds(pl.multiple_of(places[first + i], 16), piece.shape[0]), :] = piece[...]


TILE = 256


def tile_columns(ref, n, first=0):
    return ref[:, pl.ds(pl.multiple_of(n * TILE + first, LANES), TILE)]


def first_project(weights, tokens, places, channels):
    count = len(weights)
    depth, width = tokens[0].shape[1], weights[0].shape[1]
    rows = tokens[0].shape[0] * len(tokens)

    def kernel(places, *refs):
        pieces, (normed, full, input_proj, tail_proj) = refs[:-4], refs[-4:]
        n = pl.program_id(0)

        @pl.when(n == 0)
        def _():
            lay(places, pieces[:count], full)
            lay(places, pieces[count:], normed, count)
            tail_proj[...] = dot(normed[...], full[:, channels:], ((1,), (0,)))

        input_proj[...] = dot(normed[...], tile_columns(full, n), ((1,), (0,)))

    return call(
        kernel, places, channels // TILE, (*weights, *tokens),
        [fixed_block(*piece.shape) for piece in (*weights, *tokens)],
        [
            fixed_block(rows, depth), fixed_block(depth, width), pl.BlockSpec((rows, TILE), lambda n, _: (0, n)),
            fixed_block(rows, width - channels),
        ],
        [
            jax.ShapeDtypeStruct((rows, depth), bf16), jax.ShapeDtypeStruct((depth, width), bf16),
            jax.ShapeDtypeStruct((rows, channels), f32), jax.ShapeDtypeStruct((rows, width - channels), f32),
        ],
        "first_project",
    )


def second_project(weights, places, normed, cot, mixed, gain):
    count, halves = len(weights), len(mixed)
    width = weights[0].shape[1]
    rows, depth = normed.shape
    channels = width // 2
    part_rows = mixed[0].shape[0]

    def kernel(places, *refs):
        pieces, (normed_ref, cot_ref, gain_ref), mixed_refs = refs[:count], refs[count : count + 3], refs[count + 3 : -4]
        full, gate_proj, out_grad, sums = refs[-4:]
        n = pl.program_id(0)

        @pl.when(n == 0)
        def _():
            lay(places, pieces, full)
            sums[...] = jnp.zeros(sums.shape, f32)

        gate_proj[...] = dot(normed_ref[...], tile_columns(full, n), ((1,), (0,)))
        out_grad[...] = dot(cot_ref[...], tile_columns(full, n, channels), ((1,), (0,)))
        ones = jnp.ones((8, TILE), f32)
        for i in range(halves):
            at = slice(i * part_rows, (i + 1) * part_rows)
            proj = gate_proj[at, :]
            gated = mixed_refs[i][...] * (proj * sigmoid(proj))
            pulled = out_grad[at, :] * gain_ref[...] * gated
            sums[0:8, at] += dot(ones, gated * gated, ((1,), (1,)), highest)
            sums[8:16, at] += dot(ones, pulled, ((1,), (1,)), highest)

    tile = pl.BlockSpec((rows, TILE), lambda n, _: (0, n))
    return call(
        kernel, places, channels // TILE, (*weights, normed, cot, gain, *mixed),
        [fixed_block(*piece.shape) for piece in (*weights, normed, cot)]
        + [pl.BlockSpec((1, TILE), lambda n, _: (0, n))]
        + [pl.BlockSpec((part_rows, TILE), lambda n, _: (0, n)) for _ in mixed],
        [fixed_block(depth, width), tile, tile, fixed_block(16, rows)],
        [
            jax.ShapeDtypeStruct((depth, width), bf16), jax.ShapeDtypeStruct((rows, channels), f32),
            jax.ShapeDtypeStruct((rows, channels), f32), jax.ShapeDtypeStruct((16, rows), f32),
        ],
        "second_project",
    )


def store_shares(places, product, result, tops, part, columns):
    owners, rows = result.shape[0], result.shape[2] - 16
    for owner in range(owners):
        own = product[owner * rows : (owner + 1) * rows]
        result[places[owner], part, 0:rows, columns] = own
        top = jnp.max(jnp.abs(own), axis=0, keepdims=True)
        result[places[owner], part, rows : rows + 16, columns] = jnp.zeros((16, own.shape[1]), f32)
        tops[places[owner], part, :, columns] = jnp.broadcast_to(top, (8, own.shape[1]))


def gate_step(ring, places, sums, gain, mixed, gate_proj, out_grad, cot_t, normed_t, second_full, inner_total):
    depth = second_full.shape[0]
    rows, channels = gate_proj.shape
    halves, part_rows = len(mixed), mixed[0].shape[0]
    share = cot_t.shape[0] // ring.count

    def kernel(places, *refs):
        sums_ref, gain_ref, proj_ref, grad_ref, cot_ref, normed_ref, weight_ref = refs[:7]
        mixed_refs, (branch, gate_grad, mixed_grad, gain_sum, result, tops, gate_out) = refs[7 : 7 + halves], refs[7 + halves :]
        gain_sum[...] = jnp.zeros(gain_sum.shape, f32)
        scale_row = lax.rsqrt(sums_ref[0:8, :] / inner_total + epsilon)
        pull_row = scale_row * scale_row * scale_row * (sums_ref[8:16, :] / inner_total)
        scales, pulls = scale_row.T, pull_row.T
        for i in range(halves):
            at = slice(i * part_rows, (i + 1) * part_rows)
            proj, rows_mixed, grad = proj_ref[at, :], mixed_refs[i][...], grad_ref[at, :]
            sig = sigmoid(proj)
            act = proj * sig
            gated = rows_mixed * act
            scale = scales[at, 0:1]
            scaled = gated * scale
            gate_out[at, :] = (scaled * gain_ref[...]).astype(bf16)
            gain_sum[0:1, :] += jnp.sum(grad * scaled, axis=0, keepdims=True)
            gated_grad = scale * (grad * gain_ref[...]) - gated * pulls[at, 0:1]
            mixed_grad[at, :] = gated_grad * act
            gate_grad[at, :] = (gated_grad * rows_mixed * (sig * (1.0 + proj * (1.0 - sig)))).astype(bf16)
        everything = slice(0, TILE)
        first = pl.program_id(0) == 0
        for i in range(0, rows, TILE):
            at = slice(i, i + TILE)
            share_out = dot(gate_out[at, :], weight_ref[...], ((1,), (1,)))
            branch[at, :] = share_out + jnp.where(first, 0.0, branch[at, :])
        store_shares(places, dot(cot_ref[...], gate_out[...], ((1,), (0,))), result, tops, 0, everything)
        store_shares(places, dot(normed_ref[...], gate_grad[...], ((1,), (0,))), result, tops, 1, everything)

    tile = pl.BlockSpec((rows, TILE), lambda n, _: (0, n))
    return call(
        kernel, places, channels // TILE, (sums, gain, gate_proj, out_grad, cot_t, normed_t, second_full, *mixed),
        [
            fixed_block(16, rows), pl.BlockSpec((1, TILE), lambda n, _: (0, n)), tile, tile,
            fixed_block(*cot_t.shape), fixed_block(*normed_t.shape),
            pl.BlockSpec((depth, TILE), lambda n, _: (0, channels // TILE + n)),
        ] + [pl.BlockSpec((part_rows, TILE), lambda n, _: (0, n)) for _ in mixed],
        [
            fixed_block(rows, depth), tile, tile, pl.BlockSpec((8, TILE), lambda n, _: (0, n)),
            pl.BlockSpec((ring.count, 2, share + 16, TILE), lambda n, _: (0, 0, 0, n)),
            pl.BlockSpec((ring.count, 2, 8, TILE), lambda n, _: (0, 0, 0, n)),
        ],
        [
            jax.ShapeDtypeStruct((rows, depth), f32), jax.ShapeDtypeStruct((rows, channels), bf16),
            jax.ShapeDtypeStruct((rows, channels), f32), jax.ShapeDtypeStruct((8, channels), f32),
            jax.ShapeDtypeStruct((ring.count, 2, share + 16, channels), f32),
            jax.ShapeDtypeStruct((ring.count, 2, 8, channels), f32),
        ],
        "gate_step", [pltpu.VMEM((rows, TILE), bf16)],
    )


def partials(ring, places, normed_t, input_back, tail):
    halves, (part_rows, channels) = len(input_back), input_back[0].shape
    rows = halves * part_rows
    share = normed_t.shape[0] // ring.count

    def kernel(places, left, tail_ref, *refs):
        rights, result, tops = refs[:-2], refs[-2], refs[-1]
        n = pl.program_id(0)

        @pl.when(n == 0)
        def _():
            product = dot(left[...], tail_ref[...], ((1,), (0,)))
            store_shares(places, product, result, tops, 0, slice(channels, channels + LANES))

        product = dot(left[:, 0:part_rows], rights[0][...], ((1,), (0,)))
        for i in range(1, halves):
            product = product + dot(left[:, i * part_rows : (i + 1) * part_rows], rights[i][...], ((1,), (0,)))
        store_shares(places, product, result, tops, 0, pl.ds(pl.multiple_of(n * TILE, LANES), TILE))

    shape = (ring.count, 1, share + 16, channels + LANES)
    return call(
        kernel, places, channels // TILE, (normed_t, tail, *input_back),
        [fixed_block(*normed_t.shape), fixed_block(rows, LANES)]
        + [pl.BlockSpec((part_rows, TILE), lambda n, _: (0, n)) for _ in input_back],
        [fixed_block(*shape), fixed_block(ring.count, 1, 8, channels + LANES)],
        [jax.ShapeDtypeStruct(shape, f32), jax.ShapeDtypeStruct((ring.count, 1, 8, channels + LANES), f32)], "partials",
    )


def normed_kernel(halves, places, gate_rows, tail_rows, gate_tile, input_tile, tail_tile, *refs):
    inputs, results, product = refs[:halves], refs[halves:-1], refs[-1]
    part = inputs[0].shape[0]
    for i, input_rows in enumerate(inputs):
        at = slice(i * part, (i + 1) * part)
        total = dot(gate_rows[at, :], gate_tile[...], ((1,), (1,)))
        total = total + dot(tail_rows[at, :], tail_tile[...], ((1,), (1,)))
        product[at, :] = total + dot(input_rows[...], input_tile[...], ((1,), (1,)))
    rows = results[0].shape[0]
    for i, result in enumerate(results):
        result[...] = product[pl.ds(pl.multiple_of(places[i] * rows, 16), rows), :]


def normed_parts(places, gate_grad, input_back, tail, second_full, first_full):
    count = lax.axis_size("tensor")
    tokens, channels = gate_grad.shape
    width, tile = first_full.shape[0], 2 * LANES
    halves = len(input_back)

    def fixed(n, _):
        return (0, 0)

    return pl.pallas_call(
        lambda *refs: normed_kernel(halves, *refs),
        grid_spec=pltpu.PrefetchScalarGridSpec(
            num_scalar_prefetch=1, grid=(width // tile,),
            in_specs=[
                pl.BlockSpec((tokens, channels), fixed), pl.BlockSpec((tokens, LANES), fixed),
                pl.BlockSpec((tile, channels), lambda n, _: (n, 0)), pl.BlockSpec((tile, channels), lambda n, _: (n, 0)),
                pl.BlockSpec((tile, LANES), lambda n, _: (n, channels // LANES)),
            ] + [pl.BlockSpec(half.shape, fixed) for half in input_back],
            out_specs=[pl.BlockSpec((tokens // count, tile), lambda n, _: (0, n))] * count,
            scratch_shapes=[pltpu.VMEM((tokens, tile), f32)],
        ),
        out_shape=[jax.ShapeDtypeStruct((tokens // count, width), f32)] * count,
        compiler_params=params(LIM_NORMED_PARTS),
        cost_estimate=little,
        name="normed_parts",
    )(places, gate_grad, tail, second_full, first_full, first_full, *input_back)


def cycle(count):
    return list(range(0, count, 2)) + list(range(count - 1, 0, -2))


def table(numbers):
    return jnp.stack(numbers).astype(jnp.int32)


class Ring:
    def __init__(self):
        self.count = lax.axis_size("dp")
        order = cycle(self.count)
        self.up = [(order[i], order[(i + 1) % self.count]) for i in range(self.count)]
        self.down = [(b, a) for a, b in self.up]
        me = lax.axis_index("dp")
        self.place = jnp.where(me % 2 == 0, me // 2, self.count - 1 - me // 2)

    def places(self):
        order = cycle(self.count)
        return table([(order.index(i) - self.place + self.count) % self.count for i in range(self.count)])

    def owner(self, offset):
        place = (self.place + offset + self.count) % self.count
        return jnp.where(place < self.count // 2, 2 * place, 2 * (self.count - 1 - place) + 1)


def middle(rows):
    return (rows // 2 + 15) // 16 * 16


class Gather:
    def __init__(self, ring, shard):
        self.ring, self.shard, self.step = ring, shard, 0
        self.held = [(shard, 0, 0)]
        self.last = (shard, shard)

    def hop(self):
        self.step += 1
        half, cut = self.ring.count // 2, middle(self.shard.shape[0])
        up, down = self.last
        offsets = ((-self.step, 0), (self.step, 0))
        if self.step == half:
            up, down = up[:cut], down[cut:]
            offsets = ((half, 0), (half, cut))
        self.last = (lax.ppermute(up, "dp", self.ring.up), lax.ppermute(down, "dp", self.ring.down))
        self.held += [(piece, *offset) for piece, offset in zip(self.last, offsets)]

    def after(self, *marks):
        self.last, marks = fence(self.last, marks)
        self.held[-2:] = [(piece, *old[1:]) for piece, old in zip(self.last, self.held[-2:])]
        return marks if len(marks) > 1 else marks[0]

    def pieces(self):
        return [piece for piece, _, _ in self.held]

    def places(self):
        rows, half = self.shard.shape[0], self.ring.count // 2
        spots = [self.ring.owner(0) * rows]
        for step in range(1, half):
            spots += [self.ring.owner(-step) * rows, self.ring.owner(step) * rows]
        return spots + [self.ring.owner(half) * rows, self.ring.owner(half) * rows + middle(rows)]


def encode(rows, limit):
    power = jnp.ceil(jnp.log2(jnp.maximum(limit, 1e-30)))
    ours = lax.broadcasted_iota(jnp.int32, rows.shape, 1) < rows.shape[1] - 16
    return jnp.where(ours, rows * jnp.exp2(15.0 - power), power).astype(jnp.float16)


def decode(payload):
    power = payload[:, -16:-15].astype(f32)
    return payload.astype(f32) * jnp.exp2(power - 15.0), jnp.exp2(power)


class Scatter:
    def __init__(self, ring, parts, tops):
        self.ring, self.parts, self.tops = ring, parts, tops
        self.step = ring.count // 2
        self.rows = parts.shape[2] - 16
        self.cut = middle(self.rows)
        far = parts[self.step]
        top = tops[self.step, :, 0:1]
        upper = jnp.concatenate([far[:, : self.cut], far[:, -16:]], axis=1)
        self.send = (encode(upper, top), encode(far[:, self.cut :], top))

    def hop(self):
        self.send = fence(*self.send)
        self.got = (lax.ppermute(self.send[0], "dp", self.ring.up), lax.ppermute(self.send[1], "dp", self.ring.down))

    def after(self, *marks):
        self.got, marks = fence(self.got, marks)
        return marks if len(marks) > 1 else marks[0]

    def before(self, *marks):
        self.send, marks = fence(self.send, marks)
        return marks if len(marks) > 1 else marks[0]

    def add(self):
        first = self.step == self.ring.count // 2
        self.got = fence(*self.got)
        (up, up_top), (down, down_top) = (decode(g) for g in self.got)
        if first:
            up = jnp.pad(up, ((0, 0), (0, self.rows - self.cut), (0, 0)))
            down = jnp.pad(down, ((0, 0), (self.cut, 0), (0, 0)))
            up = jnp.where(lax.broadcasted_iota(jnp.int32, up.shape, 1) < self.cut, up, 0.0)
        self.step -= 1
        if self.step == 0:
            return (self.parts[0] + up + down)[:, : self.rows]
        above, below = self.parts[self.step], self.parts[self.ring.count - self.step]
        self.send = (
            encode(above + up, self.tops[self.step, :, 0:1] + up_top),
            encode(below + down, self.tops[self.ring.count - self.step, :, 0:1] + down_top),
        )
        return None


def fence(*arrays):
    flat, tree = jax.tree.flatten(arrays)
    return jax.tree.unflatten(tree, lax.optimization_barrier(flat))


def across(array, bit, axis="tensor"):
    count = lax.axis_size(axis)
    return lax.ppermute(array, axis, [(i, i ^ bit) for i in range(count)])


def group_sum(array, axis, first, count):
    terms = [array] + [across(array, first * other, axis) for other in range(1, count)]
    while len(terms) > 1:
        terms = [terms[i] + terms[i + 1] for i in range(0, len(terms), 2)]
    return terms[0]


def cube_sum(array, axis):
    bit = 1
    while bit < lax.axis_size(axis):
        array = array + across(array, bit, axis)
        bit *= 2
    return array


def shards(
    block_input, cotangent, norm_gain, gate_weight, input_weight, state_weight, step_weight, conv_input,
    conv_input_bias, conv_state, conv_state_bias, step_bias, decay_log, skip_scale, gate_gain, out_weight,
):
    group_count = lax.axis_size("tensor")
    me = lax.axis_index("tensor")
    ring = Ring()
    half = ring.count // 2
    local_rows = block_input.shape[0]
    channels = gate_gain.shape[0]
    heads = step_bias.shape[0]
    inner_total = channels * group_count
    share = 2 * STATE // group_count
    tokens = local_rows * group_count
    blocks = tokens // BLOCK
    fold = LANES // share
    folded = tokens // fold
    rows_dot = ((1,), (0,))
    back_dot = ((1,), (1,))

    state_mine = lax.dynamic_slice_in_dim(state_weight, me * share, share, 1)
    first = Gather(
        ring,
        jnp.concatenate(
            [input_weight, state_mine, jnp.pad(step_weight, ((0, 0), (0, LANES - share - heads)))], axis=1
        ).astype(bf16),
    )
    first.hop()
    row_scale = lax.rsqrt(jnp.mean(block_input * block_input, axis=1, keepdims=True) + epsilon)
    normed = (block_input * row_scale * norm_gain).astype(bf16)
    second_weight = jnp.concatenate([gate_weight, out_weight.T], axis=1).astype(bf16)
    rates = -jnp.exp(decay_log)

    def per_head(vector):
        return jnp.pad(vector, (0, LANES - heads))[None, :]

    skip = jnp.repeat(skip_scale, HEAD_DIM)[None, :]
    head_of = (
        lax.broadcasted_iota(jnp.int32, (channels, LANES), 0) // HEAD_DIM
        == lax.broadcasted_iota(jnp.int32, (channels, LANES), 1)
    ).astype(f32)
    scan_consts = (
        conv_input, conv_input_bias[None, :], conv_state, conv_state_bias[None, :], per_head(step_bias),
        per_head(rates), skip,
    )
    back_consts = (conv_input, conv_state, per_head(step_bias), per_head(rates), skip, head_of)
    carried = jnp.zeros((channels // LANES, LANES, STATE), f32)
    carry = (jnp.zeros((8, channels), f32), jnp.zeros((8, 2 * STATE), f32), carried, jnp.zeros((8, LANES), f32))
    gain = gate_gain[None, :]
    shard_places = first.places()
    token_places = [(me ^ bits) * local_rows for bits in range(4)]
    tables = (table(shard_places + token_places), table(shard_places), ring.places(), table([i ^ me for i in range(4)]))
    normed, scan_consts, back_consts, carried, carry, gain, tables = first.after(
        normed, scan_consts, back_consts, carried, carry, gain, tables
    )
    first_places, second_places, share_places, turn_places = tables
    first.hop()
    far, near = across(normed, 2), across(normed, 1)
    for _ in range(half - 3):
        first.hop()
    far, near, second_weight, cot_low = first.after(far, near, second_weight, cotangent.astype(bf16))
    first.hop()
    second_weight = first.after(second_weight)
    normed_pieces = (normed, near, far, across(far, 1))
    second = Gather(ring, second_weight)
    second.hop()
    cot_all = lax.all_gather(cot_low, "tensor", axis=0, tiled=True)
    normed_all, first_full, input_proj, tail_proj = first_project(
        first.pieces(), normed_pieces, first_places, channels
    )
    normed_all, first_full, input_proj, tail_proj = second.after(normed_all, first_full, input_proj, tail_proj)
    second.hop()
    step_proj = jnp.pad(tail_proj[:, share : share + heads], ((0, 0), (0, LANES - heads)))
    state_mine = jnp.concatenate([tail_proj[i * folded : (i + 1) * folded, :share] for i in range(fold)], axis=1)
    far = across(state_mine, 2)
    same_x, same_core, diagonal = across(state_mine, 1), far, across(far, 1)
    right_core = me % 2 == 1
    near = (jnp.where(right_core, same_x, state_mine), jnp.where(right_core, state_mine, same_x))
    away = (jnp.where(right_core, diagonal, same_core), jnp.where(right_core, same_core, diagonal))
    right_chip = me // 2 == 1
    state_parts = [jnp.where(right_chip, away[i], near[i]) for i in range(2)]
    state_parts += [jnp.where(right_chip, near[i], away[i]) for i in range(2)]
    state_proj = jnp.concatenate(
        [jnp.concatenate([p[:, i * share : (i + 1) * share] for p in state_parts], axis=1) for i in range(fold)], axis=0
    )
    span = 2
    scanned = []
    input_proj, tail_proj = second.after(input_proj, tail_proj)
    second.hop()
    normed_t, input_proj = fence(normed_all.T, input_proj)
    for start in range(0, blocks, span):
        scanned.append(run_scan(start, span, input_proj, state_proj, step_proj, carry[:2], carried, scan_consts))
        carried = scanned[-1][4]
        if second.step < half:
            carried = second.after(carried)
            second.hop()
    while second.step < half:
        second.hop()
    mixed = [block[0] for block in scanned]
    second_full, gate_proj, gate_out_grad, sums = second_project(
        second.pieces(), second_places, normed_all, cot_all, mixed, gain
    )
    sums = (sums + across(sums, 1)) + (across(sums, 2) + across(sums, 3))
    branch_part, gate_grad, mixed_grad, gain_sum, *pair_parts = gate_step(
        ring, share_places, sums, gain, mixed, gate_proj, gate_out_grad, cot_all.T, normed_t, second_full,
        float(inner_total),
    )
    pair_ring = Scatter(ring, *pair_parts)
    done = []
    for turn in range(blocks // span):
        if turn == 0:
            carry, branch_part = pair_ring.before(carry, branch_part)
            pair_ring.hop()
            branch = lax.psum_scatter(branch_part, "tensor", scatter_dimension=0, tiled=True)
        else:
            carry = pair_ring.after(carry)
            pair_ring.add()
            carry = pair_ring.before(carry)
            pair_ring.hop()
        start = blocks - span * (turn + 1)
        kept = scanned[start // span]
        kept = [kept[1], kept[2], kept[0], kept[3]]
        result = run_scan_back(
            start, span, (input_proj, state_proj, step_proj), kept, 0, mixed_grad, carry, back_consts
        )
        done.insert(0, result)
        carry = tuple(result[6:])
    done = pair_ring.after(done)
    pair_ring.add()
    done = pair_ring.before(done)
    pair_ring.hop()
    input_back, state_back = [d[0] for d in done], [d[1] for d in done]
    step_back = jnp.concatenate([d[2] for d in done], axis=0)
    input_sums, state_sums, step_sums = (sum(d[i] for d in done) for i in range(3, 6))

    packed = jnp.concatenate(
        [
            state_sums[:5].reshape(-1),
            input_sums[:5].reshape(-1),
            gain_sum[0],
            jnp.sum(input_sums[5].reshape(heads, HEAD_DIM), axis=1),
            step_sums[0, :heads],
            step_sums[1, :heads] * rates,
        ]
    )
    packed = jnp.pad(packed, (0, -packed.shape[0] % LANES)).reshape(-1, LANES)

    def state_columns(index):
        return jnp.concatenate([lax.dynamic_slice_in_dim(rows, index * share, share, 1) for rows in state_back], axis=1)

    for_far, for_me = across(state_columns(me ^ 3), 1), across(state_columns(me ^ 1), 1)
    packed, for_far, for_me = fence(packed, for_far, for_me)
    from_far = across(state_columns(me ^ 2) + for_far, 2)
    state_share = (state_columns(me) + for_me + from_far).astype(bf16)
    state_share = jnp.concatenate([state_share[:, i * share : (i + 1) * share] for i in range(fold)], axis=0)
    tail = jnp.concatenate(
        [state_share, step_back[:, :heads], jnp.zeros((tokens, LANES - share - heads), bf16)], axis=1
    )
    parts = normed_parts(turn_places, gate_grad, input_back, tail, second_full, first_full)
    branch, *parts = pair_ring.after(branch, *parts)
    block_output = block_input + branch
    for_far, for_me = across(parts[3], 1), across(parts[1], 1)
    pair_ring.add()
    pair_ring.hop()
    input_parts, pair_ring.got = fence(partials(ring, share_places, normed_t, input_back, tail), pair_ring.got)
    input_ring = Scatter(ring, *input_parts)
    for_far, for_me = input_ring.before(for_far, for_me)
    input_ring.hop()
    sent = parts[2] + for_far
    sent = jnp.pad(sent, ((0, 16), (0, 0)))[None]
    from_far = across(encode(sent, jnp.max(jnp.abs(sent), axis=1, keepdims=True)), 2)
    input_sum = input_ring.add()
    pair_sum = pair_ring.add()
    while pair_sum is None:
        pair_ring.hop()
        pair_sum = pair_ring.add()
    while input_sum is None:
        input_ring.hop()
        if input_ring.step == 1:
            from_far = input_ring.after(from_far)
        input_sum = input_ring.add()
    normed_grad = parts[0] + for_me + decode(from_far)[0][0, :local_rows]
    input_sum = input_sum[0]
    tail_sum = input_sum[:, channels:]

    weighted_grad = normed_grad * norm_gain
    norm_gain_part = jnp.sum(normed_grad * block_input * row_scale, axis=0)
    input_grad = (
        cotangent
        + row_scale * weighted_grad
        - block_input * row_scale**3 * jnp.mean(weighted_grad * block_input, axis=1, keepdims=True)
    )
    state_rows = 10 * STATE // LANES
    shared = jnp.concatenate([norm_gain_part.reshape(-1, LANES), packed[:state_rows]], axis=0)
    shared = group_sum(shared, "tensor", 1, group_count)
    packed = jnp.concatenate([shared, packed[state_rows:]], axis=0)
    packed = group_sum(group_sum(packed, "dp", 2, half), "dp", 1, 2)
    local = packed[shared.shape[0] :].reshape(-1)
    norm_gain_grad = packed[: shared.shape[0] - state_rows].reshape(-1)
    state_sum = packed[shared.shape[0] - state_rows : shared.shape[0]].reshape(5, 2 * STATE)
    spread = [jnp.where(me == i, tail_sum[:, :share], 0.0) for i in range(group_count)]
    spread = jnp.concatenate(
        [jnp.concatenate(spread[i : i + fold], axis=1) for i in range(0, group_count, fold)], axis=0
    )
    spread = cube_sum(spread, "tensor")
    rows = tail_sum.shape[0]
    state_grad = jnp.concatenate([spread[i * rows : (i + 1) * rows] for i in range(group_count // fold)], axis=1)
    at = 6 * channels
    return (
        block_output,
        input_grad,
        norm_gain_grad,
        pair_sum[1],
        input_sum[:, :channels],
        state_grad,
        tail_sum[:, share : share + heads],
        local[: 4 * channels].reshape(4, channels),
        local[4 * channels : 5 * channels],
        state_sum[:4],
        state_sum[4],
        local[at + heads : at + 2 * heads],
        local[at + 2 * heads : at + 3 * heads],
        local[at : at + heads],
        local[5 * channels : at],
        pair_sum[0].T,
    )


def solution(mesh):
    rows = P(("dp", "tensor"), None)
    both = P("dp", "tensor")
    inner = P("tensor")
    return jax.shard_map(
        shards,
        mesh=mesh,
        in_specs=(
            rows, rows, P(), both, both, P("dp", None), both, P(None, "tensor"), inner, P(), P(), inner, inner,
            inner, inner, P("tensor", "dp"),
        ),
        out_specs=(
            rows, rows, P(), both, both, P("dp", None), both, P(None, "tensor"), inner, P(), P(), inner, inner,
            inner, inner, P("tensor", "dp"),
        ),
        check_vma=False,
    )
```

```python
import jax
import jax.numpy as jnp
from jax import lax
from jax.experimental import pallas as pl
from jax.experimental.pallas import tpu as pltpu
from jax.sharding import PartitionSpec as P

HEAD_DIM = 64
STATE = 128
BLOCK = 256
SEQ = 1024
LANES = 128

LIM_SCAN = 61
LIM_SCAN_BACK = 61
LIM_NORMED_PARTS = 61

epsilon = 1e-05
high = lax.Precision.HIGH
highest = lax.Precision.HIGHEST
f32 = jnp.float32
bf16 = jnp.bfloat16


def dot(left, right, dims, precision=None):
    return lax.dot_general(
        left, right, (dims, ((), ())), precision=precision, preferred_element_type=f32
    )


def sigmoid(v):
    return 1.0 / (1.0 + jnp.exp(-v))


def softplus(v):
    return jnp.maximum(v, 0.0) + jnp.log1p(jnp.exp(-jnp.abs(v)))


def iota(shape, axis):
    return lax.broadcasted_iota(jnp.int32, shape, axis)


def split(v):
    high_half = v.astype(bf16).astype(f32)
    return high_half, v - high_half


def packed(mine, first, second):
    return jnp.where(mine, first, pltpu.roll(second, HEAD_DIM, 1)).astype(bf16)


def meet(left, right, mine):
    (left_high, left_low), (right_high, right_low) = left, right
    lefts = [packed(mine, left_high, left_low), jnp.where(mine, left_high, 0.0).astype(bf16)]
    rights = [packed(mine, right_high, right_high), jnp.where(mine, right_low, 0.0).astype(bf16)]
    return dot(jnp.concatenate(lefts, axis=1), jnp.concatenate(rights, axis=1), ((1,), (1,)))


def pair_columns(table, pair):
    lane = iota((table.shape[0], LANES), 1)
    return jnp.where(lane < HEAD_DIM, table[:, 2 * pair : 2 * pair + 1], table[:, 2 * pair + 1 : 2 * pair + 2])


def decay_tables(step_rows, step_bias, rates):
    step_size = softplus(step_rows + step_bias)
    earlier = (iota((BLOCK, BLOCK), 0) >= iota((BLOCK, BLOCK), 1)).astype(f32)
    cumulative = dot(earlier, step_size * rates, ((1,), (0,)), highest)
    return step_size, cumulative, jnp.exp(cumulative), jnp.exp(cumulative[BLOCK - 1 : BLOCK, :] - cumulative)


def state_decay(from_start, pair):
    last = from_start[BLOCK - 1 : BLOCK, :]
    row = iota((LANES, STATE), 0)
    return jnp.where(row < HEAD_DIM, last[:, 2 * pair : 2 * pair + 1], last[:, 2 * pair + 1 : 2 * pair + 2])


def shifted_conv(rows_ref, before, buffer, taps, conv_bias, first):
    @pl.when(first)
    def _():
        buffer[0:8, :] = before[...]

    @pl.when(jnp.logical_not(first))
    def _():
        buffer[0:8, :] = buffer[BLOCK : BLOCK + 8, :]

    buffer[8 : BLOCK + 8, :] = rows_ref[...]
    total = conv_bias[...] + taps[0:1, :] * buffer[8 : BLOCK + 8, :]
    for tap in range(1, 4):
        total = total + taps[tap : tap + 1, :] * buffer[8 - tap : BLOCK + 8 - tap, :]
    return total


def scan_kernel(
    input_rows, state_rows, step_rows, input_before, state_before, state_entering,
    conv_input, conv_input_bias, conv_state, conv_state_bias, step_bias, rates, skip,
    mixed, input_conv, state_conv, entering, carried, input_buffer, state_buffer,
):
    first = pl.program_id(0) == 0
    pairs = input_rows.shape[1] // LANES

    @pl.when(first)
    def _():
        carried[...] = state_entering[...]

    input_conv[...] = shifted_conv(input_rows, input_before, input_buffer, conv_input, conv_input_bias, first)
    state_pre = shifted_conv(state_rows, state_before, state_buffer, conv_state, conv_state_bias, first)
    state_conv[...] = state_pre
    state_act = state_pre * sigmoid(state_pre)
    writes, reads = state_act[:, :STATE], state_act[:, STATE:]
    meeting = dot(reads, writes, ((1,), (1,)), high)
    step_size, cumulative, from_start, to_end = decay_tables(step_rows[...], step_bias[...], rates[...])
    cumulative_t = cumulative.T
    causal = iota((BLOCK, BLOCK), 0) >= iota((BLOCK, BLOCK), 1)
    lane = iota((BLOCK, LANES), 1)
    for pair in range(pairs):
        columns = slice(pair * LANES, pair * LANES + LANES)
        pre = input_conv[:, columns]
        inputs = pre * sigmoid(pre)
        weighted = inputs * pair_columns(step_size, pair)
        state_in = carried[pair]
        entering[0, pair] = state_in
        out = dot(reads, state_in, ((1,), (1,)), high) * pair_columns(from_start, pair)
        for side in range(2):
            head = 2 * pair + side
            gap = cumulative[:, head : head + 1] - cumulative_t[head : head + 1, :]
            mixing = jnp.exp(jnp.where(causal, gap, -1e30)) * meeting
            mine = (lane < HEAD_DIM) if side == 0 else (lane >= HEAD_DIM)
            out = out + dot(mixing, jnp.where(mine, weighted, 0.0), ((1,), (0,)), high)
        fresh = dot(weighted * pair_columns(to_end, pair), writes, ((0,), (0,)), high)
        carried[pair] = state_decay(from_start, pair) * state_in + fresh
        mixed[:, columns] = out + skip[:, columns] * inputs


def scan_back_kernel(
    input_rows, state_rows, step_rows, input_conv, state_conv, mixed, entering, mixed_grad,
    input_after, state_after, state_leaving, decay_after,
    conv_input, conv_state, step_bias, rates, skip, head_of,
    input_grad, state_grad, step_grad, input_sums, state_sums, step_sums, input_first, state_first, carried, later,
    input_buffer, state_buffer, gap_grad, out_products, in_products,
):
    first = pl.program_id(0) == 0
    pairs = input_rows.shape[1] // LANES

    @pl.when(first)
    def _():
        carried[...] = state_leaving[...]
        later[...] = decay_after[...]
        input_sums[...] = jnp.zeros(input_sums.shape, f32)
        state_sums[...] = jnp.zeros(state_sums.shape, f32)
        step_sums[...] = jnp.zeros(step_sums.shape, f32)
        input_buffer[BLOCK : BLOCK + 8, :] = input_after[...]
        state_buffer[BLOCK : BLOCK + 8, :] = state_after[...]

    @pl.when(jnp.logical_not(first))
    def _():
        input_buffer[BLOCK : BLOCK + 8, :] = input_buffer[0:8, :]
        state_buffer[BLOCK : BLOCK + 8, :] = state_buffer[0:8, :]

    state_pre = state_conv[...]
    state_sig = sigmoid(state_pre)
    state_act = state_pre * state_sig
    writes, reads = state_act[:, :STATE], state_act[:, STATE:]
    meeting_t = dot(writes, reads, ((1,), (1,)), high)
    step_size, cumulative, from_start, to_end = decay_tables(step_rows[...], step_bias[...], rates[...])
    cumulative_t = cumulative.T
    causal_t = iota((BLOCK, BLOCK), 0) <= iota((BLOCK, BLOCK), 1)
    lane = iota((BLOCK, LANES), 1)
    gap_grad[...] = jnp.zeros(gap_grad.shape, f32)
    writes_grad = jnp.zeros((BLOCK, STATE), f32)
    reads_grad = jnp.zeros((BLOCK, STATE), f32)
    for pair in range(pairs):
        columns = slice(pair * LANES, pair * LANES + LANES)
        pre = input_conv[:, columns]
        sig = sigmoid(pre)
        inputs = pre * sig
        step_pair = pair_columns(step_size, pair)
        weighted = inputs * step_pair
        out_grad = mixed_grad[:, columns]
        skip_product = out_grad * inputs
        input_sums[5:6, columns] += jnp.sum(skip_product, axis=0, keepdims=True)
        end_pair = pair_columns(to_end, pair)
        leaving_grad = carried[pair]
        weighted_grad = dot(writes, leaving_grad, ((1,), (1,)), high) * end_pair
        grad_halves, weighted_halves = split(out_grad), split(weighted)
        for side in range(2):
            head = 2 * pair + side
            gap = cumulative_t[head : head + 1, :] - cumulative[:, head : head + 1]
            within = jnp.exp(jnp.where(causal_t, gap, -1e30))
            mine = (lane < HEAD_DIM) if side == 0 else (lane >= HEAD_DIM)
            own_grad = jnp.where(mine, out_grad, 0.0)
            weighted_grad = weighted_grad + dot(within * meeting_t, own_grad, ((1,), (0,)), high)
            gap_grad[...] += within * meet(weighted_halves, grad_halves, mine)
        start_grad = out_grad * pair_columns(from_start, pair)
        reads_grad = reads_grad + dot(start_grad, entering[0, pair], ((1,), (0,)), high)
        writes_grad = writes_grad + dot(weighted * end_pair, leaving_grad, ((1,), (0,)), high)
        carried[pair] = state_decay(from_start, pair) * leaving_grad + dot(start_grad, reads, ((0,), (0,)), high)
        out_products[:, columns] = out_grad * mixed[:, columns] - skip[:, columns] * skip_product
        in_products[:, columns] = inputs * weighted_grad
        inputs_grad = skip[:, columns] * out_grad + step_pair * weighted_grad
        input_buffer[0:BLOCK, columns] = inputs_grad * (sig * (1.0 + pre * (1.0 - sig)))
    reads_grad = reads_grad + dot(gap_grad[...], writes, ((0,), (0,)), high)
    writes_grad = writes_grad + dot(gap_grad[...], reads, ((1,), (0,)), high)
    state_slope = state_sig * (1.0 + state_pre * (1.0 - state_sig))
    state_buffer[0:BLOCK, 0:STATE] = writes_grad * state_slope[:, :STATE]
    state_buffer[0:BLOCK, STATE : 2 * STATE] = reads_grad * state_slope[:, STATE:]

    for buffer, rows, taps, sums, result in (
        (input_buffer, input_rows, conv_input, input_sums, input_grad),
        (state_buffer, state_rows, conv_state, state_sums, state_grad),
    ):
        raw = rows[...]
        total = jnp.zeros(raw.shape, f32)
        for tap in range(4):
            ahead = buffer[tap : tap + BLOCK, :]
            total = total + taps[tap : tap + 1, :] * ahead
            sums[tap : tap + 1, :] += jnp.sum(ahead * raw, axis=0, keepdims=True)
        sums[4:5, :] += jnp.sum(buffer[0:BLOCK, :], axis=0, keepdims=True)
        result[...] = total.astype(result.dtype)
    input_first[...] = input_buffer[0:8, :]
    state_first[...] = state_buffer[0:8, :]

    out_head = dot(out_products[...], head_of[...], ((1,), (0,)), high)
    in_head = dot(in_products[...], head_of[...], ((1,), (0,)), high)
    upper = (iota((BLOCK, BLOCK), 0) <= iota((BLOCK, BLOCK), 1)).astype(f32)
    decay_grad = dot(upper, out_head - step_size * in_head, ((1,), (0,)), highest) + later[0:1, :]
    later[0:1, :] = decay_grad[0:1, :]
    step_sig = sigmoid(step_rows[...] + step_bias[...])
    step_back = (rates[...] * decay_grad + in_head) * step_sig
    step_grad[...] = step_back.astype(step_grad.dtype)
    step_sums[0:1, :] += jnp.sum(step_back, axis=0, keepdims=True)
    step_sums[1:2, :] += jnp.sum(step_size * decay_grad, axis=0, keepdims=True)


def whole(array):
    zeros = (0,) * array.ndim
    return pl.BlockSpec(array.shape, lambda k: zeros)


def params(mebibytes):
    return pltpu.CompilerParams(dimension_semantics=("arbitrary",), vmem_limit_bytes=mebibytes * 1024 * 1024)


little = pl.CostEstimate(flops=10**6, bytes_accessed=2**16, transcendentals=0)


def run_scan(start, span, input_rows, state_rows, step_rows, zeros, state_entering, consts):
    channels = input_rows.shape[1]
    pairs = channels // LANES
    rows = span * BLOCK
    edge = start * BLOCK // 8 - 1

    def tokens(width):
        return pl.BlockSpec((BLOCK, width), lambda k: (start + k, 0))

    def results(width):
        return pl.BlockSpec((BLOCK, width), lambda k: (k, 0))

    if start == 0:
        before = zeros
        before_specs = [whole(c) for c in before]
    else:
        before = (input_rows, state_rows)
        before_specs = [pl.BlockSpec((8, c.shape[1]), lambda k: (edge, 0)) for c in before]
    return pl.pallas_call(
        scan_kernel,
        grid=(span,),
        in_specs=[tokens(channels), tokens(2 * STATE), tokens(LANES)] + before_specs + [whole(state_entering)]
        + [whole(c) for c in consts],
        out_specs=[
            results(channels), results(channels), results(2 * STATE),
            pl.BlockSpec((1, pairs, LANES, STATE), lambda k: (k, 0, 0, 0)), whole(state_entering),
        ],
        out_shape=[
            jax.ShapeDtypeStruct((rows, channels), f32),
            jax.ShapeDtypeStruct((rows, channels), f32),
            jax.ShapeDtypeStruct((rows, 2 * STATE), f32),
            jax.ShapeDtypeStruct((span, pairs, LANES, STATE), f32),
            jax.ShapeDtypeStruct((pairs, LANES, STATE), f32),
        ],
        scratch_shapes=[pltpu.VMEM((BLOCK + 8, channels), f32), pltpu.VMEM((BLOCK + 8, 2 * STATE), f32)],
        compiler_params=params(LIM_SCAN),
        cost_estimate=little,
        name="scan",
    )(input_rows, state_rows, step_rows, *before, state_entering, *consts)


def run_scan_back(start, span, projections, kept, at, mixed_grad, carry, consts):
    channels = mixed_grad.shape[1]
    pairs = channels // LANES
    rows = span * BLOCK

    def tokens(width):
        return pl.BlockSpec((BLOCK, width), lambda k: (start + span - 1 - k, 0))

    def own(width, first=0):
        return pl.BlockSpec((BLOCK, width), lambda k: (first + span - 1 - k, 0))

    def shape(*dims):
        return jax.ShapeDtypeStruct(dims, f32)

    sums = [shape(8, channels), shape(8, 2 * STATE), shape(8, LANES)]
    ends = [jax.ShapeDtypeStruct(c.shape, f32) for c in carry]
    return pl.pallas_call(
        scan_back_kernel,
        grid=(span,),
        in_specs=[
            tokens(channels), tokens(2 * STATE), tokens(LANES), own(channels, at),
            own(2 * STATE, at), own(channels, at),
            pl.BlockSpec((1, pairs, LANES, STATE), lambda k: (at + span - 1 - k, 0, 0, 0)), tokens(channels),
        ] + [whole(c) for c in carry] + [whole(c) for c in consts],
        out_specs=[own(channels), own(2 * STATE), own(LANES)] + [whole(c) for c in sums + ends],
        out_shape=[
            jax.ShapeDtypeStruct((rows, channels), bf16), shape(rows, 2 * STATE),
            jax.ShapeDtypeStruct((rows, LANES), bf16),
        ] + sums + ends,
        scratch_shapes=[
            pltpu.VMEM((BLOCK + 8, channels), f32), pltpu.VMEM((BLOCK + 8, 2 * STATE), f32),
            pltpu.VMEM((BLOCK, BLOCK), f32), pltpu.VMEM((BLOCK, channels), f32), pltpu.VMEM((BLOCK, channels), f32),
        ],
        compiler_params=params(LIM_SCAN_BACK),
        cost_estimate=little,
        name="scan_back",
    )(*projections, *kept, mixed_grad, *carry, *consts)


def fixed_block(*shape):
    zeros = (0,) * len(shape)
    return pl.BlockSpec(shape, lambda n, *_: zeros)


def call(kernel, places, steps, operands, in_specs, out_specs, out_shape, name, scratch=(), aliases={}):
    return pl.pallas_call(
        kernel,
        grid_spec=pltpu.PrefetchScalarGridSpec(
            num_scalar_prefetch=1, grid=(steps,), in_specs=in_specs, out_specs=out_specs, scratch_shapes=list(scratch)
        ),
        out_shape=out_shape,
        input_output_aliases=aliases,
        compiler_params=params(61),
        cost_estimate=little,
        name=name,
    )(places, *operands)


def lay(places, pieces, result, first=0):
    for i, piece in enumerate(pieces):
        result[pl.ds(pl.multiple_of(places[first + i], 16), piece.shape[0]), :] = piece[...]


TILE = 256


def tile_columns(ref, n, first=0):
    return ref[:, pl.ds(pl.multiple_of(n * TILE + first, LANES), TILE)]


def first_project(weights, tokens, places, channels):
    count = len(weights)
    depth, width = tokens[0].shape[1], weights[0].shape[1]
    rows = tokens[0].shape[0] * len(tokens)

    def kernel(places, *refs):
        pieces, (normed, full, input_proj, tail_proj) = refs[:-4], refs[-4:]
        n = pl.program_id(0)

        @pl.when(n == 0)
        def _():
            lay(places, pieces[:count], full)
            lay(places, pieces[count:], normed, count)
            tail_proj[...] = dot(normed[...], full[:, channels:], ((1,), (0,)))

        input_proj[...] = dot(normed[...], tile_columns(full, n), ((1,), (0,)))

    return call(
        kernel, places, channels // TILE, (*weights, *tokens),
        [fixed_block(*piece.shape) for piece in (*weights, *tokens)],
        [
            fixed_block(rows, depth), fixed_block(depth, width), pl.BlockSpec((rows, TILE), lambda n, _: (0, n)),
            fixed_block(rows, width - channels),
        ],
        [
            jax.ShapeDtypeStruct((rows, depth), bf16), jax.ShapeDtypeStruct((depth, width), bf16),
            jax.ShapeDtypeStruct((rows, channels), f32), jax.ShapeDtypeStruct((rows, width - channels), f32),
        ],
        "first_project",
    )


def second_project(weights, places, normed, cot, mixed, gain):
    count, halves = len(weights), len(mixed)
    width = weights[0].shape[1]
    rows, depth = normed.shape
    channels = width // 2
    part_rows = mixed[0].shape[0]

    def kernel(places, *refs):
        pieces, (normed_ref, cot_ref, gain_ref), mixed_refs = refs[:count], refs[count : count + 3], refs[count + 3 : -4]
        full, gate_proj, out_grad, sums = refs[-4:]
        n = pl.program_id(0)

        @pl.when(n == 0)
        def _():
            lay(places, pieces, full)
            sums[...] = jnp.zeros(sums.shape, f32)

        gate_proj[...] = dot(normed_ref[...], tile_columns(full, n), ((1,), (0,)))
        out_grad[...] = dot(cot_ref[...], tile_columns(full, n, channels), ((1,), (0,)))
        ones = jnp.ones((8, TILE), f32)
        for i in range(halves):
            at = slice(i * part_rows, (i + 1) * part_rows)
            proj = gate_proj[at, :]
            gated = mixed_refs[i][...] * (proj * sigmoid(proj))
            pulled = out_grad[at, :] * gain_ref[...] * gated
            sums[0:8, at] += dot(ones, gated * gated, ((1,), (1,)), highest)
            sums[8:16, at] += dot(ones, pulled, ((1,), (1,)), highest)

    tile = pl.BlockSpec((rows, TILE), lambda n, _: (0, n))
    return call(
        kernel, places, channels // TILE, (*weights, normed, cot, gain, *mixed),
        [fixed_block(*piece.shape) for piece in (*weights, normed, cot)]
        + [pl.BlockSpec((1, TILE), lambda n, _: (0, n))]
        + [pl.BlockSpec((part_rows, TILE), lambda n, _: (0, n)) for _ in mixed],
        [fixed_block(depth, width), tile, tile, fixed_block(16, rows)],
        [
            jax.ShapeDtypeStruct((depth, width), bf16), jax.ShapeDtypeStruct((rows, channels), f32),
            jax.ShapeDtypeStruct((rows, channels), f32), jax.ShapeDtypeStruct((16, rows), f32),
        ],
        "second_project",
    )


def store_shares(places, product, result, tops, part, columns):
    owners, rows = result.shape[0], result.shape[2] - 16
    for owner in range(owners):
        own = product[owner * rows : (owner + 1) * rows]
        result[places[owner], part, 0:rows, columns] = own
        top = jnp.max(jnp.abs(own), axis=0, keepdims=True)
        result[places[owner], part, rows : rows + 16, columns] = jnp.zeros((16, own.shape[1]), f32)
        tops[places[owner], part, :, columns] = jnp.broadcast_to(top, (8, own.shape[1]))


def gate_step(ring, places, sums, gain, mixed, gate_proj, out_grad, cot_t, normed_t, second_full, inner_total):
    depth = second_full.shape[0]
    rows, channels = gate_proj.shape
    halves, part_rows = len(mixed), mixed[0].shape[0]
    share = cot_t.shape[0] // ring.count

    def kernel(places, *refs):
        sums_ref, gain_ref, proj_ref, grad_ref, cot_ref, normed_ref, weight_ref = refs[:7]
        mixed_refs, (branch, gate_grad, mixed_grad, gain_sum, result, tops, gate_out) = refs[7 : 7 + halves], refs[7 + halves :]
        gain_sum[...] = jnp.zeros(gain_sum.shape, f32)
        scale_row = lax.rsqrt(sums_ref[0:8, :] / inner_total + epsilon)
        pull_row = scale_row * scale_row * scale_row * (sums_ref[8:16, :] / inner_total)
        scales, pulls = scale_row.T, pull_row.T
        for i in range(halves):
            at = slice(i * part_rows, (i + 1) * part_rows)
            proj, rows_mixed, grad = proj_ref[at, :], mixed_refs[i][...], grad_ref[at, :]
            sig = sigmoid(proj)
            act = proj * sig
            gated = rows_mixed * act
            scale = scales[at, 0:1]
            scaled = gated * scale
            gate_out[at, :] = (scaled * gain_ref[...]).astype(bf16)
            gain_sum[0:1, :] += jnp.sum(grad * scaled, axis=0, keepdims=True)
            gated_grad = scale * (grad * gain_ref[...]) - gated * pulls[at, 0:1]
            mixed_grad[at, :] = gated_grad * act
            gate_grad[at, :] = (gated_grad * rows_mixed * (sig * (1.0 + proj * (1.0 - sig)))).astype(bf16)
        everything = slice(0, TILE)
        first = pl.program_id(0) == 0
        for i in range(0, rows, TILE):
            at = slice(i, i + TILE)
            share_out = dot(gate_out[at, :], weight_ref[...], ((1,), (1,)))
            branch[at, :] = share_out + jnp.where(first, 0.0, branch[at, :])
        store_shares(places, dot(cot_ref[...], gate_out[...], ((1,), (0,))), result, tops, 0, everything)
        store_shares(places, dot(normed_ref[...], gate_grad[...], ((1,), (0,))), result, tops, 1, everything)

    tile = pl.BlockSpec((rows, TILE), lambda n, _: (0, n))
    return call(
        kernel, places, channels // TILE, (sums, gain, gate_proj, out_grad, cot_t, normed_t, second_full, *mixed),
        [
            fixed_block(16, rows), pl.BlockSpec((1, TILE), lambda n, _: (0, n)), tile, tile,
            fixed_block(*cot_t.shape), fixed_block(*normed_t.shape),
            pl.BlockSpec((depth, TILE), lambda n, _: (0, channels // TILE + n)),
        ] + [pl.BlockSpec((part_rows, TILE), lambda n, _: (0, n)) for _ in mixed],
        [
            fixed_block(rows, depth), tile, tile, pl.BlockSpec((8, TILE), lambda n, _: (0, n)),
            pl.BlockSpec((ring.count, 2, share + 16, TILE), lambda n, _: (0, 0, 0, n)),
            pl.BlockSpec((ring.count, 2, 8, TILE), lambda n, _: (0, 0, 0, n)),
        ],
        [
            jax.ShapeDtypeStruct((rows, depth), f32), jax.ShapeDtypeStruct((rows, channels), bf16),
            jax.ShapeDtypeStruct((rows, channels), f32), jax.ShapeDtypeStruct((8, channels), f32),
            jax.ShapeDtypeStruct((ring.count, 2, share + 16, channels), f32),
            jax.ShapeDtypeStruct((ring.count, 2, 8, channels), f32),
        ],
        "gate_step", [pltpu.VMEM((rows, TILE), bf16)],
    )


def input_partials(ring, places, normed_t, input_back):
    halves, (part_rows, channels) = len(input_back), input_back[0].shape
    share = normed_t.shape[0] // ring.count

    def kernel(places, left, *refs):
        rights, result, tops = refs[:-2], refs[-2], refs[-1]
        product = dot(left[:, 0:part_rows], rights[0][...], ((1,), (0,)))
        for i in range(1, halves):
            product = product + dot(left[:, i * part_rows : (i + 1) * part_rows], rights[i][...], ((1,), (0,)))
        store_shares(places, product, result, tops, 0, slice(0, TILE))

    def block(rows):
        return pl.BlockSpec((ring.count, 1, rows, TILE), lambda n, _: (0, 0, 0, n))

    return call(
        kernel, places, channels // TILE, (normed_t, *input_back),
        [fixed_block(*normed_t.shape)] + [pl.BlockSpec((part_rows, TILE), lambda n, _: (0, n)) for _ in input_back],
        [block(share + 16), block(8)],
        [jax.ShapeDtypeStruct((ring.count, 1, rows, channels + LANES), f32) for rows in (share + 16, 8)],
        "input_partials",
    )


def tail_partials(places, normed_t, tail, parts, tops):
    def kernel(places, left, right, parts_in, tops_in, result, tops_out):
        product = dot(left[...], right[...], ((1,), (0,)))
        store_shares(places, product, result, tops_out, 0, slice(0, LANES))

    last = parts.shape[3] // LANES - 1
    specs = [pl.BlockSpec((*array.shape[:3], LANES), lambda n, _: (0, 0, 0, last)) for array in (parts, tops)]
    anywhere = pl.BlockSpec(memory_space=pl.ANY)
    return call(
        kernel, places, 1, (normed_t, tail, parts, tops),
        [fixed_block(*normed_t.shape), fixed_block(*tail.shape), anywhere, anywhere], specs,
        [jax.ShapeDtypeStruct(array.shape, f32) for array in (parts, tops)], "tail_partials", aliases={3: 0, 4: 1},
    )


def normed_kernel(halves, places, gate_rows, tail_rows, gate_tile, input_tile, tail_tile, *refs):
    inputs, results, product = refs[:halves], refs[halves:-1], refs[-1]
    part = inputs[0].shape[0]
    for i, input_rows in enumerate(inputs):
        at = slice(i * part, (i + 1) * part)
        total = dot(gate_rows[at, :], gate_tile[...], ((1,), (1,)))
        total = total + dot(tail_rows[at, :], tail_tile[...], ((1,), (1,)))
        product[at, :] = total + dot(input_rows[...], input_tile[...], ((1,), (1,)))
    rows = results[0].shape[0]
    for i, result in enumerate(results):
        result[...] = product[pl.ds(pl.multiple_of(places[i] * rows, 16), rows), :]


def normed_parts(places, gate_grad, input_back, tail, second_full, first_full):
    count = lax.axis_size("tensor")
    tokens, channels = gate_grad.shape
    width, tile = first_full.shape[0], 2 * LANES
    halves = len(input_back)

    def fixed(n, _):
        return (0, 0)

    return pl.pallas_call(
        lambda *refs: normed_kernel(halves, *refs),
        grid_spec=pltpu.PrefetchScalarGridSpec(
            num_scalar_prefetch=1, grid=(width // tile,),
            in_specs=[
                pl.BlockSpec((tokens, channels), fixed), pl.BlockSpec((tokens, LANES), fixed),
                pl.BlockSpec((tile, channels), lambda n, _: (n, 0)), pl.BlockSpec((tile, channels), lambda n, _: (n, 0)),
                pl.BlockSpec((tile, LANES), lambda n, _: (n, channels // LANES)),
            ] + [pl.BlockSpec(half.shape, fixed) for half in input_back],
            out_specs=[pl.BlockSpec((tokens // count, tile), lambda n, _: (0, n))] * count,
            scratch_shapes=[pltpu.VMEM((tokens, tile), f32)],
        ),
        out_shape=[jax.ShapeDtypeStruct((tokens // count, width), f32)] * count,
        compiler_params=params(LIM_NORMED_PARTS),
        cost_estimate=little,
        name="normed_parts",
    )(places, gate_grad, tail, second_full, first_full, first_full, *input_back)


def cycle(count):
    return list(range(0, count, 2)) + list(range(count - 1, 0, -2))


def table(numbers):
    return jnp.stack(numbers).astype(jnp.int32)


class Ring:
    def __init__(self):
        self.count = lax.axis_size("dp")
        order = cycle(self.count)
        self.up = [(order[i], order[(i + 1) % self.count]) for i in range(self.count)]
        self.down = [(b, a) for a, b in self.up]
        me = lax.axis_index("dp")
        self.place = jnp.where(me % 2 == 0, me // 2, self.count - 1 - me // 2)

    def places(self):
        order = cycle(self.count)
        return table([(order.index(i) - self.place + self.count) % self.count for i in range(self.count)])

    def owner(self, offset):
        place = (self.place + offset + self.count) % self.count
        return jnp.where(place < self.count // 2, 2 * place, 2 * (self.count - 1 - place) + 1)


def middle(rows):
    return (rows // 2 + 15) // 16 * 16


class Gather:
    def __init__(self, ring, shard):
        self.ring, self.shard, self.step = ring, shard, 0
        self.held = [(shard, 0, 0)]
        self.last = (shard, shard)

    def hop(self):
        self.step += 1
        half, cut = self.ring.count // 2, middle(self.shard.shape[0])
        up, down = self.last
        offsets = ((-self.step, 0), (self.step, 0))
        if self.step == half:
            up, down = up[:cut], down[cut:]
            offsets = ((half, 0), (half, cut))
        self.last = (lax.ppermute(up, "dp", self.ring.up), lax.ppermute(down, "dp", self.ring.down))
        self.held += [(piece, *offset) for piece, offset in zip(self.last, offsets)]

    def after(self, *marks):
        self.last, marks = fence(self.last, marks)
        self.held[-2:] = [(piece, *old[1:]) for piece, old in zip(self.last, self.held[-2:])]
        return marks if len(marks) > 1 else marks[0]

    def pieces(self):
        return [piece for piece, _, _ in self.held]

    def places(self):
        rows, half = self.shard.shape[0], self.ring.count // 2
        spots = [self.ring.owner(0) * rows]
        for step in range(1, half):
            spots += [self.ring.owner(-step) * rows, self.ring.owner(step) * rows]
        return spots + [self.ring.owner(half) * rows, self.ring.owner(half) * rows + middle(rows)]


def encode(rows, limit):
    power = jnp.ceil(jnp.log2(jnp.maximum(limit, 1e-30)))
    ours = lax.broadcasted_iota(jnp.int32, rows.shape, 1) < rows.shape[1] - 16
    return jnp.where(ours, rows * jnp.exp2(15.0 - power), power).astype(jnp.float16)


def decode(payload):
    power = payload[:, -16:-15].astype(f32)
    return payload.astype(f32) * jnp.exp2(power - 15.0), jnp.exp2(power)


class Scatter:
    def __init__(self, ring, parts, tops):
        self.ring, self.parts, self.tops = ring, parts, tops
        self.step = ring.count // 2
        self.rows = parts.shape[2] - 16
        self.cut = middle(self.rows)
        far = parts[self.step]
        top = tops[self.step, :, 0:1]
        upper = jnp.concatenate([far[:, : self.cut], far[:, -16:]], axis=1)
        self.send = (encode(upper, top), encode(far[:, self.cut :], top))

    def hop(self):
        self.send = fence(*self.send)
        self.got = (lax.ppermute(self.send[0], "dp", self.ring.up), lax.ppermute(self.send[1], "dp", self.ring.down))

    def after(self, *marks):
        self.got, marks = fence(self.got, marks)
        return marks if len(marks) > 1 else marks[0]

    def before(self, *marks):
        self.send, marks = fence(self.send, marks)
        return marks if len(marks) > 1 else marks[0]

    def add(self):
        first = self.step == self.ring.count // 2
        self.got = fence(*self.got)
        (up, up_top), (down, down_top) = (decode(g) for g in self.got)
        if first:
            up = jnp.pad(up, ((0, 0), (0, self.rows - self.cut), (0, 0)))
            down = jnp.pad(down, ((0, 0), (self.cut, 0), (0, 0)))
            up = jnp.where(lax.broadcasted_iota(jnp.int32, up.shape, 1) < self.cut, up, 0.0)
        self.step -= 1
        if self.step == 0:
            return (self.parts[0] + up + down)[:, : self.rows]
        above, below = self.parts[self.step], self.parts[self.ring.count - self.step]
        self.send = (
            encode(above + up, self.tops[self.step, :, 0:1] + up_top),
            encode(below + down, self.tops[self.ring.count - self.step, :, 0:1] + down_top),
        )
        return None


def fence(*arrays):
    flat, tree = jax.tree.flatten(arrays)
    return jax.tree.unflatten(tree, lax.optimization_barrier(flat))


def across(array, bit, axis="tensor"):
    count = lax.axis_size(axis)
    return lax.ppermute(array, axis, [(i, i ^ bit) for i in range(count)])


def group_sum(array, axis, first, count):
    terms = [array] + [across(array, first * other, axis) for other in range(1, count)]
    while len(terms) > 1:
        terms = [terms[i] + terms[i + 1] for i in range(0, len(terms), 2)]
    return terms[0]


def cube_sum(array, axis):
    bit = 1
    while bit < lax.axis_size(axis):
        array = array + across(array, bit, axis)
        bit *= 2
    return array


def shards(
    block_input, cotangent, norm_gain, gate_weight, input_weight, state_weight, step_weight, conv_input,
    conv_input_bias, conv_state, conv_state_bias, step_bias, decay_log, skip_scale, gate_gain, out_weight,
):
    group_count = lax.axis_size("tensor")
    me = lax.axis_index("tensor")
    ring = Ring()
    half = ring.count // 2
    local_rows = block_input.shape[0]
    channels = gate_gain.shape[0]
    heads = step_bias.shape[0]
    inner_total = channels * group_count
    share = 2 * STATE // group_count
    tokens = local_rows * group_count
    blocks = tokens // BLOCK
    fold = LANES // share
    folded = tokens // fold
    rows_dot = ((1,), (0,))
    back_dot = ((1,), (1,))

    state_mine = lax.dynamic_slice_in_dim(state_weight, me * share, share, 1)
    first = Gather(
        ring,
        jnp.concatenate(
            [input_weight, state_mine, jnp.pad(step_weight, ((0, 0), (0, LANES - share - heads)))], axis=1
        ).astype(bf16),
    )
    first.hop()
    row_scale = lax.rsqrt(jnp.mean(block_input * block_input, axis=1, keepdims=True) + epsilon)
    normed = (block_input * row_scale * norm_gain).astype(bf16)
    second_weight = jnp.concatenate([gate_weight, out_weight.T], axis=1).astype(bf16)
    rates = -jnp.exp(decay_log)

    def per_head(vector):
        return jnp.pad(vector, (0, LANES - heads))[None, :]

    skip = jnp.repeat(skip_scale, HEAD_DIM)[None, :]
    head_of = (
        lax.broadcasted_iota(jnp.int32, (channels, LANES), 0) // HEAD_DIM
        == lax.broadcasted_iota(jnp.int32, (channels, LANES), 1)
    ).astype(f32)
    scan_consts = (
        conv_input, conv_input_bias[None, :], conv_state, conv_state_bias[None, :], per_head(step_bias),
        per_head(rates), skip,
    )
    back_consts = (conv_input, conv_state, per_head(step_bias), per_head(rates), skip, head_of)
    carried = jnp.zeros((channels // LANES, LANES, STATE), f32)
    carry = (jnp.zeros((8, channels), f32), jnp.zeros((8, 2 * STATE), f32), carried, jnp.zeros((8, LANES), f32))
    gain = gate_gain[None, :]
    shard_places = first.places()
    token_places = [(me ^ bits) * local_rows for bits in range(4)]
    tables = (table(shard_places + token_places), table(shard_places), ring.places(), table([i ^ me for i in range(4)]))
    normed, scan_consts, back_consts, carried, carry, gain, tables = first.after(
        normed, scan_consts, back_consts, carried, carry, gain, tables
    )
    first_places, second_places, share_places, turn_places = tables
    first.hop()
    far, near = across(normed, 2), across(normed, 1)
    for _ in range(half - 3):
        first.hop()
    far, near, second_weight, cot_low = first.after(far, near, second_weight, cotangent.astype(bf16))
    first.hop()
    second_weight = first.after(second_weight)
    normed_pieces = (normed, near, far, across(far, 1))
    second = Gather(ring, second_weight)
    second.hop()
    cot_all = lax.all_gather(cot_low, "tensor", axis=0, tiled=True)
    normed_all, first_full, input_proj, tail_proj = first_project(
        first.pieces(), normed_pieces, first_places, channels
    )
    normed_all, first_full, input_proj, tail_proj = second.after(normed_all, first_full, input_proj, tail_proj)
    second.hop()
    step_proj = jnp.pad(tail_proj[:, share : share + heads], ((0, 0), (0, LANES - heads)))
    state_mine = jnp.concatenate([tail_proj[i * folded : (i + 1) * folded, :share] for i in range(fold)], axis=1)
    far = across(state_mine, 2)
    same_x, same_core, diagonal = across(state_mine, 1), far, across(far, 1)
    right_core = me % 2 == 1
    near = (jnp.where(right_core, same_x, state_mine), jnp.where(right_core, state_mine, same_x))
    away = (jnp.where(right_core, diagonal, same_core), jnp.where(right_core, same_core, diagonal))
    right_chip = me // 2 == 1
    state_parts = [jnp.where(right_chip, away[i], near[i]) for i in range(2)]
    state_parts += [jnp.where(right_chip, near[i], away[i]) for i in range(2)]
    state_proj = jnp.concatenate(
        [jnp.concatenate([p[:, i * share : (i + 1) * share] for p in state_parts], axis=1) for i in range(fold)], axis=0
    )
    span = 2
    scanned, mixed = [], []
    normed_t, input_proj = fence(normed_all.T, input_proj)
    for start in range(0, blocks, span):
        scanned.append(run_scan(start, span, input_proj, state_proj, step_proj, carry[:2], carried, scan_consts))
        carried = scanned[-1][4]
        mixed.append(scanned[-1][0])
        if second.step < half:
            carried, mixed[-1] = second.after(carried, mixed[-1])
            second.hop()
    while second.step < half:
        second.hop()
    second_full, gate_proj, gate_out_grad, sums = second_project(
        second.pieces(), second_places, normed_all, cot_all, mixed, gain
    )
    sums = (sums + across(sums, 1)) + (across(sums, 2) + across(sums, 3))
    branch_part, gate_grad, mixed_grad, gain_sum, *pair_parts = gate_step(
        ring, share_places, sums, gain, mixed, gate_proj, gate_out_grad, cot_all.T, normed_t, second_full,
        float(inner_total),
    )
    pair_ring = Scatter(ring, *pair_parts)
    done = []
    for turn in range(blocks // span):
        if turn == 0:
            carry, branch_part = pair_ring.before(carry, branch_part)
            pair_ring.hop()
            branch = lax.psum_scatter(branch_part, "tensor", scatter_dimension=0, tiled=True)
        else:
            carry = pair_ring.after(carry)
            pair_ring.add()
            carry = pair_ring.before(carry)
            pair_ring.hop()
        start = blocks - span * (turn + 1)
        kept = scanned[start // span]
        kept = [kept[1], kept[2], kept[0], kept[3]]
        result = run_scan_back(
            start, span, (input_proj, state_proj, step_proj), kept, 0, mixed_grad, carry, back_consts
        )
        done.insert(0, result)
        carry = tuple(result[6:])
    done = pair_ring.after(done)
    pair_ring.add()
    done = pair_ring.before(done)
    pair_ring.hop()
    input_back, state_back = [d[0] for d in done], [d[1] for d in done]
    step_back = jnp.concatenate([d[2] for d in done], axis=0)
    input_sums, state_sums, step_sums = (sum(d[i] for d in done) for i in range(3, 6))

    packed = jnp.concatenate(
        [
            state_sums[:5].reshape(-1),
            input_sums[:5].reshape(-1),
            gain_sum[0],
            jnp.sum(input_sums[5].reshape(heads, HEAD_DIM), axis=1),
            step_sums[0, :heads],
            step_sums[1, :heads] * rates,
        ]
    )
    packed = jnp.pad(packed, (0, -packed.shape[0] % LANES)).reshape(-1, LANES)

    def state_columns(index):
        return jnp.concatenate([lax.dynamic_slice_in_dim(rows, index * share, share, 1) for rows in state_back], axis=1)

    for_far, for_me = across(state_columns(me ^ 3), 1), across(state_columns(me ^ 1), 1)
    packed, for_far, for_me = fence(packed, for_far, for_me)
    far, input_back = fence(state_columns(me ^ 2) + for_far, input_back)
    from_far = across(far, 2)
    input_parts, from_far = fence(input_partials(ring, share_places, normed_t, input_back), from_far)
    state_share = (state_columns(me) + for_me + from_far).astype(bf16)
    state_share = jnp.concatenate([state_share[:, i * share : (i + 1) * share] for i in range(fold)], axis=0)
    tail = jnp.concatenate(
        [state_share, step_back[:, :heads], jnp.zeros((tokens, LANES - share - heads), bf16)], axis=1
    )
    parts = normed_parts(turn_places, gate_grad, input_back, tail, second_full, first_full)
    branch, *parts = pair_ring.after(branch, *parts)
    block_output = block_input + branch
    for_far, for_me = across(parts[3], 1), across(parts[1], 1)
    pair_ring.add()
    pair_ring.hop()
    input_parts, pair_ring.got = fence(tail_partials(share_places, normed_t, tail, *input_parts), pair_ring.got)
    input_ring = Scatter(ring, *input_parts)
    for_far, for_me = input_ring.before(for_far, for_me)
    input_ring.hop()
    sent = parts[2] + for_far
    sent = jnp.pad(sent, ((0, 16), (0, 0)))[None]
    from_far = across(encode(sent, jnp.max(jnp.abs(sent), axis=1, keepdims=True)), 2)
    input_sum = input_ring.add()
    pair_sum = pair_ring.add()
    while pair_sum is None:
        pair_ring.hop()
        pair_sum = pair_ring.add()
    while input_sum is None:
        input_ring.hop()
        if input_ring.step == 1:
            from_far = input_ring.after(from_far)
        input_sum = input_ring.add()
    normed_grad = parts[0] + for_me + decode(from_far)[0][0, :local_rows]
    input_sum = input_sum[0]
    tail_sum = input_sum[:, channels:]

    weighted_grad = normed_grad * norm_gain
    norm_gain_part = jnp.sum(normed_grad * block_input * row_scale, axis=0)
    input_grad = (
        cotangent
        + row_scale * weighted_grad
        - block_input * row_scale**3 * jnp.mean(weighted_grad * block_input, axis=1, keepdims=True)
    )
    spread = [jnp.where(me == i, tail_sum[:, :share], 0.0) for i in range(group_count)]
    spread = jnp.concatenate(
        [jnp.concatenate(spread[i : i + fold], axis=1) for i in range(0, group_count, fold)], axis=0
    )
    state_rows = 10 * STATE // LANES
    shared = jnp.concatenate([norm_gain_part.reshape(-1, LANES), packed[:state_rows]], axis=0)
    shared = group_sum(shared, "tensor", 1, group_count)
    shared, spread = fence(shared, spread + across(spread, 1))
    packed = jnp.concatenate([shared, packed[state_rows:]], axis=0)
    packed, spread = fence(group_sum(packed, "dp", 2, half), spread + across(spread, 2))
    packed = group_sum(packed, "dp", 1, 2)
    rows = tail_sum.shape[0]
    state_grad = jnp.concatenate([spread[i * rows : (i + 1) * rows] for i in range(group_count // fold)], axis=1)
    local = packed[shared.shape[0] :].reshape(-1)
    norm_gain_grad = packed[: shared.shape[0] - state_rows].reshape(-1)
    state_sum = packed[shared.shape[0] - state_rows : shared.shape[0]].reshape(5, 2 * STATE)
    at = 6 * channels
    return (
        block_output,
        input_grad,
        norm_gain_grad,
        pair_sum[1],
        input_sum[:, :channels],
        state_grad,
        tail_sum[:, share : share + heads],
        local[: 4 * channels].reshape(4, channels),
        local[4 * channels : 5 * channels],
        state_sum[:4],
        state_sum[4],
        local[at + heads : at + 2 * heads],
        local[at + 2 * heads : at + 3 * heads],
        local[at : at + heads],
        local[5 * channels : at],
        pair_sum[0].T,
    )


def solution(mesh):
    rows = P(("dp", "tensor"), None)
    both = P("dp", "tensor")
    inner = P("tensor")
    return jax.shard_map(
        shards,
        mesh=mesh,
        in_specs=(
            rows, rows, P(), both, both, P("dp", None), both, P(None, "tensor"), inner, P(), P(), inner, inner,
            inner, inner, P("tensor", "dp"),
        ),
        out_specs=(
            rows, rows, P(), both, both, P("dp", None), both, P(None, "tensor"), inner, P(), P(), inner, inner,
            inner, inner, P("tensor", "dp"),
        ),
        check_vma=False,
    )
```

```python
import jax
import jax.numpy as jnp
from jax import lax
from jax.experimental import pallas as pl
from jax.experimental.pallas import tpu as pltpu
from jax.sharding import PartitionSpec as P

HEAD_DIM = 64
STATE = 128
BLOCK = 256
SEQ = 1024
LANES = 128

LIM_SCAN = 61
LIM_SCAN_BACK = 61
LIM_NORMED_PARTS = 61

epsilon = 1e-05
high = lax.Precision.HIGH
highest = lax.Precision.HIGHEST
f32 = jnp.float32
bf16 = jnp.bfloat16


def dot(left, right, dims, precision=None):
    return lax.dot_general(
        left, right, (dims, ((), ())), precision=precision, preferred_element_type=f32
    )


def sigmoid(v):
    return 1.0 / (1.0 + jnp.exp(-v))


def softplus(v):
    return jnp.maximum(v, 0.0) + jnp.log1p(jnp.exp(-jnp.abs(v)))


def iota(shape, axis):
    return lax.broadcasted_iota(jnp.int32, shape, axis)


def split(v):
    high_half = v.astype(bf16).astype(f32)
    return high_half, v - high_half


def packed(mine, first, second):
    return jnp.where(mine, first, pltpu.roll(second, HEAD_DIM, 1)).astype(bf16)


def meet(left, right, mine):
    (left_high, left_low), (right_high, right_low) = left, right
    lefts = [packed(mine, left_high, left_low), jnp.where(mine, left_high, 0.0).astype(bf16)]
    rights = [packed(mine, right_high, right_high), jnp.where(mine, right_low, 0.0).astype(bf16)]
    return dot(jnp.concatenate(lefts, axis=1), jnp.concatenate(rights, axis=1), ((1,), (1,)))


def pair_columns(table, pair):
    lane = iota((table.shape[0], LANES), 1)
    return jnp.where(lane < HEAD_DIM, table[:, 2 * pair : 2 * pair + 1], table[:, 2 * pair + 1 : 2 * pair + 2])


def decay_tables(step_rows, step_bias, rates):
    step_size = softplus(step_rows + step_bias)
    earlier = (iota((BLOCK, BLOCK), 0) >= iota((BLOCK, BLOCK), 1)).astype(f32)
    cumulative = dot(earlier, step_size * rates, ((1,), (0,)), highest)
    return step_size, cumulative, jnp.exp(cumulative), jnp.exp(cumulative[BLOCK - 1 : BLOCK, :] - cumulative)


def state_decay(from_start, pair):
    last = from_start[BLOCK - 1 : BLOCK, :]
    row = iota((LANES, STATE), 0)
    return jnp.where(row < HEAD_DIM, last[:, 2 * pair : 2 * pair + 1], last[:, 2 * pair + 1 : 2 * pair + 2])


def shifted_conv(rows_ref, before, buffer, taps, conv_bias, first):
    @pl.when(first)
    def _():
        buffer[0:8, :] = before[...]

    @pl.when(jnp.logical_not(first))
    def _():
        buffer[0:8, :] = buffer[BLOCK : BLOCK + 8, :]

    buffer[8 : BLOCK + 8, :] = rows_ref[...]
    total = conv_bias[...] + taps[0:1, :] * buffer[8 : BLOCK + 8, :]
    for tap in range(1, 4):
        total = total + taps[tap : tap + 1, :] * buffer[8 - tap : BLOCK + 8 - tap, :]
    return total


def scan_kernel(
    input_rows, state_rows, step_rows, input_before, state_before, state_entering,
    conv_input, conv_input_bias, conv_state, conv_state_bias, step_bias, rates, skip,
    mixed, input_conv, state_conv, entering, carried, input_buffer, state_buffer,
):
    first = pl.program_id(0) == 0
    pairs = input_rows.shape[1] // LANES

    @pl.when(first)
    def _():
        carried[...] = state_entering[...]

    input_conv[...] = shifted_conv(input_rows, input_before, input_buffer, conv_input, conv_input_bias, first)
    state_pre = shifted_conv(state_rows, state_before, state_buffer, conv_state, conv_state_bias, first)
    state_conv[...] = state_pre
    state_act = state_pre * sigmoid(state_pre)
    writes, reads = state_act[:, :STATE], state_act[:, STATE:]
    meeting = dot(reads, writes, ((1,), (1,)), high)
    step_size, cumulative, from_start, to_end = decay_tables(step_rows[...], step_bias[...], rates[...])
    cumulative_t = cumulative.T
    causal = iota((BLOCK, BLOCK), 0) >= iota((BLOCK, BLOCK), 1)
    lane = iota((BLOCK, LANES), 1)
    for pair in range(pairs):
        columns = slice(pair * LANES, pair * LANES + LANES)
        pre = input_conv[:, columns]
        inputs = pre * sigmoid(pre)
        weighted = inputs * pair_columns(step_size, pair)
        state_in = carried[pair]
        entering[0, pair] = state_in
        out = dot(reads, state_in, ((1,), (1,)), high) * pair_columns(from_start, pair)
        for side in range(2):
            head = 2 * pair + side
            gap = cumulative[:, head : head + 1] - cumulative_t[head : head + 1, :]
            mixing = jnp.exp(jnp.where(causal, gap, -1e30)) * meeting
            mine = (lane < HEAD_DIM) if side == 0 else (lane >= HEAD_DIM)
            out = out + dot(mixing, jnp.where(mine, weighted, 0.0), ((1,), (0,)), high)
        fresh = dot(weighted * pair_columns(to_end, pair), writes, ((0,), (0,)), high)
        carried[pair] = state_decay(from_start, pair) * state_in + fresh
        mixed[:, columns] = out + skip[:, columns] * inputs


def scan_back_kernel(
    input_rows, state_rows, step_rows, input_conv, state_conv, mixed, entering, mixed_grad,
    input_after, state_after, state_leaving, decay_after,
    conv_input, conv_state, step_bias, rates, skip, head_of,
    input_grad, state_grad, step_grad, input_sums, state_sums, step_sums, input_first, state_first, carried, later,
    input_buffer, state_buffer, gap_grad, out_products, in_products,
):
    first = pl.program_id(0) == 0
    pairs = input_rows.shape[1] // LANES

    @pl.when(first)
    def _():
        carried[...] = state_leaving[...]
        later[...] = decay_after[...]
        input_sums[...] = jnp.zeros(input_sums.shape, f32)
        state_sums[...] = jnp.zeros(state_sums.shape, f32)
        step_sums[...] = jnp.zeros(step_sums.shape, f32)
        input_buffer[BLOCK : BLOCK + 8, :] = input_after[...]
        state_buffer[BLOCK : BLOCK + 8, :] = state_after[...]

    @pl.when(jnp.logical_not(first))
    def _():
        input_buffer[BLOCK : BLOCK + 8, :] = input_buffer[0:8, :]
        state_buffer[BLOCK : BLOCK + 8, :] = state_buffer[0:8, :]

    state_pre = state_conv[...]
    state_sig = sigmoid(state_pre)
    state_act = state_pre * state_sig
    writes, reads = state_act[:, :STATE], state_act[:, STATE:]
    meeting_t = dot(writes, reads, ((1,), (1,)), high)
    step_size, cumulative, from_start, to_end = decay_tables(step_rows[...], step_bias[...], rates[...])
    cumulative_t = cumulative.T
    causal_t = iota((BLOCK, BLOCK), 0) <= iota((BLOCK, BLOCK), 1)
    lane = iota((BLOCK, LANES), 1)
    gap_grad[...] = jnp.zeros(gap_grad.shape, f32)
    writes_grad = jnp.zeros((BLOCK, STATE), f32)
    reads_grad = jnp.zeros((BLOCK, STATE), f32)
    for pair in range(pairs):
        columns = slice(pair * LANES, pair * LANES + LANES)
        pre = input_conv[:, columns]
        sig = sigmoid(pre)
        inputs = pre * sig
        step_pair = pair_columns(step_size, pair)
        weighted = inputs * step_pair
        out_grad = mixed_grad[:, columns]
        skip_product = out_grad * inputs
        input_sums[5:6, columns] += jnp.sum(skip_product, axis=0, keepdims=True)
        end_pair = pair_columns(to_end, pair)
        leaving_grad = carried[pair]
        weighted_grad = dot(writes, leaving_grad, ((1,), (1,)), high) * end_pair
        grad_halves, weighted_halves = split(out_grad), split(weighted)
        for side in range(2):
            head = 2 * pair + side
            gap = cumulative_t[head : head + 1, :] - cumulative[:, head : head + 1]
            within = jnp.exp(jnp.where(causal_t, gap, -1e30))
            mine = (lane < HEAD_DIM) if side == 0 else (lane >= HEAD_DIM)
            own_grad = jnp.where(mine, out_grad, 0.0)
            weighted_grad = weighted_grad + dot(within * meeting_t, own_grad, ((1,), (0,)), high)
            gap_grad[...] += within * meet(weighted_halves, grad_halves, mine)
        start_grad = out_grad * pair_columns(from_start, pair)
        reads_grad = reads_grad + dot(start_grad, entering[0, pair], ((1,), (0,)), high)
        writes_grad = writes_grad + dot(weighted * end_pair, leaving_grad, ((1,), (0,)), high)
        carried[pair] = state_decay(from_start, pair) * leaving_grad + dot(start_grad, reads, ((0,), (0,)), high)
        out_products[:, columns] = out_grad * mixed[:, columns] - skip[:, columns] * skip_product
        in_products[:, columns] = inputs * weighted_grad
        inputs_grad = skip[:, columns] * out_grad + step_pair * weighted_grad
        input_buffer[0:BLOCK, columns] = inputs_grad * (sig * (1.0 + pre * (1.0 - sig)))
    reads_grad = reads_grad + dot(gap_grad[...], writes, ((0,), (0,)), high)
    writes_grad = writes_grad + dot(gap_grad[...], reads, ((1,), (0,)), high)
    state_slope = state_sig * (1.0 + state_pre * (1.0 - state_sig))
    state_buffer[0:BLOCK, 0:STATE] = writes_grad * state_slope[:, :STATE]
    state_buffer[0:BLOCK, STATE : 2 * STATE] = reads_grad * state_slope[:, STATE:]

    for buffer, rows, taps, sums, result in (
        (input_buffer, input_rows, conv_input, input_sums, input_grad),
        (state_buffer, state_rows, conv_state, state_sums, state_grad),
    ):
        raw = rows[...]
        total = jnp.zeros(raw.shape, f32)
        for tap in range(4):
            ahead = buffer[tap : tap + BLOCK, :]
            total = total + taps[tap : tap + 1, :] * ahead
            sums[tap : tap + 1, :] += jnp.sum(ahead * raw, axis=0, keepdims=True)
        sums[4:5, :] += jnp.sum(buffer[0:BLOCK, :], axis=0, keepdims=True)
        result[...] = total.astype(result.dtype)
    input_first[...] = input_buffer[0:8, :]
    state_first[...] = state_buffer[0:8, :]

    out_head = dot(out_products[...], head_of[...], ((1,), (0,)), high)
    in_head = dot(in_products[...], head_of[...], ((1,), (0,)), high)
    upper = (iota((BLOCK, BLOCK), 0) <= iota((BLOCK, BLOCK), 1)).astype(f32)
    decay_grad = dot(upper, out_head - step_size * in_head, ((1,), (0,)), highest) + later[0:1, :]
    later[0:1, :] = decay_grad[0:1, :]
    step_sig = sigmoid(step_rows[...] + step_bias[...])
    step_back = (rates[...] * decay_grad + in_head) * step_sig
    step_grad[...] = step_back.astype(step_grad.dtype)
    step_sums[0:1, :] += jnp.sum(step_back, axis=0, keepdims=True)
    step_sums[1:2, :] += jnp.sum(step_size * decay_grad, axis=0, keepdims=True)


def whole(array):
    zeros = (0,) * array.ndim
    return pl.BlockSpec(array.shape, lambda k: zeros)


def params(mebibytes):
    return pltpu.CompilerParams(dimension_semantics=("arbitrary",), vmem_limit_bytes=mebibytes * 1024 * 1024)


little = pl.CostEstimate(flops=10**6, bytes_accessed=2**16, transcendentals=0)


def run_scan(start, span, input_rows, state_rows, step_rows, zeros, state_entering, consts):
    channels = input_rows.shape[1]
    pairs = channels // LANES
    rows = span * BLOCK
    edge = start * BLOCK // 8 - 1

    def tokens(width):
        return pl.BlockSpec((BLOCK, width), lambda k: (start + k, 0))

    def results(width):
        return pl.BlockSpec((BLOCK, width), lambda k: (k, 0))

    if start == 0:
        before = zeros
        before_specs = [whole(c) for c in before]
    else:
        before = (input_rows, state_rows)
        before_specs = [pl.BlockSpec((8, c.shape[1]), lambda k: (edge, 0)) for c in before]
    return pl.pallas_call(
        scan_kernel,
        grid=(span,),
        in_specs=[tokens(channels), tokens(2 * STATE), tokens(LANES)] + before_specs + [whole(state_entering)]
        + [whole(c) for c in consts],
        out_specs=[
            results(channels), results(channels), results(2 * STATE),
            pl.BlockSpec((1, pairs, LANES, STATE), lambda k: (k, 0, 0, 0)), whole(state_entering),
        ],
        out_shape=[
            jax.ShapeDtypeStruct((rows, channels), f32),
            jax.ShapeDtypeStruct((rows, channels), f32),
            jax.ShapeDtypeStruct((rows, 2 * STATE), f32),
            jax.ShapeDtypeStruct((span, pairs, LANES, STATE), f32),
            jax.ShapeDtypeStruct((pairs, LANES, STATE), f32),
        ],
        scratch_shapes=[pltpu.VMEM((BLOCK + 8, channels), f32), pltpu.VMEM((BLOCK + 8, 2 * STATE), f32)],
        compiler_params=params(LIM_SCAN),
        cost_estimate=little,
        name="scan",
    )(input_rows, state_rows, step_rows, *before, state_entering, *consts)


def run_scan_back(start, span, projections, kept, at, mixed_grad, carry, consts):
    channels = mixed_grad.shape[1]
    pairs = channels // LANES
    rows = span * BLOCK

    def tokens(width):
        return pl.BlockSpec((BLOCK, width), lambda k: (start + span - 1 - k, 0))

    def own(width, first=0):
        return pl.BlockSpec((BLOCK, width), lambda k: (first + span - 1 - k, 0))

    def shape(*dims):
        return jax.ShapeDtypeStruct(dims, f32)

    sums = [shape(8, channels), shape(8, 2 * STATE), shape(8, LANES)]
    ends = [jax.ShapeDtypeStruct(c.shape, f32) for c in carry]
    return pl.pallas_call(
        scan_back_kernel,
        grid=(span,),
        in_specs=[
            tokens(channels), tokens(2 * STATE), tokens(LANES), own(channels, at),
            own(2 * STATE, at), own(channels, at),
            pl.BlockSpec((1, pairs, LANES, STATE), lambda k: (at + span - 1 - k, 0, 0, 0)), tokens(channels),
        ] + [whole(c) for c in carry] + [whole(c) for c in consts],
        out_specs=[own(channels), own(2 * STATE), own(LANES)] + [whole(c) for c in sums + ends],
        out_shape=[
            jax.ShapeDtypeStruct((rows, channels), bf16), shape(rows, 2 * STATE),
            jax.ShapeDtypeStruct((rows, LANES), bf16),
        ] + sums + ends,
        scratch_shapes=[
            pltpu.VMEM((BLOCK + 8, channels), f32), pltpu.VMEM((BLOCK + 8, 2 * STATE), f32),
            pltpu.VMEM((BLOCK, BLOCK), f32), pltpu.VMEM((BLOCK, channels), f32), pltpu.VMEM((BLOCK, channels), f32),
        ],
        compiler_params=params(LIM_SCAN_BACK),
        cost_estimate=little,
        name="scan_back",
    )(*projections, *kept, mixed_grad, *carry, *consts)


def fixed_block(*shape):
    zeros = (0,) * len(shape)
    return pl.BlockSpec(shape, lambda n, *_: zeros)


def call(kernel, places, steps, operands, in_specs, out_specs, out_shape, name, scratch=(), aliases={}):
    return pl.pallas_call(
        kernel,
        grid_spec=pltpu.PrefetchScalarGridSpec(
            num_scalar_prefetch=1, grid=(steps,), in_specs=in_specs, out_specs=out_specs, scratch_shapes=list(scratch)
        ),
        out_shape=out_shape,
        input_output_aliases=aliases,
        compiler_params=params(61),
        cost_estimate=little,
        name=name,
    )(places, *operands)


def lay(places, pieces, result, first=0):
    for i, piece in enumerate(pieces):
        result[pl.ds(pl.multiple_of(places[first + i], 16), piece.shape[0]), :] = piece[...]


TILE = 256


def tile_columns(ref, n, first=0):
    return ref[:, pl.ds(pl.multiple_of(n * TILE + first, LANES), TILE)]


def first_project(weights, tokens, places, channels):
    count = len(weights)
    depth, width = tokens[0].shape[1], weights[0].shape[1]
    rows = tokens[0].shape[0] * len(tokens)

    def kernel(places, *refs):
        pieces, (normed, full, input_proj, tail_proj) = refs[:-4], refs[-4:]
        n = pl.program_id(0)

        @pl.when(n == 0)
        def _():
            lay(places, pieces[:count], full)
            lay(places, pieces[count:], normed, count)
            tail_proj[...] = dot(normed[...], full[:, channels:], ((1,), (0,)))

        input_proj[...] = dot(normed[...], tile_columns(full, n), ((1,), (0,)))

    return call(
        kernel, places, channels // TILE, (*weights, *tokens),
        [fixed_block(*piece.shape) for piece in (*weights, *tokens)],
        [
            fixed_block(rows, depth), fixed_block(depth, width), pl.BlockSpec((rows, TILE), lambda n, _: (0, n)),
            fixed_block(rows, width - channels),
        ],
        [
            jax.ShapeDtypeStruct((rows, depth), bf16), jax.ShapeDtypeStruct((depth, width), bf16),
            jax.ShapeDtypeStruct((rows, channels), f32), jax.ShapeDtypeStruct((rows, width - channels), f32),
        ],
        "first_project",
    )


def second_project(weights, places, normed, cot, mixed, gain):
    count, halves = len(weights), len(mixed)
    width = weights[0].shape[1]
    rows, depth = normed.shape
    channels = width // 2
    part_rows = mixed[0].shape[0]

    def kernel(places, *refs):
        pieces, (normed_ref, cot_ref, gain_ref), mixed_refs = refs[:count], refs[count : count + 3], refs[count + 3 : -4]
        full, gate_proj, out_grad, sums = refs[-4:]
        n = pl.program_id(0)

        @pl.when(n == 0)
        def _():
            lay(places, pieces, full)
            sums[...] = jnp.zeros(sums.shape, f32)

        gate_proj[...] = dot(normed_ref[...], tile_columns(full, n), ((1,), (0,)))
        out_grad[...] = dot(cot_ref[...], tile_columns(full, n, channels), ((1,), (0,)))
        ones = jnp.ones((8, TILE), f32)
        for i in range(halves):
            at = slice(i * part_rows, (i + 1) * part_rows)
            proj = gate_proj[at, :]
            gated = mixed_refs[i][...] * (proj * sigmoid(proj))
            pulled = out_grad[at, :] * gain_ref[...] * gated
            sums[0:8, at] += dot(ones, gated * gated, ((1,), (1,)), highest)
            sums[8:16, at] += dot(ones, pulled, ((1,), (1,)), highest)

    tile = pl.BlockSpec((rows, TILE), lambda n, _: (0, n))
    return call(
        kernel, places, channels // TILE, (*weights, normed, cot, gain, *mixed),
        [fixed_block(*piece.shape) for piece in (*weights, normed, cot)]
        + [pl.BlockSpec((1, TILE), lambda n, _: (0, n))]
        + [pl.BlockSpec((part_rows, TILE), lambda n, _: (0, n)) for _ in mixed],
        [fixed_block(depth, width), tile, tile, fixed_block(16, rows)],
        [
            jax.ShapeDtypeStruct((depth, width), bf16), jax.ShapeDtypeStruct((rows, channels), f32),
            jax.ShapeDtypeStruct((rows, channels), f32), jax.ShapeDtypeStruct((16, rows), f32),
        ],
        "second_project",
    )


def store_shares(places, product, result, tops, part, columns):
    owners, rows = result.shape[0], result.shape[2] - 16
    for owner in range(owners):
        own = product[owner * rows : (owner + 1) * rows]
        result[places[owner], part, 0:rows, columns] = own
        top = jnp.max(jnp.abs(own), axis=0, keepdims=True)
        result[places[owner], part, rows : rows + 16, columns] = jnp.zeros((16, own.shape[1]), f32)
        tops[places[owner], part, :, columns] = jnp.broadcast_to(top, (8, own.shape[1]))


def gate_step(ring, places, sums, gain, mixed, gate_proj, out_grad, cot_t, normed_t, second_full, inner_total):
    depth = second_full.shape[0]
    rows, channels = gate_proj.shape
    halves, part_rows = len(mixed), mixed[0].shape[0]
    share = cot_t.shape[0] // ring.count

    def kernel(places, *refs):
        sums_ref, gain_ref, proj_ref, grad_ref, cot_ref, normed_ref, weight_ref = refs[:7]
        mixed_refs, (branch, gate_grad, mixed_grad, gain_sum, result, tops, gate_out) = refs[7 : 7 + halves], refs[7 + halves :]
        gain_sum[...] = jnp.zeros(gain_sum.shape, f32)
        scale_row = lax.rsqrt(sums_ref[0:8, :] / inner_total + epsilon)
        pull_row = scale_row * scale_row * scale_row * (sums_ref[8:16, :] / inner_total)
        scales, pulls = scale_row.T, pull_row.T
        for i in range(halves):
            at = slice(i * part_rows, (i + 1) * part_rows)
            proj, rows_mixed, grad = proj_ref[at, :], mixed_refs[i][...], grad_ref[at, :]
            sig = sigmoid(proj)
            act = proj * sig
            gated = rows_mixed * act
            scale = scales[at, 0:1]
            scaled = gated * scale
            gate_out[at, :] = (scaled * gain_ref[...]).astype(bf16)
            gain_sum[0:1, :] += jnp.sum(grad * scaled, axis=0, keepdims=True)
            gated_grad = scale * (grad * gain_ref[...]) - gated * pulls[at, 0:1]
            mixed_grad[at, :] = gated_grad * act
            gate_grad[at, :] = (gated_grad * rows_mixed * (sig * (1.0 + proj * (1.0 - sig)))).astype(bf16)
        everything = slice(0, TILE)
        first = pl.program_id(0) == 0
        for i in range(0, rows, TILE):
            at = slice(i, i + TILE)
            share_out = dot(gate_out[at, :], weight_ref[...], ((1,), (1,)))
            branch[at, :] = share_out + jnp.where(first, 0.0, branch[at, :])
        store_shares(places, dot(cot_ref[...], gate_out[...], ((1,), (0,))), result, tops, 0, everything)
        store_shares(places, dot(normed_ref[...], gate_grad[...], ((1,), (0,))), result, tops, 1, everything)

    tile = pl.BlockSpec((rows, TILE), lambda n, _: (0, n))
    return call(
        kernel, places, channels // TILE, (sums, gain, gate_proj, out_grad, cot_t, normed_t, second_full, *mixed),
        [
            fixed_block(16, rows), pl.BlockSpec((1, TILE), lambda n, _: (0, n)), tile, tile,
            fixed_block(*cot_t.shape), fixed_block(*normed_t.shape),
            pl.BlockSpec((depth, TILE), lambda n, _: (0, channels // TILE + n)),
        ] + [pl.BlockSpec((part_rows, TILE), lambda n, _: (0, n)) for _ in mixed],
        [
            fixed_block(rows, depth), tile, tile, pl.BlockSpec((8, TILE), lambda n, _: (0, n)),
            pl.BlockSpec((ring.count, 2, share + 16, TILE), lambda n, _: (0, 0, 0, n)),
            pl.BlockSpec((ring.count, 2, 8, TILE), lambda n, _: (0, 0, 0, n)),
        ],
        [
            jax.ShapeDtypeStruct((rows, depth), f32), jax.ShapeDtypeStruct((rows, channels), bf16),
            jax.ShapeDtypeStruct((rows, channels), f32), jax.ShapeDtypeStruct((8, channels), f32),
            jax.ShapeDtypeStruct((ring.count, 2, share + 16, channels), f32),
            jax.ShapeDtypeStruct((ring.count, 2, 8, channels), f32),
        ],
        "gate_step", [pltpu.VMEM((rows, TILE), bf16)],
    )


def input_partials(ring, places, normed_t, input_back):
    halves, (part_rows, channels) = len(input_back), input_back[0].shape
    share = normed_t.shape[0] // ring.count

    def kernel(places, left, *refs):
        rights, result, tops = refs[:-2], refs[-2], refs[-1]
        product = dot(left[:, 0:part_rows], rights[0][...], ((1,), (0,)))
        for i in range(1, halves):
            product = product + dot(left[:, i * part_rows : (i + 1) * part_rows], rights[i][...], ((1,), (0,)))
        store_shares(places, product, result, tops, 0, slice(0, TILE))

    def block(rows):
        return pl.BlockSpec((ring.count, 1, rows, TILE), lambda n, _: (0, 0, 0, n))

    return call(
        kernel, places, channels // TILE, (normed_t, *input_back),
        [fixed_block(*normed_t.shape)] + [pl.BlockSpec((part_rows, TILE), lambda n, _: (0, n)) for _ in input_back],
        [block(share + 16), block(8)],
        [jax.ShapeDtypeStruct((ring.count, 1, rows, channels + LANES), f32) for rows in (share + 16, 8)],
        "input_partials",
    )


def tail_partials(places, normed_t, tail, parts, tops):
    def kernel(places, left, right, parts_in, tops_in, result, tops_out):
        product = dot(left[...], right[...], ((1,), (0,)))
        store_shares(places, product, result, tops_out, 0, slice(0, LANES))

    last = parts.shape[3] // LANES - 1
    specs = [pl.BlockSpec((*array.shape[:3], LANES), lambda n, _: (0, 0, 0, last)) for array in (parts, tops)]
    anywhere = pl.BlockSpec(memory_space=pl.ANY)
    return call(
        kernel, places, 1, (normed_t, tail, parts, tops),
        [fixed_block(*normed_t.shape), fixed_block(*tail.shape), anywhere, anywhere], specs,
        [jax.ShapeDtypeStruct(array.shape, f32) for array in (parts, tops)], "tail_partials", aliases={3: 0, 4: 1},
    )


def normed_kernel(halves, places, gate_rows, tail_rows, gate_tile, input_tile, tail_tile, *refs):
    inputs, results, product = refs[:halves], refs[halves:-1], refs[-1]
    part = inputs[0].shape[0]
    for i, input_rows in enumerate(inputs):
        at = slice(i * part, (i + 1) * part)
        total = dot(gate_rows[at, :], gate_tile[...], ((1,), (1,)))
        total = total + dot(tail_rows[at, :], tail_tile[...], ((1,), (1,)))
        product[at, :] = total + dot(input_rows[...], input_tile[...], ((1,), (1,)))
    rows = results[0].shape[0]
    for i, result in enumerate(results):
        result[...] = product[pl.ds(pl.multiple_of(places[i] * rows, 16), rows), :]


def normed_parts(places, gate_grad, input_back, tail, second_full, first_full):
    count = lax.axis_size("tensor")
    tokens, channels = gate_grad.shape
    width, tile = first_full.shape[0], 2 * LANES
    halves = len(input_back)

    def fixed(n, _):
        return (0, 0)

    return pl.pallas_call(
        lambda *refs: normed_kernel(halves, *refs),
        grid_spec=pltpu.PrefetchScalarGridSpec(
            num_scalar_prefetch=1, grid=(width // tile,),
            in_specs=[
                pl.BlockSpec((tokens, channels), fixed), pl.BlockSpec((tokens, LANES), fixed),
                pl.BlockSpec((tile, channels), lambda n, _: (n, 0)), pl.BlockSpec((tile, channels), lambda n, _: (n, 0)),
                pl.BlockSpec((tile, LANES), lambda n, _: (n, channels // LANES)),
            ] + [pl.BlockSpec(half.shape, fixed) for half in input_back],
            out_specs=[pl.BlockSpec((tokens // count, tile), lambda n, _: (0, n))] * count,
            scratch_shapes=[pltpu.VMEM((tokens, tile), f32)],
        ),
        out_shape=[jax.ShapeDtypeStruct((tokens // count, width), f32)] * count,
        compiler_params=params(LIM_NORMED_PARTS),
        cost_estimate=little,
        name="normed_parts",
    )(places, gate_grad, tail, second_full, first_full, first_full, *input_back)


def cycle(count):
    return list(range(0, count, 2)) + list(range(count - 1, 0, -2))


def table(numbers):
    return jnp.stack(numbers).astype(jnp.int32)


class Ring:
    def __init__(self):
        self.count = lax.axis_size("dp")
        order = cycle(self.count)
        self.up = [(order[i], order[(i + 1) % self.count]) for i in range(self.count)]
        self.down = [(b, a) for a, b in self.up]
        me = lax.axis_index("dp")
        self.place = jnp.where(me % 2 == 0, me // 2, self.count - 1 - me // 2)

    def places(self):
        order = cycle(self.count)
        return table([(order.index(i) - self.place + self.count) % self.count for i in range(self.count)])

    def owner(self, offset):
        place = (self.place + offset + self.count) % self.count
        return jnp.where(place < self.count // 2, 2 * place, 2 * (self.count - 1 - place) + 1)


def middle(rows):
    return (rows // 2 + 15) // 16 * 16


class Gather:
    def __init__(self, ring, shard):
        self.ring, self.shard, self.step = ring, shard, 0
        self.held = [(shard, 0, 0)]
        self.last = (shard, shard)

    def hop(self):
        self.step += 1
        half, cut = self.ring.count // 2, middle(self.shard.shape[0])
        up, down = self.last
        offsets = ((-self.step, 0), (self.step, 0))
        if self.step == half:
            up, down = up[:cut], down[cut:]
            offsets = ((half, 0), (half, cut))
        self.last = (lax.ppermute(up, "dp", self.ring.up), lax.ppermute(down, "dp", self.ring.down))
        self.held += [(piece, *offset) for piece, offset in zip(self.last, offsets)]

    def after(self, *marks):
        self.last, marks = fence(self.last, marks)
        self.held[-2:] = [(piece, *old[1:]) for piece, old in zip(self.last, self.held[-2:])]
        return marks if len(marks) > 1 else marks[0]

    def pieces(self):
        return [piece for piece, _, _ in self.held]

    def places(self):
        rows, half = self.shard.shape[0], self.ring.count // 2
        spots = [self.ring.owner(0) * rows]
        for step in range(1, half):
            spots += [self.ring.owner(-step) * rows, self.ring.owner(step) * rows]
        return spots + [self.ring.owner(half) * rows, self.ring.owner(half) * rows + middle(rows)]


def encode(rows, limit):
    power = jnp.ceil(jnp.log2(jnp.maximum(limit, 1e-30)))
    ours = lax.broadcasted_iota(jnp.int32, rows.shape, 1) < rows.shape[1] - 16
    return jnp.where(ours, rows * jnp.exp2(15.0 - power), power).astype(jnp.float16)


def decode(payload):
    power = payload[:, -16:-15].astype(f32)
    return payload.astype(f32) * jnp.exp2(power - 15.0), jnp.exp2(power)


class Scatter:
    def __init__(self, ring, parts, tops):
        self.ring, self.parts, self.tops = ring, parts, tops
        self.step = ring.count // 2
        self.rows = parts.shape[2] - 16
        self.cut = middle(self.rows)
        far = parts[self.step]
        top = tops[self.step, :, 0:1]
        upper = jnp.concatenate([far[:, : self.cut], far[:, -16:]], axis=1)
        self.send = (encode(upper, top), encode(far[:, self.cut :], top))

    def hop(self):
        self.send = fence(*self.send)
        self.got = (lax.ppermute(self.send[0], "dp", self.ring.up), lax.ppermute(self.send[1], "dp", self.ring.down))

    def after(self, *marks):
        self.got, marks = fence(self.got, marks)
        return marks if len(marks) > 1 else marks[0]

    def before(self, *marks):
        self.send, marks = fence(self.send, marks)
        return marks if len(marks) > 1 else marks[0]

    def add(self):
        first = self.step == self.ring.count // 2
        self.got = fence(*self.got)
        (up, up_top), (down, down_top) = (decode(g) for g in self.got)
        if first:
            up = jnp.pad(up, ((0, 0), (0, self.rows - self.cut), (0, 0)))
            down = jnp.pad(down, ((0, 0), (self.cut, 0), (0, 0)))
            up = jnp.where(lax.broadcasted_iota(jnp.int32, up.shape, 1) < self.cut, up, 0.0)
        self.step -= 1
        if self.step == 0:
            return (self.parts[0] + up + down)[:, : self.rows]
        above, below = self.parts[self.step], self.parts[self.ring.count - self.step]
        self.send = (
            encode(above + up, self.tops[self.step, :, 0:1] + up_top),
            encode(below + down, self.tops[self.ring.count - self.step, :, 0:1] + down_top),
        )
        return None


def fence(*arrays):
    flat, tree = jax.tree.flatten(arrays)
    return jax.tree.unflatten(tree, lax.optimization_barrier(flat))


def across(array, bit, axis="tensor"):
    count = lax.axis_size(axis)
    return lax.ppermute(array, axis, [(i, i ^ bit) for i in range(count)])


def group_sum(array, axis, first, count):
    terms = [array] + [across(array, first * other, axis) for other in range(1, count)]
    while len(terms) > 1:
        terms = [terms[i] + terms[i + 1] for i in range(0, len(terms), 2)]
    return terms[0]


def cube_sum(array, axis):
    bit = 1
    while bit < lax.axis_size(axis):
        array = array + across(array, bit, axis)
        bit *= 2
    return array


def shards(
    block_input, cotangent, norm_gain, gate_weight, input_weight, state_weight, step_weight, conv_input,
    conv_input_bias, conv_state, conv_state_bias, step_bias, decay_log, skip_scale, gate_gain, out_weight,
):
    group_count = lax.axis_size("tensor")
    me = lax.axis_index("tensor")
    ring = Ring()
    half = ring.count // 2
    local_rows = block_input.shape[0]
    channels = gate_gain.shape[0]
    heads = step_bias.shape[0]
    inner_total = channels * group_count
    share = 2 * STATE // group_count
    tokens = local_rows * group_count
    blocks = tokens // BLOCK
    fold = LANES // share
    folded = tokens // fold
    rows_dot = ((1,), (0,))
    back_dot = ((1,), (1,))

    state_mine = lax.dynamic_slice_in_dim(state_weight, me * share, share, 1)
    first = Gather(
        ring,
        jnp.concatenate(
            [input_weight, state_mine, jnp.pad(step_weight, ((0, 0), (0, LANES - share - heads)))], axis=1
        ).astype(bf16),
    )
    first.hop()
    row_scale = lax.rsqrt(jnp.mean(block_input * block_input, axis=1, keepdims=True) + epsilon)
    normed = (block_input * row_scale * norm_gain).astype(bf16)
    second_weight = jnp.concatenate([gate_weight, out_weight.T], axis=1).astype(bf16)
    rates = -jnp.exp(decay_log)

    def per_head(vector):
        return jnp.pad(vector, (0, LANES - heads))[None, :]

    skip = jnp.repeat(skip_scale, HEAD_DIM)[None, :]
    head_of = (
        lax.broadcasted_iota(jnp.int32, (channels, LANES), 0) // HEAD_DIM
        == lax.broadcasted_iota(jnp.int32, (channels, LANES), 1)
    ).astype(f32)
    scan_consts = (
        conv_input, conv_input_bias[None, :], conv_state, conv_state_bias[None, :], per_head(step_bias),
        per_head(rates), skip,
    )
    back_consts = (conv_input, conv_state, per_head(step_bias), per_head(rates), skip, head_of)
    carried = jnp.zeros((channels // LANES, LANES, STATE), f32)
    carry = (jnp.zeros((8, channels), f32), jnp.zeros((8, 2 * STATE), f32), carried, jnp.zeros((8, LANES), f32))
    gain = gate_gain[None, :]
    shard_places = first.places()
    token_places = [(me ^ bits) * local_rows for bits in range(4)]
    tables = (table(shard_places + token_places), table(shard_places), ring.places(), table([i ^ me for i in range(4)]))
    normed, scan_consts, back_consts, carried, carry, gain, tables = first.after(
        normed, scan_consts, back_consts, carried, carry, gain, tables
    )
    first_places, second_places, share_places, turn_places = tables
    first.hop()
    far, near = across(normed, 2), across(normed, 1)
    for _ in range(half - 3):
        first.hop()
    far, near, second_weight, cot_low = first.after(far, near, second_weight, cotangent.astype(bf16))
    first.hop()
    second_weight = first.after(second_weight)
    normed_pieces = (normed, near, far, across(far, 1))
    second = Gather(ring, second_weight)
    second.hop()
    cot_all = lax.all_gather(cot_low, "tensor", axis=0, tiled=True)
    normed_all, first_full, input_proj, tail_proj = first_project(
        first.pieces(), normed_pieces, first_places, channels
    )
    normed_all, first_full, input_proj, tail_proj = second.after(normed_all, first_full, input_proj, tail_proj)
    second.hop()
    step_proj = jnp.pad(tail_proj[:, share : share + heads], ((0, 0), (0, LANES - heads)))
    state_mine = jnp.concatenate([tail_proj[i * folded : (i + 1) * folded, :share] for i in range(fold)], axis=1)
    far = across(state_mine, 2)
    same_x, same_core, diagonal = across(state_mine, 1), far, across(far, 1)
    right_core = me % 2 == 1
    near = (jnp.where(right_core, same_x, state_mine), jnp.where(right_core, state_mine, same_x))
    away = (jnp.where(right_core, diagonal, same_core), jnp.where(right_core, same_core, diagonal))
    right_chip = me // 2 == 1
    state_parts = [jnp.where(right_chip, away[i], near[i]) for i in range(2)]
    state_parts += [jnp.where(right_chip, near[i], away[i]) for i in range(2)]
    state_proj = jnp.concatenate(
        [jnp.concatenate([p[:, i * share : (i + 1) * share] for p in state_parts], axis=1) for i in range(fold)], axis=0
    )
    span = 2
    scanned, mixed = [], []
    for start in range(0, blocks, span):
        scanned.append(run_scan(start, span, input_proj, state_proj, step_proj, carry[:2], carried, scan_consts))
        carried = scanned[-1][4]
        mixed.append(scanned[-1][0])
        if second.step < half:
            carried, mixed[-1] = second.after(carried, mixed[-1])
            second.hop()
    while second.step < half:
        second.hop()
    second_full, gate_proj, gate_out_grad, sums = second_project(
        second.pieces(), second_places, normed_all, cot_all, mixed, gain
    )
    sums = (sums + across(sums, 1)) + (across(sums, 2) + across(sums, 3))
    normed_t = normed_all.T
    branch_part, gate_grad, mixed_grad, gain_sum, *pair_parts = gate_step(
        ring, share_places, sums, gain, mixed, gate_proj, gate_out_grad, cot_all.T, normed_t, second_full,
        float(inner_total),
    )
    pair_ring = Scatter(ring, *pair_parts)
    done = []
    for turn in range(blocks // span):
        if turn == 0:
            carry, branch_part = pair_ring.before(carry, branch_part)
            pair_ring.hop()
            branch = lax.psum_scatter(branch_part, "tensor", scatter_dimension=0, tiled=True)
        else:
            carry = pair_ring.after(carry)
            pair_ring.add()
            carry = pair_ring.before(carry)
            pair_ring.hop()
        start = blocks - span * (turn + 1)
        kept = scanned[start // span]
        kept = [kept[1], kept[2], kept[0], kept[3]]
        result = run_scan_back(
            start, span, (input_proj, state_proj, step_proj), kept, 0, mixed_grad, carry, back_consts
        )
        done.insert(0, result)
        carry = tuple(result[6:])
    done = pair_ring.after(done)
    pair_ring.add()
    done = pair_ring.before(done)
    pair_ring.hop()
    input_back, state_back = [d[0] for d in done], [d[1] for d in done]
    step_back = jnp.concatenate([d[2] for d in done], axis=0)
    input_sums, state_sums, step_sums = (sum(d[i] for d in done) for i in range(3, 6))

    packed = jnp.concatenate(
        [
            state_sums[:5].reshape(-1),
            input_sums[:5].reshape(-1),
            gain_sum[0],
            jnp.sum(input_sums[5].reshape(heads, HEAD_DIM), axis=1),
            step_sums[0, :heads],
            step_sums[1, :heads] * rates,
        ]
    )
    packed = jnp.pad(packed, (0, -packed.shape[0] % LANES)).reshape(-1, LANES)

    def state_columns(index):
        return jnp.concatenate([lax.dynamic_slice_in_dim(rows, index * share, share, 1) for rows in state_back], axis=1)

    for_far, for_me = across(state_columns(me ^ 3), 1), across(state_columns(me ^ 1), 1)
    packed, for_far, for_me = fence(packed, for_far, for_me)
    far, input_back = fence(state_columns(me ^ 2) + for_far, input_back)
    from_far = across(far, 2)
    input_parts, from_far, pair_ring.got = fence(
        input_partials(ring, share_places, normed_t, input_back), from_far, pair_ring.got
    )
    pair_ring.add()
    from_far = pair_ring.before(from_far)
    pair_ring.hop()
    state_share = (state_columns(me) + for_me + from_far).astype(bf16)
    state_share = jnp.concatenate([state_share[:, i * share : (i + 1) * share] for i in range(fold)], axis=0)
    tail = jnp.concatenate(
        [state_share, step_back[:, :heads], jnp.zeros((tokens, LANES - share - heads), bf16)], axis=1
    )
    parts = normed_parts(turn_places, gate_grad, input_back, tail, second_full, first_full)
    branch, *parts = pair_ring.after(branch, *parts)
    block_output = block_input + branch
    for_far, for_me = across(parts[3], 1), across(parts[1], 1)
    input_parts = tail_partials(share_places, normed_t, tail, *input_parts)
    input_ring = Scatter(ring, *input_parts)
    for_far, for_me = input_ring.before(for_far, for_me)
    input_ring.hop()
    sent = parts[2] + for_far
    sent = jnp.pad(sent, ((0, 16), (0, 0)))[None]
    from_far = across(encode(sent, jnp.max(jnp.abs(sent), axis=1, keepdims=True)), 2)
    input_sum = input_ring.add()
    pair_sum = pair_ring.add()
    while pair_sum is None:
        pair_ring.hop()
        pair_sum = pair_ring.add()
    while input_sum is None:
        input_ring.hop()
        if input_ring.step == 1:
            from_far = input_ring.after(from_far)
        input_sum = input_ring.add()
    normed_grad = parts[0] + for_me + decode(from_far)[0][0, :local_rows]
    input_sum = input_sum[0]
    tail_sum = input_sum[:, channels:]

    weighted_grad = normed_grad * norm_gain
    norm_gain_part = jnp.sum(normed_grad * block_input * row_scale, axis=0)
    input_grad = (
        cotangent
        + row_scale * weighted_grad
        - block_input * row_scale**3 * jnp.mean(weighted_grad * block_input, axis=1, keepdims=True)
    )
    mine = tail_sum[:, :share]
    other = across(mine, 1)
    pair = jnp.concatenate([jnp.where(right_core, other, mine), jnp.where(right_core, mine, other)], axis=1)
    state_rows = 10 * STATE // LANES
    shared = jnp.concatenate([norm_gain_part.reshape(-1, LANES), packed[:state_rows]], axis=0)
    shared = group_sum(shared, "tensor", 1, group_count)
    shared, pair = fence(shared, pair)
    other = across(pair, 2)
    packed = jnp.concatenate([shared, packed[state_rows:]], axis=0)
    packed, other = fence(group_sum(packed, "dp", 2, half), other)
    packed = group_sum(packed, "dp", 1, 2)
    state_grad = jnp.concatenate([jnp.where(right_chip, other, pair), jnp.where(right_chip, pair, other)], axis=1)
    local = packed[shared.shape[0] :].reshape(-1)
    norm_gain_grad = packed[: shared.shape[0] - state_rows].reshape(-1)
    state_sum = packed[shared.shape[0] - state_rows : shared.shape[0]].reshape(5, 2 * STATE)
    at = 6 * channels
    return (
        block_output,
        input_grad,
        norm_gain_grad,
        pair_sum[1],
        input_sum[:, :channels],
        state_grad,
        tail_sum[:, share : share + heads],
        local[: 4 * channels].reshape(4, channels),
        local[4 * channels : 5 * channels],
        state_sum[:4],
        state_sum[4],
        local[at + heads : at + 2 * heads],
        local[at + 2 * heads : at + 3 * heads],
        local[at : at + heads],
        local[5 * channels : at],
        pair_sum[0].T,
    )


def solution(mesh):
    rows = P(("dp", "tensor"), None)
    both = P("dp", "tensor")
    inner = P("tensor")
    return jax.shard_map(
        shards,
        mesh=mesh,
        in_specs=(
            rows, rows, P(), both, both, P("dp", None), both, P(None, "tensor"), inner, P(), P(), inner, inner,
            inner, inner, P("tensor", "dp"),
        ),
        out_specs=(
            rows, rows, P(), both, both, P("dp", None), both, P(None, "tensor"), inner, P(), P(), inner, inner,
            inner, inner, P("tensor", "dp"),
        ),
        check_vma=False,
    )
```

```python
import jax
import jax.numpy as jnp
from jax import lax
from jax.experimental import pallas as pl
from jax.experimental.pallas import tpu as pltpu
from jax.sharding import PartitionSpec as P

HEAD_DIM = 64
STATE = 128
BLOCK = 256
SEQ = 1024
LANES = 128

LIM_SCAN = 61
LIM_SCAN_BACK = 61
LIM_NORMED_PARTS = 61

epsilon = 1e-05
high = lax.Precision.HIGH
highest = lax.Precision.HIGHEST
f32 = jnp.float32
bf16 = jnp.bfloat16


def dot(left, right, dims, precision=None):
    return lax.dot_general(
        left, right, (dims, ((), ())), precision=precision, preferred_element_type=f32
    )


def sigmoid(v):
    return 1.0 / (1.0 + jnp.exp(-v))


def softplus(v):
    return jnp.maximum(v, 0.0) + jnp.log1p(jnp.exp(-jnp.abs(v)))


def iota(shape, axis):
    return lax.broadcasted_iota(jnp.int32, shape, axis)


def split(v):
    high_half = v.astype(bf16).astype(f32)
    return high_half, v - high_half


def packed(mine, first, second):
    return jnp.where(mine, first, pltpu.roll(second, HEAD_DIM, 1)).astype(bf16)


def meet(left, right, mine):
    (left_high, left_low), (right_high, right_low) = left, right
    lefts = [packed(mine, left_high, left_low), jnp.where(mine, left_high, 0.0).astype(bf16)]
    rights = [packed(mine, right_high, right_high), jnp.where(mine, right_low, 0.0).astype(bf16)]
    return dot(jnp.concatenate(lefts, axis=1), jnp.concatenate(rights, axis=1), ((1,), (1,)))


def pair_columns(table, pair):
    lane = iota((table.shape[0], LANES), 1)
    return jnp.where(lane < HEAD_DIM, table[:, 2 * pair : 2 * pair + 1], table[:, 2 * pair + 1 : 2 * pair + 2])


def decay_tables(step_rows, step_bias, rates):
    step_size = softplus(step_rows + step_bias)
    earlier = (iota((BLOCK, BLOCK), 0) >= iota((BLOCK, BLOCK), 1)).astype(f32)
    cumulative = dot(earlier, step_size * rates, ((1,), (0,)), highest)
    return step_size, cumulative, jnp.exp(cumulative), jnp.exp(cumulative[BLOCK - 1 : BLOCK, :] - cumulative)


def state_decay(from_start, pair):
    last = from_start[BLOCK - 1 : BLOCK, :]
    row = iota((LANES, STATE), 0)
    return jnp.where(row < HEAD_DIM, last[:, 2 * pair : 2 * pair + 1], last[:, 2 * pair + 1 : 2 * pair + 2])


def shifted_conv(rows_ref, before, buffer, taps, conv_bias, first):
    @pl.when(first)
    def _():
        buffer[0:8, :] = before[...]

    @pl.when(jnp.logical_not(first))
    def _():
        buffer[0:8, :] = buffer[BLOCK : BLOCK + 8, :]

    buffer[8 : BLOCK + 8, :] = rows_ref[...]
    total = conv_bias[...] + taps[0:1, :] * buffer[8 : BLOCK + 8, :]
    for tap in range(1, 4):
        total = total + taps[tap : tap + 1, :] * buffer[8 - tap : BLOCK + 8 - tap, :]
    return total


def scan_kernel(
    input_rows, state_rows, step_rows, input_before, state_before, state_entering,
    conv_input, conv_input_bias, conv_state, conv_state_bias, step_bias, rates, skip,
    mixed, input_conv, state_conv, entering, carried, input_buffer, state_buffer,
):
    first = pl.program_id(0) == 0
    pairs = input_rows.shape[1] // LANES

    @pl.when(first)
    def _():
        carried[...] = state_entering[...]

    input_conv[...] = shifted_conv(input_rows, input_before, input_buffer, conv_input, conv_input_bias, first)
    state_pre = shifted_conv(state_rows, state_before, state_buffer, conv_state, conv_state_bias, first)
    state_conv[...] = state_pre
    state_act = state_pre * sigmoid(state_pre)
    writes, reads = state_act[:, :STATE], state_act[:, STATE:]
    meeting = dot(reads, writes, ((1,), (1,)), high)
    step_size, cumulative, from_start, to_end = decay_tables(step_rows[...], step_bias[...], rates[...])
    cumulative_t = cumulative.T
    causal = iota((BLOCK, BLOCK), 0) >= iota((BLOCK, BLOCK), 1)
    lane = iota((BLOCK, LANES), 1)
    for pair in range(pairs):
        columns = slice(pair * LANES, pair * LANES + LANES)
        pre = input_conv[:, columns]
        inputs = pre * sigmoid(pre)
        weighted = inputs * pair_columns(step_size, pair)
        state_in = carried[pair]
        entering[0, pair] = state_in
        out = dot(reads, state_in, ((1,), (1,)), high) * pair_columns(from_start, pair)
        for side in range(2):
            head = 2 * pair + side
            gap = cumulative[:, head : head + 1] - cumulative_t[head : head + 1, :]
            mixing = jnp.exp(jnp.where(causal, gap, -1e30)) * meeting
            mine = (lane < HEAD_DIM) if side == 0 else (lane >= HEAD_DIM)
            out = out + dot(mixing, jnp.where(mine, weighted, 0.0), ((1,), (0,)), high)
        fresh = dot(weighted * pair_columns(to_end, pair), writes, ((0,), (0,)), high)
        carried[pair] = state_decay(from_start, pair) * state_in + fresh
        mixed[:, columns] = out + skip[:, columns] * inputs


def scan_back_kernel(
    input_rows, state_rows, step_rows, input_conv, state_conv, mixed, entering, mixed_grad,
    input_after, state_after, state_leaving, decay_after,
    conv_input, conv_state, step_bias, rates, skip, head_of,
    input_grad, state_grad, step_grad, input_sums, state_sums, step_sums, input_first, state_first, carried, later,
    input_buffer, state_buffer, gap_grad, out_products, in_products,
):
    first = pl.program_id(0) == 0
    pairs = input_rows.shape[1] // LANES

    @pl.when(first)
    def _():
        carried[...] = state_leaving[...]
        later[...] = decay_after[...]
        input_sums[...] = jnp.zeros(input_sums.shape, f32)
        state_sums[...] = jnp.zeros(state_sums.shape, f32)
        step_sums[...] = jnp.zeros(step_sums.shape, f32)
        input_buffer[BLOCK : BLOCK + 8, :] = input_after[...]
        state_buffer[BLOCK : BLOCK + 8, :] = state_after[...]

    @pl.when(jnp.logical_not(first))
    def _():
        input_buffer[BLOCK : BLOCK + 8, :] = input_buffer[0:8, :]
        state_buffer[BLOCK : BLOCK + 8, :] = state_buffer[0:8, :]

    state_pre = state_conv[...]
    state_sig = sigmoid(state_pre)
    state_act = state_pre * state_sig
    writes, reads = state_act[:, :STATE], state_act[:, STATE:]
    meeting_t = dot(writes, reads, ((1,), (1,)), high)
    step_size, cumulative, from_start, to_end = decay_tables(step_rows[...], step_bias[...], rates[...])
    cumulative_t = cumulative.T
    causal_t = iota((BLOCK, BLOCK), 0) <= iota((BLOCK, BLOCK), 1)
    lane = iota((BLOCK, LANES), 1)
    gap_grad[...] = jnp.zeros(gap_grad.shape, f32)
    writes_grad = jnp.zeros((BLOCK, STATE), f32)
    reads_grad = jnp.zeros((BLOCK, STATE), f32)
    for pair in range(pairs):
        columns = slice(pair * LANES, pair * LANES + LANES)
        pre = input_conv[:, columns]
        sig = sigmoid(pre)
        inputs = pre * sig
        step_pair = pair_columns(step_size, pair)
        weighted = inputs * step_pair
        out_grad = mixed_grad[:, columns]
        skip_product = out_grad * inputs
        input_sums[5:6, columns] += jnp.sum(skip_product, axis=0, keepdims=True)
        end_pair = pair_columns(to_end, pair)
        leaving_grad = carried[pair]
        weighted_grad = dot(writes, leaving_grad, ((1,), (1,)), high) * end_pair
        grad_halves, weighted_halves = split(out_grad), split(weighted)
        for side in range(2):
            head = 2 * pair + side
            gap = cumulative_t[head : head + 1, :] - cumulative[:, head : head + 1]
            within = jnp.exp(jnp.where(causal_t, gap, -1e30))
            mine = (lane < HEAD_DIM) if side == 0 else (lane >= HEAD_DIM)
            own_grad = jnp.where(mine, out_grad, 0.0)
            weighted_grad = weighted_grad + dot(within * meeting_t, own_grad, ((1,), (0,)), high)
            gap_grad[...] += within * meet(weighted_halves, grad_halves, mine)
        start_grad = out_grad * pair_columns(from_start, pair)
        reads_grad = reads_grad + dot(start_grad, entering[0, pair], ((1,), (0,)), high)
        writes_grad = writes_grad + dot(weighted * end_pair, leaving_grad, ((1,), (0,)), high)
        carried[pair] = state_decay(from_start, pair) * leaving_grad + dot(start_grad, reads, ((0,), (0,)), high)
        out_products[:, columns] = out_grad * mixed[:, columns] - skip[:, columns] * skip_product
        in_products[:, columns] = inputs * weighted_grad
        inputs_grad = skip[:, columns] * out_grad + step_pair * weighted_grad
        input_buffer[0:BLOCK, columns] = inputs_grad * (sig * (1.0 + pre * (1.0 - sig)))
    reads_grad = reads_grad + dot(gap_grad[...], writes, ((0,), (0,)), high)
    writes_grad = writes_grad + dot(gap_grad[...], reads, ((1,), (0,)), high)
    state_slope = state_sig * (1.0 + state_pre * (1.0 - state_sig))
    state_buffer[0:BLOCK, 0:STATE] = writes_grad * state_slope[:, :STATE]
    state_buffer[0:BLOCK, STATE : 2 * STATE] = reads_grad * state_slope[:, STATE:]

    for buffer, rows, taps, sums, result in (
        (input_buffer, input_rows, conv_input, input_sums, input_grad),
        (state_buffer, state_rows, conv_state, state_sums, state_grad),
    ):
        raw = rows[...]
        total = jnp.zeros(raw.shape, f32)
        for tap in range(4):
            ahead = buffer[tap : tap + BLOCK, :]
            total = total + taps[tap : tap + 1, :] * ahead
            sums[tap : tap + 1, :] += jnp.sum(ahead * raw, axis=0, keepdims=True)
        sums[4:5, :] += jnp.sum(buffer[0:BLOCK, :], axis=0, keepdims=True)
        result[...] = total.astype(result.dtype)
    input_first[...] = input_buffer[0:8, :]
    state_first[...] = state_buffer[0:8, :]

    out_head = dot(out_products[...], head_of[...], ((1,), (0,)), high)
    in_head = dot(in_products[...], head_of[...], ((1,), (0,)), high)
    upper = (iota((BLOCK, BLOCK), 0) <= iota((BLOCK, BLOCK), 1)).astype(f32)
    decay_grad = dot(upper, out_head - step_size * in_head, ((1,), (0,)), highest) + later[0:1, :]
    later[0:1, :] = decay_grad[0:1, :]
    step_sig = sigmoid(step_rows[...] + step_bias[...])
    step_back = (rates[...] * decay_grad + in_head) * step_sig
    step_grad[...] = step_back.astype(step_grad.dtype)
    step_sums[0:1, :] += jnp.sum(step_back, axis=0, keepdims=True)
    step_sums[1:2, :] += jnp.sum(step_size * decay_grad, axis=0, keepdims=True)


def whole(array):
    zeros = (0,) * array.ndim
    return pl.BlockSpec(array.shape, lambda k: zeros)


def params(mebibytes):
    return pltpu.CompilerParams(dimension_semantics=("arbitrary",), vmem_limit_bytes=mebibytes * 1024 * 1024)


little = pl.CostEstimate(flops=10**6, bytes_accessed=2**16, transcendentals=0)


def run_scan(start, span, input_rows, state_rows, step_rows, zeros, state_entering, consts):
    channels = input_rows.shape[1]
    pairs = channels // LANES
    rows = span * BLOCK
    edge = start * BLOCK // 8 - 1

    def tokens(width):
        return pl.BlockSpec((BLOCK, width), lambda k: (start + k, 0))

    def results(width):
        return pl.BlockSpec((BLOCK, width), lambda k: (k, 0))

    if start == 0:
        before = zeros
        before_specs = [whole(c) for c in before]
    else:
        before = (input_rows, state_rows)
        before_specs = [pl.BlockSpec((8, c.shape[1]), lambda k: (edge, 0)) for c in before]
    return pl.pallas_call(
        scan_kernel,
        grid=(span,),
        in_specs=[tokens(channels), tokens(2 * STATE), tokens(LANES)] + before_specs + [whole(state_entering)]
        + [whole(c) for c in consts],
        out_specs=[
            results(channels), results(channels), results(2 * STATE),
            pl.BlockSpec((1, pairs, LANES, STATE), lambda k: (k, 0, 0, 0)), whole(state_entering),
        ],
        out_shape=[
            jax.ShapeDtypeStruct((rows, channels), f32),
            jax.ShapeDtypeStruct((rows, channels), f32),
            jax.ShapeDtypeStruct((rows, 2 * STATE), f32),
            jax.ShapeDtypeStruct((span, pairs, LANES, STATE), f32),
            jax.ShapeDtypeStruct((pairs, LANES, STATE), f32),
        ],
        scratch_shapes=[pltpu.VMEM((BLOCK + 8, channels), f32), pltpu.VMEM((BLOCK + 8, 2 * STATE), f32)],
        compiler_params=params(LIM_SCAN),
        cost_estimate=little,
        name="scan",
    )(input_rows, state_rows, step_rows, *before, state_entering, *consts)


def run_scan_back(start, span, projections, kept, at, mixed_grad, carry, consts):
    channels = mixed_grad.shape[1]
    pairs = channels // LANES
    rows = span * BLOCK

    def tokens(width):
        return pl.BlockSpec((BLOCK, width), lambda k: (start + span - 1 - k, 0))

    def own(width, first=0):
        return pl.BlockSpec((BLOCK, width), lambda k: (first + span - 1 - k, 0))

    def shape(*dims):
        return jax.ShapeDtypeStruct(dims, f32)

    sums = [shape(8, channels), shape(8, 2 * STATE), shape(8, LANES)]
    ends = [jax.ShapeDtypeStruct(c.shape, f32) for c in carry]
    return pl.pallas_call(
        scan_back_kernel,
        grid=(span,),
        in_specs=[
            tokens(channels), tokens(2 * STATE), tokens(LANES), own(channels, at),
            own(2 * STATE, at), own(channels, at),
            pl.BlockSpec((1, pairs, LANES, STATE), lambda k: (at + span - 1 - k, 0, 0, 0)), tokens(channels),
        ] + [whole(c) for c in carry] + [whole(c) for c in consts],
        out_specs=[own(channels), own(2 * STATE), own(LANES)] + [whole(c) for c in sums + ends],
        out_shape=[
            jax.ShapeDtypeStruct((rows, channels), bf16), shape(rows, 2 * STATE),
            jax.ShapeDtypeStruct((rows, LANES), bf16),
        ] + sums + ends,
        scratch_shapes=[
            pltpu.VMEM((BLOCK + 8, channels), f32), pltpu.VMEM((BLOCK + 8, 2 * STATE), f32),
            pltpu.VMEM((BLOCK, BLOCK), f32), pltpu.VMEM((BLOCK, channels), f32), pltpu.VMEM((BLOCK, channels), f32),
        ],
        compiler_params=params(LIM_SCAN_BACK),
        cost_estimate=little,
        name="scan_back",
    )(*projections, *kept, mixed_grad, *carry, *consts)


def fixed_block(*shape):
    zeros = (0,) * len(shape)
    return pl.BlockSpec(shape, lambda n, *_: zeros)


def call(kernel, places, steps, operands, in_specs, out_specs, out_shape, name, scratch=(), aliases={}):
    return pl.pallas_call(
        kernel,
        grid_spec=pltpu.PrefetchScalarGridSpec(
            num_scalar_prefetch=1, grid=(steps,), in_specs=in_specs, out_specs=out_specs, scratch_shapes=list(scratch)
        ),
        out_shape=out_shape,
        input_output_aliases=aliases,
        compiler_params=params(61),
        cost_estimate=little,
        name=name,
    )(places, *operands)


def lay(places, pieces, result, first=0):
    for i, piece in enumerate(pieces):
        result[pl.ds(pl.multiple_of(places[first + i], 16), piece.shape[0]), :] = piece[...]


TILE = 256


def tile_columns(ref, n, first=0):
    return ref[:, pl.ds(pl.multiple_of(n * TILE + first, LANES), TILE)]


def first_project(weights, tokens, places, channels):
    count = len(weights)
    depth, width = tokens[0].shape[1], weights[0].shape[1]
    rows = tokens[0].shape[0] * len(tokens)

    def kernel(places, *refs):
        pieces, (normed, full, tail_proj) = refs[:-3], refs[-3:]
        lay(places, pieces[:count], full)
        lay(places, pieces[count:], normed, count)
        tail_proj[...] = dot(normed[...], full[:, channels:], ((1,), (0,)))

    return call(
        kernel, places, 1, (*weights, *tokens), [fixed_block(*piece.shape) for piece in (*weights, *tokens)],
        [fixed_block(rows, depth), fixed_block(depth, width), fixed_block(rows, width - channels)],
        [
            jax.ShapeDtypeStruct((rows, depth), bf16), jax.ShapeDtypeStruct((depth, width), bf16),
            jax.ShapeDtypeStruct((rows, width - channels), f32),
        ],
        "first_project",
    )


def input_project(places, normed, first_full, channels):
    rows, depth = normed.shape

    def kernel(places, left, right, result):
        result[...] = dot(left[...], right[...], ((1,), (0,)))

    return call(
        kernel, places, channels // TILE, (normed, first_full),
        [fixed_block(rows, depth), pl.BlockSpec((depth, TILE), lambda n, _: (0, n))],
        pl.BlockSpec((rows, TILE), lambda n, _: (0, n)), jax.ShapeDtypeStruct((rows, channels), f32), "input_project",
    )


def second_project(weights, places, normed, cot, mixed, gain):
    count, halves = len(weights), len(mixed)
    width = weights[0].shape[1]
    rows, depth = normed.shape
    channels = width // 2
    part_rows = mixed[0].shape[0]

    def kernel(places, *refs):
        pieces, (normed_ref, cot_ref, gain_ref), mixed_refs = refs[:count], refs[count : count + 3], refs[count + 3 : -4]
        full, gate_proj, out_grad, sums = refs[-4:]
        n = pl.program_id(0)

        @pl.when(n == 0)
        def _():
            lay(places, pieces, full)
            sums[...] = jnp.zeros(sums.shape, f32)

        gate_proj[...] = dot(normed_ref[...], tile_columns(full, n), ((1,), (0,)))
        out_grad[...] = dot(cot_ref[...], tile_columns(full, n, channels), ((1,), (0,)))
        ones = jnp.ones((8, TILE), f32)
        for i in range(halves):
            at = slice(i * part_rows, (i + 1) * part_rows)
            proj = gate_proj[at, :]
            gated = mixed_refs[i][...] * (proj * sigmoid(proj))
            pulled = out_grad[at, :] * gain_ref[...] * gated
            sums[0:8, at] += dot(ones, gated * gated, ((1,), (1,)), highest)
            sums[8:16, at] += dot(ones, pulled, ((1,), (1,)), highest)

    tile = pl.BlockSpec((rows, TILE), lambda n, _: (0, n))
    return call(
        kernel, places, channels // TILE, (*weights, normed, cot, gain, *mixed),
        [fixed_block(*piece.shape) for piece in (*weights, normed, cot)]
        + [pl.BlockSpec((1, TILE), lambda n, _: (0, n))]
        + [pl.BlockSpec((part_rows, TILE), lambda n, _: (0, n)) for _ in mixed],
        [fixed_block(depth, width), tile, tile, fixed_block(16, rows)],
        [
            jax.ShapeDtypeStruct((depth, width), bf16), jax.ShapeDtypeStruct((rows, channels), f32),
            jax.ShapeDtypeStruct((rows, channels), f32), jax.ShapeDtypeStruct((16, rows), f32),
        ],
        "second_project",
    )


def store_shares(places, product, result, tops, part, columns):
    owners, rows = result.shape[0], result.shape[2] - 16
    for owner in range(owners):
        own = product[owner * rows : (owner + 1) * rows]
        result[places[owner], part, 0:rows, columns] = own
        top = jnp.max(jnp.abs(own), axis=0, keepdims=True)
        result[places[owner], part, rows : rows + 16, columns] = jnp.zeros((16, own.shape[1]), f32)
        tops[places[owner], part, :, columns] = jnp.broadcast_to(top, (8, own.shape[1]))


def gate_step(ring, places, sums, gain, mixed, gate_proj, out_grad, cot_t, normed_t, second_full, inner_total):
    depth = second_full.shape[0]
    rows, channels = gate_proj.shape
    halves, part_rows = len(mixed), mixed[0].shape[0]
    share = cot_t.shape[0] // ring.count

    def kernel(places, *refs):
        sums_ref, gain_ref, proj_ref, grad_ref, cot_ref, normed_ref, weight_ref = refs[:7]
        mixed_refs, (branch, gate_grad, mixed_grad, gain_sum, result, tops, gate_out) = refs[7 : 7 + halves], refs[7 + halves :]
        gain_sum[...] = jnp.zeros(gain_sum.shape, f32)
        scale_row = lax.rsqrt(sums_ref[0:8, :] / inner_total + epsilon)
        pull_row = scale_row * scale_row * scale_row * (sums_ref[8:16, :] / inner_total)
        scales, pulls = scale_row.T, pull_row.T
        for i in range(halves):
            at = slice(i * part_rows, (i + 1) * part_rows)
            proj, rows_mixed, grad = proj_ref[at, :], mixed_refs[i][...], grad_ref[at, :]
            sig = sigmoid(proj)
            act = proj * sig
            gated = rows_mixed * act
            scale = scales[at, 0:1]
            scaled = gated * scale
            gate_out[at, :] = (scaled * gain_ref[...]).astype(bf16)
            gain_sum[0:1, :] += jnp.sum(grad * scaled, axis=0, keepdims=True)
            gated_grad = scale * (grad * gain_ref[...]) - gated * pulls[at, 0:1]
            mixed_grad[at, :] = gated_grad * act
            gate_grad[at, :] = (gated_grad * rows_mixed * (sig * (1.0 + proj * (1.0 - sig)))).astype(bf16)
        everything = slice(0, TILE)
        first = pl.program_id(0) == 0
        for i in range(0, rows, TILE):
            at = slice(i, i + TILE)
            share_out = dot(gate_out[at, :], weight_ref[...], ((1,), (1,)))
            branch[at, :] = share_out + jnp.where(first, 0.0, branch[at, :])
        store_shares(places, dot(cot_ref[...], gate_out[...], ((1,), (0,))), result, tops, 0, everything)
        store_shares(places, dot(normed_ref[...], gate_grad[...], ((1,), (0,))), result, tops, 1, everything)

    tile = pl.BlockSpec((rows, TILE), lambda n, _: (0, n))
    return call(
        kernel, places, channels // TILE, (sums, gain, gate_proj, out_grad, cot_t, normed_t, second_full, *mixed),
        [
            fixed_block(16, rows), pl.BlockSpec((1, TILE), lambda n, _: (0, n)), tile, tile,
            fixed_block(*cot_t.shape), fixed_block(*normed_t.shape),
            pl.BlockSpec((depth, TILE), lambda n, _: (0, channels // TILE + n)),
        ] + [pl.BlockSpec((part_rows, TILE), lambda n, _: (0, n)) for _ in mixed],
        [
            fixed_block(rows, depth), tile, tile, pl.BlockSpec((8, TILE), lambda n, _: (0, n)),
            pl.BlockSpec((ring.count, 2, share + 16, TILE), lambda n, _: (0, 0, 0, n)),
            pl.BlockSpec((ring.count, 2, 8, TILE), lambda n, _: (0, 0, 0, n)),
        ],
        [
            jax.ShapeDtypeStruct((rows, depth), f32), jax.ShapeDtypeStruct((rows, channels), bf16),
            jax.ShapeDtypeStruct((rows, channels), f32), jax.ShapeDtypeStruct((8, channels), f32),
            jax.ShapeDtypeStruct((ring.count, 2, share + 16, channels), f32),
            jax.ShapeDtypeStruct((ring.count, 2, 8, channels), f32),
        ],
        "gate_step", [pltpu.VMEM((rows, TILE), bf16)],
    )


def input_partials(ring, places, normed_t, input_back):
    halves, (part_rows, channels) = len(input_back), input_back[0].shape
    share = normed_t.shape[0] // ring.count

    def kernel(places, left, *refs):
        rights, result, tops = refs[:-2], refs[-2], refs[-1]
        product = dot(left[:, 0:part_rows], rights[0][...], ((1,), (0,)))
        for i in range(1, halves):
            product = product + dot(left[:, i * part_rows : (i + 1) * part_rows], rights[i][...], ((1,), (0,)))
        store_shares(places, product, result, tops, 0, slice(0, TILE))

    def block(rows):
        return pl.BlockSpec((ring.count, 1, rows, TILE), lambda n, _: (0, 0, 0, n))

    return call(
        kernel, places, channels // TILE, (normed_t, *input_back),
        [fixed_block(*normed_t.shape)] + [pl.BlockSpec((part_rows, TILE), lambda n, _: (0, n)) for _ in input_back],
        [block(share + 16), block(8)],
        [jax.ShapeDtypeStruct((ring.count, 1, rows, channels + LANES), f32) for rows in (share + 16, 8)],
        "input_partials",
    )


def tail_partials(places, normed_t, tail, parts, tops):
    def kernel(places, left, right, parts_in, tops_in, result, tops_out):
        product = dot(left[...], right[...], ((1,), (0,)))
        store_shares(places, product, result, tops_out, 0, slice(0, LANES))

    last = parts.shape[3] // LANES - 1
    specs = [pl.BlockSpec((*array.shape[:3], LANES), lambda n, _: (0, 0, 0, last)) for array in (parts, tops)]
    anywhere = pl.BlockSpec(memory_space=pl.ANY)
    return call(
        kernel, places, 1, (normed_t, tail, parts, tops),
        [fixed_block(*normed_t.shape), fixed_block(*tail.shape), anywhere, anywhere], specs,
        [jax.ShapeDtypeStruct(array.shape, f32) for array in (parts, tops)], "tail_partials", aliases={3: 0, 4: 1},
    )


def normed_kernel(halves, places, gate_rows, tail_rows, gate_tile, input_tile, tail_tile, *refs):
    inputs, results, product = refs[:halves], refs[halves:-1], refs[-1]
    part = inputs[0].shape[0]
    for i, input_rows in enumerate(inputs):
        at = slice(i * part, (i + 1) * part)
        total = dot(gate_rows[at, :], gate_tile[...], ((1,), (1,)))
        total = total + dot(tail_rows[at, :], tail_tile[...], ((1,), (1,)))
        product[at, :] = total + dot(input_rows[...], input_tile[...], ((1,), (1,)))
    rows = results[0].shape[0]
    for i, result in enumerate(results):
        result[...] = product[pl.ds(pl.multiple_of(places[i] * rows, 16), rows), :]


def normed_parts(places, gate_grad, input_back, tail, second_full, first_full):
    count = lax.axis_size("tensor")
    tokens, channels = gate_grad.shape
    width, tile = first_full.shape[0], 2 * LANES
    halves = len(input_back)

    def fixed(n, _):
        return (0, 0)

    return pl.pallas_call(
        lambda *refs: normed_kernel(halves, *refs),
        grid_spec=pltpu.PrefetchScalarGridSpec(
            num_scalar_prefetch=1, grid=(width // tile,),
            in_specs=[
                pl.BlockSpec((tokens, channels), fixed), pl.BlockSpec((tokens, LANES), fixed),
                pl.BlockSpec((tile, channels), lambda n, _: (n, 0)), pl.BlockSpec((tile, channels), lambda n, _: (n, 0)),
                pl.BlockSpec((tile, LANES), lambda n, _: (n, channels // LANES)),
            ] + [pl.BlockSpec(half.shape, fixed) for half in input_back],
            out_specs=[pl.BlockSpec((tokens // count, tile), lambda n, _: (0, n))] * count,
            scratch_shapes=[pltpu.VMEM((tokens, tile), f32)],
        ),
        out_shape=[jax.ShapeDtypeStruct((tokens // count, width), f32)] * count,
        compiler_params=params(LIM_NORMED_PARTS),
        cost_estimate=little,
        name="normed_parts",
    )(places, gate_grad, tail, second_full, first_full, first_full, *input_back)


def cycle(count):
    return list(range(0, count, 2)) + list(range(count - 1, 0, -2))


def table(numbers):
    return jnp.stack(numbers).astype(jnp.int32)


class Ring:
    def __init__(self):
        self.count = lax.axis_size("dp")
        order = cycle(self.count)
        self.up = [(order[i], order[(i + 1) % self.count]) for i in range(self.count)]
        self.down = [(b, a) for a, b in self.up]
        me = lax.axis_index("dp")
        self.place = jnp.where(me % 2 == 0, me // 2, self.count - 1 - me // 2)

    def places(self):
        order = cycle(self.count)
        return table([(order.index(i) - self.place + self.count) % self.count for i in range(self.count)])

    def owner(self, offset):
        place = (self.place + offset + self.count) % self.count
        return jnp.where(place < self.count // 2, 2 * place, 2 * (self.count - 1 - place) + 1)


def middle(rows):
    return (rows // 2 + 15) // 16 * 16


class Gather:
    def __init__(self, ring, shard):
        self.ring, self.shard, self.step = ring, shard, 0
        self.held = [(shard, 0, 0)]
        self.last = (shard, shard)

    def hop(self):
        self.step += 1
        half, cut = self.ring.count // 2, middle(self.shard.shape[0])
        up, down = self.last
        offsets = ((-self.step, 0), (self.step, 0))
        if self.step == half:
            up, down = up[:cut], down[cut:]
            offsets = ((half, 0), (half, cut))
        self.last = (lax.ppermute(up, "dp", self.ring.up), lax.ppermute(down, "dp", self.ring.down))
        self.held += [(piece, *offset) for piece, offset in zip(self.last, offsets)]

    def after(self, *marks):
        self.last, marks = fence(self.last, marks)
        self.held[-2:] = [(piece, *old[1:]) for piece, old in zip(self.last, self.held[-2:])]
        return marks if len(marks) > 1 else marks[0]

    def pieces(self):
        return [piece for piece, _, _ in self.held]

    def places(self):
        rows, half = self.shard.shape[0], self.ring.count // 2
        spots = [self.ring.owner(0) * rows]
        for step in range(1, half):
            spots += [self.ring.owner(-step) * rows, self.ring.owner(step) * rows]
        return spots + [self.ring.owner(half) * rows, self.ring.owner(half) * rows + middle(rows)]


def encode(rows, limit):
    power = jnp.ceil(jnp.log2(jnp.maximum(limit, 1e-30)))
    ours = lax.broadcasted_iota(jnp.int32, rows.shape, 1) < rows.shape[1] - 16
    return jnp.where(ours, rows * jnp.exp2(15.0 - power), power).astype(jnp.float16)


def decode(payload):
    power = payload[:, -16:-15].astype(f32)
    return payload.astype(f32) * jnp.exp2(power - 15.0), jnp.exp2(power)


class Scatter:
    def __init__(self, ring, parts, tops):
        self.ring, self.parts, self.tops = ring, parts, tops
        self.step = ring.count // 2
        self.rows = parts.shape[2] - 16
        self.cut = middle(self.rows)
        far = parts[self.step]
        top = tops[self.step, :, 0:1]
        upper = jnp.concatenate([far[:, : self.cut], far[:, -16:]], axis=1)
        self.send = (encode(upper, top), encode(far[:, self.cut :], top))

    def hop(self):
        self.send = fence(*self.send)
        self.got = (lax.ppermute(self.send[0], "dp", self.ring.up), lax.ppermute(self.send[1], "dp", self.ring.down))

    def after(self, *marks):
        self.got, marks = fence(self.got, marks)
        return marks if len(marks) > 1 else marks[0]

    def before(self, *marks):
        self.send, marks = fence(self.send, marks)
        return marks if len(marks) > 1 else marks[0]

    def add(self):
        first = self.step == self.ring.count // 2
        self.got = fence(*self.got)
        (up, up_top), (down, down_top) = (decode(g) for g in self.got)
        if first:
            up = jnp.pad(up, ((0, 0), (0, self.rows - self.cut), (0, 0)))
            down = jnp.pad(down, ((0, 0), (self.cut, 0), (0, 0)))
            up = jnp.where(lax.broadcasted_iota(jnp.int32, up.shape, 1) < self.cut, up, 0.0)
        self.step -= 1
        if self.step == 0:
            return (self.parts[0] + up + down)[:, : self.rows]
        above, below = self.parts[self.step], self.parts[self.ring.count - self.step]
        self.send = (
            encode(above + up, self.tops[self.step, :, 0:1] + up_top),
            encode(below + down, self.tops[self.ring.count - self.step, :, 0:1] + down_top),
        )
        return None


def fence(*arrays):
    flat, tree = jax.tree.flatten(arrays)
    return jax.tree.unflatten(tree, lax.optimization_barrier(flat))


def across(array, bit, axis="tensor"):
    count = lax.axis_size(axis)
    return lax.ppermute(array, axis, [(i, i ^ bit) for i in range(count)])


def group_sum(array, axis, first, count):
    terms = [array] + [across(array, first * other, axis) for other in range(1, count)]
    while len(terms) > 1:
        terms = [terms[i] + terms[i + 1] for i in range(0, len(terms), 2)]
    return terms[0]


def cube_sum(array, axis):
    bit = 1
    while bit < lax.axis_size(axis):
        array = array + across(array, bit, axis)
        bit *= 2
    return array


def shards(
    block_input, cotangent, norm_gain, gate_weight, input_weight, state_weight, step_weight, conv_input,
    conv_input_bias, conv_state, conv_state_bias, step_bias, decay_log, skip_scale, gate_gain, out_weight,
):
    group_count = lax.axis_size("tensor")
    me = lax.axis_index("tensor")
    ring = Ring()
    half = ring.count // 2
    local_rows = block_input.shape[0]
    channels = gate_gain.shape[0]
    heads = step_bias.shape[0]
    inner_total = channels * group_count
    share = 2 * STATE // group_count
    tokens = local_rows * group_count
    blocks = tokens // BLOCK
    fold = LANES // share
    folded = tokens // fold
    rows_dot = ((1,), (0,))
    back_dot = ((1,), (1,))

    state_mine = lax.dynamic_slice_in_dim(state_weight, me * share, share, 1)
    first = Gather(
        ring,
        jnp.concatenate(
            [input_weight, state_mine, jnp.pad(step_weight, ((0, 0), (0, LANES - share - heads)))], axis=1
        ).astype(bf16),
    )
    first.hop()
    row_scale = lax.rsqrt(jnp.mean(block_input * block_input, axis=1, keepdims=True) + epsilon)
    normed = (block_input * row_scale * norm_gain).astype(bf16)
    second_weight = jnp.concatenate([gate_weight, out_weight.T], axis=1).astype(bf16)
    rates = -jnp.exp(decay_log)

    def per_head(vector):
        return jnp.pad(vector, (0, LANES - heads))[None, :]

    skip = jnp.repeat(skip_scale, HEAD_DIM)[None, :]
    head_of = (
        lax.broadcasted_iota(jnp.int32, (channels, LANES), 0) // HEAD_DIM
        == lax.broadcasted_iota(jnp.int32, (channels, LANES), 1)
    ).astype(f32)
    scan_consts = (
        conv_input, conv_input_bias[None, :], conv_state, conv_state_bias[None, :], per_head(step_bias),
        per_head(rates), skip,
    )
    back_consts = (conv_input, conv_state, per_head(step_bias), per_head(rates), skip, head_of)
    carried = jnp.zeros((channels // LANES, LANES, STATE), f32)
    carry = (jnp.zeros((8, channels), f32), jnp.zeros((8, 2 * STATE), f32), carried, jnp.zeros((8, LANES), f32))
    gain = gate_gain[None, :]
    shard_places = first.places()
    token_places = [(me ^ bits) * local_rows for bits in range(4)]
    tables = (table(shard_places + token_places), table(shard_places), ring.places(), table([i ^ me for i in range(4)]))
    normed, scan_consts, back_consts, carried, carry, gain, tables = first.after(
        normed, scan_consts, back_consts, carried, carry, gain, tables
    )
    first_places, second_places, share_places, turn_places = tables
    first.hop()
    far, near = across(normed, 2), across(normed, 1)
    for _ in range(half - 3):
        first.hop()
    far, near, second_weight, cot_low = first.after(far, near, second_weight, cotangent.astype(bf16))
    first.hop()
    second_weight = first.after(second_weight)
    normed_pieces = (normed, near, far, across(far, 1))
    second = Gather(ring, second_weight)
    second.hop()
    cot_all = lax.all_gather(cot_low, "tensor", axis=0, tiled=True)
    normed_all, first_full, tail_proj = first_project(first.pieces(), normed_pieces, first_places, channels)
    step_proj = jnp.pad(tail_proj[:, share : share + heads], ((0, 0), (0, LANES - heads)))
    state_mine = jnp.concatenate([tail_proj[i * folded : (i + 1) * folded, :share] for i in range(fold)], axis=1)
    normed_all, state_mine = fence(normed_all, state_mine)
    far = across(state_mine, 2)
    input_proj, far = second.after(input_project(share_places, normed_all, first_full, channels), far)
    second.hop()
    same_x, same_core, diagonal = across(state_mine, 1), far, across(far, 1)
    right_core = me % 2 == 1
    near = (jnp.where(right_core, same_x, state_mine), jnp.where(right_core, state_mine, same_x))
    away = (jnp.where(right_core, diagonal, same_core), jnp.where(right_core, same_core, diagonal))
    right_chip = me // 2 == 1
    state_parts = [jnp.where(right_chip, away[i], near[i]) for i in range(2)]
    state_parts += [jnp.where(right_chip, near[i], away[i]) for i in range(2)]
    state_proj = jnp.concatenate(
        [jnp.concatenate([p[:, i * share : (i + 1) * share] for p in state_parts], axis=1) for i in range(fold)], axis=0
    )
    span = 2
    scanned, mixed = [], []
    for start in range(0, blocks, span):
        scanned.append(run_scan(start, span, input_proj, state_proj, step_proj, carry[:2], carried, scan_consts))
        carried = scanned[-1][4]
        mixed.append(scanned[-1][0])
        if second.step < half:
            carried, mixed[-1] = second.after(carried, mixed[-1])
            second.hop()
    while second.step < half:
        second.hop()
    second_full, gate_proj, gate_out_grad, sums = second_project(
        second.pieces(), second_places, normed_all, cot_all, mixed, gain
    )
    sums = (sums + across(sums, 1)) + (across(sums, 2) + across(sums, 3))
    normed_t = normed_all.T
    branch_part, gate_grad, mixed_grad, gain_sum, *pair_parts = gate_step(
        ring, share_places, sums, gain, mixed, gate_proj, gate_out_grad, cot_all.T, normed_t, second_full,
        float(inner_total),
    )
    pair_ring = Scatter(ring, *pair_parts)
    done = []
    for turn in range(blocks // span):
        if turn == 0:
            carry, branch_part = pair_ring.before(carry, branch_part)
            pair_ring.hop()
            branch = lax.psum_scatter(branch_part, "tensor", scatter_dimension=0, tiled=True)
        else:
            carry = pair_ring.after(carry)
            pair_ring.add()
            carry = pair_ring.before(carry)
            pair_ring.hop()
        start = blocks - span * (turn + 1)
        kept = scanned[start // span]
        kept = [kept[1], kept[2], kept[0], kept[3]]
        result = run_scan_back(
            start, span, (input_proj, state_proj, step_proj), kept, 0, mixed_grad, carry, back_consts
        )
        done.insert(0, result)
        carry = tuple(result[6:])
    done = pair_ring.after(done)
    pair_ring.add()
    done = pair_ring.before(done)
    pair_ring.hop()
    input_back, state_back = [d[0] for d in done], [d[1] for d in done]
    step_back = jnp.concatenate([d[2] for d in done], axis=0)
    input_sums, state_sums, step_sums = (sum(d[i] for d in done) for i in range(3, 6))

    packed = jnp.concatenate(
        [
            state_sums[:5].reshape(-1),
            input_sums[:5].reshape(-1),
            gain_sum[0],
            jnp.sum(input_sums[5].reshape(heads, HEAD_DIM), axis=1),
            step_sums[0, :heads],
            step_sums[1, :heads] * rates,
        ]
    )
    packed = jnp.pad(packed, (0, -packed.shape[0] % LANES)).reshape(-1, LANES)

    def state_columns(index):
        return jnp.concatenate([lax.dynamic_slice_in_dim(rows, index * share, share, 1) for rows in state_back], axis=1)

    for_far, for_me = across(state_columns(me ^ 3), 1), across(state_columns(me ^ 1), 1)
    packed, for_far, for_me = fence(packed, for_far, for_me)
    far, input_back = fence(state_columns(me ^ 2) + for_far, input_back)
    from_far = across(far, 2)
    input_parts, from_far, pair_ring.got = fence(
        input_partials(ring, share_places, normed_t, input_back), from_far, pair_ring.got
    )
    pair_ring.add()
    from_far = pair_ring.before(from_far)
    pair_ring.hop()
    state_share = (state_columns(me) + for_me + from_far).astype(bf16)
    state_share = jnp.concatenate([state_share[:, i * share : (i + 1) * share] for i in range(fold)], axis=0)
    tail = jnp.concatenate(
        [state_share, step_back[:, :heads], jnp.zeros((tokens, LANES - share - heads), bf16)], axis=1
    )
    parts = normed_parts(turn_places, gate_grad, input_back, tail, second_full, first_full)
    branch, *parts = pair_ring.after(branch, *parts)
    block_output = block_input + branch
    for_far, for_me = across(parts[3], 1), across(parts[1], 1)
    input_parts = tail_partials(share_places, normed_t, tail, *input_parts)
    input_ring = Scatter(ring, *input_parts)
    for_far, for_me = input_ring.before(for_far, for_me)
    input_ring.hop()
    sent = parts[2] + for_far
    sent = jnp.pad(sent, ((0, 16), (0, 0)))[None]
    from_far = across(encode(sent, jnp.max(jnp.abs(sent), axis=1, keepdims=True)), 2)
    input_sum = input_ring.add()
    pair_sum = pair_ring.add()
    while pair_sum is None:
        pair_ring.hop()
        pair_sum = pair_ring.add()
    while input_sum is None:
        input_ring.hop()
        if input_ring.step == 1:
            from_far = input_ring.after(from_far)
        input_sum = input_ring.add()
    normed_grad = parts[0] + for_me + decode(from_far)[0][0, :local_rows]
    input_sum = input_sum[0]
    tail_sum = input_sum[:, channels:]

    weighted_grad = normed_grad * norm_gain
    norm_gain_part = jnp.sum(normed_grad * block_input * row_scale, axis=0)
    input_grad = (
        cotangent
        + row_scale * weighted_grad
        - block_input * row_scale**3 * jnp.mean(weighted_grad * block_input, axis=1, keepdims=True)
    )
    mine = tail_sum[:, :share]
    other = across(mine, 1)
    pair = jnp.concatenate([jnp.where(right_core, other, mine), jnp.where(right_core, mine, other)], axis=1)
    state_rows = 10 * STATE // LANES
    shared = jnp.concatenate([norm_gain_part.reshape(-1, LANES), packed[:state_rows]], axis=0)
    shared = group_sum(shared, "tensor", 1, group_count)
    shared, pair = fence(shared, pair)
    other = across(pair, 2)
    packed = jnp.concatenate([shared, packed[state_rows:]], axis=0)
    packed, other = fence(group_sum(packed, "dp", 2, half), other)
    packed = group_sum(packed, "dp", 1, 2)
    state_grad = jnp.concatenate([jnp.where(right_chip, other, pair), jnp.where(right_chip, pair, other)], axis=1)
    local = packed[shared.shape[0] :].reshape(-1)
    norm_gain_grad = packed[: shared.shape[0] - state_rows].reshape(-1)
    state_sum = packed[shared.shape[0] - state_rows : shared.shape[0]].reshape(5, 2 * STATE)
    at = 6 * channels
    return (
        block_output,
        input_grad,
        norm_gain_grad,
        pair_sum[1],
        input_sum[:, :channels],
        state_grad,
        tail_sum[:, share : share + heads],
        local[: 4 * channels].reshape(4, channels),
        local[4 * channels : 5 * channels],
        state_sum[:4],
        state_sum[4],
        local[at + heads : at + 2 * heads],
        local[at + 2 * heads : at + 3 * heads],
        local[at : at + heads],
        local[5 * channels : at],
        pair_sum[0].T,
    )


def solution(mesh):
    rows = P(("dp", "tensor"), None)
    both = P("dp", "tensor")
    inner = P("tensor")
    return jax.shard_map(
        shards,
        mesh=mesh,
        in_specs=(
            rows, rows, P(), both, both, P("dp", None), both, P(None, "tensor"), inner, P(), P(), inner, inner,
            inner, inner, P("tensor", "dp"),
        ),
        out_specs=(
            rows, rows, P(), both, both, P("dp", None), both, P(None, "tensor"), inner, P(), P(), inner, inner,
            inner, inner, P("tensor", "dp"),
        ),
        check_vma=False,
    )
```

```python
import jax
import jax.numpy as jnp
from jax import lax
from jax.experimental import pallas as pl
from jax.experimental.pallas import tpu as pltpu
from jax.sharding import PartitionSpec as P

HEAD_DIM = 64
STATE = 128
BLOCK = 256
SEQ = 1024
LANES = 128

LIM_SCAN = 61
LIM_SCAN_BACK = 61
LIM_NORMED_PARTS = 61

epsilon = 1e-05
high = lax.Precision.HIGH
highest = lax.Precision.HIGHEST
f32 = jnp.float32
bf16 = jnp.bfloat16


def dot(left, right, dims, precision=None):
    return lax.dot_general(
        left, right, (dims, ((), ())), precision=precision, preferred_element_type=f32
    )


def sigmoid(v):
    return 1.0 / (1.0 + jnp.exp(-v))


def softplus(v):
    return jnp.maximum(v, 0.0) + jnp.log1p(jnp.exp(-jnp.abs(v)))


def iota(shape, axis):
    return lax.broadcasted_iota(jnp.int32, shape, axis)


def split(v):
    high_half = v.astype(bf16).astype(f32)
    return high_half, v - high_half


def packed(mine, first, second):
    return jnp.where(mine, first, pltpu.roll(second, HEAD_DIM, 1)).astype(bf16)


def meet(left, right, mine):
    (left_high, left_low), (right_high, right_low) = left, right
    lefts = [packed(mine, left_high, left_low), jnp.where(mine, left_high, 0.0).astype(bf16)]
    rights = [packed(mine, right_high, right_high), jnp.where(mine, right_low, 0.0).astype(bf16)]
    return dot(jnp.concatenate(lefts, axis=1), jnp.concatenate(rights, axis=1), ((1,), (1,)))


def pair_columns(table, pair):
    lane = iota((table.shape[0], LANES), 1)
    return jnp.where(lane < HEAD_DIM, table[:, 2 * pair : 2 * pair + 1], table[:, 2 * pair + 1 : 2 * pair + 2])


def decay_tables(step_rows, step_bias, rates):
    step_size = softplus(step_rows + step_bias)
    earlier = (iota((BLOCK, BLOCK), 0) >= iota((BLOCK, BLOCK), 1)).astype(f32)
    cumulative = dot(earlier, step_size * rates, ((1,), (0,)), highest)
    return step_size, cumulative, jnp.exp(cumulative), jnp.exp(cumulative[BLOCK - 1 : BLOCK, :] - cumulative)


def state_decay(from_start, pair):
    last = from_start[BLOCK - 1 : BLOCK, :]
    row = iota((LANES, STATE), 0)
    return jnp.where(row < HEAD_DIM, last[:, 2 * pair : 2 * pair + 1], last[:, 2 * pair + 1 : 2 * pair + 2])


def shifted_conv(rows_ref, before, buffer, taps, conv_bias, first):
    @pl.when(first)
    def _():
        buffer[0:8, :] = before[...]

    @pl.when(jnp.logical_not(first))
    def _():
        buffer[0:8, :] = buffer[BLOCK : BLOCK + 8, :]

    buffer[8 : BLOCK + 8, :] = rows_ref[...]
    total = conv_bias[...] + taps[0:1, :] * buffer[8 : BLOCK + 8, :]
    for tap in range(1, 4):
        total = total + taps[tap : tap + 1, :] * buffer[8 - tap : BLOCK + 8 - tap, :]
    return total


def scan_kernel(
    input_rows, state_rows, step_rows, input_before, state_before, state_entering,
    conv_input, conv_input_bias, conv_state, conv_state_bias, step_bias, rates, skip,
    mixed, input_conv, state_conv, entering, carried, input_buffer, state_buffer,
):
    first = pl.program_id(0) == 0
    pairs = input_rows.shape[1] // LANES

    @pl.when(first)
    def _():
        carried[...] = state_entering[...]

    input_conv[...] = shifted_conv(input_rows, input_before, input_buffer, conv_input, conv_input_bias, first)
    state_pre = shifted_conv(state_rows, state_before, state_buffer, conv_state, conv_state_bias, first)
    state_conv[...] = state_pre
    state_act = state_pre * sigmoid(state_pre)
    writes, reads = state_act[:, :STATE], state_act[:, STATE:]
    meeting = dot(reads, writes, ((1,), (1,)), high)
    step_size, cumulative, from_start, to_end = decay_tables(step_rows[...], step_bias[...], rates[...])
    cumulative_t = cumulative.T
    causal = iota((BLOCK, BLOCK), 0) >= iota((BLOCK, BLOCK), 1)
    lane = iota((BLOCK, LANES), 1)
    for pair in range(pairs):
        columns = slice(pair * LANES, pair * LANES + LANES)
        pre = input_conv[:, columns]
        inputs = pre * sigmoid(pre)
        weighted = inputs * pair_columns(step_size, pair)
        state_in = carried[pair]
        entering[0, pair] = state_in
        out = dot(reads, state_in, ((1,), (1,)), high) * pair_columns(from_start, pair)
        for side in range(2):
            head = 2 * pair + side
            gap = cumulative[:, head : head + 1] - cumulative_t[head : head + 1, :]
            mixing = jnp.exp(jnp.where(causal, gap, -1e30)) * meeting
            mine = (lane < HEAD_DIM) if side == 0 else (lane >= HEAD_DIM)
            out = out + dot(mixing, jnp.where(mine, weighted, 0.0), ((1,), (0,)), high)
        fresh = dot(weighted * pair_columns(to_end, pair), writes, ((0,), (0,)), high)
        carried[pair] = state_decay(from_start, pair) * state_in + fresh
        mixed[:, columns] = out + skip[:, columns] * inputs


def scan_back_kernel(
    input_rows, state_rows, step_rows, input_conv, state_conv, mixed, entering, mixed_grad,
    input_after, state_after, state_leaving, decay_after,
    conv_input, conv_state, step_bias, rates, skip, head_of,
    input_grad, state_grad, step_grad, input_sums, state_sums, step_sums, input_first, state_first, carried, later,
    input_buffer, state_buffer, gap_grad, out_products, in_products,
):
    first = pl.program_id(0) == 0
    pairs = input_rows.shape[1] // LANES

    @pl.when(first)
    def _():
        carried[...] = state_leaving[...]
        later[...] = decay_after[...]
        input_sums[...] = jnp.zeros(input_sums.shape, f32)
        state_sums[...] = jnp.zeros(state_sums.shape, f32)
        step_sums[...] = jnp.zeros(step_sums.shape, f32)
        input_buffer[BLOCK : BLOCK + 8, :] = input_after[...]
        state_buffer[BLOCK : BLOCK + 8, :] = state_after[...]

    @pl.when(jnp.logical_not(first))
    def _():
        input_buffer[BLOCK : BLOCK + 8, :] = input_buffer[0:8, :]
        state_buffer[BLOCK : BLOCK + 8, :] = state_buffer[0:8, :]

    state_pre = state_conv[...]
    state_sig = sigmoid(state_pre)
    state_act = state_pre * state_sig
    writes, reads = state_act[:, :STATE], state_act[:, STATE:]
    meeting_t = dot(writes, reads, ((1,), (1,)), high)
    step_size, cumulative, from_start, to_end = decay_tables(step_rows[...], step_bias[...], rates[...])
    cumulative_t = cumulative.T
    causal_t = iota((BLOCK, BLOCK), 0) <= iota((BLOCK, BLOCK), 1)
    lane = iota((BLOCK, LANES), 1)
    gap_grad[...] = jnp.zeros(gap_grad.shape, f32)
    writes_grad = jnp.zeros((BLOCK, STATE), f32)
    reads_grad = jnp.zeros((BLOCK, STATE), f32)
    for pair in range(pairs):
        columns = slice(pair * LANES, pair * LANES + LANES)
        pre = input_conv[:, columns]
        sig = sigmoid(pre)
        inputs = pre * sig
        step_pair = pair_columns(step_size, pair)
        weighted = inputs * step_pair
        out_grad = mixed_grad[:, columns]
        skip_product = out_grad * inputs
        input_sums[5:6, columns] += jnp.sum(skip_product, axis=0, keepdims=True)
        end_pair = pair_columns(to_end, pair)
        leaving_grad = carried[pair]
        weighted_grad = dot(writes, leaving_grad, ((1,), (1,)), high) * end_pair
        grad_halves, weighted_halves = split(out_grad), split(weighted)
        for side in range(2):
            head = 2 * pair + side
            gap = cumulative_t[head : head + 1, :] - cumulative[:, head : head + 1]
            within = jnp.exp(jnp.where(causal_t, gap, -1e30))
            mine = (lane < HEAD_DIM) if side == 0 else (lane >= HEAD_DIM)
            own_grad = jnp.where(mine, out_grad, 0.0)
            weighted_grad = weighted_grad + dot(within * meeting_t, own_grad, ((1,), (0,)), high)
            gap_grad[...] += within * meet(weighted_halves, grad_halves, mine)
        start_grad = out_grad * pair_columns(from_start, pair)
        reads_grad = reads_grad + dot(start_grad, entering[0, pair], ((1,), (0,)), high)
        writes_grad = writes_grad + dot(weighted * end_pair, leaving_grad, ((1,), (0,)), high)
        carried[pair] = state_decay(from_start, pair) * leaving_grad + dot(start_grad, reads, ((0,), (0,)), high)
        out_products[:, columns] = out_grad * mixed[:, columns] - skip[:, columns] * skip_product
        in_products[:, columns] = inputs * weighted_grad
        inputs_grad = skip[:, columns] * out_grad + step_pair * weighted_grad
        input_buffer[0:BLOCK, columns] = inputs_grad * (sig * (1.0 + pre * (1.0 - sig)))
    reads_grad = reads_grad + dot(gap_grad[...], writes, ((0,), (0,)), high)
    writes_grad = writes_grad + dot(gap_grad[...], reads, ((1,), (0,)), high)
    state_slope = state_sig * (1.0 + state_pre * (1.0 - state_sig))
    state_buffer[0:BLOCK, 0:STATE] = writes_grad * state_slope[:, :STATE]
    state_buffer[0:BLOCK, STATE : 2 * STATE] = reads_grad * state_slope[:, STATE:]

    for buffer, rows, taps, sums, result in (
        (input_buffer, input_rows, conv_input, input_sums, input_grad),
        (state_buffer, state_rows, conv_state, state_sums, state_grad),
    ):
        raw = rows[...]
        total = jnp.zeros(raw.shape, f32)
        for tap in range(4):
            ahead = buffer[tap : tap + BLOCK, :]
            total = total + taps[tap : tap + 1, :] * ahead
            sums[tap : tap + 1, :] += jnp.sum(ahead * raw, axis=0, keepdims=True)
        sums[4:5, :] += jnp.sum(buffer[0:BLOCK, :], axis=0, keepdims=True)
        result[...] = total.astype(result.dtype)
    input_first[...] = input_buffer[0:8, :]
    state_first[...] = state_buffer[0:8, :]

    out_head = dot(out_products[...], head_of[...], ((1,), (0,)), high)
    in_head = dot(in_products[...], head_of[...], ((1,), (0,)), high)
    upper = (iota((BLOCK, BLOCK), 0) <= iota((BLOCK, BLOCK), 1)).astype(f32)
    decay_grad = dot(upper, out_head - step_size * in_head, ((1,), (0,)), highest) + later[0:1, :]
    later[0:1, :] = decay_grad[0:1, :]
    step_sig = sigmoid(step_rows[...] + step_bias[...])
    step_back = (rates[...] * decay_grad + in_head) * step_sig
    step_grad[...] = step_back.astype(step_grad.dtype)
    step_sums[0:1, :] += jnp.sum(step_back, axis=0, keepdims=True)
    step_sums[1:2, :] += jnp.sum(step_size * decay_grad, axis=0, keepdims=True)


def whole(array):
    zeros = (0,) * array.ndim
    return pl.BlockSpec(array.shape, lambda k: zeros)


def params(mebibytes):
    return pltpu.CompilerParams(dimension_semantics=("arbitrary",), vmem_limit_bytes=mebibytes * 1024 * 1024)


little = pl.CostEstimate(flops=10**6, bytes_accessed=2**16, transcendentals=0)


def run_scan(start, span, input_rows, state_rows, step_rows, zeros, state_entering, consts):
    channels = input_rows.shape[1]
    pairs = channels // LANES
    rows = span * BLOCK
    edge = start * BLOCK // 8 - 1

    def tokens(width):
        return pl.BlockSpec((BLOCK, width), lambda k: (start + k, 0))

    def results(width):
        return pl.BlockSpec((BLOCK, width), lambda k: (k, 0))

    if start == 0:
        before = zeros
        before_specs = [whole(c) for c in before]
    else:
        before = (input_rows, state_rows)
        before_specs = [pl.BlockSpec((8, c.shape[1]), lambda k: (edge, 0)) for c in before]
    return pl.pallas_call(
        scan_kernel,
        grid=(span,),
        in_specs=[tokens(channels), tokens(2 * STATE), tokens(LANES)] + before_specs + [whole(state_entering)]
        + [whole(c) for c in consts],
        out_specs=[
            results(channels), results(channels), results(2 * STATE),
            pl.BlockSpec((1, pairs, LANES, STATE), lambda k: (k, 0, 0, 0)), whole(state_entering),
        ],
        out_shape=[
            jax.ShapeDtypeStruct((rows, channels), f32),
            jax.ShapeDtypeStruct((rows, channels), f32),
            jax.ShapeDtypeStruct((rows, 2 * STATE), f32),
            jax.ShapeDtypeStruct((span, pairs, LANES, STATE), f32),
            jax.ShapeDtypeStruct((pairs, LANES, STATE), f32),
        ],
        scratch_shapes=[pltpu.VMEM((BLOCK + 8, channels), f32), pltpu.VMEM((BLOCK + 8, 2 * STATE), f32)],
        compiler_params=params(LIM_SCAN),
        cost_estimate=little,
        name="scan",
    )(input_rows, state_rows, step_rows, *before, state_entering, *consts)


def run_scan_back(start, span, projections, kept, at, mixed_grad, carry, consts):
    channels = mixed_grad.shape[1]
    pairs = channels // LANES
    rows = span * BLOCK

    def tokens(width):
        return pl.BlockSpec((BLOCK, width), lambda k: (start + span - 1 - k, 0))

    def own(width, first=0):
        return pl.BlockSpec((BLOCK, width), lambda k: (first + span - 1 - k, 0))

    def shape(*dims):
        return jax.ShapeDtypeStruct(dims, f32)

    sums = [shape(8, channels), shape(8, 2 * STATE), shape(8, LANES)]
    ends = [jax.ShapeDtypeStruct(c.shape, f32) for c in carry]
    return pl.pallas_call(
        scan_back_kernel,
        grid=(span,),
        in_specs=[
            tokens(channels), tokens(2 * STATE), tokens(LANES), own(channels, at),
            own(2 * STATE, at), own(channels, at),
            pl.BlockSpec((1, pairs, LANES, STATE), lambda k: (at + span - 1 - k, 0, 0, 0)), tokens(channels),
        ] + [whole(c) for c in carry] + [whole(c) for c in consts],
        out_specs=[own(channels), own(2 * STATE), own(LANES)] + [whole(c) for c in sums + ends],
        out_shape=[
            jax.ShapeDtypeStruct((rows, channels), bf16), shape(rows, 2 * STATE),
            jax.ShapeDtypeStruct((rows, LANES), bf16),
        ] + sums + ends,
        scratch_shapes=[
            pltpu.VMEM((BLOCK + 8, channels), f32), pltpu.VMEM((BLOCK + 8, 2 * STATE), f32),
            pltpu.VMEM((BLOCK, BLOCK), f32), pltpu.VMEM((BLOCK, channels), f32), pltpu.VMEM((BLOCK, channels), f32),
        ],
        compiler_params=params(LIM_SCAN_BACK),
        cost_estimate=little,
        name="scan_back",
    )(*projections, *kept, mixed_grad, *carry, *consts)


def fixed_block(*shape):
    zeros = (0,) * len(shape)
    return pl.BlockSpec(shape, lambda n, *_: zeros)


def call(kernel, places, steps, operands, in_specs, out_specs, out_shape, name, scratch=(), aliases={}):
    return pl.pallas_call(
        kernel,
        grid_spec=pltpu.PrefetchScalarGridSpec(
            num_scalar_prefetch=1, grid=(steps,), in_specs=in_specs, out_specs=out_specs, scratch_shapes=list(scratch)
        ),
        out_shape=out_shape,
        input_output_aliases=aliases,
        compiler_params=params(61),
        cost_estimate=little,
        name=name,
    )(places, *operands)


def lay(places, pieces, result, first=0):
    for i, piece in enumerate(pieces):
        result[pl.ds(pl.multiple_of(places[first + i], 16), piece.shape[0]), :] = piece[...]


TILE = 256


def tile_columns(ref, n, first=0):
    return ref[:, pl.ds(pl.multiple_of(n * TILE + first, LANES), TILE)]


def first_project(weights, tokens, places, channels):
    count = len(weights)
    depth, width = tokens[0].shape[1], weights[0].shape[1]
    rows = tokens[0].shape[0] * len(tokens)

    def kernel(places, *refs):
        pieces, (normed, full, tail_proj) = refs[:-3], refs[-3:]
        lay(places, pieces[:count], full)
        lay(places, pieces[count:], normed, count)
        tail_proj[...] = dot(normed[...], full[:, channels:], ((1,), (0,)))

    return call(
        kernel, places, 1, (*weights, *tokens), [fixed_block(*piece.shape) for piece in (*weights, *tokens)],
        [fixed_block(rows, depth), fixed_block(depth, width), fixed_block(rows, width - channels)],
        [
            jax.ShapeDtypeStruct((rows, depth), bf16), jax.ShapeDtypeStruct((depth, width), bf16),
            jax.ShapeDtypeStruct((rows, width - channels), f32),
        ],
        "first_project",
    )


def input_project(places, normed, first_full, channels):
    rows, depth = normed.shape

    def kernel(places, left, right, result):
        result[...] = dot(left[...], right[...], ((1,), (0,)))

    return call(
        kernel, places, channels // TILE, (normed, first_full),
        [fixed_block(rows, depth), pl.BlockSpec((depth, TILE), lambda n, _: (0, n))],
        pl.BlockSpec((rows, TILE), lambda n, _: (0, n)), jax.ShapeDtypeStruct((rows, channels), f32), "input_project",
    )


def second_project(weights, places, normed, cot, mixed, gain):
    count, halves = len(weights), len(mixed)
    width = weights[0].shape[1]
    rows, depth = normed.shape
    channels = width // 2
    part_rows = mixed[0].shape[0]

    def kernel(places, *refs):
        pieces, (normed_ref, cot_ref, gain_ref), mixed_refs = refs[:count], refs[count : count + 3], refs[count + 3 : -4]
        full, gate_proj, out_grad, sums = refs[-4:]
        n = pl.program_id(0)

        @pl.when(n == 0)
        def _():
            lay(places, pieces, full)
            sums[...] = jnp.zeros(sums.shape, f32)

        gate_proj[...] = dot(normed_ref[...], tile_columns(full, n), ((1,), (0,)))
        out_grad[...] = dot(cot_ref[...], tile_columns(full, n, channels), ((1,), (0,)))
        ones = jnp.ones((8, TILE), f32)
        for i in range(halves):
            at = slice(i * part_rows, (i + 1) * part_rows)
            proj = gate_proj[at, :]
            gated = mixed_refs[i][...] * (proj * sigmoid(proj))
            pulled = out_grad[at, :] * gain_ref[...] * gated
            sums[0:8, at] += dot(ones, gated * gated, ((1,), (1,)), highest)
            sums[8:16, at] += dot(ones, pulled, ((1,), (1,)), highest)

    tile = pl.BlockSpec((rows, TILE), lambda n, _: (0, n))
    return call(
        kernel, places, channels // TILE, (*weights, normed, cot, gain, *mixed),
        [fixed_block(*piece.shape) for piece in (*weights, normed, cot)]
        + [pl.BlockSpec((1, TILE), lambda n, _: (0, n))]
        + [pl.BlockSpec((part_rows, TILE), lambda n, _: (0, n)) for _ in mixed],
        [fixed_block(depth, width), tile, tile, fixed_block(16, rows)],
        [
            jax.ShapeDtypeStruct((depth, width), bf16), jax.ShapeDtypeStruct((rows, channels), f32),
            jax.ShapeDtypeStruct((rows, channels), f32), jax.ShapeDtypeStruct((16, rows), f32),
        ],
        "second_project",
    )


def store_shares(places, product, result, tops, part, columns):
    owners, rows = result.shape[0], result.shape[2] - 16
    for owner in range(owners):
        own = product[owner * rows : (owner + 1) * rows]
        result[places[owner], part, 0:rows, columns] = own
        top = jnp.max(jnp.abs(own), axis=0, keepdims=True)
        result[places[owner], part, rows : rows + 16, columns] = jnp.zeros((16, own.shape[1]), f32)
        tops[places[owner], part, :, columns] = jnp.broadcast_to(top, (8, own.shape[1]))


def gate_step(ring, places, sums, gain, mixed, gate_proj, out_grad, cot_t, normed_t, second_full, inner_total):
    depth = second_full.shape[0]
    rows, channels = gate_proj.shape
    halves, part_rows = len(mixed), mixed[0].shape[0]
    share = cot_t.shape[0] // ring.count

    def kernel(places, *refs):
        sums_ref, gain_ref, proj_ref, grad_ref, cot_ref, normed_ref, weight_ref = refs[:7]
        mixed_refs, (branch, gate_grad, mixed_grad, gain_sum, result, tops, gate_out) = refs[7 : 7 + halves], refs[7 + halves :]
        gain_sum[...] = jnp.zeros(gain_sum.shape, f32)
        scale_row = lax.rsqrt(sums_ref[0:8, :] / inner_total + epsilon)
        pull_row = scale_row * scale_row * scale_row * (sums_ref[8:16, :] / inner_total)
        scales, pulls = scale_row.T, pull_row.T
        for i in range(halves):
            at = slice(i * part_rows, (i + 1) * part_rows)
            proj, rows_mixed, grad = proj_ref[at, :], mixed_refs[i][...], grad_ref[at, :]
            sig = sigmoid(proj)
            act = proj * sig
            gated = rows_mixed * act
            scale = scales[at, 0:1]
            scaled = gated * scale
            gate_out[at, :] = (scaled * gain_ref[...]).astype(bf16)
            gain_sum[0:1, :] += jnp.sum(grad * scaled, axis=0, keepdims=True)
            gated_grad = scale * (grad * gain_ref[...]) - gated * pulls[at, 0:1]
            mixed_grad[at, :] = gated_grad * act
            gate_grad[at, :] = (gated_grad * rows_mixed * (sig * (1.0 + proj * (1.0 - sig)))).astype(bf16)
        everything = slice(0, TILE)
        first = pl.program_id(0) == 0
        for i in range(0, rows, TILE):
            at = slice(i, i + TILE)
            share_out = dot(gate_out[at, :], weight_ref[...], ((1,), (1,)))
            branch[at, :] = share_out + jnp.where(first, 0.0, branch[at, :])
        store_shares(places, dot(cot_ref[...], gate_out[...], ((1,), (0,))), result, tops, 0, everything)
        store_shares(places, dot(normed_ref[...], gate_grad[...], ((1,), (0,))), result, tops, 1, everything)

    tile = pl.BlockSpec((rows, TILE), lambda n, _: (0, n))
    return call(
        kernel, places, channels // TILE, (sums, gain, gate_proj, out_grad, cot_t, normed_t, second_full, *mixed),
        [
            fixed_block(16, rows), pl.BlockSpec((1, TILE), lambda n, _: (0, n)), tile, tile,
            fixed_block(*cot_t.shape), fixed_block(*normed_t.shape),
            pl.BlockSpec((depth, TILE), lambda n, _: (0, channels // TILE + n)),
        ] + [pl.BlockSpec((part_rows, TILE), lambda n, _: (0, n)) for _ in mixed],
        [
            fixed_block(rows, depth), tile, tile, pl.BlockSpec((8, TILE), lambda n, _: (0, n)),
            pl.BlockSpec((ring.count, 2, share + 16, TILE), lambda n, _: (0, 0, 0, n)),
            pl.BlockSpec((ring.count, 2, 8, TILE), lambda n, _: (0, 0, 0, n)),
        ],
        [
            jax.ShapeDtypeStruct((rows, depth), f32), jax.ShapeDtypeStruct((rows, channels), bf16),
            jax.ShapeDtypeStruct((rows, channels), f32), jax.ShapeDtypeStruct((8, channels), f32),
            jax.ShapeDtypeStruct((ring.count, 2, share + 16, channels), f32),
            jax.ShapeDtypeStruct((ring.count, 2, 8, channels), f32),
        ],
        "gate_step", [pltpu.VMEM((rows, TILE), bf16)],
    )


def input_partials(ring, places, normed_t, input_back):
    halves, (part_rows, channels) = len(input_back), input_back[0].shape
    share = normed_t.shape[0] // ring.count

    def kernel(places, left, *refs):
        rights, result, tops = refs[:-2], refs[-2], refs[-1]
        product = dot(left[:, 0:part_rows], rights[0][...], ((1,), (0,)))
        for i in range(1, halves):
            product = product + dot(left[:, i * part_rows : (i + 1) * part_rows], rights[i][...], ((1,), (0,)))
        store_shares(places, product, result, tops, 0, slice(0, TILE))

    def block(rows):
        return pl.BlockSpec((ring.count, 1, rows, TILE), lambda n, _: (0, 0, 0, n))

    return call(
        kernel, places, channels // TILE, (normed_t, *input_back),
        [fixed_block(*normed_t.shape)] + [pl.BlockSpec((part_rows, TILE), lambda n, _: (0, n)) for _ in input_back],
        [block(share + 16), block(8)],
        [jax.ShapeDtypeStruct((ring.count, 1, rows, channels + LANES), f32) for rows in (share + 16, 8)],
        "input_partials",
    )


def tail_partials(places, normed_t, tail, parts, tops):
    def kernel(places, left, right, parts_in, tops_in, result, tops_out):
        product = dot(left[...], right[...], ((1,), (0,)))
        store_shares(places, product, result, tops_out, 0, slice(0, LANES))

    last = parts.shape[3] // LANES - 1
    specs = [pl.BlockSpec((*array.shape[:3], LANES), lambda n, _: (0, 0, 0, last)) for array in (parts, tops)]
    anywhere = pl.BlockSpec(memory_space=pl.ANY)
    return call(
        kernel, places, 1, (normed_t, tail, parts, tops),
        [fixed_block(*normed_t.shape), fixed_block(*tail.shape), anywhere, anywhere], specs,
        [jax.ShapeDtypeStruct(array.shape, f32) for array in (parts, tops)], "tail_partials", aliases={3: 0, 4: 1},
    )


def normed_kernel(halves, places, gate_rows, tail_rows, gate_tile, input_tile, tail_tile, *refs):
    inputs, results, product = refs[:halves], refs[halves:-1], refs[-1]
    part = inputs[0].shape[0]
    for i, input_rows in enumerate(inputs):
        at = slice(i * part, (i + 1) * part)
        total = dot(gate_rows[at, :], gate_tile[...], ((1,), (1,)))
        total = total + dot(tail_rows[at, :], tail_tile[...], ((1,), (1,)))
        product[at, :] = total + dot(input_rows[...], input_tile[...], ((1,), (1,)))
    rows = results[0].shape[0]
    for i, result in enumerate(results):
        result[...] = product[pl.ds(pl.multiple_of(places[i] * rows, 16), rows), :]


def normed_parts(places, gate_grad, input_back, tail, second_full, first_full):
    count = lax.axis_size("tensor")
    tokens, channels = gate_grad.shape
    width, tile = first_full.shape[0], 2 * LANES
    halves = len(input_back)

    def fixed(n, _):
        return (0, 0)

    return pl.pallas_call(
        lambda *refs: normed_kernel(halves, *refs),
        grid_spec=pltpu.PrefetchScalarGridSpec(
            num_scalar_prefetch=1, grid=(width // tile,),
            in_specs=[
                pl.BlockSpec((tokens, channels), fixed), pl.BlockSpec((tokens, LANES), fixed),
                pl.BlockSpec((tile, channels), lambda n, _: (n, 0)), pl.BlockSpec((tile, channels), lambda n, _: (n, 0)),
                pl.BlockSpec((tile, LANES), lambda n, _: (n, channels // LANES)),
            ] + [pl.BlockSpec(half.shape, fixed) for half in input_back],
            out_specs=[pl.BlockSpec((tokens // count, tile), lambda n, _: (0, n))] * count,
            scratch_shapes=[pltpu.VMEM((tokens, tile), f32)],
        ),
        out_shape=[jax.ShapeDtypeStruct((tokens // count, width), f32)] * count,
        compiler_params=params(LIM_NORMED_PARTS),
        cost_estimate=little,
        name="normed_parts",
    )(places, gate_grad, tail, second_full, first_full, first_full, *input_back)


def cycle(count):
    return list(range(0, count, 2)) + list(range(count - 1, 0, -2))


def table(numbers):
    return jnp.stack(numbers).astype(jnp.int32)


class Ring:
    def __init__(self):
        self.count = lax.axis_size("dp")
        order = cycle(self.count)
        self.up = [(order[i], order[(i + 1) % self.count]) for i in range(self.count)]
        self.down = [(b, a) for a, b in self.up]
        me = lax.axis_index("dp")
        self.place = jnp.where(me % 2 == 0, me // 2, self.count - 1 - me // 2)

    def places(self):
        order = cycle(self.count)
        return table([(order.index(i) - self.place + self.count) % self.count for i in range(self.count)])

    def owner(self, offset):
        place = (self.place + offset + self.count) % self.count
        return jnp.where(place < self.count // 2, 2 * place, 2 * (self.count - 1 - place) + 1)


def middle(rows):
    return (rows // 2 + 15) // 16 * 16


class Gather:
    def __init__(self, ring, shard):
        self.ring, self.shard, self.step = ring, shard, 0
        self.held = [(shard, 0, 0)]
        self.last = (shard, shard)

    def hop(self):
        self.step += 1
        half, cut = self.ring.count // 2, middle(self.shard.shape[0])
        up, down = self.last
        offsets = ((-self.step, 0), (self.step, 0))
        if self.step == half:
            up, down = up[:cut], down[cut:]
            offsets = ((half, 0), (half, cut))
        self.last = (lax.ppermute(up, "dp", self.ring.up), lax.ppermute(down, "dp", self.ring.down))
        self.held += [(piece, *offset) for piece, offset in zip(self.last, offsets)]

    def after(self, *marks):
        self.last, marks = fence(self.last, marks)
        self.held[-2:] = [(piece, *old[1:]) for piece, old in zip(self.last, self.held[-2:])]
        return marks if len(marks) > 1 else marks[0]

    def pieces(self):
        return [piece for piece, _, _ in self.held]

    def places(self):
        rows, half = self.shard.shape[0], self.ring.count // 2
        spots = [self.ring.owner(0) * rows]
        for step in range(1, half):
            spots += [self.ring.owner(-step) * rows, self.ring.owner(step) * rows]
        return spots + [self.ring.owner(half) * rows, self.ring.owner(half) * rows + middle(rows)]


def encode(rows, limit):
    power = jnp.ceil(jnp.log2(jnp.maximum(limit, 1e-30)))
    ours = lax.broadcasted_iota(jnp.int32, rows.shape, 1) < rows.shape[1] - 16
    return jnp.where(ours, rows * jnp.exp2(15.0 - power), power).astype(jnp.float16)


def decode(payload):
    power = payload[:, -16:-15].astype(f32)
    return payload.astype(f32) * jnp.exp2(power - 15.0), jnp.exp2(power)


class Scatter:
    def __init__(self, ring, parts, tops):
        self.ring, self.parts, self.tops = ring, parts, tops
        self.step = ring.count // 2
        self.rows = parts.shape[2] - 16
        self.cut = middle(self.rows)
        far = parts[self.step]
        top = tops[self.step, :, 0:1]
        upper = jnp.concatenate([far[:, : self.cut], far[:, -16:]], axis=1)
        self.send = (encode(upper, top), encode(far[:, self.cut :], top))

    def hop(self):
        self.send = fence(*self.send)
        self.got = (lax.ppermute(self.send[0], "dp", self.ring.up), lax.ppermute(self.send[1], "dp", self.ring.down))

    def after(self, *marks):
        self.got, marks = fence(self.got, marks)
        return marks if len(marks) > 1 else marks[0]

    def before(self, *marks):
        self.send, marks = fence(self.send, marks)
        return marks if len(marks) > 1 else marks[0]

    def add(self):
        first = self.step == self.ring.count // 2
        self.got = fence(*self.got)
        (up, up_top), (down, down_top) = (decode(g) for g in self.got)
        if first:
            up = jnp.pad(up, ((0, 0), (0, self.rows - self.cut), (0, 0)))
            down = jnp.pad(down, ((0, 0), (self.cut, 0), (0, 0)))
            up = jnp.where(lax.broadcasted_iota(jnp.int32, up.shape, 1) < self.cut, up, 0.0)
        self.step -= 1
        if self.step == 0:
            return (self.parts[0] + up + down)[:, : self.rows]
        above, below = self.parts[self.step], self.parts[self.ring.count - self.step]
        self.send = (
            encode(above + up, self.tops[self.step, :, 0:1] + up_top),
            encode(below + down, self.tops[self.ring.count - self.step, :, 0:1] + down_top),
        )
        return None


def fence(*arrays):
    flat, tree = jax.tree.flatten(arrays)
    return jax.tree.unflatten(tree, lax.optimization_barrier(flat))


def across(array, bit, axis="tensor"):
    count = lax.axis_size(axis)
    return lax.ppermute(array, axis, [(i, i ^ bit) for i in range(count)])


def group_sum(array, axis, first, count):
    terms = [array] + [across(array, first * other, axis) for other in range(1, count)]
    while len(terms) > 1:
        terms = [terms[i] + terms[i + 1] for i in range(0, len(terms), 2)]
    return terms[0]


def cube_sum(array, axis):
    bit = 1
    while bit < lax.axis_size(axis):
        array = array + across(array, bit, axis)
        bit *= 2
    return array


def shards(
    block_input, cotangent, norm_gain, gate_weight, input_weight, state_weight, step_weight, conv_input,
    conv_input_bias, conv_state, conv_state_bias, step_bias, decay_log, skip_scale, gate_gain, out_weight,
):
    group_count = lax.axis_size("tensor")
    me = lax.axis_index("tensor")
    ring = Ring()
    half = ring.count // 2
    local_rows = block_input.shape[0]
    channels = gate_gain.shape[0]
    heads = step_bias.shape[0]
    inner_total = channels * group_count
    share = 2 * STATE // group_count
    tokens = local_rows * group_count
    blocks = tokens // BLOCK
    fold = LANES // share
    folded = tokens // fold
    rows_dot = ((1,), (0,))
    back_dot = ((1,), (1,))

    state_mine = lax.dynamic_slice_in_dim(state_weight, me * share, share, 1)
    first = Gather(
        ring,
        jnp.concatenate(
            [input_weight, state_mine, jnp.pad(step_weight, ((0, 0), (0, LANES - share - heads)))], axis=1
        ).astype(bf16),
    )
    first.hop()
    row_scale = lax.rsqrt(jnp.mean(block_input * block_input, axis=1, keepdims=True) + epsilon)
    normed = (block_input * row_scale * norm_gain).astype(bf16)
    second_weight = jnp.concatenate([gate_weight, out_weight.T], axis=1).astype(bf16)
    rates = -jnp.exp(decay_log)

    def per_head(vector):
        return jnp.pad(vector, (0, LANES - heads))[None, :]

    skip = jnp.repeat(skip_scale, HEAD_DIM)[None, :]
    head_of = (
        lax.broadcasted_iota(jnp.int32, (channels, LANES), 0) // HEAD_DIM
        == lax.broadcasted_iota(jnp.int32, (channels, LANES), 1)
    ).astype(f32)
    scan_consts = (
        conv_input, conv_input_bias[None, :], conv_state, conv_state_bias[None, :], per_head(step_bias),
        per_head(rates), skip,
    )
    back_consts = (conv_input, conv_state, per_head(step_bias), per_head(rates), skip, head_of)
    carried = jnp.zeros((channels // LANES, LANES, STATE), f32)
    carry = (jnp.zeros((8, channels), f32), jnp.zeros((8, 2 * STATE), f32), carried, jnp.zeros((8, LANES), f32))
    gain = gate_gain[None, :]
    shard_places = first.places()
    token_places = [(me ^ bits) * local_rows for bits in range(4)]
    tables = (table(shard_places + token_places), table(shard_places), ring.places(), table([i ^ me for i in range(4)]))
    normed, scan_consts, back_consts, carried, carry, gain, tables = first.after(
        normed, scan_consts, back_consts, carried, carry, gain, tables
    )
    first_places, second_places, share_places, turn_places = tables
    first.hop()
    far, near = across(normed, 2), across(normed, 1)
    for _ in range(half - 3):
        first.hop()
    far, near, second_weight, cot_low = first.after(far, near, second_weight, cotangent.astype(bf16))
    first.hop()
    second_weight = first.after(second_weight)
    normed_pieces = (normed, near, far, across(far, 1))
    second = Gather(ring, second_weight)
    second.hop()
    normed_all, first_full, tail_proj = first_project(first.pieces(), normed_pieces, first_places, channels)
    step_proj = jnp.pad(tail_proj[:, share : share + heads], ((0, 0), (0, LANES - heads)))
    state_mine = jnp.concatenate([tail_proj[i * folded : (i + 1) * folded, :share] for i in range(fold)], axis=1)
    normed_all, state_mine = fence(normed_all, state_mine)
    far = across(state_mine, 2)
    input_proj, far, cot_low = second.after(input_project(share_places, normed_all, first_full, channels), far, cot_low)
    second.hop()
    cot_all = lax.all_gather(cot_low, "tensor", axis=0, tiled=True)
    same_x, same_core, diagonal = across(state_mine, 1), far, across(far, 1)
    right_core = me % 2 == 1
    near = (jnp.where(right_core, same_x, state_mine), jnp.where(right_core, state_mine, same_x))
    away = (jnp.where(right_core, diagonal, same_core), jnp.where(right_core, same_core, diagonal))
    right_chip = me // 2 == 1
    state_parts = [jnp.where(right_chip, away[i], near[i]) for i in range(2)]
    state_parts += [jnp.where(right_chip, near[i], away[i]) for i in range(2)]
    state_proj = jnp.concatenate(
        [jnp.concatenate([p[:, i * share : (i + 1) * share] for p in state_parts], axis=1) for i in range(fold)], axis=0
    )
    span = 2
    scanned, mixed = [], []
    for start in range(0, blocks, span):
        scanned.append(run_scan(start, span, input_proj, state_proj, step_proj, carry[:2], carried, scan_consts))
        carried = scanned[-1][4]
        mixed.append(scanned[-1][0])
        if second.step < half:
            carried, mixed[-1] = second.after(carried, mixed[-1])
            second.hop()
    while second.step < half:
        second.hop()
    second_full, gate_proj, gate_out_grad, sums = second_project(
        second.pieces(), second_places, normed_all, cot_all, mixed, gain
    )
    sums = (sums + across(sums, 1)) + (across(sums, 2) + across(sums, 3))
    normed_t = normed_all.T
    branch_part, gate_grad, mixed_grad, gain_sum, *pair_parts = gate_step(
        ring, share_places, sums, gain, mixed, gate_proj, gate_out_grad, cot_all.T, normed_t, second_full,
        float(inner_total),
    )
    pair_ring = Scatter(ring, *pair_parts)
    done = []
    for turn in range(blocks // span):
        if turn == 0:
            carry, branch_part = pair_ring.before(carry, branch_part)
            pair_ring.hop()
            branch = lax.psum_scatter(branch_part, "tensor", scatter_dimension=0, tiled=True)
        else:
            carry = pair_ring.after(carry)
            pair_ring.add()
            carry = pair_ring.before(carry)
            pair_ring.hop()
        start = blocks - span * (turn + 1)
        kept = scanned[start // span]
        kept = [kept[1], kept[2], kept[0], kept[3]]
        result = run_scan_back(
            start, span, (input_proj, state_proj, step_proj), kept, 0, mixed_grad, carry, back_consts
        )
        done.insert(0, result)
        carry = tuple(result[6:])
    done = pair_ring.after(done)
    pair_ring.add()
    done = pair_ring.before(done)
    pair_ring.hop()
    input_back, state_back = [d[0] for d in done], [d[1] for d in done]
    step_back = jnp.concatenate([d[2] for d in done], axis=0)
    input_sums, state_sums, step_sums = (sum(d[i] for d in done) for i in range(3, 6))

    packed = jnp.concatenate(
        [
            state_sums[:5].reshape(-1),
            input_sums[:5].reshape(-1),
            gain_sum[0],
            jnp.sum(input_sums[5].reshape(heads, HEAD_DIM), axis=1),
            step_sums[0, :heads],
            step_sums[1, :heads] * rates,
        ]
    )
    packed = jnp.pad(packed, (0, -packed.shape[0] % LANES)).reshape(-1, LANES)

    def state_columns(index):
        return jnp.concatenate([lax.dynamic_slice_in_dim(rows, index * share, share, 1) for rows in state_back], axis=1)

    for_far, for_me = across(state_columns(me ^ 3), 1), across(state_columns(me ^ 1), 1)
    packed, for_far, for_me = fence(packed, for_far, for_me)
    far, input_back = fence(state_columns(me ^ 2) + for_far, input_back)
    from_far = across(far, 2)
    input_parts, from_far, pair_ring.got = fence(
        input_partials(ring, share_places, normed_t, input_back), from_far, pair_ring.got
    )
    pair_ring.add()
    from_far = pair_ring.before(from_far)
    pair_ring.hop()
    state_share = (state_columns(me) + for_me + from_far).astype(bf16)
    state_share = jnp.concatenate([state_share[:, i * share : (i + 1) * share] for i in range(fold)], axis=0)
    tail = jnp.concatenate(
        [state_share, step_back[:, :heads], jnp.zeros((tokens, LANES - share - heads), bf16)], axis=1
    )
    parts = normed_parts(turn_places, gate_grad, input_back, tail, second_full, first_full)
    branch, *parts = pair_ring.after(branch, *parts)
    block_output = block_input + branch
    for_far, for_me = across(parts[3], 1), across(parts[1], 1)
    input_parts = tail_partials(share_places, normed_t, tail, *input_parts)
    input_ring = Scatter(ring, *input_parts)
    for_far, for_me = input_ring.before(for_far, for_me)
    input_ring.hop()
    sent = parts[2] + for_far
    sent = jnp.pad(sent, ((0, 16), (0, 0)))[None]
    from_far = across(encode(sent, jnp.max(jnp.abs(sent), axis=1, keepdims=True)), 2)
    input_sum = input_ring.add()
    pair_sum = pair_ring.add()
    while pair_sum is None:
        pair_ring.hop()
        pair_sum = pair_ring.add()
    while input_sum is None:
        input_ring.hop()
        if input_ring.step == 1:
            from_far = input_ring.after(from_far)
        input_sum = input_ring.add()
    normed_grad = parts[0] + for_me + decode(from_far)[0][0, :local_rows]
    input_sum = input_sum[0]
    tail_sum = input_sum[:, channels:]

    weighted_grad = normed_grad * norm_gain
    norm_gain_part = jnp.sum(normed_grad * block_input * row_scale, axis=0)
    input_grad = (
        cotangent
        + row_scale * weighted_grad
        - block_input * row_scale**3 * jnp.mean(weighted_grad * block_input, axis=1, keepdims=True)
    )
    mine = tail_sum[:, :share]
    other = across(mine, 1)
    pair = jnp.concatenate([jnp.where(right_core, other, mine), jnp.where(right_core, mine, other)], axis=1)
    state_rows = 10 * STATE // LANES
    shared = jnp.concatenate([norm_gain_part.reshape(-1, LANES), packed[:state_rows]], axis=0)
    shared = group_sum(shared, "tensor", 1, group_count)
    shared, pair = fence(shared, pair)
    other = across(pair, 2)
    packed = jnp.concatenate([shared, packed[state_rows:]], axis=0)
    packed, other = fence(group_sum(packed, "dp", 2, half), other)
    packed = group_sum(packed, "dp", 1, 2)
    state_grad = jnp.concatenate([jnp.where(right_chip, other, pair), jnp.where(right_chip, pair, other)], axis=1)
    local = packed[shared.shape[0] :].reshape(-1)
    norm_gain_grad = packed[: shared.shape[0] - state_rows].reshape(-1)
    state_sum = packed[shared.shape[0] - state_rows : shared.shape[0]].reshape(5, 2 * STATE)
    at = 6 * channels
    return (
        block_output,
        input_grad,
        norm_gain_grad,
        pair_sum[1],
        input_sum[:, :channels],
        state_grad,
        tail_sum[:, share : share + heads],
        local[: 4 * channels].reshape(4, channels),
        local[4 * channels : 5 * channels],
        state_sum[:4],
        state_sum[4],
        local[at + heads : at + 2 * heads],
        local[at + 2 * heads : at + 3 * heads],
        local[at : at + heads],
        local[5 * channels : at],
        pair_sum[0].T,
    )


def solution(mesh):
    rows = P(("dp", "tensor"), None)
    both = P("dp", "tensor")
    inner = P("tensor")
    return jax.shard_map(
        shards,
        mesh=mesh,
        in_specs=(
            rows, rows, P(), both, both, P("dp", None), both, P(None, "tensor"), inner, P(), P(), inner, inner,
            inner, inner, P("tensor", "dp"),
        ),
        out_specs=(
            rows, rows, P(), both, both, P("dp", None), both, P(None, "tensor"), inner, P(), P(), inner, inner,
            inner, inner, P("tensor", "dp"),
        ),
        check_vma=False,
    )
```

```python
import jax
import jax.numpy as jnp
from jax import lax
from jax.experimental import pallas as pl
from jax.experimental.pallas import tpu as pltpu
from jax.sharding import PartitionSpec as P

HEAD_DIM = 64
STATE = 128
BLOCK = 256
SEQ = 1024
LANES = 128

LIM_SCAN = 61
LIM_SCAN_BACK = 61
LIM_NORMED_PARTS = 61

epsilon = 1e-05
high = lax.Precision.HIGH
highest = lax.Precision.HIGHEST
f32 = jnp.float32
bf16 = jnp.bfloat16


def dot(left, right, dims, precision=None):
    return lax.dot_general(
        left, right, (dims, ((), ())), precision=precision, preferred_element_type=f32
    )


def sigmoid(v):
    return 1.0 / (1.0 + jnp.exp(-v))


def softplus(v):
    return jnp.maximum(v, 0.0) + jnp.log1p(jnp.exp(-jnp.abs(v)))


def iota(shape, axis):
    return lax.broadcasted_iota(jnp.int32, shape, axis)


def split(v):
    high_half = v.astype(bf16).astype(f32)
    return high_half, v - high_half


def packed(mine, first, second):
    return jnp.where(mine, first, pltpu.roll(second, HEAD_DIM, 1)).astype(bf16)


def meet(left, right, mine):
    (left_high, left_low), (right_high, right_low) = left, right
    lefts = [packed(mine, left_high, left_low), jnp.where(mine, left_high, 0.0).astype(bf16)]
    rights = [packed(mine, right_high, right_high), jnp.where(mine, right_low, 0.0).astype(bf16)]
    return dot(jnp.concatenate(lefts, axis=1), jnp.concatenate(rights, axis=1), ((1,), (1,)))


def pair_columns(table, pair):
    lane = iota((table.shape[0], LANES), 1)
    return jnp.where(lane < HEAD_DIM, table[:, 2 * pair : 2 * pair + 1], table[:, 2 * pair + 1 : 2 * pair + 2])


def decay_tables(step_rows, step_bias, rates):
    step_size = softplus(step_rows + step_bias)
    earlier = (iota((BLOCK, BLOCK), 0) >= iota((BLOCK, BLOCK), 1)).astype(f32)
    cumulative = dot(earlier, step_size * rates, ((1,), (0,)), highest)
    return step_size, cumulative, jnp.exp(cumulative), jnp.exp(cumulative[BLOCK - 1 : BLOCK, :] - cumulative)


def state_decay(from_start, pair):
    last = from_start[BLOCK - 1 : BLOCK, :]
    row = iota((LANES, STATE), 0)
    return jnp.where(row < HEAD_DIM, last[:, 2 * pair : 2 * pair + 1], last[:, 2 * pair + 1 : 2 * pair + 2])


def shifted_conv(rows_ref, before, buffer, taps, conv_bias, first):
    @pl.when(first)
    def _():
        buffer[0:8, :] = before[...]

    @pl.when(jnp.logical_not(first))
    def _():
        buffer[0:8, :] = buffer[BLOCK : BLOCK + 8, :]

    buffer[8 : BLOCK + 8, :] = rows_ref[...]
    total = conv_bias[...] + taps[0:1, :] * buffer[8 : BLOCK + 8, :]
    for tap in range(1, 4):
        total = total + taps[tap : tap + 1, :] * buffer[8 - tap : BLOCK + 8 - tap, :]
    return total


def scan_kernel(
    input_rows, state_rows, step_rows, input_before, state_before, state_entering,
    conv_input, conv_input_bias, conv_state, conv_state_bias, step_bias, rates, skip,
    mixed, input_conv, state_conv, entering, carried, input_buffer, state_buffer,
):
    first = pl.program_id(0) == 0
    pairs = input_rows.shape[1] // LANES

    @pl.when(first)
    def _():
        carried[...] = state_entering[...]

    input_conv[...] = shifted_conv(input_rows, input_before, input_buffer, conv_input, conv_input_bias, first)
    state_pre = shifted_conv(state_rows, state_before, state_buffer, conv_state, conv_state_bias, first)
    state_conv[...] = state_pre
    state_act = state_pre * sigmoid(state_pre)
    writes, reads = state_act[:, :STATE], state_act[:, STATE:]
    meeting = dot(reads, writes, ((1,), (1,)), high)
    step_size, cumulative, from_start, to_end = decay_tables(step_rows[...], step_bias[...], rates[...])
    cumulative_t = cumulative.T
    causal = iota((BLOCK, BLOCK), 0) >= iota((BLOCK, BLOCK), 1)
    lane = iota((BLOCK, LANES), 1)
    for pair in range(pairs):
        columns = slice(pair * LANES, pair * LANES + LANES)
        pre = input_conv[:, columns]
        inputs = pre * sigmoid(pre)
        weighted = inputs * pair_columns(step_size, pair)
        state_in = carried[pair]
        entering[0, pair] = state_in
        out = dot(reads, state_in, ((1,), (1,)), high) * pair_columns(from_start, pair)
        for side in range(2):
            head = 2 * pair + side
            gap = cumulative[:, head : head + 1] - cumulative_t[head : head + 1, :]
            mixing = jnp.exp(jnp.where(causal, gap, -1e30)) * meeting
            mine = (lane < HEAD_DIM) if side == 0 else (lane >= HEAD_DIM)
            out = out + dot(mixing, jnp.where(mine, weighted, 0.0), ((1,), (0,)), high)
        fresh = dot(weighted * pair_columns(to_end, pair), writes, ((0,), (0,)), high)
        carried[pair] = state_decay(from_start, pair) * state_in + fresh
        mixed[:, columns] = out + skip[:, columns] * inputs


def scan_back_kernel(
    input_rows, state_rows, step_rows, input_conv, state_conv, mixed, entering, mixed_grad,
    input_after, state_after, state_leaving, decay_after,
    conv_input, conv_state, step_bias, rates, skip, head_of,
    input_grad, state_grad, step_grad, input_sums, state_sums, step_sums, input_first, state_first, carried, later,
    input_buffer, state_buffer, gap_grad, out_products, in_products,
):
    first = pl.program_id(0) == 0
    pairs = input_rows.shape[1] // LANES

    @pl.when(first)
    def _():
        carried[...] = state_leaving[...]
        later[...] = decay_after[...]
        input_sums[...] = jnp.zeros(input_sums.shape, f32)
        state_sums[...] = jnp.zeros(state_sums.shape, f32)
        step_sums[...] = jnp.zeros(step_sums.shape, f32)
        input_buffer[BLOCK : BLOCK + 8, :] = input_after[...]
        state_buffer[BLOCK : BLOCK + 8, :] = state_after[...]

    @pl.when(jnp.logical_not(first))
    def _():
        input_buffer[BLOCK : BLOCK + 8, :] = input_buffer[0:8, :]
        state_buffer[BLOCK : BLOCK + 8, :] = state_buffer[0:8, :]

    state_pre = state_conv[...]
    state_sig = sigmoid(state_pre)
    state_act = state_pre * state_sig
    writes, reads = state_act[:, :STATE], state_act[:, STATE:]
    meeting_t = dot(writes, reads, ((1,), (1,)), high)
    step_size, cumulative, from_start, to_end = decay_tables(step_rows[...], step_bias[...], rates[...])
    cumulative_t = cumulative.T
    causal_t = iota((BLOCK, BLOCK), 0) <= iota((BLOCK, BLOCK), 1)
    lane = iota((BLOCK, LANES), 1)
    gap_grad[...] = jnp.zeros(gap_grad.shape, f32)
    writes_grad = jnp.zeros((BLOCK, STATE), f32)
    reads_grad = jnp.zeros((BLOCK, STATE), f32)
    for pair in range(pairs):
        columns = slice(pair * LANES, pair * LANES + LANES)
        pre = input_conv[:, columns]
        sig = sigmoid(pre)
        inputs = pre * sig
        step_pair = pair_columns(step_size, pair)
        weighted = inputs * step_pair
        out_grad = mixed_grad[:, columns]
        skip_product = out_grad * inputs
        input_sums[5:6, columns] += jnp.sum(skip_product, axis=0, keepdims=True)
        end_pair = pair_columns(to_end, pair)
        leaving_grad = carried[pair]
        weighted_grad = dot(writes, leaving_grad, ((1,), (1,)), high) * end_pair
        grad_halves, weighted_halves = split(out_grad), split(weighted)
        for side in range(2):
            head = 2 * pair + side
            gap = cumulative_t[head : head + 1, :] - cumulative[:, head : head + 1]
            within = jnp.exp(jnp.where(causal_t, gap, -1e30))
            mine = (lane < HEAD_DIM) if side == 0 else (lane >= HEAD_DIM)
            own_grad = jnp.where(mine, out_grad, 0.0)
            weighted_grad = weighted_grad + dot(within * meeting_t, own_grad, ((1,), (0,)), high)
            gap_grad[...] += within * meet(weighted_halves, grad_halves, mine)
        start_grad = out_grad * pair_columns(from_start, pair)
        reads_grad = reads_grad + dot(start_grad, entering[0, pair], ((1,), (0,)), high)
        writes_grad = writes_grad + dot(weighted * end_pair, leaving_grad, ((1,), (0,)), high)
        carried[pair] = state_decay(from_start, pair) * leaving_grad + dot(start_grad, reads, ((0,), (0,)), high)
        out_products[:, columns] = out_grad * mixed[:, columns] - skip[:, columns] * skip_product
        in_products[:, columns] = inputs * weighted_grad
        inputs_grad = skip[:, columns] * out_grad + step_pair * weighted_grad
        input_buffer[0:BLOCK, columns] = inputs_grad * (sig * (1.0 + pre * (1.0 - sig)))
    reads_grad = reads_grad + dot(gap_grad[...], writes, ((0,), (0,)), high)
    writes_grad = writes_grad + dot(gap_grad[...], reads, ((1,), (0,)), high)
    state_slope = state_sig * (1.0 + state_pre * (1.0 - state_sig))
    state_buffer[0:BLOCK, 0:STATE] = writes_grad * state_slope[:, :STATE]
    state_buffer[0:BLOCK, STATE : 2 * STATE] = reads_grad * state_slope[:, STATE:]

    for buffer, rows, taps, sums, result in (
        (input_buffer, input_rows, conv_input, input_sums, input_grad),
        (state_buffer, state_rows, conv_state, state_sums, state_grad),
    ):
        raw = rows[...]
        total = jnp.zeros(raw.shape, f32)
        for tap in range(4):
            ahead = buffer[tap : tap + BLOCK, :]
            total = total + taps[tap : tap + 1, :] * ahead
            sums[tap : tap + 1, :] += jnp.sum(ahead * raw, axis=0, keepdims=True)
        sums[4:5, :] += jnp.sum(buffer[0:BLOCK, :], axis=0, keepdims=True)
        result[...] = total.astype(result.dtype)
    input_first[...] = input_buffer[0:8, :]
    state_first[...] = state_buffer[0:8, :]

    out_head = dot(out_products[...], head_of[...], ((1,), (0,)), high)
    in_head = dot(in_products[...], head_of[...], ((1,), (0,)), high)
    upper = (iota((BLOCK, BLOCK), 0) <= iota((BLOCK, BLOCK), 1)).astype(f32)
    decay_grad = dot(upper, out_head - step_size * in_head, ((1,), (0,)), highest) + later[0:1, :]
    later[0:1, :] = decay_grad[0:1, :]
    step_sig = sigmoid(step_rows[...] + step_bias[...])
    step_back = (rates[...] * decay_grad + in_head) * step_sig
    step_grad[...] = step_back.astype(step_grad.dtype)
    step_sums[0:1, :] += jnp.sum(step_back, axis=0, keepdims=True)
    step_sums[1:2, :] += jnp.sum(step_size * decay_grad, axis=0, keepdims=True)


def whole(array):
    zeros = (0,) * array.ndim
    return pl.BlockSpec(array.shape, lambda k: zeros)


def params(mebibytes):
    return pltpu.CompilerParams(dimension_semantics=("arbitrary",), vmem_limit_bytes=mebibytes * 1024 * 1024)


little = pl.CostEstimate(flops=10**6, bytes_accessed=2**16, transcendentals=0)


def run_scan(start, span, input_rows, state_rows, step_rows, zeros, state_entering, consts):
    channels = input_rows.shape[1]
    pairs = channels // LANES
    rows = span * BLOCK
    edge = start * BLOCK // 8 - 1

    def tokens(width):
        return pl.BlockSpec((BLOCK, width), lambda k: (start + k, 0))

    def results(width):
        return pl.BlockSpec((BLOCK, width), lambda k: (k, 0))

    if start == 0:
        before = zeros
        before_specs = [whole(c) for c in before]
    else:
        before = (input_rows, state_rows)
        before_specs = [pl.BlockSpec((8, c.shape[1]), lambda k: (edge, 0)) for c in before]
    return pl.pallas_call(
        scan_kernel,
        grid=(span,),
        in_specs=[tokens(channels), tokens(2 * STATE), tokens(LANES)] + before_specs + [whole(state_entering)]
        + [whole(c) for c in consts],
        out_specs=[
            results(channels), results(channels), results(2 * STATE),
            pl.BlockSpec((1, pairs, LANES, STATE), lambda k: (k, 0, 0, 0)), whole(state_entering),
        ],
        out_shape=[
            jax.ShapeDtypeStruct((rows, channels), f32),
            jax.ShapeDtypeStruct((rows, channels), f32),
            jax.ShapeDtypeStruct((rows, 2 * STATE), f32),
            jax.ShapeDtypeStruct((span, pairs, LANES, STATE), f32),
            jax.ShapeDtypeStruct((pairs, LANES, STATE), f32),
        ],
        scratch_shapes=[pltpu.VMEM((BLOCK + 8, channels), f32), pltpu.VMEM((BLOCK + 8, 2 * STATE), f32)],
        compiler_params=params(LIM_SCAN),
        cost_estimate=little,
        name="scan",
    )(input_rows, state_rows, step_rows, *before, state_entering, *consts)


def run_scan_back(start, span, projections, kept, at, mixed_grad, carry, consts):
    channels = mixed_grad.shape[1]
    pairs = channels // LANES
    rows = span * BLOCK

    def tokens(width):
        return pl.BlockSpec((BLOCK, width), lambda k: (start + span - 1 - k, 0))

    def own(width, first=0):
        return pl.BlockSpec((BLOCK, width), lambda k: (first + span - 1 - k, 0))

    def shape(*dims):
        return jax.ShapeDtypeStruct(dims, f32)

    sums = [shape(8, channels), shape(8, 2 * STATE), shape(8, LANES)]
    ends = [jax.ShapeDtypeStruct(c.shape, f32) for c in carry]
    return pl.pallas_call(
        scan_back_kernel,
        grid=(span,),
        in_specs=[
            tokens(channels), tokens(2 * STATE), tokens(LANES), own(channels, at),
            own(2 * STATE, at), own(channels, at),
            pl.BlockSpec((1, pairs, LANES, STATE), lambda k: (at + span - 1 - k, 0, 0, 0)), tokens(channels),
        ] + [whole(c) for c in carry] + [whole(c) for c in consts],
        out_specs=[own(channels), own(2 * STATE), own(LANES)] + [whole(c) for c in sums + ends],
        out_shape=[
            jax.ShapeDtypeStruct((rows, channels), bf16), shape(rows, 2 * STATE),
            jax.ShapeDtypeStruct((rows, LANES), bf16),
        ] + sums + ends,
        scratch_shapes=[
            pltpu.VMEM((BLOCK + 8, channels), f32), pltpu.VMEM((BLOCK + 8, 2 * STATE), f32),
            pltpu.VMEM((BLOCK, BLOCK), f32), pltpu.VMEM((BLOCK, channels), f32), pltpu.VMEM((BLOCK, channels), f32),
        ],
        compiler_params=params(LIM_SCAN_BACK),
        cost_estimate=little,
        name="scan_back",
    )(*projections, *kept, mixed_grad, *carry, *consts)


def fixed_block(*shape):
    zeros = (0,) * len(shape)
    return pl.BlockSpec(shape, lambda n, *_: zeros)


def call(kernel, places, steps, operands, in_specs, out_specs, out_shape, name, scratch=(), aliases={}):
    return pl.pallas_call(
        kernel,
        grid_spec=pltpu.PrefetchScalarGridSpec(
            num_scalar_prefetch=1, grid=(steps,), in_specs=in_specs, out_specs=out_specs, scratch_shapes=list(scratch)
        ),
        out_shape=out_shape,
        input_output_aliases=aliases,
        compiler_params=params(61),
        cost_estimate=little,
        name=name,
    )(places, *operands)


def lay(places, pieces, result, first=0):
    for i, piece in enumerate(pieces):
        result[pl.ds(pl.multiple_of(places[first + i], 16), piece.shape[0]), :] = piece[...]


TILE = 256


def tile_columns(ref, n, first=0):
    return ref[:, pl.ds(pl.multiple_of(n * TILE + first, LANES), TILE)]


def first_project(weights, tokens, places, channels):
    count = len(weights)
    depth, width = tokens[0].shape[1], weights[0].shape[1]
    rows = tokens[0].shape[0] * len(tokens)

    def kernel(places, *refs):
        pieces, (normed, full, tail_proj) = refs[:-3], refs[-3:]
        lay(places, pieces[:count], full)
        lay(places, pieces[count:], normed, count)
        tail_proj[...] = dot(normed[...], full[:, channels:], ((1,), (0,)))

    return call(
        kernel, places, 1, (*weights, *tokens), [fixed_block(*piece.shape) for piece in (*weights, *tokens)],
        [fixed_block(rows, depth), fixed_block(depth, width), fixed_block(rows, width - channels)],
        [
            jax.ShapeDtypeStruct((rows, depth), bf16), jax.ShapeDtypeStruct((depth, width), bf16),
            jax.ShapeDtypeStruct((rows, width - channels), f32),
        ],
        "first_project",
    )


def input_project(places, normed, first_full, channels):
    rows, depth = normed.shape

    def kernel(places, left, right, result):
        result[...] = dot(left[...], right[...], ((1,), (0,)))

    return call(
        kernel, places, channels // TILE, (normed, first_full),
        [fixed_block(rows, depth), pl.BlockSpec((depth, TILE), lambda n, _: (0, n))],
        pl.BlockSpec((rows, TILE), lambda n, _: (0, n)), jax.ShapeDtypeStruct((rows, channels), f32), "input_project",
    )


def second_project(weights, places, normed, cot, mixed, gain):
    count, halves = len(weights), len(mixed)
    width = weights[0].shape[1]
    rows, depth = normed.shape
    channels = width // 2
    part_rows = mixed[0].shape[0]

    def kernel(places, *refs):
        pieces, (normed_ref, cot_ref, gain_ref), mixed_refs = refs[:count], refs[count : count + 3], refs[count + 3 : -4]
        full, gate_proj, out_grad, sums = refs[-4:]
        n = pl.program_id(0)

        @pl.when(n == 0)
        def _():
            lay(places, pieces, full)
            sums[...] = jnp.zeros(sums.shape, f32)

        gate_proj[...] = dot(normed_ref[...], tile_columns(full, n), ((1,), (0,)))
        out_grad[...] = dot(cot_ref[...], tile_columns(full, n, channels), ((1,), (0,)))
        ones = jnp.ones((8, TILE), f32)
        for i in range(halves):
            at = slice(i * part_rows, (i + 1) * part_rows)
            proj = gate_proj[at, :]
            gated = mixed_refs[i][...] * (proj * sigmoid(proj))
            pulled = out_grad[at, :] * gain_ref[...] * gated
            sums[0:8, at] += dot(ones, gated * gated, ((1,), (1,)), highest)
            sums[8:16, at] += dot(ones, pulled, ((1,), (1,)), highest)

    tile = pl.BlockSpec((rows, TILE), lambda n, _: (0, n))
    return call(
        kernel, places, channels // TILE, (*weights, normed, cot, gain, *mixed),
        [fixed_block(*piece.shape) for piece in (*weights, normed, cot)]
        + [pl.BlockSpec((1, TILE), lambda n, _: (0, n))]
        + [pl.BlockSpec((part_rows, TILE), lambda n, _: (0, n)) for _ in mixed],
        [fixed_block(depth, width), tile, tile, fixed_block(16, rows)],
        [
            jax.ShapeDtypeStruct((depth, width), bf16), jax.ShapeDtypeStruct((rows, channels), f32),
            jax.ShapeDtypeStruct((rows, channels), f32), jax.ShapeDtypeStruct((16, rows), f32),
        ],
        "second_project",
    )


def store_shares(places, product, result, tops, part, columns):
    owners, rows = result.shape[0], result.shape[2] - 16
    for owner in range(owners):
        own = product[owner * rows : (owner + 1) * rows]
        result[places[owner], part, 0:rows, columns] = own
        top = jnp.max(jnp.abs(own), axis=0, keepdims=True)
        result[places[owner], part, rows : rows + 16, columns] = jnp.zeros((16, own.shape[1]), f32)
        tops[places[owner], part, :, columns] = jnp.broadcast_to(top, (8, own.shape[1]))


def gate_step(ring, places, sums, gain, mixed, gate_proj, out_grad, cot_t, normed_t, second_full, inner_total):
    depth = second_full.shape[0]
    rows, channels = gate_proj.shape
    halves, part_rows = len(mixed), mixed[0].shape[0]
    share = cot_t.shape[0] // ring.count

    def kernel(places, *refs):
        sums_ref, gain_ref, proj_ref, grad_ref, cot_ref, normed_ref, weight_ref = refs[:7]
        mixed_refs, (branch, gate_grad, mixed_grad, gain_sum, result, tops, gate_out) = refs[7 : 7 + halves], refs[7 + halves :]
        gain_sum[...] = jnp.zeros(gain_sum.shape, f32)
        scale_row = lax.rsqrt(sums_ref[0:8, :] / inner_total + epsilon)
        pull_row = scale_row * scale_row * scale_row * (sums_ref[8:16, :] / inner_total)
        scales, pulls = scale_row.T, pull_row.T
        for i in range(halves):
            at = slice(i * part_rows, (i + 1) * part_rows)
            proj, rows_mixed, grad = proj_ref[at, :], mixed_refs[i][...], grad_ref[at, :]
            sig = sigmoid(proj)
            act = proj * sig
            gated = rows_mixed * act
            scale = scales[at, 0:1]
            scaled = gated * scale
            gate_out[at, :] = (scaled * gain_ref[...]).astype(bf16)
            gain_sum[0:1, :] += jnp.sum(grad * scaled, axis=0, keepdims=True)
            gated_grad = scale * (grad * gain_ref[...]) - gated * pulls[at, 0:1]
            mixed_grad[at, :] = gated_grad * act
            gate_grad[at, :] = (gated_grad * rows_mixed * (sig * (1.0 + proj * (1.0 - sig)))).astype(bf16)
        everything = slice(0, TILE)
        first = pl.program_id(0) == 0
        for i in range(0, rows, TILE):
            at = slice(i, i + TILE)
            share_out = dot(gate_out[at, :], weight_ref[...], ((1,), (1,)))
            branch[at, :] = share_out + jnp.where(first, 0.0, branch[at, :])
        store_shares(places, dot(cot_ref[...], gate_out[...], ((1,), (0,))), result, tops, 0, everything)
        store_shares(places, dot(normed_ref[...], gate_grad[...], ((1,), (0,))), result, tops, 1, everything)

    tile = pl.BlockSpec((rows, TILE), lambda n, _: (0, n))
    return call(
        kernel, places, channels // TILE, (sums, gain, gate_proj, out_grad, cot_t, normed_t, second_full, *mixed),
        [
            fixed_block(16, rows), pl.BlockSpec((1, TILE), lambda n, _: (0, n)), tile, tile,
            fixed_block(*cot_t.shape), fixed_block(*normed_t.shape),
            pl.BlockSpec((depth, TILE), lambda n, _: (0, channels // TILE + n)),
        ] + [pl.BlockSpec((part_rows, TILE), lambda n, _: (0, n)) for _ in mixed],
        [
            fixed_block(rows, depth), tile, tile, pl.BlockSpec((8, TILE), lambda n, _: (0, n)),
            pl.BlockSpec((ring.count, 2, share + 16, TILE), lambda n, _: (0, 0, 0, n)),
            pl.BlockSpec((ring.count, 2, 8, TILE), lambda n, _: (0, 0, 0, n)),
        ],
        [
            jax.ShapeDtypeStruct((rows, depth), f32), jax.ShapeDtypeStruct((rows, channels), bf16),
            jax.ShapeDtypeStruct((rows, channels), f32), jax.ShapeDtypeStruct((8, channels), f32),
            jax.ShapeDtypeStruct((ring.count, 2, share + 16, channels), f32),
            jax.ShapeDtypeStruct((ring.count, 2, 8, channels), f32),
        ],
        "gate_step", [pltpu.VMEM((rows, TILE), bf16)],
    )


def input_partials(ring, places, normed_t, input_back):
    halves, (part_rows, channels) = len(input_back), input_back[0].shape
    share = normed_t.shape[0] // ring.count

    def kernel(places, left, *refs):
        rights, result, tops = refs[:-2], refs[-2], refs[-1]
        product = dot(left[:, 0:part_rows], rights[0][...], ((1,), (0,)))
        for i in range(1, halves):
            product = product + dot(left[:, i * part_rows : (i + 1) * part_rows], rights[i][...], ((1,), (0,)))
        store_shares(places, product, result, tops, 0, slice(0, TILE))

    def block(rows):
        return pl.BlockSpec((ring.count, 1, rows, TILE), lambda n, _: (0, 0, 0, n))

    return call(
        kernel, places, channels // TILE, (normed_t, *input_back),
        [fixed_block(*normed_t.shape)] + [pl.BlockSpec((part_rows, TILE), lambda n, _: (0, n)) for _ in input_back],
        [block(share + 16), block(8)],
        [jax.ShapeDtypeStruct((ring.count, 1, rows, channels + LANES), f32) for rows in (share + 16, 8)],
        "input_partials",
    )


def tail_partials(places, normed_t, tail, parts, tops):
    def kernel(places, left, right, parts_in, tops_in, result, tops_out):
        product = dot(left[...], right[...], ((1,), (0,)))
        store_shares(places, product, result, tops_out, 0, slice(0, LANES))

    last = parts.shape[3] // LANES - 1
    specs = [pl.BlockSpec((*array.shape[:3], LANES), lambda n, _: (0, 0, 0, last)) for array in (parts, tops)]
    anywhere = pl.BlockSpec(memory_space=pl.ANY)
    return call(
        kernel, places, 1, (normed_t, tail, parts, tops),
        [fixed_block(*normed_t.shape), fixed_block(*tail.shape), anywhere, anywhere], specs,
        [jax.ShapeDtypeStruct(array.shape, f32) for array in (parts, tops)], "tail_partials", aliases={3: 0, 4: 1},
    )


def normed_kernel(halves, places, gate_rows, tail_rows, gate_tile, input_tile, tail_tile, *refs):
    inputs, results, product = refs[:halves], refs[halves:-1], refs[-1]
    part = inputs[0].shape[0]
    for i, input_rows in enumerate(inputs):
        at = slice(i * part, (i + 1) * part)
        total = dot(gate_rows[at, :], gate_tile[...], ((1,), (1,)))
        total = total + dot(tail_rows[at, :], tail_tile[...], ((1,), (1,)))
        product[at, :] = total + dot(input_rows[...], input_tile[...], ((1,), (1,)))
    rows = results[0].shape[0]
    for i, result in enumerate(results):
        result[...] = product[pl.ds(pl.multiple_of(places[i] * rows, 16), rows), :]


def normed_parts(places, gate_grad, input_back, tail, second_full, first_full):
    count = lax.axis_size("tensor")
    tokens, channels = gate_grad.shape
    width, tile = first_full.shape[0], 2 * LANES
    halves = len(input_back)

    def fixed(n, _):
        return (0, 0)

    return pl.pallas_call(
        lambda *refs: normed_kernel(halves, *refs),
        grid_spec=pltpu.PrefetchScalarGridSpec(
            num_scalar_prefetch=1, grid=(width // tile,),
            in_specs=[
                pl.BlockSpec((tokens, channels), fixed), pl.BlockSpec((tokens, LANES), fixed),
                pl.BlockSpec((tile, channels), lambda n, _: (n, 0)), pl.BlockSpec((tile, channels), lambda n, _: (n, 0)),
                pl.BlockSpec((tile, LANES), lambda n, _: (n, channels // LANES)),
            ] + [pl.BlockSpec(half.shape, fixed) for half in input_back],
            out_specs=[pl.BlockSpec((tokens // count, tile), lambda n, _: (0, n))] * count,
            scratch_shapes=[pltpu.VMEM((tokens, tile), f32)],
        ),
        out_shape=[jax.ShapeDtypeStruct((tokens // count, width), f32)] * count,
        compiler_params=params(LIM_NORMED_PARTS),
        cost_estimate=little,
        name="normed_parts",
    )(places, gate_grad, tail, second_full, first_full, first_full, *input_back)


def cycle(count):
    return list(range(0, count, 2)) + list(range(count - 1, 0, -2))


def table(numbers):
    return jnp.stack(numbers).astype(jnp.int32)


class Ring:
    def __init__(self):
        self.count = lax.axis_size("dp")
        order = cycle(self.count)
        self.up = [(order[i], order[(i + 1) % self.count]) for i in range(self.count)]
        self.down = [(b, a) for a, b in self.up]
        me = lax.axis_index("dp")
        self.place = jnp.where(me % 2 == 0, me // 2, self.count - 1 - me // 2)

    def places(self):
        order = cycle(self.count)
        return table([(order.index(i) - self.place + self.count) % self.count for i in range(self.count)])

    def owner(self, offset):
        place = (self.place + offset + self.count) % self.count
        return jnp.where(place < self.count // 2, 2 * place, 2 * (self.count - 1 - place) + 1)


def middle(rows):
    return (rows // 2 + 15) // 16 * 16


class Gather:
    def __init__(self, ring, shard):
        self.ring, self.shard, self.step = ring, shard, 0
        self.held = [(shard, 0, 0)]
        self.last = (shard, shard)

    def hop(self):
        self.step += 1
        half, cut = self.ring.count // 2, middle(self.shard.shape[0])
        up, down = self.last
        offsets = ((-self.step, 0), (self.step, 0))
        if self.step == half:
            up, down = up[:cut], down[cut:]
            offsets = ((half, 0), (half, cut))
        self.last = (lax.ppermute(up, "dp", self.ring.up), lax.ppermute(down, "dp", self.ring.down))
        self.held += [(piece, *offset) for piece, offset in zip(self.last, offsets)]

    def after(self, *marks):
        self.last, marks = fence(self.last, marks)
        self.held[-2:] = [(piece, *old[1:]) for piece, old in zip(self.last, self.held[-2:])]
        return marks if len(marks) > 1 else marks[0]

    def pieces(self):
        return [piece for piece, _, _ in self.held]

    def places(self):
        rows, half = self.shard.shape[0], self.ring.count // 2
        spots = [self.ring.owner(0) * rows]
        for step in range(1, half):
            spots += [self.ring.owner(-step) * rows, self.ring.owner(step) * rows]
        return spots + [self.ring.owner(half) * rows, self.ring.owner(half) * rows + middle(rows)]


def encode(rows, limit):
    power = jnp.ceil(jnp.log2(jnp.maximum(limit, 1e-30)))
    ours = lax.broadcasted_iota(jnp.int32, rows.shape, 1) < rows.shape[1] - 16
    return jnp.where(ours, rows * jnp.exp2(15.0 - power), power).astype(jnp.float16)


def decode(payload):
    power = payload[:, -16:-15].astype(f32)
    return payload.astype(f32) * jnp.exp2(power - 15.0), jnp.exp2(power)


class Scatter:
    def __init__(self, ring, parts, tops):
        self.ring, self.parts, self.tops = ring, parts, tops
        self.step = ring.count // 2
        self.rows = parts.shape[2] - 16
        self.cut = middle(self.rows)
        far = parts[self.step]
        top = tops[self.step, :, 0:1]
        upper = jnp.concatenate([far[:, : self.cut], far[:, -16:]], axis=1)
        self.send = (encode(upper, top), encode(far[:, self.cut :], top))

    def hop(self):
        self.send = fence(*self.send)
        self.got = (lax.ppermute(self.send[0], "dp", self.ring.up), lax.ppermute(self.send[1], "dp", self.ring.down))

    def after(self, *marks):
        self.got, marks = fence(self.got, marks)
        return marks if len(marks) > 1 else marks[0]

    def before(self, *marks):
        self.send, marks = fence(self.send, marks)
        return marks if len(marks) > 1 else marks[0]

    def add(self):
        first = self.step == self.ring.count // 2
        self.got = fence(*self.got)
        (up, up_top), (down, down_top) = (decode(g) for g in self.got)
        if first:
            up = jnp.pad(up, ((0, 0), (0, self.rows - self.cut), (0, 0)))
            down = jnp.pad(down, ((0, 0), (self.cut, 0), (0, 0)))
            up = jnp.where(lax.broadcasted_iota(jnp.int32, up.shape, 1) < self.cut, up, 0.0)
        self.step -= 1
        if self.step == 0:
            return (self.parts[0] + up + down)[:, : self.rows]
        above, below = self.parts[self.step], self.parts[self.ring.count - self.step]
        self.send = (
            encode(above + up, self.tops[self.step, :, 0:1] + up_top),
            encode(below + down, self.tops[self.ring.count - self.step, :, 0:1] + down_top),
        )
        return None


def fence(*arrays):
    flat, tree = jax.tree.flatten(arrays)
    return jax.tree.unflatten(tree, lax.optimization_barrier(flat))


def across(array, bit, axis="tensor"):
    count = lax.axis_size(axis)
    return lax.ppermute(array, axis, [(i, i ^ bit) for i in range(count)])


def group_sum(array, axis, first, count):
    terms = [array] + [across(array, first * other, axis) for other in range(1, count)]
    while len(terms) > 1:
        terms = [terms[i] + terms[i + 1] for i in range(0, len(terms), 2)]
    return terms[0]


def cube_sum(array, axis):
    bit = 1
    while bit < lax.axis_size(axis):
        array = array + across(array, bit, axis)
        bit *= 2
    return array


def shards(
    block_input, cotangent, norm_gain, gate_weight, input_weight, state_weight, step_weight, conv_input,
    conv_input_bias, conv_state, conv_state_bias, step_bias, decay_log, skip_scale, gate_gain, out_weight,
):
    group_count = lax.axis_size("tensor")
    me = lax.axis_index("tensor")
    ring = Ring()
    half = ring.count // 2
    local_rows = block_input.shape[0]
    channels = gate_gain.shape[0]
    heads = step_bias.shape[0]
    inner_total = channels * group_count
    share = 2 * STATE // group_count
    tokens = local_rows * group_count
    blocks = tokens // BLOCK
    fold = LANES // share
    folded = tokens // fold
    rows_dot = ((1,), (0,))
    back_dot = ((1,), (1,))

    state_mine = lax.dynamic_slice_in_dim(state_weight, me * share, share, 1)
    first = Gather(
        ring,
        jnp.concatenate(
            [input_weight, state_mine, jnp.pad(step_weight, ((0, 0), (0, LANES - share - heads)))], axis=1
        ).astype(bf16),
    )
    first.hop()
    row_scale = lax.rsqrt(jnp.mean(block_input * block_input, axis=1, keepdims=True) + epsilon)
    normed = (block_input * row_scale * norm_gain).astype(bf16)
    second_weight = jnp.concatenate([gate_weight, out_weight.T], axis=1).astype(bf16)
    rates = -jnp.exp(decay_log)

    def per_head(vector):
        return jnp.pad(vector, (0, LANES - heads))[None, :]

    skip = jnp.repeat(skip_scale, HEAD_DIM)[None, :]
    head_of = (
        lax.broadcasted_iota(jnp.int32, (channels, LANES), 0) // HEAD_DIM
        == lax.broadcasted_iota(jnp.int32, (channels, LANES), 1)
    ).astype(f32)
    scan_consts = (
        conv_input, conv_input_bias[None, :], conv_state, conv_state_bias[None, :], per_head(step_bias),
        per_head(rates), skip,
    )
    back_consts = (conv_input, conv_state, per_head(step_bias), per_head(rates), skip, head_of)
    carried = jnp.zeros((channels // LANES, LANES, STATE), f32)
    carry = (jnp.zeros((8, channels), f32), jnp.zeros((8, 2 * STATE), f32), carried, jnp.zeros((8, LANES), f32))
    gain = gate_gain[None, :]
    shard_places = first.places()
    token_places = [(me ^ bits) * local_rows for bits in range(4)]
    tables = (table(shard_places + token_places), table(shard_places), ring.places(), table([i ^ me for i in range(4)]))
    normed, scan_consts, back_consts, carried, carry, gain, tables = first.after(
        normed, scan_consts, back_consts, carried, carry, gain, tables
    )
    first_places, second_places, share_places, turn_places = tables
    first.hop()
    far, near = across(normed, 2), across(normed, 1)
    for _ in range(half - 3):
        first.hop()
    far, near, second_weight, cot_low = first.after(far, near, second_weight, cotangent.astype(bf16))
    first.hop()
    second_weight = first.after(second_weight)
    normed_pieces = (normed, near, far, across(far, 1))
    second = Gather(ring, second_weight)
    second.hop()
    normed_all, first_full, tail_proj = first_project(first.pieces(), normed_pieces, first_places, channels)
    step_proj = jnp.pad(tail_proj[:, share : share + heads], ((0, 0), (0, LANES - heads)))
    state_mine = jnp.concatenate([tail_proj[i * folded : (i + 1) * folded, :share] for i in range(fold)], axis=1)
    normed_all, state_mine = fence(normed_all, state_mine)
    far = across(state_mine, 2)
    input_proj, far, cot_low = second.after(input_project(share_places, normed_all, first_full, channels), far, cot_low)
    second.hop()
    cot_all = lax.all_gather(cot_low, "tensor", axis=0, tiled=True)
    same_x, same_core, diagonal = across(state_mine, 1), far, across(far, 1)
    right_core = me % 2 == 1
    near = (jnp.where(right_core, same_x, state_mine), jnp.where(right_core, state_mine, same_x))
    away = (jnp.where(right_core, diagonal, same_core), jnp.where(right_core, same_core, diagonal))
    right_chip = me // 2 == 1
    state_parts = [jnp.where(right_chip, away[i], near[i]) for i in range(2)]
    state_parts += [jnp.where(right_chip, near[i], away[i]) for i in range(2)]
    state_proj = jnp.concatenate(
        [jnp.concatenate([p[:, i * share : (i + 1) * share] for p in state_parts], axis=1) for i in range(fold)], axis=0
    )
    span = 2
    scanned, mixed = [], []
    for start in range(0, blocks, span):
        scanned.append(run_scan(start, span, input_proj, state_proj, step_proj, carry[:2], carried, scan_consts))
        carried = scanned[-1][4]
        mixed.append(scanned[-1][0])
        if second.step < half:
            carried, mixed[-1] = second.after(carried, mixed[-1])
            second.hop()
    while second.step < half:
        second.hop()
    second_full, gate_proj, gate_out_grad, sums = second_project(
        second.pieces(), second_places, normed_all, cot_all, mixed, gain
    )
    sums = (sums + across(sums, 1)) + (across(sums, 2) + across(sums, 3))
    normed_t = normed_all.T
    branch_part, gate_grad, mixed_grad, gain_sum, *pair_parts = gate_step(
        ring, share_places, sums, gain, mixed, gate_proj, gate_out_grad, cot_all.T, normed_t, second_full,
        float(inner_total),
    )
    pair_ring = Scatter(ring, *pair_parts)
    done = []
    for turn in range(blocks // span):
        if turn == 0:
            carry, branch_part = pair_ring.before(carry, branch_part)
            pair_ring.hop()
            branch = lax.psum_scatter(branch_part, "tensor", scatter_dimension=0, tiled=True)
        else:
            carry = pair_ring.after(carry)
            pair_ring.add()
            carry = pair_ring.before(carry)
            pair_ring.hop()
        start = blocks - span * (turn + 1)
        kept = scanned[start // span]
        kept = [kept[1], kept[2], kept[0], kept[3]]
        result = run_scan_back(
            start, span, (input_proj, state_proj, step_proj), kept, 0, mixed_grad, carry, back_consts
        )
        done.insert(0, result)
        carry = tuple(result[6:])
    done = pair_ring.after(done)
    pair_ring.add()
    done = pair_ring.before(done)
    pair_ring.hop()
    input_back, state_back = [d[0] for d in done], [d[1] for d in done]
    step_back = jnp.concatenate([d[2] for d in done], axis=0)
    input_sums, state_sums, step_sums = (sum(d[i] for d in done) for i in range(3, 6))

    packed = jnp.concatenate(
        [
            state_sums[:5].reshape(-1),
            input_sums[:5].reshape(-1),
            gain_sum[0],
            jnp.sum(input_sums[5].reshape(heads, HEAD_DIM), axis=1),
            step_sums[0, :heads],
            step_sums[1, :heads] * rates,
        ]
    )
    packed = jnp.pad(packed, (0, -packed.shape[0] % LANES)).reshape(-1, LANES)

    def state_columns(index):
        return jnp.concatenate([lax.dynamic_slice_in_dim(rows, index * share, share, 1) for rows in state_back], axis=1)

    for_far, for_me = across(state_columns(me ^ 3), 1), across(state_columns(me ^ 1), 1)
    packed, for_far, for_me = fence(packed, for_far, for_me)
    far, input_back = fence(state_columns(me ^ 2) + for_far, input_back)
    from_far = across(far, 2)
    input_parts, from_far, pair_ring.got = fence(
        input_partials(ring, share_places, normed_t, input_back), from_far, pair_ring.got
    )
    pair_ring.add()
    from_far = pair_ring.before(from_far)
    pair_ring.hop()
    state_share = (state_columns(me) + for_me + from_far).astype(bf16)
    state_share = jnp.concatenate([state_share[:, i * share : (i + 1) * share] for i in range(fold)], axis=0)
    tail = jnp.concatenate(
        [state_share, step_back[:, :heads], jnp.zeros((tokens, LANES - share - heads), bf16)], axis=1
    )
    parts = normed_parts(turn_places, gate_grad, input_back, tail, second_full, first_full)
    branch, *parts = pair_ring.after(branch, *parts)
    block_output = block_input + branch
    for_far, for_me = across(parts[3], 1), across(parts[1], 1)
    input_parts = tail_partials(share_places, normed_t, tail, *input_parts)
    input_ring = Scatter(ring, *input_parts)
    for_far, for_me = input_ring.before(for_far, for_me)
    input_ring.hop()
    sent = parts[2] + for_far
    sent = jnp.pad(sent, ((0, 16), (0, 0)))[None]
    from_far = across(encode(sent, jnp.max(jnp.abs(sent), axis=1, keepdims=True)), 2)
    input_sum = input_ring.add()
    pair_sum = pair_ring.add()
    while pair_sum is None:
        pair_ring.hop()
        pair_sum = pair_ring.add()
    while input_sum is None:
        input_ring.hop()
        if input_ring.step == 2:
            from_far = input_ring.after(from_far)
        input_sum = input_ring.add()
    normed_grad = parts[0] + for_me + decode(from_far)[0][0, :local_rows]
    input_sum = input_sum[0]
    tail_sum = input_sum[:, channels:]

    weighted_grad = normed_grad * norm_gain
    norm_gain_part = jnp.sum(normed_grad * block_input * row_scale, axis=0)
    input_grad = (
        cotangent
        + row_scale * weighted_grad
        - block_input * row_scale**3 * jnp.mean(weighted_grad * block_input, axis=1, keepdims=True)
    )
    mine = tail_sum[:, :share]
    other = across(mine, 1)
    pair = jnp.concatenate([jnp.where(right_core, other, mine), jnp.where(right_core, mine, other)], axis=1)
    state_rows = 10 * STATE // LANES
    shared = jnp.concatenate([norm_gain_part.reshape(-1, LANES), packed[:state_rows]], axis=0)
    shared = group_sum(shared, "tensor", 1, group_count)
    shared, pair = fence(shared, pair)
    other = across(pair, 2)
    packed = jnp.concatenate([shared, packed[state_rows:]], axis=0)
    packed, other = fence(group_sum(packed, "dp", 2, half), other)
    packed = group_sum(packed, "dp", 1, 2)
    state_grad = jnp.concatenate([jnp.where(right_chip, other, pair), jnp.where(right_chip, pair, other)], axis=1)
    local = packed[shared.shape[0] :].reshape(-1)
    norm_gain_grad = packed[: shared.shape[0] - state_rows].reshape(-1)
    state_sum = packed[shared.shape[0] - state_rows : shared.shape[0]].reshape(5, 2 * STATE)
    at = 6 * channels
    return (
        block_output,
        input_grad,
        norm_gain_grad,
        pair_sum[1],
        input_sum[:, :channels],
        state_grad,
        tail_sum[:, share : share + heads],
        local[: 4 * channels].reshape(4, channels),
        local[4 * channels : 5 * channels],
        state_sum[:4],
        state_sum[4],
        local[at + heads : at + 2 * heads],
        local[at + 2 * heads : at + 3 * heads],
        local[at : at + heads],
        local[5 * channels : at],
        pair_sum[0].T,
    )


def solution(mesh):
    rows = P(("dp", "tensor"), None)
    both = P("dp", "tensor")
    inner = P("tensor")
    return jax.shard_map(
        shards,
        mesh=mesh,
        in_specs=(
            rows, rows, P(), both, both, P("dp", None), both, P(None, "tensor"), inner, P(), P(), inner, inner,
            inner, inner, P("tensor", "dp"),
        ),
        out_specs=(
            rows, rows, P(), both, both, P("dp", None), both, P(None, "tensor"), inner, P(), P(), inner, inner,
            inner, inner, P("tensor", "dp"),
        ),
        check_vma=False,
    )
```
